32 devices in a mesh: seq: 16 (over z, y, x), head: 2 (over core).
Axes of the slice: x: 2, y: 2, z: 4, core: 2. Of those that a mesh axis runs over, the one named last changes fastest.
Arguments:
- query_raw: bfloat16 [6144, 2048], P('seq', 'head'), may hold values from -6 to 6
- key_raw: bfloat16 [6144, 2048], P('seq', 'head'), may hold values from -6 to 6
- value_raw: bfloat16 [6144, 4096], P('seq', 'head'), may hold values from -6 to 6
- gate_raw: bfloat16 [6144, 4096], P('seq', 'head'), may hold values from -6 to 6
- query_taps: float32 [4, 2048], P(None, 'head'), may hold values from -3 to 3
- key_taps: float32 [4, 2048], P(None, 'head'), may hold values from -3 to 3
- value_taps: float32 [4, 4096], P(None, 'head'), may hold values from -3 to 3
- beta_logit: float32 [6144, 32], P('seq', 'head'), may hold values from -6 to 6
- decay_logit: float32 [6144, 32], P('seq', 'head'), may hold values from -14 to 0
- norm_gain: float32 [128], replicated, may hold values from 0.5 to 1.5
- out_weight: bfloat16 [4096, 2048], P('head'), may hold values from -0.09375 to 0.09375
Outputs:
- mixed: bfloat16 [6144, 2048], P(('seq', 'head'))
The draws below stay inside these ranges and needn't reach their ends.
All inputs are finite; a program needn't handle non-finite values.
Results may differ from the reference program's by a relative error of at most 0.017.
Values may be sent and summed in bfloat16 or wider, within the bound.
No kernel may reach another device: no remote copies, remote signals or barrier semaphores. Data moves between devices by JAX's collectives and lax.ppermute only.
A program may use at most 128 MiB of HBM per device.

```python
import jax
import jax.numpy as jnp
from jax import lax

D = 2048
HK = 16
VALUE_HEADS = 32
DK = 128
DV = 128
BLOCK = 64
TOK_DEV = 384
WINDOW_TOKENS = 6144
N_HEAD = 2


def draw_key_raw(key, part):
    random_subkeys = jax.random.split(key, 2)
    channel_scale = jnp.exp(jax.random.uniform(random_subkeys[0], (HK * DK,), jnp.float32, jnp.log(0.001), 0.0))
    entries = jnp.clip(jax.random.normal(random_subkeys[1], (WINDOW_TOKENS, HK * DK), jnp.float32), -6.0, 6.0)
    return (entries * channel_scale).astype(jnp.bfloat16)


def draw_decay_logit(key, part):
    random_subkeys = jax.random.split(key, 7)
    fast_heads = jax.random.randint(random_subkeys[0], (VALUE_HEADS,), 0, 2) == 0
    slow_rate = jnp.exp(jax.random.uniform(random_subkeys[1], (VALUE_HEADS,), jnp.float32, jnp.log(0.15), jnp.log(0.6))) / WINDOW_TOKENS
    fast_rate = jnp.exp(jax.random.uniform(random_subkeys[2], (VALUE_HEADS,), jnp.float32, jnp.log(1.0 / 50.0), jnp.log(1.0 / 30.0)))
    base_rate = jnp.where(fast_heads, fast_rate, slow_rate)
    shards = WINDOW_TOKENS // TOK_DEV
    shard_factor = jnp.exp(jax.random.uniform(random_subkeys[3], (shards, 1, VALUE_HEADS), jnp.float32, jnp.log(0.5), 0.0))
    roughness = jax.random.uniform(random_subkeys[4], (shards, TOK_DEV, VALUE_HEADS), jnp.float32, 0.5, 1.5)
    decay_rates = (base_rate * shard_factor * roughness).reshape(WINDOW_TOKENS, VALUE_HEADS)
    spike_positions = jax.random.randint(random_subkeys[5], (3, VALUE_HEADS), 0, WINDOW_TOKENS)
    token_positions = jnp.arange(WINDOW_TOKENS, dtype=jnp.int32)
    spike_mask = jnp.any(token_positions[:, None, None] == spike_positions[None, :, :], axis=1)
    spike_rate = jax.random.uniform(random_subkeys[6], (WINDOW_TOKENS, VALUE_HEADS), jnp.float32, 0.22, 0.41)
    decay_rates = jnp.where(spike_mask, spike_rate, decay_rates)
    return jnp.log(jnp.expm1(decay_rates))


def block_scale(own_key, dims, cuts, least, largest):
    def one(position, parts):
        heights = jax.random.uniform(jax.random.fold_in(jax.random.fold_in(own_key, 6), position), (parts,), jnp.float32, least / len(cuts), largest / len(cuts))
        return jnp.repeat(jnp.exp(heights), dims[position] // parts).reshape((-1,) + (1,) * (len(dims) - position - 1))

    level = one(*cuts[0])
    for cut in cuts[1:]:
        level = level * one(*cut)
    return level


def normal_values(key, shape, scale, bound, cuts=(), kind=jnp.bfloat16):
    array = jax.random.normal(key, shape, jnp.float32) * scale
    if len(cuts) > 0:
        array = block_scale(key, shape, cuts, -0.22, 0.18) * array
    return jnp.clip(array, min=-bound, max=bound).astype(kind)


def setup_inputs(seed: int = 0) -> dict:
    keys = jax.random.split(jax.random.key(seed), 12)
    query_raw = normal_values(keys[0], (WINDOW_TOKENS, HK * DK), 1.0, 6.0, ((0, 16), (1, 2)))
    key_raw = draw_key_raw(jax.random.fold_in(keys[11], 71), 0)
    value_raw = normal_values(keys[2], (WINDOW_TOKENS, VALUE_HEADS * DV), 1.0, 6.0, ((0, 16), (1, 2)))
    gate_raw = normal_values(keys[3], (WINDOW_TOKENS, VALUE_HEADS * DV), 1.0, 6.0, ((0, 16), (1, 2)))
    query_taps = normal_values(keys[4], (4, HK * DK), 0.5, 3.0, ((1, 2),), jnp.float32)
    key_taps = normal_values(keys[5], (4, HK * DK), 0.5, 3.0, ((1, 2),), jnp.float32)
    value_taps = normal_values(keys[6], (4, VALUE_HEADS * DV), 0.5, 3.0, ((1, 2),), jnp.float32)
    beta_logit = normal_values(keys[7], (WINDOW_TOKENS, VALUE_HEADS), 1.5, 6.0, ((0, 16), (1, 2)), jnp.float32)
    decay_logit = draw_decay_logit(jax.random.fold_in(keys[11], 71), 0)
    norm_gain = jnp.clip(1.0 + 0.1 * jax.random.normal(keys[9], (DV,), jnp.float32), 0.5, 1.5)
    out_weight = normal_values(keys[10], (VALUE_HEADS * DV, D), (VALUE_HEADS * DV) ** -0.5, 0.09375, ((0, 2),))
    return {"query_raw": query_raw, "key_raw": key_raw, "value_raw": value_raw, "gate_raw": gate_raw, "query_taps": query_taps, "key_taps": key_taps, "value_taps": value_taps, "beta_logit": beta_logit, "decay_logit": decay_logit, "norm_gain": norm_gain, "out_weight": out_weight}


PRECISE = lax.Precision.HIGHEST
EPSILON = 1e-06

def conv_silu(raw_rows, before, weight):
    extended = jnp.concatenate([before, raw_rows], 0).astype(jnp.float32)
    length = raw_rows.shape[0]
    summed = weight[0] * extended[0:length]
    for offset in range(1, 4):
        summed = summed + weight[offset] * extended[offset:offset + length]
    return jax.nn.silu(summed)

def prepare(query_conv, key_conv, value_conv, beta_logit, decay_logit):
    length = query_conv.shape[0]
    head_keys = key_conv.shape[1] // DK
    head_values = value_conv.shape[1] // DV
    repeat_by = head_values // head_keys
    blocks = length // BLOCK
    key_three = key_conv.reshape(length, head_keys, DK)
    key_three = key_three * lax.rsqrt(lax.optimization_barrier(jnp.sum(key_three * key_three, -1, keepdims=True)) + EPSILON)
    query_three = query_conv.reshape(length, head_keys, DK)

    def arrange(array_in):
        moved = jnp.moveaxis(array_in, 1, 0)
        return moved.reshape((moved.shape[0], blocks, BLOCK) + moved.shape[2:])
    queries = arrange(jnp.repeat(query_three, repeat_by, axis=1))
    key_rows = arrange(jnp.repeat(key_three, repeat_by, axis=1))
    value_rows = arrange(value_conv.reshape(length, head_values, DV))
    decays = arrange(-jax.nn.softplus(decay_logit))
    beta_rows = arrange(jax.nn.sigmoid(beta_logit))
    return (queries, key_rows, value_rows, decays, beta_rows)

def stack_mul(left, right):
    return jnp.einsum('bkl,blv->bkv', left, right, precision=PRECISE)

def block_parts(queries, key_rows, value_rows, decays, beta_rows):
    block_len = decays.shape[-1]
    log_fade = jnp.cumsum(decays, axis=-1)
    row_ids = lax.broadcasted_iota(jnp.int32, (block_len, block_len), 0)
    col_ids = lax.broadcasted_iota(jnp.int32, (block_len, block_len), 1)
    gap_log = log_fade[..., :, None] - log_fade[..., None, :]
    strict = row_ids > col_ids
    within = row_ids >= col_ids
    decay_low = jnp.where(strict, jnp.exp(jnp.where(strict, gap_log, 0.0)), 0.0)
    decay_on = jnp.where(within, jnp.exp(jnp.where(within, gap_log, 0.0)), 0.0)
    key_inner = jnp.einsum('bik,bjk->bij', key_rows, key_rows, precision=PRECISE)
    system = jnp.eye(block_len, dtype=jnp.float32) + beta_rows[..., :, None] * decay_low * key_inner
    rhs_both = jnp.concatenate([beta_rows[..., None] * value_rows, (beta_rows * jnp.exp(log_fade))[..., None] * key_rows], -1)
    solved = lax.linalg.triangular_solve(system, rhs_both, left_side=True, lower=True, unit_diagonal=True)
    value_dim = value_rows.shape[-1]
    updates = solved[..., :value_dim]
    wide = solved[..., value_dim:]
    scores = decay_on * jnp.einsum('bik,bjk->bij', queries, key_rows, precision=PRECISE)
    tail_fade = jnp.exp(log_fade[..., -1:] - log_fade)
    faded_keys = key_rows * tail_fade[..., None]
    last_fade = jnp.exp(log_fade[..., -1])
    identity = jnp.eye(key_rows.shape[-1], dtype=jnp.float32)
    transit = last_fade[..., None, None] * identity - jnp.einsum('bck,bcl->bkl', faded_keys, wide, precision=PRECISE)
    inject = jnp.einsum('bck,bcv->bkv', faded_keys, updates, precision=PRECISE)
    return (updates, wide, scores, log_fade, transit, inject)

def block_out(queries, scores, log_fade, updates, wide, state_now):
    fresh = updates - jnp.einsum('bck,bkv->bcv', wide, state_now, precision=PRECISE)
    carried = jnp.einsum('bck,bkv->bcv', queries, state_now, precision=PRECISE)
    return jnp.exp(log_fade)[..., None] * carried + jnp.einsum('bij,bjv->biv', scores, fresh, precision=PRECISE)

def gated_norm(outputs, gate_raw, norm_gain):
    gate_three = gate_raw.reshape(outputs.shape).astype(jnp.float32)
    scale_rows = lax.rsqrt(lax.optimization_barrier(jnp.mean(outputs * outputs, -1, keepdims=True)) + EPSILON)
    normed = (outputs * scale_rows * norm_gain * jax.nn.silu(gate_three)).astype(jnp.bfloat16)
    return normed.reshape(outputs.shape[0], -1)

def reference(query_raw, key_raw, value_raw, gate_raw, query_taps, key_taps, value_taps, beta_logit, decay_logit, norm_gain, out_weight):
    query_conv = conv_silu(query_raw, jnp.zeros((3, query_raw.shape[1]), jnp.bfloat16), query_taps)
    key_conv = conv_silu(key_raw, jnp.zeros((3, key_raw.shape[1]), jnp.bfloat16), key_taps)
    value_conv = conv_silu(value_raw, jnp.zeros((3, value_raw.shape[1]), jnp.bfloat16), value_taps)
    prepared = prepare(query_conv, key_conv, value_conv, beta_logit, decay_logit)
    moved = tuple((jnp.moveaxis(array_in, 1, 0) for array_in in prepared))

    def block_step(state_now, pieces):
        updates, wide, scores, log_fade, transit, inject = block_parts(pieces[0], pieces[1], pieces[2], pieces[3], pieces[4])
        outputs = block_out(pieces[0], scores, log_fade, updates, wide, state_now)
        return (stack_mul(transit, state_now) + inject, outputs)
    initial = jnp.zeros((VALUE_HEADS, DK, DV), jnp.float32)
    _, outputs = lax.scan(block_step, initial, moved)
    core = jnp.moveaxis(outputs, 0, 1).reshape(VALUE_HEADS, -1, DV)
    core = jnp.moveaxis(core, 0, 1)
    normed = gated_norm(core, gate_raw, norm_gain)
    group_width = VALUE_HEADS * DV // N_HEAD
    summed = jnp.zeros((normed.shape[0], out_weight.shape[1]), jnp.float32)
    for part_index in range(N_HEAD):
        lower_col = part_index * group_width
        partial_value = jnp.dot(normed[:, lower_col:lower_col + group_width].astype(jnp.float32), out_weight[lower_col:lower_col + group_width].astype(jnp.float32), preferred_element_type=jnp.float32)
        summed = summed + lax.optimization_barrier(partial_value.astype(jnp.bfloat16)).astype(jnp.float32)
    return summed.astype(jnp.bfloat16)
```

```python
import functools

import jax
import jax.numpy as jnp
from jax import lax
from jax.experimental import pallas as pl
from jax.experimental.pallas import tpu as pltpu
from jax.sharding import PartitionSpec as P

DK = 128
DV = 128
CHUNK = 128
EPSILON = 1e-06
F32 = jnp.float32
BF16 = jnp.bfloat16


def mul(left, right):
    return jnp.dot(left.astype(BF16), right.astype(BF16), preferred_element_type=F32)


def silu(x):
    return x * (0.5 + 0.5 * jnp.tanh(0.5 * x))


def conv_silu(raw_ref, before_ref, taps_ref, padded):
    length, width = raw_ref.shape
    padded[5:8, :width] = before_ref[...].astype(F32)
    padded[8 : 8 + length, :width] = raw_ref[...].astype(F32)
    summed = taps_ref[0:1, :] * padded[5 : 5 + length, :width]
    for offset in range(1, 4):
        summed = summed + taps_ref[offset : offset + 1, :] * padded[5 + offset : 5 + offset + length, :width]
    return silu(summed)


def delta_kernel(
    query_ref, key_ref, value_ref, query_before, key_before, value_before,
    query_taps, key_taps, value_taps, beta_ref, decay_ref,
    state_ref, parts_ref, padded,
):
    length = query_ref.shape[0]
    chunks = length // CHUNK
    heads = value_ref.shape[1] // DV
    packs = [(head, chunk) for head in range(heads) for chunk in range(chunks)]

    query = conv_silu(query_ref, query_before, query_taps, padded)
    key = conv_silu(key_ref, key_before, key_taps, padded)
    key = key * lax.rsqrt(jnp.sum(key * key, -1, keepdims=True) + EPSILON)
    value = conv_silu(value_ref, value_before, value_taps, padded)

    rows = lax.broadcasted_iota(jnp.int32, (CHUNK, CHUNK), 0)
    cols = lax.broadcasted_iota(jnp.int32, (CHUNK, CHUNK), 1)
    within = rows >= cols
    strict = rows > cols
    differ = rows ^ cols

    def stacked(ref):
        return jnp.concatenate(
            [ref[0, head : head + 1, chunk * CHUNK : (chunk + 1) * CHUNK] for head, chunk in packs], 0
        )

    logit = stacked(decay_ref)
    decay = -(jnp.maximum(logit, 0.0) + jnp.log(1.0 + jnp.exp(-jnp.abs(logit))))
    fade = jnp.dot(
        decay, (rows <= cols).astype(F32), precision=lax.Precision.HIGHEST, preferred_element_type=F32
    )
    beta = 0.5 + 0.5 * jnp.tanh(0.5 * stacked(beta_ref))
    grown = jnp.exp(fade)
    tail = jnp.exp(fade[:, CHUNK - 1 : CHUNK] - fade)
    count = len(packs)
    columns = jnp.concatenate(
        [fade, beta, grown, beta * grown, jnp.zeros((CHUNK - 4 * count, CHUNK), F32)], 0
    ).T

    def column(kind, pack):
        at = kind * count + pack
        return columns[:, at : at + 1]

    key_rows, key_cols, inner = [], [], []
    for chunk in range(chunks):
        part = slice(chunk * CHUNK, (chunk + 1) * CHUNK)
        key_rows.append(key[part])
        key_cols.append(key[part].T)
        inner.append(mul(jnp.concatenate([key[part], query[part]], 0), key_cols[-1]))

    lower, scores, inverse = [], [], []
    for pack, (head, chunk) in enumerate(packs):
        gap = column(0, pack) - fade[pack : pack + 1, :]
        ratio = jnp.exp(jnp.where(within, gap, -1e30))
        lower.append(jnp.where(strict, column(1, pack) * ratio * inner[chunk][:CHUNK], 0.0))
        scores.append((ratio * inner[chunk][CHUNK:]).astype(BF16))
        inverse.append(jnp.where(rows == cols, 1.0, jnp.where(differ == 1, -lower[-1], 0.0)))

    size = 2
    while size < CHUNK:
        band = (differ >= size) & (differ < 2 * size)
        inner_part = [
            mul(jnp.where(band, lower[pack], 0.0), inverse[pack]) for pack in range(count)
        ]
        inverse = [inverse[pack] - mul(inverse[pack], inner_part[pack]) for pack in range(count)]
        size *= 2

    solved = []
    for pack, (head, chunk) in enumerate(packs):
        part = slice(chunk * CHUNK, (chunk + 1) * CHUNK)
        right = jnp.concatenate(
            [
                column(1, pack) * value[part, head * DV : (head + 1) * DV],
                column(3, pack) * key_rows[chunk],
            ],
            1,
        )
        solved.append(mul(inverse[pack], right))

    identity = jnp.where(rows == cols, 1.0, 0.0)
    state = [jnp.concatenate([jnp.zeros((DK, DV), F32), identity], 1)] * heads
    for chunk in range(chunks):
        part = slice(chunk * CHUNK, (chunk + 1) * CHUNK)
        for head in range(heads):
            pack = head * chunks + chunk
            updates, wide = solved[pack][:, :DV], solved[pack][:, DV:]
            if chunk == 0:
                fresh = jnp.concatenate([updates, -wide], 1)
                carried = jnp.concatenate([jnp.zeros((CHUNK, DV), F32), query[part]], 1)
            else:
                both = mul(jnp.concatenate([wide, query[part]], 0), state[head])
                fresh = jnp.concatenate([updates, jnp.zeros((CHUNK, DK), F32)], 1) - both[:CHUNK]
                carried = both[CHUNK:]
            fresh = fresh.astype(BF16)
            outputs = column(2, pack) * carried + mul(scores[pack], fresh)
            parts_ref[head, part, :] = outputs.astype(parts_ref.dtype)
            state[head] = grown[pack : pack + 1, CHUNK - 1 : CHUNK] * state[head] + mul(
                key_cols[chunk] * tail[pack : pack + 1, :], fresh
            )
    for head in range(heads):
        state_ref[head] = state[head].astype(state_ref.dtype)


def delta_parts(raws, before, taps, beta_logit, decay_logit):
    length = raws[0].shape[0]
    key_heads = raws[0].shape[1] // DK
    value_heads = raws[2].shape[1] // DV
    repeat_by = value_heads // key_heads
    wide = repeat_by * DV

    def columns_of(rows, width):
        return pl.BlockSpec((rows, width), lambda step: (0, step))

    def logits(array):
        return array.T.reshape(key_heads, repeat_by, length)

    logit_spec = pl.BlockSpec((1, repeat_by, length), lambda step: (step, 0, 0))
    return pl.pallas_call(
        delta_kernel,
        grid=(key_heads,),
        in_specs=[
            columns_of(length, DK), columns_of(length, DK), columns_of(length, wide),
            columns_of(3, DK), columns_of(3, DK), columns_of(3, wide),
            columns_of(4, DK), columns_of(4, DK), columns_of(4, wide),
            logit_spec, logit_spec,
        ],
        out_specs=[
            pl.BlockSpec((repeat_by, DK, DV + DK), lambda step: (step, 0, 0)),
            pl.BlockSpec((repeat_by, length, DV + DK), lambda step: (step, 0, 0)),
        ],
        out_shape=[
            jax.ShapeDtypeStruct((value_heads, DK, DV + DK), BF16),
            jax.ShapeDtypeStruct((value_heads, length, DV + DK), BF16),
        ],
        scratch_shapes=[pltpu.VMEM((8 + length, wide), F32)],
        compiler_params=pltpu.CompilerParams(vmem_limit_bytes=48 * 1024 * 1024),
        cost_estimate=pl.CostEstimate(
            flops=2 * 30 * 128 * length * 128 * value_heads,
            bytes_accessed=12 * length * 128 * value_heads,
            transcendentals=0,
        ),
        name="delta_parts",
    )(*raws, *before, *taps, logits(beta_logit), logits(decay_logit))


def chain_kernel(pairs_ref, starts_ref):
    count, heads = pairs_ref.shape[:2]
    state = [jnp.zeros((DK, DV), F32)] * heads
    for hop in range(count):
        for head in range(heads):
            starts_ref[hop, head] = state[head].astype(starts_ref.dtype)
            if hop < count - 1:
                state[head] = pairs_ref[hop, head, :, :DV].astype(F32) + mul(
                    pairs_ref[hop, head, :, DV:], state[head]
                )


def chain(pairs):
    count, heads = pairs.shape[:2]
    return pl.pallas_call(
        chain_kernel,
        out_shape=jax.ShapeDtypeStruct((count, heads, DK, DV), BF16),
        compiler_params=pltpu.CompilerParams(vmem_limit_bytes=48 * 1024 * 1024),
        name="chain",
    )(pairs)


def passed_along(value, axis, by):
    count = lax.axis_size(axis)
    pairs = [(i, i + by) for i in range(count) if 0 <= i + by < count]
    return lax.ppermute(value, axis, pairs)


def starts_by_doubling(pairs, axis):
    count = lax.axis_size(axis)
    place = lax.axis_index(axis)
    running = pairs.astype(F32)
    by = 1
    while by < count:
        earlier = passed_along(running.astype(BF16), axis, by)
        product = jnp.einsum(
            "bkl,blv->bkv", running[..., DV:].astype(BF16), earlier, preferred_element_type=F32
        )
        joined = product + jnp.pad(running[..., :DV], ((0, 0), (0, 0), (0, DK)))
        running = jnp.where(place >= by, joined, running)
        by *= 2
    return passed_along(running[..., :DV].astype(BF16), axis, 1)


def starts_of(pairs, axis):
    count = lax.axis_size(axis)
    heads = pairs.shape[0]
    if heads % count:
        return starts_by_doubling(pairs, axis)
    by_head = lax.all_to_all(pairs, axis, 0, 0, tiled=True)
    starts = chain(by_head.reshape((count, heads // count) + pairs.shape[1:]))
    return lax.all_to_all(starts.reshape((heads, DK, DV)), axis, 0, 0, tiled=True)


def project_kernel(parts_ref, starts_ref, gate_ref, gain_ref, weight_ref, out_ref, normed):
    heads = parts_ref.shape[0]

    @pl.when(pl.program_id(0) == 0)
    def _():
        for head in range(heads):
            part = slice(head * DV, (head + 1) * DV)
            core = parts_ref[head, :, :DV].astype(F32) + mul(
                parts_ref[head, :, DV:], starts_ref[head]
            )
            scale = lax.rsqrt(jnp.mean(core * core, -1, keepdims=True) + EPSILON)
            gate = silu(gate_ref[:, part].astype(F32))
            normed[:, part] = (core * scale * gain_ref[...] * gate).astype(BF16)

    out_ref[...] = jnp.dot(
        normed[...], weight_ref[...], preferred_element_type=F32
    ).astype(out_ref.dtype)


def project(parts, starts, gate_raw, norm_gain, out_weight):
    heads, length = parts.shape[:2]
    depth, width = out_weight.shape
    block = min(512, width)
    whole = lambda *shape: pl.BlockSpec(shape, lambda step: (0,) * len(shape))
    return pl.pallas_call(
        project_kernel,
        grid=(width // block,),
        in_specs=[
            whole(*parts.shape), whole(*starts.shape), whole(*gate_raw.shape), whole(1, DV),
            pl.BlockSpec((depth, block), lambda step: (0, step)),
        ],
        out_specs=pl.BlockSpec((length, block), lambda step: (0, step)),
        out_shape=jax.ShapeDtypeStruct((length, width), BF16),
        scratch_shapes=[pltpu.VMEM((length, depth), BF16)],
        compiler_params=pltpu.CompilerParams(vmem_limit_bytes=48 * 1024 * 1024),
        name="project",
    )(parts, starts, gate_raw, norm_gain.reshape(1, DV), out_weight)


def summed_over(partial, axis):
    if lax.axis_size(axis) != 2:
        return lax.psum_scatter(partial, axis, scatter_dimension=0, tiled=True)
    half = partial.shape[0] // 2
    here = lax.axis_index(axis)
    away = lax.dynamic_slice_in_dim(partial, (1 - here) * half, half, 0)
    own = lax.dynamic_slice_in_dim(partial, here * half, half, 0)
    other = lax.ppermute(away, axis, [(0, 1), (1, 0)])
    return (own.astype(F32) + other.astype(F32)).astype(BF16)


def shards(
    query_raw, key_raw, value_raw, gate_raw, query_taps, key_taps, value_taps,
    beta_logit, decay_logit, norm_gain, out_weight,
):
    raws = (query_raw, key_raw, value_raw)
    tails = jnp.concatenate([raw[-3:] for raw in raws], 1)
    before = passed_along(tails, "seq", 1)
    at = query_raw.shape[1]
    before = (before[:, :at], before[:, at : 2 * at], before[:, 2 * at :])
    pairs, parts = delta_parts(
        raws, before, (query_taps, key_taps, value_taps), beta_logit, decay_logit
    )
    starts = starts_of(pairs, "seq")
    partial = project(parts, starts, gate_raw, norm_gain, out_weight)
    return summed_over(partial, "head")


def solution(mesh):
    placed = (
        P("seq", "head"), P("seq", "head"), P("seq", "head"), P("seq", "head"),
        P(None, "head"), P(None, "head"), P(None, "head"),
        P("seq", "head"), P("seq", "head"), P(), P("head", None),
    )
    return jax.shard_map(
        shards, mesh=mesh, in_specs=placed, out_specs=P(("seq", "head"), None), check_vma=False
    )
```

```python
import math

import jax
import jax.numpy as jnp
from jax import lax
from jax.experimental import pallas as pl
from jax.experimental.pallas import tpu as pltpu
from jax.sharding import PartitionSpec as P

DK = 128
DV = 128
CHUNK = 128
GROUP = 8
EPSILON = 1e-06
VMEM_BYTES = 60 * 1024 * 1024
F32 = jnp.float32
BF16 = jnp.bfloat16


def mul(left, right):
    return jnp.dot(left.astype(BF16), right.astype(BF16), preferred_element_type=F32)


def sigmoid(x):
    return 0.5 + 0.5 * jnp.tanh(0.5 * x)


def conv_silu(raw_ref, before_ref, taps_ref, padded):
    length, width = raw_ref.shape
    padded[5:8, :width] = before_ref[...].astype(F32)
    padded[8 : 8 + length, :width] = raw_ref[...].astype(F32)
    summed = taps_ref[0:1, :] * padded[5 : 5 + length, :width]
    for offset in range(1, 4):
        summed = summed + taps_ref[offset : offset + 1, :] * padded[5 + offset : 5 + offset + length, :width]
    return summed * sigmoid(summed)


def chunk_rows(ref, heads, chunks):
    held = ref.shape[0]
    first = (pl.program_id(0) * heads) % held
    rows = ref[:heads, :]
    for at in range(heads, held, heads):
        rows = jnp.where(first == at, ref[at : at + heads, :], rows)
    return jnp.concatenate([rows[:, c * CHUNK : (c + 1) * CHUNK] for c in range(chunks)], 0)


def log_fades(logit, upper):
    decay = -(jnp.maximum(logit, 0.0) + jnp.log(1.0 + jnp.exp(-jnp.abs(logit))))
    return jnp.dot(decay, upper, precision=lax.Precision.HIGHEST, preferred_element_type=F32)


def as_columns(blocks):
    rows = sum(block.shape[0] for block in blocks)
    return jnp.concatenate(list(blocks) + [jnp.zeros((CHUNK - rows, CHUNK), F32)], 0).T


def states_kernel(
    key_ref, value_ref, key_before, value_before, key_taps, value_taps, beta_ref, decay_ref,
    pairs_ref, fresh_ref, starts_ref, unit_ref, padded,
):
    length, width = key_ref.shape
    chunks = length // CHUNK
    key_heads = width // DK
    heads = value_ref.shape[1] // DV
    repeat_by = heads // key_heads
    packs = [(chunk, head) for chunk in range(chunks) for head in range(heads)]
    count = len(packs)

    rows = lax.broadcasted_iota(jnp.int32, (CHUNK, CHUNK), 0)
    cols = lax.broadcasted_iota(jnp.int32, (CHUNK, CHUNK), 1)
    within = rows >= cols
    strict = rows > cols
    differ = rows ^ cols
    identity = jnp.where(rows == cols, 1.0, 0.0)

    fade = log_fades(chunk_rows(decay_ref, heads, chunks), (rows <= cols).astype(F32))
    beta = sigmoid(chunk_rows(beta_ref, heads, chunks))
    last = jnp.exp(fade[:, CHUNK - 1 : CHUNK])
    tail = jnp.exp(fade[:, CHUNK - 1 : CHUNK] - fade)
    columns = as_columns((fade, beta, beta * jnp.exp(fade)))

    def column(kind, pack):
        at = kind * count + pack
        return columns[:, at : at + 1]

    def part(chunk):
        return slice(chunk * CHUNK, (chunk + 1) * CHUNK)

    key_conv = conv_silu(key_ref, key_before, key_taps, padded)
    key, key_cols, inner = {}, {}, {}
    for j in range(key_heads):
        own = key_conv[:, j * DK : (j + 1) * DK]
        unit = own * lax.rsqrt(jnp.sum(own * own, -1, keepdims=True) + EPSILON)
        unit_ref[:, j * DK : (j + 1) * DK] = unit.astype(BF16)
        for chunk in range(chunks):
            key[chunk, j] = unit[part(chunk)]
            key_cols[chunk, j] = key[chunk, j].T
            inner[chunk, j] = mul(key[chunk, j], key_cols[chunk, j])

    lower, inverse = [], []
    for pack, (chunk, head) in enumerate(packs):
        gap = column(0, pack) - fade[pack : pack + 1, :]
        ratio = jnp.exp(jnp.where(strict, gap, -1e30))
        low = column(1, pack) * ratio * inner[chunk, head // repeat_by]
        inverse.append(identity - jnp.where(differ == 1, low, 0.0))
        lower.append(low.astype(BF16))

    size = 2
    while size < CHUNK:
        band = jnp.where((differ >= size) & (differ < 4 * size), 1.0, 0.0).astype(BF16)
        inverse16 = [one.astype(BF16) for one in inverse]
        step = [mul(inverse16[p], lower[p] * band).astype(BF16) for p in range(count)]
        both = [mul(step[p], jnp.concatenate([step[p], inverse16[p]], 1)) for p in range(count)]
        inverse = [inverse[p] - both[p][:, CHUNK:] for p in range(count)]
        inverse = [inverse[p] + mul(both[p][:, :CHUNK], inverse[p]) for p in range(count)]
        size *= 4

    value = conv_silu(value_ref, value_before, value_taps, padded)
    solved = []
    for pack, (chunk, head) in enumerate(packs):
        right = jnp.concatenate(
            [
                column(1, pack) * value[part(chunk), head * DV : (head + 1) * DV],
                column(2, pack) * key[chunk, head // repeat_by],
            ],
            1,
        )
        solved.append(mul(inverse[pack], right))

    state = [None] * heads
    for chunk in range(chunks):
        for head in range(heads):
            pack = chunk * heads + head
            updates, wide = solved[pack][:, :DV], solved[pack][:, DV:]
            if chunk == 0:
                fresh = jnp.concatenate([updates, -wide], 1).astype(BF16)
                faded = jnp.concatenate(
                    [jnp.zeros((DK, DV), F32), last[pack : pack + 1, :] * identity], 1
                )
            else:
                start = state[head].astype(BF16)
                starts_ref[head, chunk - 1] = start
                fresh = (
                    jnp.concatenate([updates, jnp.zeros((CHUNK, DK), F32)], 1) - mul(wide, start)
                ).astype(BF16)
                faded = last[pack : pack + 1, :] * state[head]
            fresh_ref[head, part(chunk), :] = fresh
            state[head] = faded + mul(
                key_cols[chunk, head // repeat_by] * tail[pack : pack + 1, :], fresh
            )
    for head in range(heads):
        pairs_ref[head] = state[head].astype(BF16)


def local_kernel(
    query_ref, query_before, query_taps, unit_ref, decay_ref, fresh_ref, starts_ref, gate_ref, gain_ref,
    parts_ref, gated_ref, padded,
):
    length, width = query_ref.shape
    chunks = length // CHUNK
    key_heads = width // DK
    heads = fresh_ref.shape[0]
    repeat_by = heads // key_heads

    rows = lax.broadcasted_iota(jnp.int32, (CHUNK, CHUNK), 0)
    cols = lax.broadcasted_iota(jnp.int32, (CHUNK, CHUNK), 1)
    within = rows >= cols
    fade = log_fades(chunk_rows(decay_ref, heads, chunks), (rows <= cols).astype(F32))
    columns = as_columns((fade, jnp.exp(fade)))
    query = conv_silu(query_ref, query_before, query_taps, padded).astype(BF16)
    for head in range(heads):
        own = slice(head * DV, (head + 1) * DV)
        gate = gate_ref[:, own].astype(F32)
        gated_ref[:, own] = (gate * sigmoid(gate) * gain_ref[...]).astype(BF16)
    for chunk in range(chunks):
        part = slice(chunk * CHUNK, (chunk + 1) * CHUNK)
        for j in range(key_heads):
            own = slice(j * DK, (j + 1) * DK)
            inner = lax.dot_general(
                query[part, own], unit_ref[part, own], (((1,), (1,)), ((), ())), preferred_element_type=F32
            )
            for head in range(j * repeat_by, (j + 1) * repeat_by):
                pack = chunk * heads + head
                gap = columns[:, pack : pack + 1] - fade[pack : pack + 1, :]
                scores = inner * jnp.exp(jnp.where(within, gap, -1e30))
                grown = columns[:, chunks * heads + pack : chunks * heads + pack + 1]
                if chunk == 0:
                    carried = jnp.concatenate(
                        [jnp.zeros((CHUNK, DV), F32), grown * query[part, own].astype(F32)], 1
                    )
                else:
                    carried = grown * mul(query[part, own], starts_ref[head, chunk - 1])
                parts_ref[head, part, :] = (carried + mul(scores, fresh_ref[head, part, :])).astype(BF16)


def columns_of(rows, width, first=0):
    return pl.BlockSpec((rows, width), lambda step: (0, step + first))


def whole_of(array):
    return pl.BlockSpec(array.shape, lambda step: (0,) * array.ndim)


def local_steps(raws, before, taps, beta_logit, decay_logit, gate_raw, norm_gain):
    length = raws[0].shape[0]
    key_heads = raws[0].shape[1] // DK
    value_heads = raws[2].shape[1] // DV
    repeat_by = value_heads // key_heads
    each = 2 if key_heads % 2 == 0 else 1
    steps = key_heads // each
    heads = each * repeat_by
    narrow, wide = each * DK, heads * DV
    chunks = length // CHUNK

    def of_heads(*shape):
        return pl.BlockSpec((heads,) + shape, lambda step: (step,) + (0,) * len(shape))

    logits = (beta_logit.T, decay_logit.T)
    held = math.gcd(8, value_heads)
    logits_of = pl.BlockSpec((held, length), lambda step: (step * heads // held, 0))
    params = pltpu.CompilerParams(vmem_limit_bytes=VMEM_BYTES)
    pairs, fresh, starts, unit = pl.pallas_call(
        states_kernel,
        grid=(steps,),
        in_specs=[
            columns_of(length, narrow), columns_of(length, wide),
            columns_of(3, narrow, (repeat_by + 1) * steps), columns_of(3, wide),
            columns_of(4, narrow), columns_of(4, wide),
            logits_of, logits_of,
        ],
        out_specs=[
            of_heads(DK, DV + DK), of_heads(length, DV + DK), of_heads(chunks - 1, DK, DV + DK),
            columns_of(length, narrow),
        ],
        out_shape=[
            jax.ShapeDtypeStruct((value_heads, DK, DV + DK), BF16),
            jax.ShapeDtypeStruct((value_heads, length, DV + DK), BF16),
            jax.ShapeDtypeStruct((value_heads, chunks - 1, DK, DV + DK), BF16),
            jax.ShapeDtypeStruct(raws[1].shape, BF16),
        ],
        scratch_shapes=[pltpu.VMEM((8 + length, wide), F32)],
        compiler_params=params,
        cost_estimate=pl.CostEstimate(
            flops=40 * CHUNK * length * DV * value_heads,
            bytes_accessed=12 * length * DV * value_heads,
            transcendentals=0,
        ),
        name="states",
    )(raws[1], raws[2], before, before, taps[1], taps[2], *logits)
    gain = norm_gain.reshape(1, DV)

    def local():
        return pl.pallas_call(
            local_kernel,
            grid=(steps,),
            in_specs=[
                columns_of(length, narrow), columns_of(3, narrow, repeat_by * steps), columns_of(4, narrow),
                columns_of(length, narrow), logits_of,
                of_heads(length, DV + DK), of_heads(chunks - 1, DK, DV + DK),
                columns_of(length, wide), whole_of(gain),
            ],
            out_specs=[of_heads(length, DV + DK), columns_of(length, wide)],
            out_shape=[
                jax.ShapeDtypeStruct((value_heads, length, DV + DK), BF16),
                jax.ShapeDtypeStruct(gate_raw.shape, BF16),
            ],
            scratch_shapes=[pltpu.VMEM((8 + length, narrow), F32)],
            compiler_params=params,
            cost_estimate=pl.CostEstimate(
                flops=12 * CHUNK * length * DV * value_heads,
                bytes_accessed=16 * length * DV * value_heads,
                transcendentals=0,
            ),
            name="local",
        )(raws[0], before, taps[0], unit, logits[1], fresh, starts, gate_raw, gain)

    return pairs, local


def prefix_kernel(pairs_ref, prefix_ref, total_ref):
    count, heads = pairs_ref.shape[:2]
    running = [None] * heads
    for hop in range(count):
        for head in range(heads):
            now = pairs_ref[hop, head]
            if hop == 0:
                rows = lax.broadcasted_iota(jnp.int32, (DK, DV + DK), 0)
                cols = lax.broadcasted_iota(jnp.int32, (DK, DV + DK), 1)
                prefix_ref[hop, head] = jnp.where(cols == rows + DV, 1.0, 0.0).astype(BF16)
                running[head] = now.astype(F32)
            else:
                before = running[head].astype(BF16)
                prefix_ref[hop, head] = before
                own = jnp.concatenate([now[:, :DV].astype(F32), jnp.zeros((DK, DK), F32)], 1)
                running[head] = own + mul(now[:, DV:], before)
    for head in range(heads):
        total_ref[head] = running[head].astype(BF16)


def apply_kernel(prefix_ref, start_ref, starts_ref):
    count, heads = prefix_ref.shape[:2]
    for hop in range(count):
        for head in range(heads):
            starts_ref[hop, head] = (
                prefix_ref[hop, head, :, :DV].astype(F32)
                + mul(prefix_ref[hop, head, :, DV:], start_ref[head])
            ).astype(BF16)


def shifted(value, axis, by):
    count = lax.axis_size(axis)
    return lax.ppermute(value, axis, [(i, i + by) for i in range(count - by)])


def group_start(total, axis, group):
    groups = lax.axis_size(axis) // group
    if groups == 2:
        return shifted(total[..., :DV], axis, group)
    running = shifted(total, axis, group)
    by = 1
    while by < groups - 1:
        earlier = shifted(running, axis, by * group)
        product = jnp.einsum("bkl,blv->bkv", running[..., DV:], earlier, preferred_element_type=F32)
        own = jnp.pad(running[..., :DV], ((0, 0), (0, 0), (0, DK)))
        running = (product + own.astype(F32)).astype(BF16)
        by *= 2
    return running[..., :DV]


def starts_of(pairs, axis, beside):
    size = lax.axis_size(axis)
    heads = pairs.shape[0]
    group = math.gcd(math.gcd(size, heads), GROUP)
    groups = [[g * group + i for i in range(group)] for g in range(size // group)]
    each = heads // group
    params = pltpu.CompilerParams(vmem_limit_bytes=VMEM_BYTES)
    by_head = lax.all_to_all(pairs, axis, 0, 0, axis_index_groups=groups, tiled=True)
    by_head, done = lax.optimization_barrier((by_head, beside()))
    prefix, total = pl.pallas_call(
        prefix_kernel,
        out_shape=[
            jax.ShapeDtypeStruct((group, each, DK, DV + DK), BF16),
            jax.ShapeDtypeStruct((each, DK, DV + DK), BF16),
        ],
        compiler_params=params,
        name="prefix",
    )(by_head.reshape(group, each, DK, DV + DK))
    starts = pl.pallas_call(
        apply_kernel,
        out_shape=jax.ShapeDtypeStruct((group, each, DK, DV), BF16),
        compiler_params=params,
        name="apply",
    )(prefix, group_start(total, axis, group))
    starts = lax.all_to_all(
        starts.reshape(heads, DK, DV), axis, 0, 0, axis_index_groups=groups, tiled=True
    )
    return starts, done


def project_kernel(place_ref, parts_ref, starts_ref, gated_ref, weight_ref, out_ref, normed):
    heads = parts_ref.shape[0]

    @pl.when(pl.program_id(0) == 0)
    def _():
        for head in range(heads):
            part = slice(head * DV, (head + 1) * DV)
            core = parts_ref[head, :, :DV].astype(F32) + mul(
                parts_ref[head, :, DV:], starts_ref[head]
            )
            scale = lax.rsqrt(jnp.mean(core * core, -1, keepdims=True) + EPSILON)
            normed[:, part] = (core * scale * gated_ref[:, part].astype(F32)).astype(BF16)

    out_ref[...] = jnp.dot(
        normed[...], weight_ref[...], preferred_element_type=F32
    ).astype(out_ref.dtype)


def project(parts, starts, gated, out_weight, place, rows):
    heads = parts.shape[0]
    depth, width = out_weight.shape
    block = min(512, width)
    return pl.pallas_call(
        project_kernel,
        grid_spec=pltpu.PrefetchScalarGridSpec(
            num_scalar_prefetch=1,
            grid=(width // block,),
            in_specs=[
                pl.BlockSpec((heads, rows, DV + DK), lambda step, place: (0, place[0], 0)),
                pl.BlockSpec(starts.shape, lambda step, place: (0, 0, 0)),
                pl.BlockSpec((rows, depth), lambda step, place: (place[0], 0)),
                pl.BlockSpec((depth, block), lambda step, place: (0, step)),
            ],
            out_specs=pl.BlockSpec((rows, block), lambda step, place: (0, step)),
            scratch_shapes=[pltpu.VMEM((rows, depth), BF16)],
        ),
        out_shape=jax.ShapeDtypeStruct((rows, width), BF16),
        compiler_params=pltpu.CompilerParams(vmem_limit_bytes=VMEM_BYTES),
        cost_estimate=pl.CostEstimate(
            flops=2 * rows * depth * width, bytes_accessed=2 * depth * width, transcendentals=0
        ),
        name="project",
    )(place, parts, starts, gated, out_weight)


def projected(parts, starts, gated, out_weight, axis):
    length = parts.shape[1]
    if lax.axis_size(axis) != 2:
        partial = project(parts, starts, gated, out_weight, jnp.zeros((1,), jnp.int32), length)
        return lax.psum_scatter(partial, axis, scatter_dimension=0, tiled=True)
    here = lax.axis_index(axis).astype(jnp.int32).reshape(1)
    away = project(parts, starts, gated, out_weight, 1 - here, length // 2)
    other = lax.ppermute(away, axis, [(0, 1), (1, 0)])
    own = project(parts, starts, gated, out_weight, here, length // 2)
    return (own.astype(F32) + other.astype(F32)).astype(BF16)


def tails_kernel(value_ref, query_ref, key_ref, out_ref):
    at = 0
    for ref in (value_ref, query_ref, key_ref):
        width = ref.shape[1]
        out_ref[:, at : at + width] = ref[...].astype(F32)[13:16].astype(BF16)
        at += width


def tails(raws):
    length = raws[0].shape[0]
    order = (raws[2], raws[0], raws[1])
    width = sum(raw.shape[1] for raw in order)
    return pl.pallas_call(
        tails_kernel,
        grid=(1,),
        in_specs=[pl.BlockSpec((16, raw.shape[1]), lambda step: (length // 16 - 1, 0)) for raw in order],
        out_specs=pl.BlockSpec((3, width), lambda step: (0, 0)),
        out_shape=jax.ShapeDtypeStruct((3, width), BF16),
        compiler_params=pltpu.CompilerParams(vmem_limit_bytes=VMEM_BYTES),
        name="tails",
    )(*order)


def shards(
    query_raw, key_raw, value_raw, gate_raw, query_taps, key_taps, value_taps,
    beta_logit, decay_logit, norm_gain, out_weight,
):
    raws = (query_raw, key_raw, value_raw)
    before = shifted(tails(raws), "seq", 1)
    pairs, local = local_steps(
        raws, before, (query_taps, key_taps, value_taps), beta_logit, decay_logit, gate_raw, norm_gain
    )
    starts, (parts, gated) = starts_of(pairs, "seq", local)
    return projected(parts, starts, gated, out_weight, "head")


def solution(mesh):
    placed = (
        P("seq", "head"), P("seq", "head"), P("seq", "head"), P("seq", "head"),
        P(None, "head"), P(None, "head"), P(None, "head"),
        P("seq", "head"), P("seq", "head"), P(), P("head", None),
    )
    return jax.shard_map(
        shards, mesh=mesh, in_specs=placed, out_specs=P(("seq", "head"), None), check_vma=False
    )
```

```python
import math

import jax
import jax.numpy as jnp
from jax import lax
from jax.experimental import pallas as pl
from jax.experimental.pallas import tpu as pltpu
from jax.sharding import PartitionSpec as P

DK = 128
DV = 128
CHUNK = 128
SMALL = 32
GROUP = 8
HEADS_AT_ONCE = 4
EPSILON = 1e-06
F32 = jnp.float32
BF16 = jnp.bfloat16


def mul(left, right):
    return jnp.dot(left.astype(BF16), right.astype(BF16), preferred_element_type=F32)


def sigmoid(x):
    return 0.5 + 0.5 * jnp.tanh(0.5 * x)


def conv_silu(padded, first, rows, taps_ref):
    summed = taps_ref[0:1, :] * padded[first : first + rows, :]
    for offset in range(1, 4):
        summed = summed + taps_ref[offset : offset + 1, :] * padded[first + offset : first + offset + rows, :]
    return summed * sigmoid(summed)


def unit_rows(key):
    return key * lax.rsqrt(jnp.sum(key * key, -1, keepdims=True) + EPSILON)


def part_of(chunk):
    return slice(chunk * CHUNK, (chunk + 1) * CHUNK)


def head_of(head):
    return slice(head * DK, (head + 1) * DK)


def chunk_rows(ref, heads, chunks):
    held = ref.shape[0]
    first = (pl.program_id(0) * heads) % held
    rows = ref[:heads, :]
    for at in range(heads, held, heads):
        rows = jnp.where(first == at, ref[at : at + heads, :], rows)
    return jnp.concatenate([rows[:, part_of(c)] for c in chunks], 0)


def square_iotas(rows=CHUNK):
    return (
        lax.broadcasted_iota(jnp.int32, (rows, CHUNK), 0),
        lax.broadcasted_iota(jnp.int32, (rows, CHUNK), 1),
    )


def log_fades(logit):
    rows, cols = square_iotas()
    decay = -(jnp.maximum(logit, 0.0) + jnp.log(1.0 + jnp.exp(-jnp.abs(logit))))
    return jnp.dot(
        decay, (rows <= cols).astype(F32), precision=lax.Precision.HIGHEST, preferred_element_type=F32
    )


def as_columns(blocks):
    rows = sum(block.shape[0] for block in blocks)
    return jnp.concatenate(list(blocks) + [jnp.zeros((CHUNK - rows, CHUNK), F32)], 0).T


def solved_packs(fade, beta, keys, key_cols, values):
    count = len(keys)
    rows, cols = square_iotas()
    strict = rows > cols
    differ = rows ^ cols
    columns = as_columns((fade, beta, beta * jnp.exp(fade)))
    inner = {id(key): mul(key, turned) for key, turned in zip(keys, key_cols)}
    lower = []
    for p in range(count):
        gap = columns[:, p : p + 1] - fade[p : p + 1, :]
        ratio = jnp.exp(jnp.where(strict, gap, -1e30))
        lower.append(columns[:, count + p : count + p + 1] * ratio * inner[id(keys[p])])

    small_rows, small_cols = square_iotas(SMALL)
    small_differ = small_rows ^ (small_cols % SMALL)
    place = small_cols // SMALL
    blocks = jnp.where(rows // SMALL == cols // SMALL, 1.0, 0.0)
    blocks16 = blocks.astype(BF16)

    def spread(small):
        return jnp.concatenate([small] * (CHUNK // SMALL), 0) * (blocks16 if small.dtype == BF16 else blocks)

    small = []
    for low in lower:
        held = low[:SMALL]
        for at in range(1, CHUNK // SMALL):
            held = jnp.where(place == at, low[at * SMALL : (at + 1) * SMALL], held)
        small.append(held)
    inverse = [
        jnp.where(small_differ == 0, 1.0, jnp.where(small_differ == 1, -one, 0.0)) for one in small
    ]
    size = 2
    while size < CHUNK:
        last = size == SMALL
        if last:
            band = (differ >= size) & (differ < 4 * size)
            inside = [jnp.where(band, low, 0.0).astype(BF16) for low in lower]
            inverse16 = [spread(one.astype(BF16)) for one in inverse]
            inverse = [spread(one) for one in inverse]
            wide16 = inverse16
        else:
            band = (small_differ >= size) & (small_differ < 4 * size)
            inside = [spread(jnp.where(band, one, 0.0).astype(BF16)) for one in small]
            inverse16 = [one.astype(BF16) for one in inverse]
            wide16 = [spread(one) for one in inverse16]
        step = [mul(inverse16[p], inside[p]).astype(BF16) for p in range(count)]
        both = [
            mul(step[p], jnp.concatenate([step[p] if last else spread(step[p]), wide16[p]], 1))
            for p in range(count)
        ]
        inverse = [inverse[p] - both[p][:, CHUNK:] for p in range(count)]
        partial = [inverse[p].astype(BF16) for p in range(count)]
        inverse = [
            inverse[p] + mul(both[p][:, :CHUNK], partial[p] if last else spread(partial[p]))
            for p in range(count)
        ]
        size *= 4

    solved = []
    for p in range(count):
        right = jnp.concatenate(
            [
                columns[:, count + p : count + p + 1] * values[p],
                columns[:, 2 * count + p : 2 * count + p + 1] * keys[p],
            ],
            1,
        )
        solved.append(mul(inverse[p], right))
    return solved


def later_kernel(
    key_ref, value_ref, key_taps, value_taps, beta_ref, decay_ref,
    solved_ref, unit_ref, turned_ref, key_padded, value_padded,
):
    length, width = key_ref.shape
    chunks = range(1, length // CHUNK)
    key_heads = width // DK
    heads = value_ref.shape[1] // DV
    repeat_by = heads // key_heads
    packs = [(chunk, head) for chunk in chunks for head in range(heads)]
    skip = CHUNK - 16
    count = length - CHUNK
    key_padded[...] = key_ref[skip:, :].astype(F32)
    value_padded[...] = value_ref[skip:, :].astype(F32)
    key_conv = conv_silu(key_padded, 13, count, key_taps)
    key, turned = {}, {}
    for j in range(key_heads):
        unit = unit_rows(key_conv[:, head_of(j)])
        unit_ref[:, head_of(j)] = unit.astype(BF16)
        for chunk in chunks:
            key[chunk, j] = unit[part_of(chunk - 1)]
            turned[chunk, j] = key[chunk, j].T
            turned_ref[j, chunk - 1] = turned[chunk, j].astype(BF16)
    value = conv_silu(value_padded, 13, count, value_taps)
    solved = solved_packs(
        log_fades(chunk_rows(decay_ref, heads, chunks)),
        sigmoid(chunk_rows(beta_ref, heads, chunks)),
        [key[chunk, head // repeat_by] for chunk, head in packs],
        [turned[chunk, head // repeat_by] for chunk, head in packs],
        [value[part_of(chunk - 1), head_of(head)] for chunk, head in packs],
    )
    for (chunk, head), one in zip(packs, solved):
        solved_ref[head, part_of(chunk - 1), :] = one.astype(BF16)


def states_kernel(
    key_ref, value_ref, key_before, value_before, key_taps, value_taps, beta_ref, decay_ref,
    solved_hbm, turned_hbm,
    pairs_ref, unit_ref, fresh_hbm, starts_hbm,
    key_padded, value_padded, solved_ref, turned_ref, fresh_ref, starts_ref, in_sem, out_sem,
):
    heads, length = decay_ref.shape
    chunks = length // CHUNK
    key_heads = key_ref.shape[1] // DK
    repeat_by = heads // key_heads
    incoming = [
        pltpu.make_async_copy(solved_hbm, solved_ref, in_sem.at[0]),
        pltpu.make_async_copy(turned_hbm, turned_ref, in_sem.at[1]),
    ]
    for copy in incoming:
        copy.start()

    key_padded[5:8, :] = key_before[...].astype(F32)
    key_padded[8 : 8 + CHUNK, :] = key_ref[...].astype(F32)
    value_padded[5:8, :] = value_before[...].astype(F32)
    value_padded[8 : 8 + CHUNK, :] = value_ref[...].astype(F32)
    key_conv = conv_silu(key_padded, 5, CHUNK, key_taps)
    key, first_turned = [], []
    for j in range(key_heads):
        key.append(unit_rows(key_conv[:, head_of(j)]))
        unit_ref[:, head_of(j)] = key[j].astype(BF16)
        first_turned.append(key[j].T)
    value = conv_silu(value_padded, 5, CHUNK, value_taps)
    fade = log_fades(chunk_rows(decay_ref, heads, range(chunks)))
    solved = solved_packs(
        fade[:heads],
        sigmoid(beta_ref[:, :CHUNK]),
        [key[head // repeat_by] for head in range(heads)],
        [first_turned[head // repeat_by] for head in range(heads)],
        [value[:, head_of(head)] for head in range(heads)],
    )
    last = jnp.exp(fade[:, CHUNK - 1 : CHUNK])
    tail = jnp.exp(fade[:, CHUNK - 1 : CHUNK] - fade)
    rows, cols = square_iotas()
    identity = jnp.where(rows == cols, 1.0, 0.0)

    state = [None] * heads
    outgoing = []
    for chunk in range(chunks):
        if chunk == 1:
            for copy in incoming:
                copy.wait()
        for head in range(heads):
            pack = chunk * heads + head
            if chunk == 0:
                updates, wide = solved[head][:, :DV], solved[head][:, DV:]
                fresh = jnp.concatenate([updates, -wide], 1).astype(BF16)
                faded = jnp.concatenate(
                    [jnp.zeros((DK, DV), F32), last[pack : pack + 1, :] * identity], 1
                )
                turned = first_turned[head // repeat_by]
            else:
                held = solved_ref[head, part_of(chunk - 1), :]
                start = state[head].astype(BF16)
                starts_ref[head, chunk - 1] = start
                taken = mul(held[:, DV:], start)
                fresh = jnp.concatenate(
                    [held[:, :DV].astype(F32) - taken[:, :DV], -taken[:, DV:]], 1
                ).astype(BF16)
                faded = last[pack : pack + 1, :] * state[head]
                turned = turned_ref[head // repeat_by, chunk - 1].astype(F32)
            fresh_ref[head, part_of(chunk), :] = fresh
            state[head] = faded + mul(turned * tail[pack : pack + 1, :], fresh)
        outgoing.append(
            pltpu.make_async_copy(
                fresh_ref.at[:, pl.ds(chunk * CHUNK, CHUNK)],
                fresh_hbm.at[:, pl.ds(chunk * CHUNK, CHUNK)],
                out_sem.at[chunk],
            )
        )
        outgoing[-1].start()
    outgoing.append(pltpu.make_async_copy(starts_ref, starts_hbm, out_sem.at[chunks]))
    outgoing[-1].start()
    for head in range(heads):
        pairs_ref[head] = state[head].astype(BF16)
    for copy in outgoing:
        copy.wait()


def local_kernel(
    query_ref, query_before, query_taps, first_unit, later_unit, decay_ref, fresh_ref, starts_ref,
    gate_ref, gain_ref, parts_ref, gated_ref, padded,
):
    length, width = query_ref.shape
    chunks = length // CHUNK
    key_heads = width // DK
    heads = fresh_ref.shape[0]
    repeat_by = heads // key_heads

    rows, cols = square_iotas()
    within = rows >= cols
    fade = log_fades(chunk_rows(decay_ref, heads, range(chunks)))
    columns = as_columns((fade, jnp.exp(fade)))
    padded[5:8, :] = query_before[...].astype(F32)
    padded[8 : 8 + length, :] = query_ref[...].astype(F32)
    query = conv_silu(padded, 5, length, query_taps).astype(BF16)
    for head in range(heads):
        gate = gate_ref[:, head_of(head)].astype(F32)
        gated_ref[:, head_of(head)] = (gate * sigmoid(gate) * gain_ref[...]).astype(BF16)
    for chunk in range(chunks):
        part = part_of(chunk)
        for j in range(key_heads):
            own = head_of(j)
            unit = first_unit[:, own] if chunk == 0 else later_unit[part_of(chunk - 1), own]
            inner = lax.dot_general(
                query[part, own], unit, (((1,), (1,)), ((), ())), preferred_element_type=F32
            )
            for head in range(j * repeat_by, (j + 1) * repeat_by):
                pack = chunk * heads + head
                gap = columns[:, pack : pack + 1] - fade[pack : pack + 1, :]
                scores = inner * jnp.exp(jnp.where(within, gap, -1e30))
                grown = columns[:, chunks * heads + pack : chunks * heads + pack + 1]
                if chunk == 0:
                    carried = jnp.concatenate(
                        [jnp.zeros((CHUNK, DV), F32), grown * query[part, own].astype(F32)], 1
                    )
                else:
                    carried = grown * mul(query[part, own], starts_ref[head, chunk - 1])
                parts_ref[head, part, :] = (carried + mul(scores, fresh_ref[head, part, :])).astype(BF16)


def columns_of(rows, width, first=0):
    return pl.BlockSpec((rows, width), lambda step: (0, step + first))


def in_vmem(mib):
    return pltpu.CompilerParams(vmem_limit_bytes=mib * 1024 * 1024)


def local_steps(raws, before, taps, beta_logit, decay_logit, gate_raw, norm_gain):
    length = raws[0].shape[0]
    key_heads = raws[0].shape[1] // DK
    value_heads = raws[2].shape[1] // DV
    repeat_by = value_heads // key_heads
    chunks = length // CHUNK
    beta, decay = beta_logit.T, decay_logit.T
    work = CHUNK * length * DV * value_heads
    hbm = pl.BlockSpec(memory_space=pltpu.HBM)

    def split(each):
        heads = each * repeat_by
        held = max(heads, math.gcd(8, value_heads))
        of_heads = lambda *shape: pl.BlockSpec((heads,) + shape, lambda step: (step,) + (0,) * len(shape))
        logits = pl.BlockSpec((held, length), lambda step: (step * heads // held, 0))
        return key_heads // each, each * DK, heads * DV, of_heads, logits

    each = math.gcd(4, key_heads)
    steps, narrow, wide, of_heads, logits = split(each)
    later = length - CHUNK
    solved, later_unit, turned = pl.pallas_call(
        later_kernel,
        grid=(steps,),
        in_specs=[
            columns_of(length, narrow), columns_of(length, wide),
            columns_of(4, narrow), columns_of(4, wide), logits, logits,
        ],
        out_specs=[
            of_heads(later, DV + DK), columns_of(later, narrow),
            pl.BlockSpec((each, chunks - 1, DK, CHUNK), lambda step: (step, 0, 0, 0)),
        ],
        out_shape=[
            jax.ShapeDtypeStruct((value_heads, later, DV + DK), BF16),
            jax.ShapeDtypeStruct((later, key_heads * DK), BF16),
            jax.ShapeDtypeStruct((key_heads, chunks - 1, DK, CHUNK), BF16),
        ],
        scratch_shapes=[pltpu.VMEM((later + 16, narrow), F32), pltpu.VMEM((later + 16, wide), F32)],
        compiler_params=in_vmem(60),
        cost_estimate=pl.CostEstimate(flops=30 * work, bytes_accessed=0, transcendentals=0),
        name="later",
    )(raws[1], raws[2], taps[1], taps[2], beta, decay)

    narrow, wide = key_heads * DK, value_heads * DV
    whole = lambda shape, *at: pl.BlockSpec(shape, lambda step: at or (0,) * len(shape))
    pairs, first_unit, fresh, starts = pl.pallas_call(
        states_kernel,
        grid=(1,),
        in_specs=[
            whole((CHUNK, narrow)), whole((CHUNK, wide)),
            whole((3, narrow), 0, repeat_by + 1), whole((3, wide)),
            whole(taps[1].shape), whole(taps[2].shape), whole(beta.shape), whole(decay.shape),
            hbm, hbm,
        ],
        out_specs=[whole((value_heads, DK, DV + DK)), whole((CHUNK, narrow)), hbm, hbm],
        out_shape=[
            jax.ShapeDtypeStruct((value_heads, DK, DV + DK), BF16),
            jax.ShapeDtypeStruct((CHUNK, narrow), BF16),
            jax.ShapeDtypeStruct((value_heads, length, DV + DK), BF16),
            jax.ShapeDtypeStruct((value_heads, chunks - 1, DK, DV + DK), BF16),
        ],
        scratch_shapes=[
            pltpu.VMEM((8 + CHUNK, narrow), F32),
            pltpu.VMEM((8 + CHUNK, wide), F32),
            pltpu.VMEM(solved.shape, BF16),
            pltpu.VMEM(turned.shape, BF16),
            pltpu.VMEM((value_heads, length, DV + DK), BF16),
            pltpu.VMEM((value_heads, chunks - 1, DK, DV + DK), BF16),
            pltpu.SemaphoreType.DMA((2,)),
            pltpu.SemaphoreType.DMA((chunks + 1,)),
        ],
        compiler_params=in_vmem(54),
        cost_estimate=pl.CostEstimate(flops=20 * work, bytes_accessed=0, transcendentals=0),
        name="states",
    )(raws[1], raws[2], before, before, taps[1], taps[2], beta, decay, solved, turned)
    gain = norm_gain.reshape(1, DV)

    def local():
        steps, narrow, wide, of_heads, logits = split(math.gcd(2, key_heads))
        return pl.pallas_call(
            local_kernel,
            grid=(steps,),
            in_specs=[
                columns_of(length, narrow), columns_of(3, narrow, repeat_by * steps), columns_of(4, narrow),
                columns_of(CHUNK, narrow), columns_of(later, narrow), logits,
                of_heads(length, DV + DK), of_heads(chunks - 1, DK, DV + DK),
                columns_of(length, wide), whole(gain.shape),
            ],
            out_specs=[of_heads(length, DV + DK), columns_of(length, wide)],
            out_shape=[
                jax.ShapeDtypeStruct((value_heads, length, DV + DK), BF16),
                jax.ShapeDtypeStruct(gate_raw.shape, BF16),
            ],
            scratch_shapes=[pltpu.VMEM((8 + length, narrow), F32)],
            compiler_params=in_vmem(40),
            cost_estimate=pl.CostEstimate(flops=12 * work, bytes_accessed=0, transcendentals=0),
            name="local",
        )(raws[0], before, taps[0], first_unit, later_unit, decay, fresh, starts, gate_raw, gain)

    return pairs, local


def prefix_kernel(pairs_ref, prefix_ref, total_ref):
    count, heads = pairs_ref.shape[:2]
    running = [None] * heads
    for hop in range(count):
        for head in range(heads):
            now = pairs_ref[hop, head]
            if hop == 0:
                rows = lax.broadcasted_iota(jnp.int32, (DK, DV + DK), 0)
                cols = lax.broadcasted_iota(jnp.int32, (DK, DV + DK), 1)
                prefix_ref[hop, head] = jnp.where(cols == rows + DV, 1.0, 0.0).astype(BF16)
                running[head] = now.astype(F32)
            else:
                before = running[head].astype(BF16)
                prefix_ref[hop, head] = before
                own = jnp.concatenate([now[:, :DV].astype(F32), jnp.zeros((DK, DK), F32)], 1)
                running[head] = own + mul(now[:, DV:], before)
    for head in range(heads):
        total_ref[head] = running[head][:, : total_ref.shape[2]].astype(BF16)


def apply_kernel(prefix_ref, start_ref, starts_ref):
    count, heads = prefix_ref.shape[:2]
    for hop in range(count):
        for head in range(heads):
            starts_ref[hop, head] = (
                prefix_ref[hop, head, :, :DV].astype(F32)
                + mul(prefix_ref[hop, head, :, DV:], start_ref[head])
            ).astype(BF16)


def shifted(value, axis, by):
    count = lax.axis_size(axis)
    return lax.ppermute(value, axis, [(i, i + by) for i in range(count - by)])


def group_start(total, axis, group):
    groups = lax.axis_size(axis) // group
    running = shifted(total, axis, group)
    by = 1
    while by < groups - 1:
        earlier = shifted(running, axis, by * group)
        product = jnp.einsum("bkl,blv->bkv", running[..., DV:], earlier, preferred_element_type=F32)
        own = jnp.pad(running[..., :DV], ((0, 0), (0, 0), (0, DK)))
        running = (product + own.astype(F32)).astype(BF16)
        by *= 2
    return running[..., :DV]


def starts_of(pairs, axis, beside):
    size = lax.axis_size(axis)
    heads = pairs.shape[0]
    group = math.gcd(math.gcd(size, heads), GROUP)
    groups = [[g * group + i for i in range(group)] for g in range(size // group)]
    each = heads // group
    wide = DV if size // group == 2 else DV + DK
    by_head = lax.all_to_all(pairs, axis, 0, 0, axis_index_groups=groups, tiled=True)
    by_head, done = lax.optimization_barrier((by_head, beside()))
    prefix, total = pl.pallas_call(
        prefix_kernel,
        out_shape=[
            jax.ShapeDtypeStruct((group, each, DK, DV + DK), BF16),
            jax.ShapeDtypeStruct((each, DK, wide), BF16),
        ],
        compiler_params=in_vmem(16),
        name="prefix",
    )(by_head.reshape(group, each, DK, DV + DK))
    starts = pl.pallas_call(
        apply_kernel,
        out_shape=jax.ShapeDtypeStruct((group, each, DK, DV), BF16),
        compiler_params=in_vmem(16),
        name="apply",
    )(prefix, group_start(total, axis, group))
    starts = lax.all_to_all(
        starts.reshape(heads, DK, DV), axis, 0, 0, axis_index_groups=groups, tiled=True
    )
    return starts, done


def project_kernel(
    place_ref, starts_ref, parts_hbm, gated_hbm, weight_hbm, away_ref, own_ref,
    parts_ref, gated_ref, weight_ref, total, in_sem,
):
    heads, length = parts_ref.shape[:2]
    depth, width = weight_ref.shape
    each = min(HEADS_AT_ONCE, heads)
    block = min(512, width)
    groups = heads // each
    copies = []
    for g in range(groups):
        here, lanes = pl.ds(g * each, each), pl.ds(g * each * DV, each * DV)
        copies.append(
            [
                pltpu.make_async_copy(parts_hbm.at[here], parts_ref.at[here], in_sem.at[0, g]),
                pltpu.make_async_copy(gated_hbm.at[:, lanes], gated_ref.at[:, lanes], in_sem.at[1, g]),
                pltpu.make_async_copy(weight_hbm.at[lanes], weight_ref.at[lanes], in_sem.at[2, g]),
            ]
        )
        for copy in copies[g]:
            copy.start()
    for g in range(groups):
        copies[g][0].wait()
        copies[g][1].wait()
        normed = []
        for head in range(g * each, (g + 1) * each):
            core = parts_ref[head, :, :DV].astype(F32) + mul(
                parts_ref[head, :, DV:], starts_ref[head]
            )
            scale = lax.rsqrt(jnp.mean(core * core, -1, keepdims=True) + EPSILON)
            normed.append((core * scale * gated_ref[:, head_of(head)].astype(F32)).astype(BF16))
        normed = jnp.concatenate(normed, 1)
        copies[g][2].wait()
        for at in range(0, width, block):
            added = jnp.dot(
                normed, weight_ref[g * each * DV : (g + 1) * each * DV, at : at + block],
                preferred_element_type=F32,
            )
            if g > 0:
                added = added + total[:, at : at + block]
            if g < groups - 1:
                total[:, at : at + block] = added
            elif own_ref is None:
                away_ref[:, at : at + block] = added.astype(BF16)
            else:
                first = place_ref[0] == 0
                low, high = added[: length // 2], added[length // 2 :]
                own_ref[:, at : at + block] = jnp.where(first, low, high).astype(BF16)
                away_ref[:, at : at + block] = jnp.where(first, high, low).astype(BF16)


def whole_kernel(place_ref, starts_ref, parts_hbm, gated_hbm, weight_hbm, out_ref, *scratch):
    project_kernel(place_ref, starts_ref, parts_hbm, gated_hbm, weight_hbm, out_ref, None, *scratch)


def projected(parts, starts, gated, out_weight, axis):
    heads, length = parts.shape[:2]
    depth, width = out_weight.shape
    halves = lax.axis_size(axis) == 2
    hbm = pl.BlockSpec(memory_space=pltpu.HBM)
    vmem = pl.BlockSpec(memory_space=pltpu.VMEM)
    here = lax.axis_index(axis).astype(jnp.int32).reshape(1)
    out = jax.ShapeDtypeStruct((length // 2 if halves else length, width), BF16)
    partial = pl.pallas_call(
        project_kernel if halves else whole_kernel,
        in_specs=[pl.BlockSpec(memory_space=pltpu.SMEM), vmem, hbm, hbm, hbm],
        out_specs=[vmem, vmem] if halves else vmem,
        out_shape=[out, out] if halves else out,
        scratch_shapes=[
            pltpu.VMEM(parts.shape, BF16),
            pltpu.VMEM(gated.shape, BF16),
            pltpu.VMEM(out_weight.shape, BF16),
            pltpu.VMEM((length, width), F32),
            pltpu.SemaphoreType.DMA((3, heads // min(HEADS_AT_ONCE, heads))),
        ],
        compiler_params=in_vmem(40),
        name="project",
    )(here, starts, parts, gated, out_weight)
    if not halves:
        return lax.psum_scatter(partial, axis, scatter_dimension=0, tiled=True)
    away, own = partial
    other = lax.ppermute(away, axis, [(0, 1), (1, 0)])
    return (own.astype(F32) + other.astype(F32)).astype(BF16)


def tails_kernel(value_hbm, query_hbm, key_hbm, out_ref, value_ref, query_ref, key_ref, sem):
    pairs = ((value_hbm, value_ref), (query_hbm, query_ref), (key_hbm, key_ref))
    copies = [
        pltpu.make_async_copy(source.at[pl.ds(source.shape[0] - 16, 16)], held, sem.at[i])
        for i, (source, held) in enumerate(pairs)
    ]
    for copy in copies:
        copy.start()
    at = 0
    for copy, (_, held) in zip(copies, pairs):
        copy.wait()
        width = held.shape[1]
        out_ref[:, at : at + width] = held[...].astype(F32)[13:16].astype(BF16)
        at += width


def tails(raws):
    order = (raws[2], raws[0], raws[1])
    width = sum(raw.shape[1] for raw in order)
    return pl.pallas_call(
        tails_kernel,
        in_specs=[pl.BlockSpec(memory_space=pltpu.HBM)] * 3,
        out_shape=jax.ShapeDtypeStruct((3, width), BF16),
        scratch_shapes=[pltpu.VMEM((16, raw.shape[1]), BF16) for raw in order]
        + [pltpu.SemaphoreType.DMA((3,))],
        compiler_params=in_vmem(60),
        name="tails",
    )(*order)


def shards(
    query_raw, key_raw, value_raw, gate_raw, query_taps, key_taps, value_taps,
    beta_logit, decay_logit, norm_gain, out_weight,
):
    raws = (query_raw, key_raw, value_raw)
    before = shifted(tails(raws), "seq", 1)
    pairs, local = local_steps(
        raws, before, (query_taps, key_taps, value_taps), beta_logit, decay_logit, gate_raw, norm_gain
    )
    starts, (parts, gated) = starts_of(pairs, "seq", local)
    return projected(parts, starts, gated, out_weight, "head")


def solution(mesh):
    placed = (
        P("seq", "head"), P("seq", "head"), P("seq", "head"), P("seq", "head"),
        P(None, "head"), P(None, "head"), P(None, "head"),
        P("seq", "head"), P("seq", "head"), P(), P("head", None),
    )
    return jax.shard_map(
        shards, mesh=mesh, in_specs=placed, out_specs=P(("seq", "head"), None), check_vma=False
    )
```

```python
import math

import jax
import jax.numpy as jnp
from jax import lax
from jax.experimental import pallas as pl
from jax.experimental.pallas import tpu as pltpu
from jax.sharding import PartitionSpec as P

DK = 128
DV = 128
CHUNK = 128
SMALL = 32
GROUP = 8
HEADS_AT_ONCE = 4
EPSILON = 1e-06
F32 = jnp.float32
BF16 = jnp.bfloat16


def mul(left, right):
    return jnp.dot(left.astype(BF16), right.astype(BF16), preferred_element_type=F32)


def sigmoid(x):
    return 0.5 + 0.5 * jnp.tanh(0.5 * x)


def conv_silu(padded, first, rows, taps_ref):
    summed = taps_ref[0:1, :] * padded[first : first + rows, :]
    for offset in range(1, 4):
        summed = summed + taps_ref[offset : offset + 1, :] * padded[first + offset : first + offset + rows, :]
    return summed * sigmoid(summed)


def unit_rows(key):
    return key * lax.rsqrt(jnp.sum(key * key, -1, keepdims=True) + EPSILON)


def part_of(chunk):
    return slice(chunk * CHUNK, (chunk + 1) * CHUNK)


def head_of(head):
    return slice(head * DK, (head + 1) * DK)


def chunk_rows(ref, heads, chunks):
    held = ref.shape[0]
    first = (pl.program_id(0) * heads) % held
    rows = ref[:heads, :]
    for at in range(heads, held, heads):
        rows = jnp.where(first == at, ref[at : at + heads, :], rows)
    return jnp.concatenate([rows[:, part_of(c)] for c in chunks], 0)


def square_iotas(rows=CHUNK):
    return (
        lax.broadcasted_iota(jnp.int32, (rows, CHUNK), 0),
        lax.broadcasted_iota(jnp.int32, (rows, CHUNK), 1),
    )


def log_fades(logit):
    rows, cols = square_iotas()
    decay = -(jnp.maximum(logit, 0.0) + jnp.log(1.0 + jnp.exp(-jnp.abs(logit))))
    return jnp.dot(
        decay, (rows <= cols).astype(F32), precision=lax.Precision.HIGHEST, preferred_element_type=F32
    )


def as_columns(blocks):
    rows = sum(block.shape[0] for block in blocks)
    return jnp.concatenate(list(blocks) + [jnp.zeros((CHUNK - rows, CHUNK), F32)], 0).T


def solved_packs(fade, beta, keys, key_cols, values):
    count = len(keys)
    rows, cols = square_iotas()
    strict = rows > cols
    differ = rows ^ cols
    columns = as_columns((fade, beta, beta * jnp.exp(fade)))
    inner = {id(key): mul(key, turned) for key, turned in zip(keys, key_cols)}
    lower = []
    for p in range(count):
        gap = columns[:, p : p + 1] - fade[p : p + 1, :]
        ratio = jnp.exp(jnp.where(strict, gap, -1e30))
        lower.append(columns[:, count + p : count + p + 1] * ratio * inner[id(keys[p])])

    small_rows, small_cols = square_iotas(SMALL)
    small_differ = small_rows ^ (small_cols % SMALL)
    place = small_cols // SMALL
    blocks = jnp.where(rows // SMALL == cols // SMALL, 1.0, 0.0)
    blocks16 = blocks.astype(BF16)

    def spread(small):
        return jnp.concatenate([small] * (CHUNK // SMALL), 0) * (blocks16 if small.dtype == BF16 else blocks)

    small = []
    for low in lower:
        held = low[:SMALL]
        for at in range(1, CHUNK // SMALL):
            held = jnp.where(place == at, low[at * SMALL : (at + 1) * SMALL], held)
        small.append(held)
    inverse = [
        jnp.where(small_differ == 0, 1.0, jnp.where(small_differ == 1, -one, 0.0)) for one in small
    ]
    size = 2
    while size < CHUNK:
        last = size == SMALL
        if last:
            band = (differ >= size) & (differ < 4 * size)
            inside = [jnp.where(band, low, 0.0).astype(BF16) for low in lower]
            inverse16 = [spread(one.astype(BF16)) for one in inverse]
            inverse = [spread(one) for one in inverse]
            wide16 = inverse16
        else:
            band = (small_differ >= size) & (small_differ < 4 * size)
            inside = [spread(jnp.where(band, one, 0.0).astype(BF16)) for one in small]
            inverse16 = [one.astype(BF16) for one in inverse]
            wide16 = [spread(one) for one in inverse16]
        step = [mul(inverse16[p], inside[p]).astype(BF16) for p in range(count)]
        both = [
            mul(step[p], jnp.concatenate([step[p] if last else spread(step[p]), wide16[p]], 1))
            for p in range(count)
        ]
        inverse = [inverse[p] - both[p][:, CHUNK:] for p in range(count)]
        partial = [inverse[p].astype(BF16) for p in range(count)]
        inverse = [
            inverse[p] + mul(both[p][:, :CHUNK], partial[p] if last else spread(partial[p]))
            for p in range(count)
        ]
        size *= 4

    solved = []
    for p in range(count):
        right = jnp.concatenate(
            [
                columns[:, count + p : count + p + 1] * values[p],
                columns[:, 2 * count + p : 2 * count + p + 1] * keys[p],
            ],
            1,
        )
        solved.append(mul(inverse[p], right))
    return solved


def later_kernel(
    key_ref, value_ref, key_taps, value_taps, beta_ref, decay_ref,
    solved_ref, unit_ref, turned_ref, key_padded, value_padded,
):
    length, width = key_ref.shape
    chunks = range(1, length // CHUNK)
    key_heads = width // DK
    heads = value_ref.shape[1] // DV
    repeat_by = heads // key_heads
    packs = [(chunk, head) for chunk in chunks for head in range(heads)]
    skip = CHUNK - 16
    count = length - CHUNK
    key_padded[...] = key_ref[skip:, :].astype(F32)
    value_padded[...] = value_ref[skip:, :].astype(F32)
    key_conv = conv_silu(key_padded, 13, count, key_taps)
    key, turned = {}, {}
    for j in range(key_heads):
        unit = unit_rows(key_conv[:, head_of(j)])
        unit_ref[:, head_of(j)] = unit.astype(BF16)
        for chunk in chunks:
            key[chunk, j] = unit[part_of(chunk - 1)]
            turned[chunk, j] = key[chunk, j].T
            turned_ref[j, chunk - 1] = turned[chunk, j].astype(BF16)
    value = conv_silu(value_padded, 13, count, value_taps)
    solved = solved_packs(
        log_fades(chunk_rows(decay_ref, heads, chunks)),
        sigmoid(chunk_rows(beta_ref, heads, chunks)),
        [key[chunk, head // repeat_by] for chunk, head in packs],
        [turned[chunk, head // repeat_by] for chunk, head in packs],
        [value[part_of(chunk - 1), head_of(head)] for chunk, head in packs],
    )
    for (chunk, head), one in zip(packs, solved):
        solved_ref[head, part_of(chunk - 1), :] = one.astype(BF16)


def states_kernel(
    key_ref, value_ref, key_before, value_before, key_taps, value_taps, beta_ref, decay_ref,
    solved_hbm, turned_hbm,
    pairs_ref, unit_ref, fresh_ref, starts_ref,
    key_padded, value_padded, solved_ref, turned_ref, in_sem,
):
    heads, length = decay_ref.shape
    chunks = length // CHUNK
    key_heads = key_ref.shape[1] // DK
    repeat_by = heads // key_heads
    incoming = [
        pltpu.make_async_copy(solved_hbm, solved_ref, in_sem.at[0]),
        pltpu.make_async_copy(turned_hbm, turned_ref, in_sem.at[1]),
    ]
    for copy in incoming:
        copy.start()

    key_padded[5:8, :] = key_before[...].astype(F32)
    key_padded[8 : 8 + CHUNK, :] = key_ref[...].astype(F32)
    value_padded[5:8, :] = value_before[...].astype(F32)
    value_padded[8 : 8 + CHUNK, :] = value_ref[...].astype(F32)
    key_conv = conv_silu(key_padded, 5, CHUNK, key_taps)
    key, first_turned = [], []
    for j in range(key_heads):
        key.append(unit_rows(key_conv[:, head_of(j)]))
        unit_ref[:, head_of(j)] = key[j].astype(BF16)
        first_turned.append(key[j].T)
    value = conv_silu(value_padded, 5, CHUNK, value_taps)
    fade = log_fades(chunk_rows(decay_ref, heads, range(chunks)))
    solved = solved_packs(
        fade[:heads],
        sigmoid(beta_ref[:, :CHUNK]),
        [key[head // repeat_by] for head in range(heads)],
        [first_turned[head // repeat_by] for head in range(heads)],
        [value[:, head_of(head)] for head in range(heads)],
    )
    last = jnp.exp(fade[:, CHUNK - 1 : CHUNK])
    tail = jnp.exp(fade[:, CHUNK - 1 : CHUNK] - fade)
    rows, cols = square_iotas()
    identity = jnp.where(rows == cols, 1.0, 0.0)

    state = [None] * heads
    for chunk in range(chunks):
        if chunk == 1:
            for copy in incoming:
                copy.wait()
        for head in range(heads):
            pack = chunk * heads + head
            if chunk == 0:
                updates, wide = solved[head][:, :DV], solved[head][:, DV:]
                fresh = jnp.concatenate([updates, -wide], 1).astype(BF16)
                faded = jnp.concatenate(
                    [jnp.zeros((DK, DV), F32), last[pack : pack + 1, :] * identity], 1
                )
                turned = first_turned[head // repeat_by]
            else:
                held = solved_ref[head, part_of(chunk - 1), :]
                start = state[head].astype(BF16)
                starts_ref[head, chunk - 1] = start
                taken = mul(held[:, DV:], start)
                fresh = jnp.concatenate(
                    [held[:, :DV].astype(F32) - taken[:, :DV], -taken[:, DV:]], 1
                ).astype(BF16)
                faded = last[pack : pack + 1, :] * state[head]
                turned = turned_ref[head // repeat_by, chunk - 1].astype(F32)
            fresh_ref[head, part_of(chunk), :] = fresh
            state[head] = faded + mul(turned * tail[pack : pack + 1, :], fresh)
    for head in range(heads):
        pairs_ref[head] = state[head].astype(BF16)


def local_kernel(
    query_ref, query_before, query_taps, first_unit, later_unit, decay_ref, fresh_ref, starts_ref,
    gate_ref, gain_ref, parts_ref, gated_ref, padded,
):
    length, width = query_ref.shape
    chunks = length // CHUNK
    key_heads = width // DK
    heads = fresh_ref.shape[0]
    repeat_by = heads // key_heads

    rows, cols = square_iotas()
    within = rows >= cols
    fade = log_fades(chunk_rows(decay_ref, heads, range(chunks)))
    columns = as_columns((fade, jnp.exp(fade)))
    padded[5:8, :] = query_before[...].astype(F32)
    padded[8 : 8 + length, :] = query_ref[...].astype(F32)
    query = conv_silu(padded, 5, length, query_taps).astype(BF16)
    for head in range(heads):
        gate = gate_ref[:, head_of(head)].astype(F32)
        gated_ref[:, head_of(head)] = (gate * sigmoid(gate) * gain_ref[...]).astype(BF16)
    for chunk in range(chunks):
        part = part_of(chunk)
        for j in range(key_heads):
            own = head_of(j)
            unit = first_unit[:, own] if chunk == 0 else later_unit[part_of(chunk - 1), own]
            inner = lax.dot_general(
                query[part, own], unit, (((1,), (1,)), ((), ())), preferred_element_type=F32
            )
            for head in range(j * repeat_by, (j + 1) * repeat_by):
                pack = chunk * heads + head
                gap = columns[:, pack : pack + 1] - fade[pack : pack + 1, :]
                scores = inner * jnp.exp(jnp.where(within, gap, -1e30))
                grown = columns[:, chunks * heads + pack : chunks * heads + pack + 1]
                if chunk == 0:
                    carried = jnp.concatenate(
                        [jnp.zeros((CHUNK, DV), F32), grown * query[part, own].astype(F32)], 1
                    )
                else:
                    carried = grown * mul(query[part, own], starts_ref[head, chunk - 1])
                parts_ref[head, part, :] = (carried + mul(scores, fresh_ref[head, part, :])).astype(BF16)


def columns_of(rows, width, first=0):
    return pl.BlockSpec((rows, width), lambda step: (0, step + first))


def in_vmem(mib):
    return pltpu.CompilerParams(vmem_limit_bytes=mib * 1024 * 1024)


def local_steps(raws, before, taps, beta_logit, decay_logit, gate_raw, norm_gain):
    length = raws[0].shape[0]
    key_heads = raws[0].shape[1] // DK
    value_heads = raws[2].shape[1] // DV
    repeat_by = value_heads // key_heads
    chunks = length // CHUNK
    beta, decay = beta_logit.T, decay_logit.T
    work = CHUNK * length * DV * value_heads
    hbm = pl.BlockSpec(memory_space=pltpu.HBM)
    vmem = pl.BlockSpec(memory_space=pltpu.VMEM)

    def split(each):
        heads = each * repeat_by
        held = max(heads, math.gcd(8, value_heads))
        of_heads = lambda *shape: pl.BlockSpec((heads,) + shape, lambda step: (step,) + (0,) * len(shape))
        logits = pl.BlockSpec((held, length), lambda step: (step * heads // held, 0))
        return key_heads // each, each * DK, heads * DV, of_heads, logits

    each = math.gcd(4, key_heads)
    steps, narrow, wide, of_heads, logits = split(each)
    later = length - CHUNK
    solved, later_unit, turned = pl.pallas_call(
        later_kernel,
        grid=(steps,),
        in_specs=[
            columns_of(length, narrow), columns_of(length, wide),
            columns_of(4, narrow), columns_of(4, wide), logits, logits,
        ],
        out_specs=[
            of_heads(later, DV + DK), columns_of(later, narrow),
            pl.BlockSpec((each, chunks - 1, DK, CHUNK), lambda step: (step, 0, 0, 0)),
        ],
        out_shape=[
            jax.ShapeDtypeStruct((value_heads, later, DV + DK), BF16),
            jax.ShapeDtypeStruct((later, key_heads * DK), BF16),
            jax.ShapeDtypeStruct((key_heads, chunks - 1, DK, CHUNK), BF16),
        ],
        scratch_shapes=[pltpu.VMEM((later + 16, narrow), F32), pltpu.VMEM((later + 16, wide), F32)],
        compiler_params=in_vmem(60),
        cost_estimate=pl.CostEstimate(flops=30 * work, bytes_accessed=0, transcendentals=0),
        name="later",
    )(raws[1], raws[2], taps[1], taps[2], beta, decay)

    narrow, wide = key_heads * DK, value_heads * DV
    whole = lambda shape, *at: pl.BlockSpec(shape, lambda step: at or (0,) * len(shape))
    pairs, first_unit, fresh, starts = pl.pallas_call(
        states_kernel,
        grid=(1,),
        in_specs=[
            whole((CHUNK, narrow)), whole((CHUNK, wide)),
            whole((3, narrow), 0, repeat_by + 1), whole((3, wide)),
            whole(taps[1].shape), whole(taps[2].shape), whole(beta.shape), whole(decay.shape),
            hbm, hbm,
        ],
        out_specs=[vmem] * 4,
        out_shape=[
            jax.ShapeDtypeStruct((value_heads, DK, DV + DK), BF16),
            jax.ShapeDtypeStruct((CHUNK, narrow), BF16),
            jax.ShapeDtypeStruct((value_heads, length, DV + DK), BF16),
            jax.ShapeDtypeStruct((value_heads, chunks - 1, DK, DV + DK), BF16),
        ],
        scratch_shapes=[
            pltpu.VMEM((8 + CHUNK, narrow), F32),
            pltpu.VMEM((8 + CHUNK, wide), F32),
            pltpu.VMEM(solved.shape, BF16),
            pltpu.VMEM(turned.shape, BF16),
            pltpu.SemaphoreType.DMA((2,)),
        ],
        compiler_params=in_vmem(52),
        cost_estimate=pl.CostEstimate(flops=20 * work, bytes_accessed=0, transcendentals=0),
        name="states",
    )(raws[1], raws[2], before, before, taps[1], taps[2], beta, decay, solved, turned)
    gain = norm_gain.reshape(1, DV)

    def local():
        steps, narrow, wide, of_heads, logits = split(math.gcd(2, key_heads))
        return pl.pallas_call(
            local_kernel,
            grid=(steps,),
            in_specs=[
                columns_of(length, narrow), columns_of(3, narrow, repeat_by * steps), columns_of(4, narrow),
                columns_of(CHUNK, narrow), columns_of(later, narrow), logits,
                of_heads(length, DV + DK), of_heads(chunks - 1, DK, DV + DK),
                columns_of(length, wide), whole(gain.shape),
            ],
            out_specs=[of_heads(length, DV + DK), columns_of(length, wide)],
            out_shape=[
                jax.ShapeDtypeStruct((value_heads, length, DV + DK), BF16),
                jax.ShapeDtypeStruct(gate_raw.shape, BF16),
            ],
            scratch_shapes=[pltpu.VMEM((8 + length, narrow), F32)],
            compiler_params=in_vmem(24),
            cost_estimate=pl.CostEstimate(flops=12 * work, bytes_accessed=0, transcendentals=0),
            name="local",
        )(raws[0], before, taps[0], first_unit, later_unit, decay, fresh, starts, gate_raw, gain)

    return pairs, local


def prefix_kernel(pairs_ref, prefix_ref, total_ref):
    count, heads = pairs_ref.shape[:2]
    running = [None] * heads
    for hop in range(count):
        for head in range(heads):
            now = pairs_ref[hop, head]
            if hop == 0:
                rows = lax.broadcasted_iota(jnp.int32, (DK, DV + DK), 0)
                cols = lax.broadcasted_iota(jnp.int32, (DK, DV + DK), 1)
                prefix_ref[hop, head] = jnp.where(cols == rows + DV, 1.0, 0.0).astype(BF16)
                running[head] = now.astype(F32)
            else:
                before = running[head].astype(BF16)
                prefix_ref[hop, head] = before
                own = jnp.concatenate([now[:, :DV].astype(F32), jnp.zeros((DK, DK), F32)], 1)
                running[head] = own + mul(now[:, DV:], before)
    for head in range(heads):
        total_ref[head] = running[head][:, : total_ref.shape[2]].astype(BF16)


def apply_kernel(prefix_ref, start_ref, starts_ref):
    count, heads = prefix_ref.shape[:2]
    for hop in range(count):
        for head in range(heads):
            starts_ref[hop, head] = (
                prefix_ref[hop, head, :, :DV].astype(F32)
                + mul(prefix_ref[hop, head, :, DV:], start_ref[head])
            ).astype(BF16)


def shifted(value, axis, by):
    count = lax.axis_size(axis)
    return lax.ppermute(value, axis, [(i, i + by) for i in range(count - by)])


def group_start(total, axis, group):
    groups = lax.axis_size(axis) // group
    running = shifted(total, axis, group)
    by = 1
    while by < groups - 1:
        earlier = shifted(running, axis, by * group)
        product = jnp.einsum("bkl,blv->bkv", running[..., DV:], earlier, preferred_element_type=F32)
        own = jnp.pad(running[..., :DV], ((0, 0), (0, 0), (0, DK)))
        running = (product + own.astype(F32)).astype(BF16)
        by *= 2
    return running[..., :DV]


def starts_of(pairs, axis, beside):
    size = lax.axis_size(axis)
    heads = pairs.shape[0]
    group = math.gcd(math.gcd(size, heads), GROUP)
    groups = [[g * group + i for i in range(group)] for g in range(size // group)]
    each = heads // group
    wide = DV if size // group == 2 else DV + DK
    by_head = lax.all_to_all(pairs, axis, 0, 0, axis_index_groups=groups, tiled=True)
    by_head, done = lax.optimization_barrier((by_head, beside()))
    prefix, total = pl.pallas_call(
        prefix_kernel,
        out_shape=[
            jax.ShapeDtypeStruct((group, each, DK, DV + DK), BF16),
            jax.ShapeDtypeStruct((each, DK, wide), BF16),
        ],
        compiler_params=in_vmem(16),
        name="prefix",
    )(by_head.reshape(group, each, DK, DV + DK))
    starts = pl.pallas_call(
        apply_kernel,
        out_shape=jax.ShapeDtypeStruct((group, each, DK, DV), BF16),
        compiler_params=in_vmem(16),
        name="apply",
    )(prefix, group_start(total, axis, group))
    starts = lax.all_to_all(
        starts.reshape(heads, DK, DV), axis, 0, 0, axis_index_groups=groups, tiled=True
    )
    return starts, done


def project_kernel(place_ref, starts_ref, parts_ref, gated_ref, weight_ref, away_ref, own_ref, total):
    heads, length = parts_ref.shape[:2]
    width = weight_ref.shape[1]
    each = min(HEADS_AT_ONCE, heads)
    block = min(512, width)
    groups = heads // each
    for g in range(groups):
        normed = []
        for head in range(g * each, (g + 1) * each):
            core = parts_ref[head, :, :DV].astype(F32) + mul(
                parts_ref[head, :, DV:], starts_ref[head]
            )
            scale = lax.rsqrt(jnp.mean(core * core, -1, keepdims=True) + EPSILON)
            normed.append((core * scale * gated_ref[:, head_of(head)].astype(F32)).astype(BF16))
        normed = jnp.concatenate(normed, 1)
        for at in range(0, width, block):
            added = jnp.dot(
                normed, weight_ref[g * each * DV : (g + 1) * each * DV, at : at + block],
                preferred_element_type=F32,
            )
            if g > 0:
                added = added + total[:, at : at + block]
            if g < groups - 1:
                total[:, at : at + block] = added
            elif own_ref is None:
                away_ref[:, at : at + block] = added.astype(BF16)
            else:
                first = place_ref[0] == 0
                low, high = added[: length // 2], added[length // 2 :]
                own_ref[:, at : at + block] = jnp.where(first, low, high).astype(BF16)
                away_ref[:, at : at + block] = jnp.where(first, high, low).astype(BF16)


def whole_kernel(place_ref, starts_ref, parts_ref, gated_ref, weight_ref, out_ref, total):
    project_kernel(place_ref, starts_ref, parts_ref, gated_ref, weight_ref, out_ref, None, total)


def projected(parts, starts, gated, out_weight, axis):
    length = parts.shape[1]
    width = out_weight.shape[1]
    halves = lax.axis_size(axis) == 2
    vmem = pl.BlockSpec(memory_space=pltpu.VMEM)
    here = lax.axis_index(axis).astype(jnp.int32).reshape(1)
    out = jax.ShapeDtypeStruct((length // 2 if halves else length, width), BF16)
    partial = pl.pallas_call(
        project_kernel if halves else whole_kernel,
        in_specs=[pl.BlockSpec(memory_space=pltpu.SMEM)] + [vmem] * 4,
        out_specs=[vmem, vmem] if halves else vmem,
        out_shape=[out, out] if halves else out,
        scratch_shapes=[pltpu.VMEM((length, width), F32)],
        compiler_params=in_vmem(24),
        name="project",
    )(here, starts, parts, gated, out_weight)
    if not halves:
        return lax.psum_scatter(partial, axis, scatter_dimension=0, tiled=True)
    away, own = partial
    other = lax.ppermute(away, axis, [(0, 1), (1, 0)])
    return (own.astype(F32) + other.astype(F32)).astype(BF16)


def tails_kernel(value_hbm, query_hbm, key_hbm, out_ref, value_ref, query_ref, key_ref, sem):
    pairs = ((value_hbm, value_ref), (query_hbm, query_ref), (key_hbm, key_ref))
    copies = [
        pltpu.make_async_copy(source.at[pl.ds(source.shape[0] - 16, 16)], held, sem.at[i])
        for i, (source, held) in enumerate(pairs)
    ]
    for copy in copies:
        copy.start()
    at = 0
    for copy, (_, held) in zip(copies, pairs):
        copy.wait()
        width = held.shape[1]
        out_ref[:, at : at + width] = held[...].astype(F32)[13:16].astype(BF16)
        at += width


def tails(raws):
    order = (raws[2], raws[0], raws[1])
    width = sum(raw.shape[1] for raw in order)
    return pl.pallas_call(
        tails_kernel,
        in_specs=[pl.BlockSpec(memory_space=pltpu.HBM)] * 3,
        out_shape=jax.ShapeDtypeStruct((3, width), BF16),
        scratch_shapes=[pltpu.VMEM((16, raw.shape[1]), BF16) for raw in order]
        + [pltpu.SemaphoreType.DMA((3,))],
        compiler_params=in_vmem(60),
        name="tails",
    )(*order)


def shards(
    query_raw, key_raw, value_raw, gate_raw, query_taps, key_taps, value_taps,
    beta_logit, decay_logit, norm_gain, out_weight,
):
    raws = (query_raw, key_raw, value_raw)
    before = shifted(tails(raws), "seq", 1)
    pairs, local = local_steps(
        raws, before, (query_taps, key_taps, value_taps), beta_logit, decay_logit, gate_raw, norm_gain
    )
    starts, (parts, gated) = starts_of(pairs, "seq", local)
    return projected(parts, starts, gated, out_weight, "head")


def solution(mesh):
    placed = (
        P("seq", "head"), P("seq", "head"), P("seq", "head"), P("seq", "head"),
        P(None, "head"), P(None, "head"), P(None, "head"),
        P("seq", "head"), P("seq", "head"), P(), P("head", None),
    )
    return jax.shard_map(
        shards, mesh=mesh, in_specs=placed, out_specs=P(("seq", "head"), None), check_vma=False
    )
```

```python
import math

import jax
import jax.numpy as jnp
from jax import lax
from jax.experimental import pallas as pl
from jax.experimental.pallas import tpu as pltpu
from jax.sharding import PartitionSpec as P

DK = 128
DV = 128
CHUNK = 128
SMALL = 32
GROUP = 8
HEADS_AT_ONCE = 4
EPSILON = 1e-06
F32 = jnp.float32
BF16 = jnp.bfloat16


def mul(left, right):
    return jnp.dot(left.astype(BF16), right.astype(BF16), preferred_element_type=F32)


def sigmoid(x):
    return 0.5 + 0.5 * jnp.tanh(0.5 * x)


def conv_silu(padded, first, rows, taps_ref, head):
    taps = taps_ref[:, head_of(head)]
    summed = taps[0:1] * padded[head, first : first + rows, :]
    for offset in range(1, 4):
        summed = summed + taps[offset : offset + 1] * padded[head, first + offset : first + offset + rows, :]
    return summed * sigmoid(summed)


def widen(padded, first, rows, raw):
    for head in range(padded.shape[0]):
        padded[head, first : first + rows, :] = raw[:, head_of(head)].astype(F32)


def unit_rows(key):
    return key * lax.rsqrt(jnp.sum(key * key, -1, keepdims=True) + EPSILON)


def part_of(chunk):
    return slice(chunk * CHUNK, (chunk + 1) * CHUNK)


def head_of(head):
    return slice(head * DK, (head + 1) * DK)


def chunk_rows(ref, heads, chunks):
    held = ref.shape[0]
    first = (pl.program_id(0) * heads) % held
    rows = ref[:heads, :]
    for at in range(heads, held, heads):
        rows = jnp.where(first == at, ref[at : at + heads, :], rows)
    return jnp.concatenate([rows[:, part_of(c)] for c in chunks], 0)


def square_iotas(rows=CHUNK):
    return (
        lax.broadcasted_iota(jnp.int32, (rows, CHUNK), 0),
        lax.broadcasted_iota(jnp.int32, (rows, CHUNK), 1),
    )


def log_fades(logit):
    rows, cols = square_iotas()
    decay = -(jnp.maximum(logit, 0.0) + jnp.log(1.0 + jnp.exp(-jnp.abs(logit))))
    return jnp.dot(
        decay, (rows <= cols).astype(F32), precision=lax.Precision.HIGHEST, preferred_element_type=F32
    )


def as_columns(blocks):
    rows = sum(block.shape[0] for block in blocks)
    return jnp.concatenate(list(blocks) + [jnp.zeros((CHUNK - rows, CHUNK), F32)], 0).T


def solved_packs(fade, beta, keys, key_cols, values):
    count = len(keys)
    rows, cols = square_iotas()
    strict = rows > cols
    differ = rows ^ cols
    columns = as_columns((fade, beta, beta * jnp.exp(fade)))
    inner = {id(key): mul(key, turned) for key, turned in zip(keys, key_cols)}
    lower = []
    for p in range(count):
        gap = columns[:, p : p + 1] - fade[p : p + 1, :]
        ratio = jnp.exp(jnp.where(strict, gap, -1e30))
        lower.append(columns[:, count + p : count + p + 1] * ratio * inner[id(keys[p])])

    small_rows, small_cols = square_iotas(SMALL)
    small_differ = small_rows ^ (small_cols % SMALL)
    place = small_cols // SMALL
    blocks = jnp.where(rows // SMALL == cols // SMALL, 1.0, 0.0)
    blocks16 = blocks.astype(BF16)

    def spread(small):
        return jnp.concatenate([small] * (CHUNK // SMALL), 0) * (blocks16 if small.dtype == BF16 else blocks)

    small = []
    for low in lower:
        held = low[:SMALL]
        for at in range(1, CHUNK // SMALL):
            held = jnp.where(place == at, low[at * SMALL : (at + 1) * SMALL], held)
        small.append(held)
    inverse = [
        jnp.where(small_differ == 0, 1.0, jnp.where(small_differ == 1, -one, 0.0)) for one in small
    ]
    size = 2
    while size < CHUNK:
        last = size == SMALL
        if last:
            band = (differ >= size) & (differ < 4 * size)
            inside = [jnp.where(band, low, 0.0).astype(BF16) for low in lower]
            inverse16 = [spread(one.astype(BF16)) for one in inverse]
            inverse = [spread(one) for one in inverse]
            wide16 = inverse16
        else:
            band = (small_differ >= size) & (small_differ < 4 * size)
            inside = [spread(jnp.where(band, one, 0.0).astype(BF16)) for one in small]
            inverse16 = [one.astype(BF16) for one in inverse]
            wide16 = [spread(one) for one in inverse16]
        step = [mul(inverse16[p], inside[p]).astype(BF16) for p in range(count)]
        both = [
            mul(step[p], jnp.concatenate([step[p] if last else spread(step[p]), wide16[p]], 1))
            for p in range(count)
        ]
        inverse = [inverse[p] - both[p][:, CHUNK:] for p in range(count)]
        partial = [inverse[p].astype(BF16) for p in range(count)]
        inverse = [
            inverse[p] + mul(both[p][:, :CHUNK], partial[p] if last else spread(partial[p]))
            for p in range(count)
        ]
        size *= 4

    solved = []
    for p in range(count):
        right = jnp.concatenate(
            [
                columns[:, count + p : count + p + 1] * values[p],
                columns[:, 2 * count + p : 2 * count + p + 1] * keys[p],
            ],
            1,
        )
        solved.append(mul(inverse[p], right))
    return solved


def later_kernel(
    key_ref, value_ref, key_taps, value_taps, beta_ref, decay_ref,
    solved_ref, moves_ref, unit_ref, key_padded, value_padded,
):
    length, width = key_ref.shape
    chunks = range(1, length // CHUNK)
    key_heads = width // DK
    heads = value_ref.shape[1] // DV
    repeat_by = heads // key_heads
    packs = [(chunk, head) for chunk in chunks for head in range(heads)]
    skip = CHUNK - 16
    count = length - CHUNK
    widen(key_padded, 0, count + 16, key_ref[skip:, :])
    widen(value_padded, 0, count + 16, value_ref[skip:, :])
    key, turned = {}, {}
    for j in range(key_heads):
        unit = unit_rows(conv_silu(key_padded, 13, count, key_taps, j))
        unit_ref[:, head_of(j)] = unit.astype(BF16)
        for chunk in chunks:
            key[chunk, j] = unit[part_of(chunk - 1)]
            turned[chunk, j] = key[chunk, j].T
    value = [conv_silu(value_padded, 13, count, value_taps, head) for head in range(heads)]
    fade = log_fades(chunk_rows(decay_ref, heads, chunks))
    solved = solved_packs(
        fade,
        sigmoid(chunk_rows(beta_ref, heads, chunks)),
        [key[chunk, head // repeat_by] for chunk, head in packs],
        [turned[chunk, head // repeat_by] for chunk, head in packs],
        [value[head][part_of(chunk - 1)] for chunk, head in packs],
    )
    tail = jnp.exp(fade[:, CHUNK - 1 : CHUNK] - fade)
    for pack, (chunk, head) in enumerate(packs):
        one = solved[pack].astype(BF16)
        solved_ref[head, part_of(chunk - 1), :] = one
        moves_ref[head, chunk - 1] = mul(
            turned[chunk, head // repeat_by] * tail[pack : pack + 1, :], one
        ).astype(BF16)


def states_kernel(
    key_ref, value_ref, key_before, value_before, key_taps, value_taps, beta_ref, decay_ref, moves_hbm,
    pairs_ref, unit_ref, solved_hbm, starts_hbm,
    key_padded, value_padded, moves_ref, solved_ref, starts_ref, in_sem, out_sem,
):
    heads, length = decay_ref.shape
    chunks = length // CHUNK
    key_heads = key_ref.shape[1] // DK
    repeat_by = heads // key_heads
    incoming = pltpu.make_async_copy(moves_hbm, moves_ref, in_sem)
    incoming.start()

    widen(key_padded, 5, 3, key_before[...])
    widen(key_padded, 8, CHUNK, key_ref[...])
    widen(value_padded, 5, 3, value_before[...])
    widen(value_padded, 8, CHUNK, value_ref[...])
    key, turned = [], []
    for j in range(key_heads):
        key.append(unit_rows(conv_silu(key_padded, 5, CHUNK, key_taps, j)))
        unit_ref[:, head_of(j)] = key[j].astype(BF16)
        turned.append(key[j].T)
    fade = log_fades(chunk_rows(decay_ref, heads, range(chunks)))
    solved = solved_packs(
        fade[:heads],
        sigmoid(beta_ref[:, :CHUNK]),
        [key[head // repeat_by] for head in range(heads)],
        [turned[head // repeat_by] for head in range(heads)],
        [conv_silu(value_padded, 5, CHUNK, value_taps, head) for head in range(heads)],
    )
    last = jnp.exp(fade[:, CHUNK - 1 : CHUNK])
    tail = jnp.exp(fade[:, CHUNK - 1 : CHUNK] - fade)
    rows, cols = square_iotas()
    identity = jnp.where(rows == cols, 1.0, 0.0)

    state = []
    for head in range(heads):
        one = solved[head].astype(BF16)
        solved_ref[head] = one
        moved = mul(turned[head // repeat_by] * tail[head : head + 1, :], one)
        state.append(
            jnp.concatenate([moved[:, :DV], last[head : head + 1, :] * identity - moved[:, DV:]], 1)
        )
    outgoing = [pltpu.make_async_copy(solved_ref, solved_hbm, out_sem.at[0])]
    outgoing[0].start()
    incoming.wait()
    for chunk in range(1, chunks):
        for head in range(heads):
            pack = chunk * heads + head
            start = state[head].astype(BF16)
            starts_ref[chunk - 1, head] = start
            moves = moves_ref[head, chunk - 1]
            moved = last[pack : pack + 1, :] * state[head] - mul(moves[:, DV:], start)
            state[head] = jnp.concatenate([moved[:, :DV] + moves[:, :DV].astype(F32), moved[:, DV:]], 1)
        outgoing.append(
            pltpu.make_async_copy(
                starts_ref.at[chunk - 1], starts_hbm.at[chunk - 1], out_sem.at[chunk]
            )
        )
        outgoing[-1].start()
    for head in range(heads):
        pairs_ref[head] = state[head].astype(BF16)
    for copy in outgoing:
        copy.wait()


def local_kernel(
    query_ref, query_before, query_taps, first_unit, later_unit, decay_ref,
    first_solved, later_solved, starts_ref, gate_ref, gain_ref,
    parts_ref, gated_ref, padded,
):
    length, width = query_ref.shape
    chunks = length // CHUNK
    key_heads = width // DK
    heads = first_solved.shape[0]
    repeat_by = heads // key_heads

    rows, cols = square_iotas()
    within = rows >= cols
    fade = log_fades(chunk_rows(decay_ref, heads, range(chunks)))
    columns = as_columns((fade, jnp.exp(fade)))
    widen(padded, 5, 3, query_before[...])
    widen(padded, 8, length, query_ref[...])
    query = [conv_silu(padded, 5, length, query_taps, j).astype(BF16) for j in range(key_heads)]
    for head in range(heads):
        gate = gate_ref[:, head_of(head)].astype(F32)
        gated_ref[:, head_of(head)] = (gate * sigmoid(gate) * gain_ref[...]).astype(BF16)
    for chunk in range(chunks):
        part = part_of(chunk)
        for j in range(key_heads):
            own = query[j][part]
            unit = first_unit[:, head_of(j)] if chunk == 0 else later_unit[part_of(chunk - 1), head_of(j)]
            inner = lax.dot_general(
                own, unit, (((1,), (1,)), ((), ())), preferred_element_type=F32
            )
            for head in range(j * repeat_by, (j + 1) * repeat_by):
                pack = chunk * heads + head
                gap = columns[:, pack : pack + 1] - fade[pack : pack + 1, :]
                scores = inner * jnp.exp(jnp.where(within, gap, -1e30))
                grown = columns[:, chunks * heads + pack : chunks * heads + pack + 1]
                if chunk == 0:
                    updates, wide = first_solved[head, :, :DV], first_solved[head, :, DV:]
                    fresh = jnp.concatenate([updates, -wide], 1)
                    carried = jnp.concatenate(
                        [jnp.zeros((CHUNK, DV), F32), grown * own.astype(F32)], 1
                    )
                else:
                    solved = later_solved[head, part_of(chunk - 1), :]
                    both = mul(jnp.concatenate([solved[:, DV:], own], 0), starts_ref[chunk - 1, head])
                    taken = both[:CHUNK]
                    fresh = jnp.concatenate(
                        [solved[:, :DV].astype(F32) - taken[:, :DV], -taken[:, DV:]], 1
                    )
                    carried = grown * both[CHUNK:]
                parts_ref[head, part, :] = (carried + mul(scores, fresh)).astype(BF16)


def columns_of(rows, width, first=0):
    return pl.BlockSpec((rows, width), lambda step: (0, step + first))


def in_vmem(mib):
    return pltpu.CompilerParams(vmem_limit_bytes=mib * 1024 * 1024)


def local_steps(raws, before, taps, beta_logit, decay_logit, gate_raw, norm_gain):
    length = raws[0].shape[0]
    key_heads = raws[0].shape[1] // DK
    value_heads = raws[2].shape[1] // DV
    repeat_by = value_heads // key_heads
    chunks = length // CHUNK
    beta, decay = beta_logit.T, decay_logit.T
    work = CHUNK * length * DV * value_heads
    hbm = pl.BlockSpec(memory_space=pltpu.HBM)

    def split(each):
        heads = each * repeat_by
        held = max(heads, math.gcd(8, value_heads))
        of_heads = lambda *shape: pl.BlockSpec((heads,) + shape, lambda step: (step,) + (0,) * len(shape))
        logits = pl.BlockSpec((held, length), lambda step: (step * heads // held, 0))
        return key_heads // each, each * DK, heads * DV, of_heads, logits

    each = math.gcd(4, key_heads)
    steps, narrow, wide, of_heads, logits = split(each)
    later = length - CHUNK
    solved, moves, later_unit = pl.pallas_call(
        later_kernel,
        grid=(steps,),
        in_specs=[
            columns_of(length, narrow), columns_of(length, wide),
            columns_of(4, narrow), columns_of(4, wide), logits, logits,
        ],
        out_specs=[
            of_heads(later, DV + DK), of_heads(chunks - 1, DK, DV + DK), columns_of(later, narrow),
        ],
        out_shape=[
            jax.ShapeDtypeStruct((value_heads, later, DV + DK), BF16),
            jax.ShapeDtypeStruct((value_heads, chunks - 1, DK, DV + DK), BF16),
            jax.ShapeDtypeStruct((later, key_heads * DK), BF16),
        ],
        scratch_shapes=[
            pltpu.VMEM((each, later + 16, DK), F32),
            pltpu.VMEM((each * repeat_by, later + 16, DV), F32),
        ],
        compiler_params=in_vmem(60),
        cost_estimate=pl.CostEstimate(flops=30 * work, bytes_accessed=0, transcendentals=0),
        name="later",
    )(raws[1], raws[2], taps[1], taps[2], beta, decay)

    narrow, wide = key_heads * DK, value_heads * DV
    whole = lambda shape, *at: pl.BlockSpec(shape, lambda step: at or (0,) * len(shape))
    pairs, first_unit, first_solved, starts = pl.pallas_call(
        states_kernel,
        grid=(1,),
        in_specs=[
            whole((CHUNK, narrow)), whole((CHUNK, wide)),
            whole((3, narrow), 0, repeat_by + 1), whole((3, wide)),
            whole(taps[1].shape), whole(taps[2].shape), whole(beta.shape), whole(decay.shape), hbm,
        ],
        out_specs=[whole((value_heads, DK, DV + DK)), whole((CHUNK, narrow)), hbm, hbm],
        out_shape=[
            jax.ShapeDtypeStruct((value_heads, DK, DV + DK), BF16),
            jax.ShapeDtypeStruct((CHUNK, narrow), BF16),
            jax.ShapeDtypeStruct((value_heads, CHUNK, DV + DK), BF16),
            jax.ShapeDtypeStruct((chunks - 1, value_heads, DK, DV + DK), BF16),
        ],
        scratch_shapes=[
            pltpu.VMEM((key_heads, 8 + CHUNK, DK), F32),
            pltpu.VMEM((value_heads, 8 + CHUNK, DV), F32),
            pltpu.VMEM(moves.shape, BF16),
            pltpu.VMEM((value_heads, CHUNK, DV + DK), BF16),
            pltpu.VMEM((chunks - 1, value_heads, DK, DV + DK), BF16),
            pltpu.SemaphoreType.DMA,
            pltpu.SemaphoreType.DMA((chunks,)),
        ],
        compiler_params=in_vmem(54),
        cost_estimate=pl.CostEstimate(flops=20 * work, bytes_accessed=0, transcendentals=0),
        name="states",
    )(raws[1], raws[2], before, before, taps[1], taps[2], beta, decay, moves)
    gain = norm_gain.reshape(1, DV)

    def local():
        steps, narrow, wide, of_heads, logits = split(math.gcd(2, key_heads))
        heads = wide // DV
        return pl.pallas_call(
            local_kernel,
            grid=(steps,),
            in_specs=[
                columns_of(length, narrow), columns_of(3, narrow, repeat_by * steps), columns_of(4, narrow),
                columns_of(CHUNK, narrow), columns_of(later, narrow), logits,
                of_heads(CHUNK, DV + DK), of_heads(later, DV + DK),
                pl.BlockSpec((chunks - 1, heads, DK, DV + DK), lambda step: (0, step, 0, 0)),
                columns_of(length, wide), whole(gain.shape),
            ],
            out_specs=[of_heads(length, DV + DK), columns_of(length, wide)],
            out_shape=[
                jax.ShapeDtypeStruct((value_heads, length, DV + DK), BF16),
                jax.ShapeDtypeStruct(gate_raw.shape, BF16),
            ],
            scratch_shapes=[pltpu.VMEM((narrow // DK, 8 + length, DK), F32)],
            compiler_params=in_vmem(60),
            cost_estimate=pl.CostEstimate(flops=12 * work, bytes_accessed=0, transcendentals=0),
            name="local",
        )(
            raws[0], before, taps[0], first_unit, later_unit, decay,
            first_solved, solved, starts, gate_raw, gain,
        )

    return pairs, local


def prefix_kernel(pairs_ref, prefix_ref, total_ref):
    count, heads = pairs_ref.shape[:2]
    running = [None] * heads
    for hop in range(count):
        for head in range(heads):
            now = pairs_ref[hop, head]
            if hop == 0:
                rows = lax.broadcasted_iota(jnp.int32, (DK, DV + DK), 0)
                cols = lax.broadcasted_iota(jnp.int32, (DK, DV + DK), 1)
                prefix_ref[hop, head] = jnp.where(cols == rows + DV, 1.0, 0.0).astype(BF16)
                running[head] = now.astype(F32)
            else:
                before = running[head].astype(BF16)
                prefix_ref[hop, head] = before
                own = jnp.concatenate([now[:, :DV].astype(F32), jnp.zeros((DK, DK), F32)], 1)
                running[head] = own + mul(now[:, DV:], before)
    for head in range(heads):
        total_ref[head] = running[head][:, : total_ref.shape[2]].astype(BF16)


def apply_kernel(prefix_ref, start_ref, starts_ref):
    count, heads = prefix_ref.shape[:2]
    for hop in range(count):
        for head in range(heads):
            starts_ref[hop, head] = (
                prefix_ref[hop, head, :, :DV].astype(F32)
                + mul(prefix_ref[hop, head, :, DV:], start_ref[head])
            ).astype(BF16)


def shifted(value, axis, by):
    count = lax.axis_size(axis)
    return lax.ppermute(value, axis, [(i, i + by) for i in range(count - by)])


def group_start(total, axis, group):
    groups = lax.axis_size(axis) // group
    running = shifted(total, axis, group)
    by = 1
    while by < groups - 1:
        earlier = shifted(running, axis, by * group)
        product = jnp.einsum("bkl,blv->bkv", running[..., DV:], earlier, preferred_element_type=F32)
        own = jnp.pad(running[..., :DV], ((0, 0), (0, 0), (0, DK)))
        running = (product + own.astype(F32)).astype(BF16)
        by *= 2
    return running[..., :DV]


def starts_of(pairs, axis, beside):
    size = lax.axis_size(axis)
    heads = pairs.shape[0]
    group = math.gcd(math.gcd(size, heads), GROUP)
    groups = [[g * group + i for i in range(group)] for g in range(size // group)]
    each = heads // group
    wide = DV if size // group == 2 else DV + DK
    by_head = lax.all_to_all(pairs, axis, 0, 0, axis_index_groups=groups, tiled=True)
    by_head, done = lax.optimization_barrier((by_head, beside()))
    prefix, total = pl.pallas_call(
        prefix_kernel,
        out_shape=[
            jax.ShapeDtypeStruct((group, each, DK, DV + DK), BF16),
            jax.ShapeDtypeStruct((each, DK, wide), BF16),
        ],
        compiler_params=in_vmem(16),
        name="prefix",
    )(by_head.reshape(group, each, DK, DV + DK))
    starts = pl.pallas_call(
        apply_kernel,
        out_shape=jax.ShapeDtypeStruct((group, each, DK, DV), BF16),
        compiler_params=in_vmem(16),
        name="apply",
    )(prefix, group_start(total, axis, group))
    starts = lax.all_to_all(
        starts.reshape(heads, DK, DV), axis, 0, 0, axis_index_groups=groups, tiled=True
    )
    return starts, done


def project_kernel(
    place_ref, starts_ref, parts_hbm, gated_hbm, weight_hbm, away_ref, own_ref,
    parts_ref, gated_ref, weight_ref, total, in_sem,
):
    heads, length = parts_ref.shape[:2]
    depth, width = weight_ref.shape
    each = min(HEADS_AT_ONCE, heads)
    block = min(512, width)
    groups = heads // each
    copies = []
    for g in range(groups):
        here, lanes = pl.ds(g * each, each), pl.ds(g * each * DV, each * DV)
        copies.append(
            [
                pltpu.make_async_copy(parts_hbm.at[here], parts_ref.at[here], in_sem.at[0, g]),
                pltpu.make_async_copy(gated_hbm.at[:, lanes], gated_ref.at[:, lanes], in_sem.at[1, g]),
                pltpu.make_async_copy(weight_hbm.at[lanes], weight_ref.at[lanes], in_sem.at[2, g]),
            ]
        )
        for copy in copies[g]:
            copy.start()
    for g in range(groups):
        copies[g][0].wait()
        copies[g][1].wait()
        normed = []
        for head in range(g * each, (g + 1) * each):
            core = parts_ref[head, :, :DV].astype(F32) + mul(
                parts_ref[head, :, DV:], starts_ref[head]
            )
            scale = lax.rsqrt(jnp.mean(core * core, -1, keepdims=True) + EPSILON)
            normed.append((core * scale * gated_ref[:, head_of(head)].astype(F32)).astype(BF16))
        normed = jnp.concatenate(normed, 1)
        copies[g][2].wait()
        for at in range(0, width, block):
            added = jnp.dot(
                normed, weight_ref[g * each * DV : (g + 1) * each * DV, at : at + block],
                preferred_element_type=F32,
            )
            if g > 0:
                added = added + total[:, at : at + block]
            if g < groups - 1:
                total[:, at : at + block] = added
            elif own_ref is None:
                away_ref[:, at : at + block] = added.astype(BF16)
            else:
                first = place_ref[0] == 0
                low, high = added[: length // 2], added[length // 2 :]
                own_ref[:, at : at + block] = jnp.where(first, low, high).astype(BF16)
                away_ref[:, at : at + block] = jnp.where(first, high, low).astype(BF16)


def whole_kernel(place_ref, starts_ref, parts_hbm, gated_hbm, weight_hbm, out_ref, *scratch):
    project_kernel(place_ref, starts_ref, parts_hbm, gated_hbm, weight_hbm, out_ref, None, *scratch)


def projected(parts, starts, gated, out_weight, axis):
    heads, length = parts.shape[:2]
    depth, width = out_weight.shape
    halves = lax.axis_size(axis) == 2
    hbm = pl.BlockSpec(memory_space=pltpu.HBM)
    vmem = pl.BlockSpec(memory_space=pltpu.VMEM)
    here = lax.axis_index(axis).astype(jnp.int32).reshape(1)
    out = jax.ShapeDtypeStruct((length // 2 if halves else length, width), BF16)
    partial = pl.pallas_call(
        project_kernel if halves else whole_kernel,
        in_specs=[pl.BlockSpec(memory_space=pltpu.SMEM), vmem, hbm, hbm, hbm],
        out_specs=[vmem, vmem] if halves else vmem,
        out_shape=[out, out] if halves else out,
        scratch_shapes=[
            pltpu.VMEM(parts.shape, BF16),
            pltpu.VMEM(gated.shape, BF16),
            pltpu.VMEM(out_weight.shape, BF16),
            pltpu.VMEM((length, width), F32),
            pltpu.SemaphoreType.DMA((3, heads // min(HEADS_AT_ONCE, heads))),
        ],
        compiler_params=in_vmem(60),
        name="project",
    )(here, starts, parts, gated, out_weight)
    if not halves:
        return lax.psum_scatter(partial, axis, scatter_dimension=0, tiled=True)
    away, own = partial
    other = lax.ppermute(away, axis, [(0, 1), (1, 0)])
    return (own.astype(F32) + other.astype(F32)).astype(BF16)


def tails_kernel(value_hbm, query_hbm, key_hbm, out_ref, value_ref, query_ref, key_ref, sem):
    pairs = ((value_hbm, value_ref), (query_hbm, query_ref), (key_hbm, key_ref))
    copies = [
        pltpu.make_async_copy(source.at[pl.ds(source.shape[0] - 16, 16)], held, sem.at[i])
        for i, (source, held) in enumerate(pairs)
    ]
    for copy in copies:
        copy.start()
    at = 0
    for copy, (_, held) in zip(copies, pairs):
        copy.wait()
        width = held.shape[1]
        out_ref[:, at : at + width] = held[...].astype(F32)[13:16].astype(BF16)
        at += width


def tails(raws):
    order = (raws[2], raws[0], raws[1])
    width = sum(raw.shape[1] for raw in order)
    return pl.pallas_call(
        tails_kernel,
        in_specs=[pl.BlockSpec(memory_space=pltpu.HBM)] * 3,
        out_shape=jax.ShapeDtypeStruct((3, width), BF16),
        scratch_shapes=[pltpu.VMEM((16, raw.shape[1]), BF16) for raw in order]
        + [pltpu.SemaphoreType.DMA((3,))],
        compiler_params=in_vmem(60),
        name="tails",
    )(*order)


def shards(
    query_raw, key_raw, value_raw, gate_raw, query_taps, key_taps, value_taps,
    beta_logit, decay_logit, norm_gain, out_weight,
):
    raws = (query_raw, key_raw, value_raw)
    before = shifted(tails(raws), "seq", 1)
    pairs, local = local_steps(
        raws, before, (query_taps, key_taps, value_taps), beta_logit, decay_logit, gate_raw, norm_gain
    )
    starts, (parts, gated) = starts_of(pairs, "seq", local)
    return projected(parts, starts, gated, out_weight, "head")


def solution(mesh):
    placed = (
        P("seq", "head"), P("seq", "head"), P("seq", "head"), P("seq", "head"),
        P(None, "head"), P(None, "head"), P(None, "head"),
        P("seq", "head"), P("seq", "head"), P(), P("head", None),
    )
    return jax.shard_map(
        shards, mesh=mesh, in_specs=placed, out_specs=P(("seq", "head"), None), check_vma=False
    )
```

```python
import math

import jax
import jax.numpy as jnp
from jax import lax
from jax.experimental import pallas as pl
from jax.experimental.pallas import tpu as pltpu
from jax.sharding import PartitionSpec as P

DK = 128
DV = 128
CHUNK = 128
SMALL = 32
GROUP = 8
HEADS_AT_ONCE = 4
EPSILON = 1e-06
F32 = jnp.float32
BF16 = jnp.bfloat16


def mul(left, right):
    return jnp.dot(left.astype(BF16), right.astype(BF16), preferred_element_type=F32)


def sigmoid(x):
    return 0.5 + 0.5 * jnp.tanh(0.5 * x)


def conv_silu(padded, first, rows, taps_ref, head):
    taps = taps_ref[:, head_of(head)]
    summed = taps[0:1] * padded[head, first : first + rows, :]
    for offset in range(1, 4):
        summed = summed + taps[offset : offset + 1] * padded[head, first + offset : first + offset + rows, :]
    return summed * sigmoid(summed)


def widen(padded, first, rows, raw):
    for head in range(padded.shape[0]):
        padded[head, first : first + rows, :] = raw[:, head_of(head)].astype(F32)


def unit_rows(key):
    return key * lax.rsqrt(jnp.sum(key * key, -1, keepdims=True) + EPSILON)


def part_of(chunk):
    return slice(chunk * CHUNK, (chunk + 1) * CHUNK)


def head_of(head):
    return slice(head * DK, (head + 1) * DK)


def chunk_rows(ref, heads, chunks):
    held = ref.shape[0]
    first = (pl.program_id(0) * heads) % held
    rows = ref[:heads, :]
    for at in range(heads, held, heads):
        rows = jnp.where(first == at, ref[at : at + heads, :], rows)
    return jnp.concatenate([rows[:, part_of(c)] for c in chunks], 0)


def square_iotas(rows=CHUNK):
    return (
        lax.broadcasted_iota(jnp.int32, (rows, CHUNK), 0),
        lax.broadcasted_iota(jnp.int32, (rows, CHUNK), 1),
    )


def log_fades(logit):
    rows, cols = square_iotas()
    decay = -(jnp.maximum(logit, 0.0) + jnp.log(1.0 + jnp.exp(-jnp.abs(logit))))
    return jnp.dot(
        decay, (rows <= cols).astype(F32), precision=lax.Precision.HIGHEST, preferred_element_type=F32
    )


def as_columns(blocks):
    rows = sum(block.shape[0] for block in blocks)
    return jnp.concatenate(list(blocks) + [jnp.zeros((CHUNK - rows, CHUNK), F32)], 0).T


def solved_packs(fade, beta, keys, key_cols, values):
    count = len(keys)
    rows, cols = square_iotas()
    strict = rows > cols
    differ = rows ^ cols
    columns = as_columns((fade, beta, beta * jnp.exp(fade)))
    inner = {id(key): mul(key, turned) for key, turned in zip(keys, key_cols)}
    lower = []
    for p in range(count):
        gap = columns[:, p : p + 1] - fade[p : p + 1, :]
        ratio = jnp.exp(jnp.where(strict, gap, -1e30))
        lower.append(columns[:, count + p : count + p + 1] * ratio * inner[id(keys[p])])

    small_rows, small_cols = square_iotas(SMALL)
    small_differ = small_rows ^ (small_cols % SMALL)
    place = small_cols // SMALL
    blocks = jnp.where(rows // SMALL == cols // SMALL, 1.0, 0.0)
    blocks16 = blocks.astype(BF16)

    def spread(small):
        return jnp.concatenate([small] * (CHUNK // SMALL), 0) * (blocks16 if small.dtype == BF16 else blocks)

    small = []
    for low in lower:
        held = low[:SMALL]
        for at in range(1, CHUNK // SMALL):
            held = jnp.where(place == at, low[at * SMALL : (at + 1) * SMALL], held)
        small.append(held)
    inverse = [
        jnp.where(small_differ == 0, 1.0, jnp.where(small_differ == 1, -one, 0.0)) for one in small
    ]
    size = 2
    while size < CHUNK:
        last = size == SMALL
        if last:
            band = (differ >= size) & (differ < 4 * size)
            inside = [jnp.where(band, low, 0.0).astype(BF16) for low in lower]
            inverse16 = [spread(one.astype(BF16)) for one in inverse]
            inverse = [spread(one) for one in inverse]
            wide16 = inverse16
        else:
            band = (small_differ >= size) & (small_differ < 4 * size)
            inside = [spread(jnp.where(band, one, 0.0).astype(BF16)) for one in small]
            inverse16 = [one.astype(BF16) for one in inverse]
            wide16 = [spread(one) for one in inverse16]
        step = [mul(inverse16[p], inside[p]).astype(BF16) for p in range(count)]
        both = [
            mul(step[p], jnp.concatenate([step[p] if last else spread(step[p]), wide16[p]], 1))
            for p in range(count)
        ]
        inverse = [inverse[p] - both[p][:, CHUNK:] for p in range(count)]
        partial = [inverse[p].astype(BF16) for p in range(count)]
        inverse = [
            inverse[p] + mul(both[p][:, :CHUNK], partial[p] if last else spread(partial[p]))
            for p in range(count)
        ]
        size *= 4

    solved = []
    for p in range(count):
        right = jnp.concatenate(
            [
                columns[:, count + p : count + p + 1] * values[p],
                columns[:, 2 * count + p : 2 * count + p + 1] * keys[p],
            ],
            1,
        )
        solved.append(mul(inverse[p], right))
    return solved


def later_kernel(
    key_ref, value_ref, key_taps, value_taps, beta_ref, decay_ref,
    solved_ref, moves_ref, unit_ref, key_padded, value_padded,
):
    length, width = key_ref.shape
    chunks = range(1, length // CHUNK)
    key_heads = width // DK
    heads = value_ref.shape[1] // DV
    repeat_by = heads // key_heads
    packs = [(chunk, head) for chunk in chunks for head in range(heads)]
    skip = CHUNK - 16
    count = length - CHUNK
    widen(key_padded, 0, count + 16, key_ref[skip:, :])
    widen(value_padded, 0, count + 16, value_ref[skip:, :])
    key, turned = {}, {}
    for j in range(key_heads):
        unit = unit_rows(conv_silu(key_padded, 13, count, key_taps, j))
        unit_ref[:, head_of(j)] = unit.astype(BF16)
        for chunk in chunks:
            key[chunk, j] = unit[part_of(chunk - 1)]
            turned[chunk, j] = key[chunk, j].T
    value = [conv_silu(value_padded, 13, count, value_taps, head) for head in range(heads)]
    fade = log_fades(chunk_rows(decay_ref, heads, chunks))
    solved = solved_packs(
        fade,
        sigmoid(chunk_rows(beta_ref, heads, chunks)),
        [key[chunk, head // repeat_by] for chunk, head in packs],
        [turned[chunk, head // repeat_by] for chunk, head in packs],
        [value[head][part_of(chunk - 1)] for chunk, head in packs],
    )
    tail = jnp.exp(fade[:, CHUNK - 1 : CHUNK] - fade)
    for pack, (chunk, head) in enumerate(packs):
        one = solved[pack].astype(BF16)
        solved_ref[head, part_of(chunk - 1), :] = one
        moves_ref[head, chunk - 1] = mul(
            turned[chunk, head // repeat_by] * tail[pack : pack + 1, :], one
        ).astype(BF16)


def states_kernel(
    key_ref, value_ref, key_before, value_before, key_taps, value_taps, beta_ref, decay_ref, moves_hbm,
    pairs_ref, unit_ref, solved_hbm, starts_hbm,
    key_padded, value_padded, moves_ref, solved_ref, starts_ref, in_sem, out_sem,
):
    heads, length = decay_ref.shape
    chunks = length // CHUNK
    key_heads = key_ref.shape[1] // DK
    repeat_by = heads // key_heads
    incoming = pltpu.make_async_copy(moves_hbm, moves_ref, in_sem)
    incoming.start()

    widen(key_padded, 5, 3, key_before[...])
    widen(key_padded, 8, CHUNK, key_ref[...])
    widen(value_padded, 5, 3, value_before[...])
    widen(value_padded, 8, CHUNK, value_ref[...])
    key, turned = [], []
    for j in range(key_heads):
        key.append(unit_rows(conv_silu(key_padded, 5, CHUNK, key_taps, j)))
        unit_ref[:, head_of(j)] = key[j].astype(BF16)
        turned.append(key[j].T)
    fade = log_fades(chunk_rows(decay_ref, heads, range(chunks)))
    solved = solved_packs(
        fade[:heads],
        sigmoid(beta_ref[:, :CHUNK]),
        [key[head // repeat_by] for head in range(heads)],
        [turned[head // repeat_by] for head in range(heads)],
        [conv_silu(value_padded, 5, CHUNK, value_taps, head) for head in range(heads)],
    )
    last = jnp.exp(fade[:, CHUNK - 1 : CHUNK])
    tail = jnp.exp(fade[:, CHUNK - 1 : CHUNK] - fade)
    rows, cols = square_iotas()
    identity = jnp.where(rows == cols, 1.0, 0.0)

    state = []
    for head in range(heads):
        one = solved[head].astype(BF16)
        solved_ref[head] = one
        moved = mul(turned[head // repeat_by] * tail[head : head + 1, :], one)
        state.append(
            jnp.concatenate([moved[:, :DV], last[head : head + 1, :] * identity - moved[:, DV:]], 1)
        )
    outgoing = [pltpu.make_async_copy(solved_ref, solved_hbm, out_sem.at[0])]
    outgoing[0].start()
    incoming.wait()
    for chunk in range(1, chunks):
        for head in range(heads):
            pack = chunk * heads + head
            start = state[head].astype(BF16)
            starts_ref[chunk - 1, head] = start
            moves = moves_ref[head, chunk - 1]
            moved = last[pack : pack + 1, :] * state[head] - mul(moves[:, DV:], start)
            state[head] = jnp.concatenate([moved[:, :DV] + moves[:, :DV].astype(F32), moved[:, DV:]], 1)
        outgoing.append(
            pltpu.make_async_copy(
                starts_ref.at[chunk - 1], starts_hbm.at[chunk - 1], out_sem.at[chunk]
            )
        )
        outgoing[-1].start()
    for head in range(heads):
        pairs_ref[head] = state[head].astype(BF16)
    for copy in outgoing:
        copy.wait()


def local_kernel(
    query_ref, query_before, query_taps, first_unit, later_unit, decay_ref,
    first_solved, later_solved, starts_ref, gate_ref, gain_ref,
    parts_ref, gated_ref, padded,
):
    length, width = query_ref.shape
    chunks = length // CHUNK
    key_heads = width // DK
    heads = first_solved.shape[0]
    repeat_by = heads // key_heads

    rows, cols = square_iotas()
    within = rows >= cols
    fade = log_fades(chunk_rows(decay_ref, heads, range(chunks)))
    columns = as_columns((fade, jnp.exp(fade)))
    widen(padded, 5, 3, query_before[...])
    widen(padded, 8, length, query_ref[...])
    query = [conv_silu(padded, 5, length, query_taps, j).astype(BF16) for j in range(key_heads)]
    for head in range(heads):
        gate = gate_ref[:, head_of(head)].astype(F32)
        gated_ref[:, head_of(head)] = (gate * sigmoid(gate) * gain_ref[...]).astype(BF16)
    for chunk in range(chunks):
        part = part_of(chunk)
        for j in range(key_heads):
            own = query[j][part]
            unit = first_unit[:, head_of(j)] if chunk == 0 else later_unit[part_of(chunk - 1), head_of(j)]
            inner = lax.dot_general(
                own, unit, (((1,), (1,)), ((), ())), preferred_element_type=F32
            )
            for head in range(j * repeat_by, (j + 1) * repeat_by):
                pack = chunk * heads + head
                gap = columns[:, pack : pack + 1] - fade[pack : pack + 1, :]
                scores = inner * jnp.exp(jnp.where(within, gap, -1e30))
                grown = columns[:, chunks * heads + pack : chunks * heads + pack + 1]
                if chunk == 0:
                    updates, wide = first_solved[head, :, :DV], first_solved[head, :, DV:]
                    fresh = jnp.concatenate([updates, -wide], 1)
                    carried = jnp.concatenate(
                        [jnp.zeros((CHUNK, DV), F32), grown * own.astype(F32)], 1
                    )
                else:
                    solved = later_solved[head, part_of(chunk - 1), :]
                    both = mul(jnp.concatenate([solved[:, DV:], own], 0), starts_ref[chunk - 1, head])
                    taken = both[:CHUNK]
                    fresh = jnp.concatenate(
                        [solved[:, :DV].astype(F32) - taken[:, :DV], -taken[:, DV:]], 1
                    )
                    carried = grown * both[CHUNK:]
                parts_ref[head, part, :] = (carried + mul(scores, fresh)).astype(BF16)


def columns_of(rows, width, first=0):
    return pl.BlockSpec((rows, width), lambda step: (0, step + first))


def in_vmem(mib):
    return pltpu.CompilerParams(vmem_limit_bytes=mib * 1024 * 1024)


def local_steps(raws, before, taps, beta_logit, decay_logit, gate_raw, norm_gain):
    length = raws[0].shape[0]
    key_heads = raws[0].shape[1] // DK
    value_heads = raws[2].shape[1] // DV
    repeat_by = value_heads // key_heads
    chunks = length // CHUNK
    beta, decay = beta_logit.T, decay_logit.T
    work = CHUNK * length * DV * value_heads
    hbm = pl.BlockSpec(memory_space=pltpu.HBM)

    def split(each):
        heads = each * repeat_by
        held = max(heads, math.gcd(8, value_heads))
        of_heads = lambda *shape: pl.BlockSpec((heads,) + shape, lambda step: (step,) + (0,) * len(shape))
        logits = pl.BlockSpec((held, length), lambda step: (step * heads // held, 0))
        return key_heads // each, each * DK, heads * DV, of_heads, logits

    each = math.gcd(4, key_heads)
    steps, narrow, wide, of_heads, logits = split(each)
    later = length - CHUNK
    solved, moves, later_unit = pl.pallas_call(
        later_kernel,
        grid=(steps,),
        in_specs=[
            columns_of(length, narrow), columns_of(length, wide),
            columns_of(4, narrow), columns_of(4, wide), logits, logits,
        ],
        out_specs=[
            of_heads(later, DV + DK), of_heads(chunks - 1, DK, DV + DK), columns_of(later, narrow),
        ],
        out_shape=[
            jax.ShapeDtypeStruct((value_heads, later, DV + DK), BF16),
            jax.ShapeDtypeStruct((value_heads, chunks - 1, DK, DV + DK), BF16),
            jax.ShapeDtypeStruct((later, key_heads * DK), BF16),
        ],
        scratch_shapes=[
            pltpu.VMEM((each, later + 16, DK), F32),
            pltpu.VMEM((each * repeat_by, later + 16, DV), F32),
        ],
        compiler_params=in_vmem(60),
        cost_estimate=pl.CostEstimate(flops=30 * work, bytes_accessed=0, transcendentals=0),
        name="later",
    )(raws[1], raws[2], taps[1], taps[2], beta, decay)

    narrow, wide = key_heads * DK, value_heads * DV
    whole = lambda shape, *at: pl.BlockSpec(shape, lambda step: at or (0,) * len(shape))
    pairs, first_unit, first_solved, starts = pl.pallas_call(
        states_kernel,
        grid=(1,),
        in_specs=[
            whole((CHUNK, narrow)), whole((CHUNK, wide)),
            whole((3, narrow), 0, repeat_by + 1), whole((3, wide)),
            whole(taps[1].shape), whole(taps[2].shape), whole(beta.shape), whole(decay.shape), hbm,
        ],
        out_specs=[whole((value_heads, DK, DV + DK)), whole((CHUNK, narrow)), hbm, hbm],
        out_shape=[
            jax.ShapeDtypeStruct((value_heads, DK, DV + DK), BF16),
            jax.ShapeDtypeStruct((CHUNK, narrow), BF16),
            jax.ShapeDtypeStruct((value_heads, CHUNK, DV + DK), BF16),
            jax.ShapeDtypeStruct((chunks - 1, value_heads, DK, DV + DK), BF16),
        ],
        scratch_shapes=[
            pltpu.VMEM((key_heads, 8 + CHUNK, DK), F32),
            pltpu.VMEM((value_heads, 8 + CHUNK, DV), F32),
            pltpu.VMEM(moves.shape, BF16),
            pltpu.VMEM((value_heads, CHUNK, DV + DK), BF16),
            pltpu.VMEM((chunks - 1, value_heads, DK, DV + DK), BF16),
            pltpu.SemaphoreType.DMA,
            pltpu.SemaphoreType.DMA((chunks,)),
        ],
        compiler_params=in_vmem(54),
        cost_estimate=pl.CostEstimate(flops=20 * work, bytes_accessed=0, transcendentals=0),
        name="states",
    )(raws[1], raws[2], before, before, taps[1], taps[2], beta, decay, moves)
    gain = norm_gain.reshape(1, DV)

    def local():
        steps, narrow, wide, of_heads, logits = split(math.gcd(2, key_heads))
        heads = wide // DV
        return pl.pallas_call(
            local_kernel,
            grid=(steps,),
            in_specs=[
                columns_of(length, narrow), columns_of(3, narrow, repeat_by * steps), columns_of(4, narrow),
                columns_of(CHUNK, narrow), columns_of(later, narrow), logits,
                of_heads(CHUNK, DV + DK), of_heads(later, DV + DK),
                pl.BlockSpec((chunks - 1, heads, DK, DV + DK), lambda step: (0, step, 0, 0)),
                columns_of(length, wide), whole(gain.shape),
            ],
            out_specs=[of_heads(length, DV + DK), columns_of(length, wide)],
            out_shape=[
                jax.ShapeDtypeStruct((value_heads, length, DV + DK), BF16),
                jax.ShapeDtypeStruct(gate_raw.shape, BF16),
            ],
            scratch_shapes=[pltpu.VMEM((narrow // DK, 8 + length, DK), F32)],
            compiler_params=in_vmem(60),
            cost_estimate=pl.CostEstimate(flops=12 * work, bytes_accessed=0, transcendentals=0),
            name="local",
        )(
            raws[0], before, taps[0], first_unit, later_unit, decay,
            first_solved, solved, starts, gate_raw, gain,
        )

    return pairs, local


def prefix_kernel(pairs_ref, prefix_ref, total_ref):
    count, heads = pairs_ref.shape[:2]
    running = [None] * heads
    for hop in range(count):
        for head in range(heads):
            now = pairs_ref[hop, head]
            if hop == 0:
                rows = lax.broadcasted_iota(jnp.int32, (DK, DV + DK), 0)
                cols = lax.broadcasted_iota(jnp.int32, (DK, DV + DK), 1)
                prefix_ref[hop, head] = jnp.where(cols == rows + DV, 1.0, 0.0).astype(BF16)
                running[head] = now.astype(F32)
            else:
                before = running[head].astype(BF16)
                prefix_ref[hop, head] = before
                own = jnp.concatenate([now[:, :DV].astype(F32), jnp.zeros((DK, DK), F32)], 1)
                running[head] = own + mul(now[:, DV:], before)
    for head in range(heads):
        total_ref[head] = running[head][:, : total_ref.shape[2]].astype(BF16)


def apply_kernel(prefix_ref, start_ref, starts_ref):
    count, heads = prefix_ref.shape[:2]
    for hop in range(count):
        for head in range(heads):
            starts_ref[hop, head] = (
                prefix_ref[hop, head, :, :DV].astype(F32)
                + mul(prefix_ref[hop, head, :, DV:], start_ref[head])
            ).astype(BF16)


def shifted(value, axis, by):
    count = lax.axis_size(axis)
    return lax.ppermute(value, axis, [(i, i + by) for i in range(count - by)])


def group_start(total, axis, group):
    groups = lax.axis_size(axis) // group
    running = shifted(total, axis, group)
    by = 1
    while by < groups - 1:
        earlier = shifted(running, axis, by * group)
        product = jnp.einsum("bkl,blv->bkv", running[..., DV:], earlier, preferred_element_type=F32)
        own = jnp.pad(running[..., :DV], ((0, 0), (0, 0), (0, DK)))
        running = (product + own.astype(F32)).astype(BF16)
        by *= 2
    return running[..., :DV]


def starts_of(pairs, axis, beside):
    size = lax.axis_size(axis)
    heads = pairs.shape[0]
    group = math.gcd(math.gcd(size, heads), GROUP)
    groups = [[g * group + i for i in range(group)] for g in range(size // group)]
    each = heads // group
    wide = DV if size // group == 2 else DV + DK
    by_head = lax.all_to_all(pairs, axis, 0, 0, axis_index_groups=groups, tiled=True)
    by_head, done = lax.optimization_barrier((by_head, beside()))
    prefix, total = pl.pallas_call(
        prefix_kernel,
        out_shape=[
            jax.ShapeDtypeStruct((group, each, DK, DV + DK), BF16),
            jax.ShapeDtypeStruct((each, DK, wide), BF16),
        ],
        compiler_params=in_vmem(16),
        name="prefix",
    )(by_head.reshape(group, each, DK, DV + DK))
    starts = pl.pallas_call(
        apply_kernel,
        out_shape=jax.ShapeDtypeStruct((group, each, DK, DV), BF16),
        compiler_params=in_vmem(16),
        name="apply",
    )(prefix, group_start(total, axis, group))
    starts = lax.all_to_all(
        starts.reshape(heads, DK, DV), axis, 0, 0, axis_index_groups=groups, tiled=True
    )
    return starts, done


def project_kernel(
    place_ref, starts_ref, gated_ref, parts_hbm, weight_hbm, away_ref, own_ref,
    parts_ref, weight_ref, total, parts_sem, weight_sem,
):
    heads, length = parts_ref.shape[:2]
    width = weight_ref.shape[1]
    each = min(HEADS_AT_ONCE, heads)
    block = min(512, width)
    groups = heads // each

    def parts(g):
        here = pl.ds(g * each, each)
        return pltpu.make_async_copy(parts_hbm.at[here], parts_ref.at[here], parts_sem.at[g])

    def weights(g):
        rows = pl.ds(g * each * DV, each * DV)
        return pltpu.make_async_copy(weight_hbm.at[rows], weight_ref.at[rows], weight_sem.at[g])

    def normed_group(g):
        normed = []
        for head in range(g * each, (g + 1) * each):
            core = parts_ref[head, :, :DV].astype(F32) + mul(
                parts_ref[head, :, DV:], starts_ref[head]
            )
            scale = lax.rsqrt(jnp.mean(core * core, -1, keepdims=True) + EPSILON)
            normed.append((core * scale * gated_ref[:, head_of(head)].astype(F32)).astype(BF16))
        return jnp.concatenate(normed, 1)

    parts(0).start()
    weights(0).start()
    parts(0).wait()
    if groups > 1:
        parts(1).start()
    following = normed_group(0)
    for g in range(groups):
        weights(g).wait()
        if g + 1 < groups:
            weights(g + 1).start()
            parts(g + 1).wait()
        if g + 2 < groups:
            parts(g + 2).start()
        normed = following
        if g + 1 < groups:
            following = normed_group(g + 1)
        for at in range(0, width, block):
            added = jnp.dot(
                normed, weight_ref[g * each * DV : (g + 1) * each * DV, at : at + block],
                preferred_element_type=F32,
            )
            if g > 0:
                added = added + total[:, at : at + block]
            if g < groups - 1:
                total[:, at : at + block] = added
            elif own_ref is None:
                away_ref[:, at : at + block] = added.astype(BF16)
            else:
                first = place_ref[0] == 0
                low, high = added[: length // 2], added[length // 2 :]
                own_ref[:, at : at + block] = jnp.where(first, low, high).astype(BF16)
                away_ref[:, at : at + block] = jnp.where(first, high, low).astype(BF16)


def whole_kernel(place_ref, starts_ref, gated_ref, parts_hbm, weight_hbm, out_ref, *scratch):
    project_kernel(place_ref, starts_ref, gated_ref, parts_hbm, weight_hbm, out_ref, None, *scratch)


def projected(parts, starts, gated, out_weight, axis):
    heads, length = parts.shape[:2]
    width = out_weight.shape[1]
    halves = lax.axis_size(axis) == 2
    vmem = pl.BlockSpec(memory_space=pltpu.VMEM)
    hbm = pl.BlockSpec(memory_space=pltpu.HBM)
    groups = heads // min(HEADS_AT_ONCE, heads)
    here = lax.axis_index(axis).astype(jnp.int32).reshape(1)
    out = jax.ShapeDtypeStruct((length // 2 if halves else length, width), BF16)
    partial = pl.pallas_call(
        project_kernel if halves else whole_kernel,
        in_specs=[pl.BlockSpec(memory_space=pltpu.SMEM), vmem, vmem, hbm, hbm],
        out_specs=[vmem, vmem] if halves else vmem,
        out_shape=[out, out] if halves else out,
        scratch_shapes=[
            pltpu.VMEM(parts.shape, BF16),
            pltpu.VMEM(out_weight.shape, BF16),
            pltpu.VMEM((length, width), F32),
            pltpu.SemaphoreType.DMA((groups,)),
            pltpu.SemaphoreType.DMA((groups,)),
        ],
        compiler_params=in_vmem(50),
        name="project",
    )(here, starts, gated, parts, out_weight)
    if not halves:
        return lax.psum_scatter(partial, axis, scatter_dimension=0, tiled=True)
    away, own = partial
    other = lax.ppermute(away, axis, [(0, 1), (1, 0)])
    return (own.astype(F32) + other.astype(F32)).astype(BF16)


def tails_kernel(value_hbm, query_hbm, key_hbm, out_ref, value_ref, query_ref, key_ref, sem):
    pairs = ((value_hbm, value_ref), (query_hbm, query_ref), (key_hbm, key_ref))
    copies = [
        pltpu.make_async_copy(source.at[pl.ds(source.shape[0] - 16, 16)], held, sem.at[i])
        for i, (source, held) in enumerate(pairs)
    ]
    for copy in copies:
        copy.start()
    at = 0
    for copy, (_, held) in zip(copies, pairs):
        copy.wait()
        width = held.shape[1]
        out_ref[:, at : at + width] = held[...].astype(F32)[13:16].astype(BF16)
        at += width


def tails(raws):
    order = (raws[2], raws[0], raws[1])
    width = sum(raw.shape[1] for raw in order)
    return pl.pallas_call(
        tails_kernel,
        in_specs=[pl.BlockSpec(memory_space=pltpu.HBM)] * 3,
        out_shape=jax.ShapeDtypeStruct((3, width), BF16),
        scratch_shapes=[pltpu.VMEM((16, raw.shape[1]), BF16) for raw in order]
        + [pltpu.SemaphoreType.DMA((3,))],
        compiler_params=in_vmem(60),
        name="tails",
    )(*order)


def shards(
    query_raw, key_raw, value_raw, gate_raw, query_taps, key_taps, value_taps,
    beta_logit, decay_logit, norm_gain, out_weight,
):
    raws = (query_raw, key_raw, value_raw)
    before = shifted(tails(raws), "seq", 1)
    pairs, local = local_steps(
        raws, before, (query_taps, key_taps, value_taps), beta_logit, decay_logit, gate_raw, norm_gain
    )
    starts, (parts, gated) = starts_of(pairs, "seq", local)
    return projected(parts, starts, gated, out_weight, "head")


def solution(mesh):
    placed = (
        P("seq", "head"), P("seq", "head"), P("seq", "head"), P("seq", "head"),
        P(None, "head"), P(None, "head"), P(None, "head"),
        P("seq", "head"), P("seq", "head"), P(), P("head", None),
    )
    return jax.shard_map(
        shards, mesh=mesh, in_specs=placed, out_specs=P(("seq", "head"), None), check_vma=False
    )
```

```python
import functools
import math

import jax
import jax.numpy as jnp
from jax import lax
from jax.experimental import pallas as pl
from jax.experimental.pallas import tpu as pltpu
from jax.sharding import PartitionSpec as P

DK = 128
DV = 128
CHUNK = 128
SMALL = 32
GROUP = 8
HEADS_AT_ONCE = 4
EPSILON = 1e-06
F32 = jnp.float32
BF16 = jnp.bfloat16


def mul(left, right):
    return jnp.dot(left.astype(BF16), right.astype(BF16), preferred_element_type=F32)


def sigmoid(x):
    return 0.5 + 0.5 * jnp.tanh(0.5 * x)


def conv_silu(padded, first, rows, taps_ref, head):
    taps = taps_ref[:, head_of(head)]
    summed = taps[0:1] * padded[head, first : first + rows, :]
    for offset in range(1, 4):
        summed = summed + taps[offset : offset + 1] * padded[head, first + offset : first + offset + rows, :]
    return summed * sigmoid(summed)


def widen(padded, first, rows, raw):
    for head in range(padded.shape[0]):
        padded[head, first : first + rows, :] = raw[:, head_of(head)].astype(F32)


def unit_rows(key):
    return key * lax.rsqrt(jnp.sum(key * key, -1, keepdims=True) + EPSILON)


def part_of(chunk):
    return slice(chunk * CHUNK, (chunk + 1) * CHUNK)


def head_of(head):
    return slice(head * DK, (head + 1) * DK)


def chunk_rows(ref, heads, chunks):
    held = ref.shape[0]
    first = (pl.program_id(0) * heads) % held
    rows = ref[:heads, :]
    for at in range(heads, held, heads):
        rows = jnp.where(first == at, ref[at : at + heads, :], rows)
    return jnp.concatenate([rows[:, part_of(c)] for c in chunks], 0)


def square_iotas(rows=CHUNK):
    return (
        lax.broadcasted_iota(jnp.int32, (rows, CHUNK), 0),
        lax.broadcasted_iota(jnp.int32, (rows, CHUNK), 1),
    )


def log_fades(logit):
    rows, cols = square_iotas()
    decay = -(jnp.maximum(logit, 0.0) + jnp.log(1.0 + jnp.exp(-jnp.abs(logit))))
    return jnp.dot(
        decay, (rows <= cols).astype(F32), precision=lax.Precision.HIGHEST, preferred_element_type=F32
    )


def as_columns(blocks):
    rows = sum(block.shape[0] for block in blocks)
    return jnp.concatenate(list(blocks) + [jnp.zeros((CHUNK - rows, CHUNK), F32)], 0).T


def solved_packs(fade, beta, keys, key_cols, value_work, value_of):
    count = len(keys)
    stages = 9
    done = [0, 0]

    def between():
        done[1] += 1
        while done[0] < len(value_work) and done[0] * stages < len(value_work) * done[1]:
            value_work[done[0]]()
            done[0] += 1

    rows, cols = square_iotas()
    strict = rows > cols
    differ = rows ^ cols
    columns = as_columns((fade, beta, beta * jnp.exp(fade)))
    inner = {id(key): mul(key, turned) for key, turned in zip(keys, key_cols)}
    lower = []
    for p in range(count):
        gap = columns[:, p : p + 1] - fade[p : p + 1, :]
        ratio = jnp.exp(jnp.where(strict, gap, -1e30))
        lower.append(columns[:, count + p : count + p + 1] * ratio * inner[id(keys[p])])

    small_rows, small_cols = square_iotas(SMALL)
    small_differ = small_rows ^ (small_cols % SMALL)
    place = small_cols // SMALL
    blocks = jnp.where(rows // SMALL == cols // SMALL, 1.0, 0.0)
    blocks16 = blocks.astype(BF16)

    def spread(small):
        return jnp.concatenate([small] * (CHUNK // SMALL), 0) * (blocks16 if small.dtype == BF16 else blocks)

    small = []
    for low in lower:
        held = low[:SMALL]
        for at in range(1, CHUNK // SMALL):
            held = jnp.where(place == at, low[at * SMALL : (at + 1) * SMALL], held)
        small.append(held)
    inverse = [
        jnp.where(small_differ == 0, 1.0, jnp.where(small_differ == 1, -one, 0.0)) for one in small
    ]
    size = 2
    while size < CHUNK:
        last = size == SMALL
        if last:
            band = (differ >= size) & (differ < 4 * size)
            inside = [jnp.where(band, low, 0.0).astype(BF16) for low in lower]
            inverse16 = [spread(one.astype(BF16)) for one in inverse]
            inverse = [spread(one) for one in inverse]
            wide16 = inverse16
        else:
            band = (small_differ >= size) & (small_differ < 4 * size)
            inside = [spread(jnp.where(band, one, 0.0).astype(BF16)) for one in small]
            inverse16 = [one.astype(BF16) for one in inverse]
            wide16 = [spread(one) for one in inverse16]
        between()
        step = [mul(inverse16[p], inside[p]).astype(BF16) for p in range(count)]
        between()
        both = [
            mul(step[p], jnp.concatenate([step[p] if last else spread(step[p]), wide16[p]], 1))
            for p in range(count)
        ]
        between()
        inverse = [inverse[p] - both[p][:, CHUNK:] for p in range(count)]
        partial = [inverse[p].astype(BF16) for p in range(count)]
        inverse = [
            inverse[p] + mul(both[p][:, :CHUNK], partial[p] if last else spread(partial[p]))
            for p in range(count)
        ]
        size *= 4

    solved = []
    for p in range(count):
        right = jnp.concatenate(
            [
                columns[:, count + p : count + p + 1] * value_of(p),
                columns[:, 2 * count + p : 2 * count + p + 1] * keys[p],
            ],
            1,
        )
        solved.append(mul(inverse[p], right))
    return solved


def later_kernel(
    key_ref, value_ref, key_taps, value_taps, beta_ref, decay_ref,
    solved_ref, moves_ref, unit_ref, key_padded, value_padded,
):
    length, width = key_ref.shape
    chunks = range(1, length // CHUNK)
    key_heads = width // DK
    heads = value_ref.shape[1] // DV
    repeat_by = heads // key_heads
    packs = [(chunk, head) for chunk in chunks for head in range(heads)]
    skip = CHUNK - 16
    count = length - CHUNK
    widen(key_padded, 0, count + 16, key_ref[skip:, :])
    widen(value_padded, 0, count + 16, value_ref[skip:, :])
    key, turned = {}, {}
    for j in range(key_heads):
        unit = unit_rows(conv_silu(key_padded, 13, count, key_taps, j))
        unit_ref[:, head_of(j)] = unit.astype(BF16)
        for chunk in chunks:
            key[chunk, j] = unit[part_of(chunk - 1)]
            turned[chunk, j] = key[chunk, j].T
    value = {}

    def make_value(head):
        value[head] = conv_silu(value_padded, 13, count, value_taps, head)

    def value_of(pack):
        chunk, head = packs[pack]
        return value[head][part_of(chunk - 1)]

    fade = log_fades(chunk_rows(decay_ref, heads, chunks))
    solved = solved_packs(
        fade,
        sigmoid(chunk_rows(beta_ref, heads, chunks)),
        [key[chunk, head // repeat_by] for chunk, head in packs],
        [turned[chunk, head // repeat_by] for chunk, head in packs],
        [functools.partial(make_value, head) for head in range(heads)],
        value_of,
    )
    tail = jnp.exp(fade[:, CHUNK - 1 : CHUNK] - fade)
    for pack, (chunk, head) in enumerate(packs):
        one = solved[pack].astype(BF16)
        solved_ref[head, part_of(chunk - 1), :] = one
        moves_ref[head, chunk - 1] = mul(
            turned[chunk, head // repeat_by] * tail[pack : pack + 1, :], one
        ).astype(BF16)


def states_kernel(
    key_ref, value_ref, key_before, value_before, key_taps, value_taps, beta_ref, decay_ref, moves_hbm,
    pairs_ref, unit_ref, solved_hbm, starts_hbm,
    key_padded, value_padded, moves_ref, solved_ref, starts_ref, in_sem, out_sem,
):
    heads, length = decay_ref.shape
    chunks = length // CHUNK
    key_heads = key_ref.shape[1] // DK
    repeat_by = heads // key_heads
    incoming = pltpu.make_async_copy(moves_hbm, moves_ref, in_sem)
    incoming.start()

    widen(key_padded, 5, 3, key_before[...])
    widen(key_padded, 8, CHUNK, key_ref[...])
    widen(value_padded, 5, 3, value_before[...])
    widen(value_padded, 8, CHUNK, value_ref[...])
    key, turned = [], []
    for j in range(key_heads):
        key.append(unit_rows(conv_silu(key_padded, 5, CHUNK, key_taps, j)))
        unit_ref[:, head_of(j)] = key[j].astype(BF16)
        turned.append(key[j].T)
    fade = log_fades(chunk_rows(decay_ref, heads, range(chunks)))
    value = {}

    def make_value(head):
        value[head] = conv_silu(value_padded, 5, CHUNK, value_taps, head)

    solved = solved_packs(
        fade[:heads],
        sigmoid(beta_ref[:, :CHUNK]),
        [key[head // repeat_by] for head in range(heads)],
        [turned[head // repeat_by] for head in range(heads)],
        [functools.partial(make_value, head) for head in range(heads)],
        lambda head: value[head],
    )
    last = jnp.exp(fade[:, CHUNK - 1 : CHUNK])
    tail = jnp.exp(fade[:, CHUNK - 1 : CHUNK] - fade)
    rows, cols = square_iotas()
    identity = jnp.where(rows == cols, 1.0, 0.0)

    state = []
    for head in range(heads):
        one = solved[head].astype(BF16)
        solved_ref[head] = one
        moved = mul(turned[head // repeat_by] * tail[head : head + 1, :], one)
        state.append(
            jnp.concatenate([moved[:, :DV], last[head : head + 1, :] * identity - moved[:, DV:]], 1)
        )
    outgoing = [pltpu.make_async_copy(solved_ref, solved_hbm, out_sem.at[0])]
    outgoing[0].start()
    incoming.wait()
    for chunk in range(1, chunks):
        for head in range(heads):
            pack = chunk * heads + head
            start = state[head].astype(BF16)
            starts_ref[chunk - 1, head] = start
            moves = moves_ref[head, chunk - 1]
            moved = last[pack : pack + 1, :] * state[head] - mul(moves[:, DV:], start)
            state[head] = jnp.concatenate([moved[:, :DV] + moves[:, :DV].astype(F32), moved[:, DV:]], 1)
        outgoing.append(
            pltpu.make_async_copy(
                starts_ref.at[chunk - 1], starts_hbm.at[chunk - 1], out_sem.at[chunk]
            )
        )
        outgoing[-1].start()
    for head in range(heads):
        pairs_ref[head] = state[head].astype(BF16)
    for copy in outgoing:
        copy.wait()


def local_kernel(
    query_ref, query_before, query_taps, first_unit, later_unit, decay_ref,
    first_solved, later_solved, starts_ref, gate_ref, gain_ref,
    parts_ref, gated_ref, padded,
):
    length, width = query_ref.shape
    chunks = length // CHUNK
    key_heads = width // DK
    heads = first_solved.shape[0]
    repeat_by = heads // key_heads

    rows, cols = square_iotas()
    within = rows >= cols
    fade = log_fades(chunk_rows(decay_ref, heads, range(chunks)))
    columns = as_columns((fade, jnp.exp(fade)))
    widen(padded, 5, 3, query_before[...])
    widen(padded, 8, length, query_ref[...])
    query = [conv_silu(padded, 5, length, query_taps, j).astype(BF16) for j in range(key_heads)]
    for head in range(heads):
        gate = gate_ref[:, head_of(head)].astype(F32)
        gated_ref[:, head_of(head)] = (gate * sigmoid(gate) * gain_ref[...]).astype(BF16)
    for chunk in range(chunks):
        part = part_of(chunk)
        for j in range(key_heads):
            own = query[j][part]
            unit = first_unit[:, head_of(j)] if chunk == 0 else later_unit[part_of(chunk - 1), head_of(j)]
            inner = lax.dot_general(
                own, unit, (((1,), (1,)), ((), ())), preferred_element_type=F32
            )
            for head in range(j * repeat_by, (j + 1) * repeat_by):
                pack = chunk * heads + head
                gap = columns[:, pack : pack + 1] - fade[pack : pack + 1, :]
                scores = inner * jnp.exp(jnp.where(within, gap, -1e30))
                grown = columns[:, chunks * heads + pack : chunks * heads + pack + 1]
                if chunk == 0:
                    updates, wide = first_solved[head, :, :DV], first_solved[head, :, DV:]
                    fresh = jnp.concatenate([updates, -wide], 1)
                    carried = jnp.concatenate(
                        [jnp.zeros((CHUNK, DV), F32), grown * own.astype(F32)], 1
                    )
                else:
                    solved = later_solved[head, part_of(chunk - 1), :]
                    both = mul(jnp.concatenate([solved[:, DV:], own], 0), starts_ref[chunk - 1, head])
                    taken = both[:CHUNK]
                    fresh = jnp.concatenate(
                        [solved[:, :DV].astype(F32) - taken[:, :DV], -taken[:, DV:]], 1
                    )
                    carried = grown * both[CHUNK:]
                parts_ref[head, part, :] = (carried + mul(scores, fresh)).astype(BF16)


def columns_of(rows, width, first=0):
    return pl.BlockSpec((rows, width), lambda step: (0, step + first))


def in_vmem(mib):
    return pltpu.CompilerParams(vmem_limit_bytes=mib * 1024 * 1024)


def local_steps(raws, before, taps, beta_logit, decay_logit, gate_raw, norm_gain):
    length = raws[0].shape[0]
    key_heads = raws[0].shape[1] // DK
    value_heads = raws[2].shape[1] // DV
    repeat_by = value_heads // key_heads
    chunks = length // CHUNK
    beta, decay = beta_logit.T, decay_logit.T
    work = CHUNK * length * DV * value_heads
    hbm = pl.BlockSpec(memory_space=pltpu.HBM)

    def split(each):
        heads = each * repeat_by
        held = max(heads, math.gcd(8, value_heads))
        of_heads = lambda *shape: pl.BlockSpec((heads,) + shape, lambda step: (step,) + (0,) * len(shape))
        logits = pl.BlockSpec((held, length), lambda step: (step * heads // held, 0))
        return key_heads // each, each * DK, heads * DV, of_heads, logits

    each = math.gcd(4, key_heads)
    steps, narrow, wide, of_heads, logits = split(each)
    later = length - CHUNK
    solved, moves, later_unit = pl.pallas_call(
        later_kernel,
        grid=(steps,),
        in_specs=[
            columns_of(length, narrow), columns_of(length, wide),
            columns_of(4, narrow), columns_of(4, wide), logits, logits,
        ],
        out_specs=[
            of_heads(later, DV + DK), of_heads(chunks - 1, DK, DV + DK), columns_of(later, narrow),
        ],
        out_shape=[
            jax.ShapeDtypeStruct((value_heads, later, DV + DK), BF16),
            jax.ShapeDtypeStruct((value_heads, chunks - 1, DK, DV + DK), BF16),
            jax.ShapeDtypeStruct((later, key_heads * DK), BF16),
        ],
        scratch_shapes=[
            pltpu.VMEM((each, later + 16, DK), F32),
            pltpu.VMEM((each * repeat_by, later + 16, DV), F32),
        ],
        compiler_params=in_vmem(60),
        cost_estimate=pl.CostEstimate(flops=30 * work, bytes_accessed=0, transcendentals=0),
        name="later",
    )(raws[1], raws[2], taps[1], taps[2], beta, decay)

    narrow, wide = key_heads * DK, value_heads * DV
    whole = lambda shape, *at: pl.BlockSpec(shape, lambda step: at or (0,) * len(shape))
    pairs, first_unit, first_solved, starts = pl.pallas_call(
        states_kernel,
        grid=(1,),
        in_specs=[
            whole((CHUNK, narrow)), whole((CHUNK, wide)),
            whole((3, narrow), 0, repeat_by + 1), whole((3, wide)),
            whole(taps[1].shape), whole(taps[2].shape), whole(beta.shape), whole(decay.shape), hbm,
        ],
        out_specs=[whole((value_heads, DK, DV + DK)), whole((CHUNK, narrow)), hbm, hbm],
        out_shape=[
            jax.ShapeDtypeStruct((value_heads, DK, DV + DK), BF16),
            jax.ShapeDtypeStruct((CHUNK, narrow), BF16),
            jax.ShapeDtypeStruct((value_heads, CHUNK, DV + DK), BF16),
            jax.ShapeDtypeStruct((chunks - 1, value_heads, DK, DV + DK), BF16),
        ],
        scratch_shapes=[
            pltpu.VMEM((key_heads, 8 + CHUNK, DK), F32),
            pltpu.VMEM((value_heads, 8 + CHUNK, DV), F32),
            pltpu.VMEM(moves.shape, BF16),
            pltpu.VMEM((value_heads, CHUNK, DV + DK), BF16),
            pltpu.VMEM((chunks - 1, value_heads, DK, DV + DK), BF16),
            pltpu.SemaphoreType.DMA,
            pltpu.SemaphoreType.DMA((chunks,)),
        ],
        compiler_params=in_vmem(54),
        cost_estimate=pl.CostEstimate(flops=20 * work, bytes_accessed=0, transcendentals=0),
        name="states",
    )(raws[1], raws[2], before, before, taps[1], taps[2], beta, decay, moves)
    gain = norm_gain.reshape(1, DV)

    def local():
        steps, narrow, wide, of_heads, logits = split(math.gcd(2, key_heads))
        heads = wide // DV
        return pl.pallas_call(
            local_kernel,
            grid=(steps,),
            in_specs=[
                columns_of(length, narrow), columns_of(3, narrow, repeat_by * steps), columns_of(4, narrow),
                columns_of(CHUNK, narrow), columns_of(later, narrow), logits,
                of_heads(CHUNK, DV + DK), of_heads(later, DV + DK),
                pl.BlockSpec((chunks - 1, heads, DK, DV + DK), lambda step: (0, step, 0, 0)),
                columns_of(length, wide), whole(gain.shape),
            ],
            out_specs=[of_heads(length, DV + DK), columns_of(length, wide)],
            out_shape=[
                jax.ShapeDtypeStruct((value_heads, length, DV + DK), BF16),
                jax.ShapeDtypeStruct(gate_raw.shape, BF16),
            ],
            scratch_shapes=[pltpu.VMEM((narrow // DK, 8 + length, DK), F32)],
            compiler_params=in_vmem(60),
            cost_estimate=pl.CostEstimate(flops=12 * work, bytes_accessed=0, transcendentals=0),
            name="local",
        )(
            raws[0], before, taps[0], first_unit, later_unit, decay,
            first_solved, solved, starts, gate_raw, gain,
        )

    return pairs, local


def prefix_kernel(pairs_ref, prefix_ref, total_ref):
    count, heads = pairs_ref.shape[:2]
    running = [None] * heads
    for hop in range(count):
        for head in range(heads):
            now = pairs_ref[hop, head]
            if hop == 0:
                rows = lax.broadcasted_iota(jnp.int32, (DK, DV + DK), 0)
                cols = lax.broadcasted_iota(jnp.int32, (DK, DV + DK), 1)
                prefix_ref[hop, head] = jnp.where(cols == rows + DV, 1.0, 0.0).astype(BF16)
                running[head] = now.astype(F32)
            else:
                before = running[head].astype(BF16)
                prefix_ref[hop, head] = before
                own = jnp.concatenate([now[:, :DV].astype(F32), jnp.zeros((DK, DK), F32)], 1)
                running[head] = own + mul(now[:, DV:], before)
    for head in range(heads):
        total_ref[head] = running[head][:, : total_ref.shape[2]].astype(BF16)


def apply_kernel(prefix_ref, start_ref, starts_ref):
    count, heads = prefix_ref.shape[:2]
    for hop in range(count):
        for head in range(heads):
            starts_ref[hop, head] = (
                prefix_ref[hop, head, :, :DV].astype(F32)
                + mul(prefix_ref[hop, head, :, DV:], start_ref[head])
            ).astype(BF16)


def shifted(value, axis, by):
    count = lax.axis_size(axis)
    return lax.ppermute(value, axis, [(i, i + by) for i in range(count - by)])


def group_start(total, axis, group):
    groups = lax.axis_size(axis) // group
    running = shifted(total, axis, group)
    by = 1
    while by < groups - 1:
        earlier = shifted(running, axis, by * group)
        product = jnp.einsum("bkl,blv->bkv", running[..., DV:], earlier, preferred_element_type=F32)
        own = jnp.pad(running[..., :DV], ((0, 0), (0, 0), (0, DK)))
        running = (product + own.astype(F32)).astype(BF16)
        by *= 2
    return running[..., :DV]


def starts_of(pairs, axis, beside):
    size = lax.axis_size(axis)
    heads = pairs.shape[0]
    group = math.gcd(math.gcd(size, heads), GROUP)
    groups = [[g * group + i for i in range(group)] for g in range(size // group)]
    each = heads // group
    wide = DV if size // group == 2 else DV + DK
    by_head = lax.all_to_all(pairs, axis, 0, 0, axis_index_groups=groups, tiled=True)
    by_head, done = lax.optimization_barrier((by_head, beside()))
    prefix, total = pl.pallas_call(
        prefix_kernel,
        out_shape=[
            jax.ShapeDtypeStruct((group, each, DK, DV + DK), BF16),
            jax.ShapeDtypeStruct((each, DK, wide), BF16),
        ],
        compiler_params=in_vmem(16),
        name="prefix",
    )(by_head.reshape(group, each, DK, DV + DK))
    starts = pl.pallas_call(
        apply_kernel,
        out_shape=jax.ShapeDtypeStruct((group, each, DK, DV), BF16),
        compiler_params=in_vmem(16),
        name="apply",
    )(prefix, group_start(total, axis, group))
    starts = lax.all_to_all(
        starts.reshape(heads, DK, DV), axis, 0, 0, axis_index_groups=groups, tiled=True
    )
    return starts, done


def project_kernel(
    place_ref, starts_ref, gated_ref, parts_hbm, weight_hbm, away_ref, own_ref,
    parts_ref, weight_ref, total, parts_sem, weight_sem,
):
    heads, length = parts_ref.shape[:2]
    width = weight_ref.shape[1]
    each = min(HEADS_AT_ONCE, heads)
    block = min(512, width)
    groups = heads // each

    def parts(g):
        here = pl.ds(g * each, each)
        return pltpu.make_async_copy(parts_hbm.at[here], parts_ref.at[here], parts_sem.at[g])

    def weights(g):
        rows = pl.ds(g * each * DV, each * DV)
        return pltpu.make_async_copy(weight_hbm.at[rows], weight_ref.at[rows], weight_sem.at[g])

    def normed_group(g):
        normed = []
        for head in range(g * each, (g + 1) * each):
            core = parts_ref[head, :, :DV].astype(F32) + mul(
                parts_ref[head, :, DV:], starts_ref[head]
            )
            scale = lax.rsqrt(jnp.mean(core * core, -1, keepdims=True) + EPSILON)
            normed.append((core * scale * gated_ref[:, head_of(head)].astype(F32)).astype(BF16))
        return jnp.concatenate(normed, 1)

    parts(0).start()
    weights(0).start()
    parts(0).wait()
    if groups > 1:
        parts(1).start()
        weights(1).start()
    following = normed_group(0)
    for g in range(groups):
        weights(g).wait()
        if g + 2 < groups:
            weights(g + 2).start()
        if g + 1 < groups:
            parts(g + 1).wait()
        if g + 2 < groups:
            parts(g + 2).start()
        normed = following
        if g + 1 < groups:
            following = normed_group(g + 1)
        for at in range(0, width, block):
            added = jnp.dot(
                normed, weight_ref[g * each * DV : (g + 1) * each * DV, at : at + block],
                preferred_element_type=F32,
            )
            if g > 0:
                added = added + total[:, at : at + block]
            if g < groups - 1:
                total[:, at : at + block] = added
            elif own_ref is None:
                away_ref[:, at : at + block] = added.astype(BF16)
            else:
                first = place_ref[0] == 0
                low, high = added[: length // 2], added[length // 2 :]
                own_ref[:, at : at + block] = jnp.where(first, low, high).astype(BF16)
                away_ref[:, at : at + block] = jnp.where(first, high, low).astype(BF16)


def whole_kernel(place_ref, starts_ref, gated_ref, parts_hbm, weight_hbm, out_ref, *scratch):
    project_kernel(place_ref, starts_ref, gated_ref, parts_hbm, weight_hbm, out_ref, None, *scratch)


def projected(parts, starts, gated, out_weight, axis):
    heads, length = parts.shape[:2]
    width = out_weight.shape[1]
    halves = lax.axis_size(axis) == 2
    vmem = pl.BlockSpec(memory_space=pltpu.VMEM)
    hbm = pl.BlockSpec(memory_space=pltpu.HBM)
    groups = heads // min(HEADS_AT_ONCE, heads)
    here = lax.axis_index(axis).astype(jnp.int32).reshape(1)
    out = jax.ShapeDtypeStruct((length // 2 if halves else length, width), BF16)
    partial = pl.pallas_call(
        project_kernel if halves else whole_kernel,
        in_specs=[pl.BlockSpec(memory_space=pltpu.SMEM), vmem, vmem, hbm, hbm],
        out_specs=[vmem, vmem] if halves else vmem,
        out_shape=[out, out] if halves else out,
        scratch_shapes=[
            pltpu.VMEM(parts.shape, BF16),
            pltpu.VMEM(out_weight.shape, BF16),
            pltpu.VMEM((length, width), F32),
            pltpu.SemaphoreType.DMA((groups,)),
            pltpu.SemaphoreType.DMA((groups,)),
        ],
        compiler_params=in_vmem(50),
        name="project",
    )(here, starts, gated, parts, out_weight)
    if not halves:
        return lax.psum_scatter(partial, axis, scatter_dimension=0, tiled=True)
    away, own = partial
    other = lax.ppermute(away, axis, [(0, 1), (1, 0)])
    return (own.astype(F32) + other.astype(F32)).astype(BF16)


def tails_kernel(value_hbm, query_hbm, key_hbm, out_ref, value_ref, query_ref, key_ref, sem):
    pairs = ((value_hbm, value_ref), (query_hbm, query_ref), (key_hbm, key_ref))
    copies = [
        pltpu.make_async_copy(source.at[pl.ds(source.shape[0] - 16, 16)], held, sem.at[i])
        for i, (source, held) in enumerate(pairs)
    ]
    for copy in copies:
        copy.start()
    at = 0
    for copy, (_, held) in zip(copies, pairs):
        copy.wait()
        width = held.shape[1]
        out_ref[:, at : at + width] = held[...].astype(F32)[13:16].astype(BF16)
        at += width


def tails(raws):
    order = (raws[2], raws[0], raws[1])
    width = sum(raw.shape[1] for raw in order)
    return pl.pallas_call(
        tails_kernel,
        in_specs=[pl.BlockSpec(memory_space=pltpu.HBM)] * 3,
        out_shape=jax.ShapeDtypeStruct((3, width), BF16),
        scratch_shapes=[pltpu.VMEM((16, raw.shape[1]), BF16) for raw in order]
        + [pltpu.SemaphoreType.DMA((3,))],
        compiler_params=in_vmem(60),
        name="tails",
    )(*order)


def shards(
    query_raw, key_raw, value_raw, gate_raw, query_taps, key_taps, value_taps,
    beta_logit, decay_logit, norm_gain, out_weight,
):
    raws = (query_raw, key_raw, value_raw)
    before = shifted(tails(raws), "seq", 1)
    pairs, local = local_steps(
        raws, before, (query_taps, key_taps, value_taps), beta_logit, decay_logit, gate_raw, norm_gain
    )
    starts, (parts, gated) = starts_of(pairs, "seq", local)
    return projected(parts, starts, gated, out_weight, "head")


def solution(mesh):
    placed = (
        P("seq", "head"), P("seq", "head"), P("seq", "head"), P("seq", "head"),
        P(None, "head"), P(None, "head"), P(None, "head"),
        P("seq", "head"), P("seq", "head"), P(), P("head", None),
    )
    return jax.shard_map(
        shards, mesh=mesh, in_specs=placed, out_specs=P(("seq", "head"), None), check_vma=False
    )
```

```python
import functools
import math

import jax
import jax.numpy as jnp
from jax import lax
from jax.experimental import pallas as pl
from jax.experimental.pallas import tpu as pltpu
from jax.sharding import PartitionSpec as P

DK = 128
DV = 128
CHUNK = 128
SMALL = 32
GROUP = 8
HEADS_AT_ONCE = 4
EPSILON = 1e-06
F32 = jnp.float32
BF16 = jnp.bfloat16


def mul(left, right):
    return jnp.dot(left.astype(BF16), right.astype(BF16), preferred_element_type=F32)


def sigmoid(x):
    return 0.5 + 0.5 * jnp.tanh(0.5 * x)


def conv_silu(padded, first, rows, taps_ref, head):
    taps = taps_ref[:, head_of(head)]
    summed = taps[0:1] * padded[head, first : first + rows, :]
    for offset in range(1, 4):
        summed = summed + taps[offset : offset + 1] * padded[head, first + offset : first + offset + rows, :]
    return summed * sigmoid(summed)


def widen(padded, first, rows, raw):
    for head in range(padded.shape[0]):
        padded[head, first : first + rows, :] = raw[:, head_of(head)].astype(F32)


def unit_rows(key):
    return key * lax.rsqrt(jnp.sum(key * key, -1, keepdims=True) + EPSILON)


def part_of(chunk):
    return slice(chunk * CHUNK, (chunk + 1) * CHUNK)


def head_of(head):
    return slice(head * DK, (head + 1) * DK)


def chunk_rows(ref, heads, chunks):
    held = ref.shape[0]
    first = (pl.program_id(0) * heads) % held
    rows = ref[:heads, :]
    for at in range(heads, held, heads):
        rows = jnp.where(first == at, ref[at : at + heads, :], rows)
    return jnp.concatenate([rows[:, part_of(c)] for c in chunks], 0)


def square_iotas(rows=CHUNK):
    return (
        lax.broadcasted_iota(jnp.int32, (rows, CHUNK), 0),
        lax.broadcasted_iota(jnp.int32, (rows, CHUNK), 1),
    )


def log_fades(logit):
    rows, cols = square_iotas()
    decay = -(jnp.maximum(logit, 0.0) + jnp.log(1.0 + jnp.exp(-jnp.abs(logit))))
    return jnp.dot(
        decay, (rows <= cols).astype(F32), precision=lax.Precision.HIGHEST, preferred_element_type=F32
    )


def as_columns(blocks):
    rows = sum(block.shape[0] for block in blocks)
    return jnp.concatenate(list(blocks) + [jnp.zeros((CHUNK - rows, CHUNK), F32)], 0).T


def each_mul(lefts, rights):
    return [mul(left, right) for left, right in zip(lefts, rights)]


def paired_mul(lefts, rights):
    products = []
    for p in range(0, len(lefts), 2):
        if p + 1 == len(lefts):
            return products + [mul(lefts[p], rights[p])]
        rows = lefts[p].shape[0]
        both = mul(
            jnp.concatenate([lefts[p], lefts[p + 1]], 0), jnp.concatenate([rights[p], rights[p + 1]], 1)
        )
        products += [both[:rows, :CHUNK], both[rows:, CHUNK:]]
    return products


def solved_packs(fade, beta, keys, key_cols, value_work, value_of):
    count = len(keys)
    stages = 9
    done = [0, 0]

    def between():
        done[1] += 1
        while done[0] < len(value_work) and done[0] * stages < len(value_work) * done[1]:
            value_work[done[0]]()
            done[0] += 1

    rows, cols = square_iotas()
    strict = rows > cols
    differ = rows ^ cols
    columns = as_columns((fade, beta, beta * jnp.exp(fade)))
    inner = {id(key): mul(key, turned) for key, turned in zip(keys, key_cols)}
    lower = []
    for p in range(count):
        gap = columns[:, p : p + 1] - fade[p : p + 1, :]
        ratio = jnp.exp(jnp.where(strict, gap, -1e30))
        lower.append(columns[:, count + p : count + p + 1] * ratio * inner[id(keys[p])])

    small_rows, small_cols = square_iotas(SMALL)
    small_differ = small_rows ^ (small_cols % SMALL)
    place = small_cols // SMALL
    blocks = jnp.where(rows // SMALL == cols // SMALL, 1.0, 0.0)
    blocks16 = blocks.astype(BF16)

    def spread(small):
        return jnp.concatenate([small] * (CHUNK // SMALL), 0) * (blocks16 if small.dtype == BF16 else blocks)

    small = []
    for low in lower:
        held = low[:SMALL]
        for at in range(1, CHUNK // SMALL):
            held = jnp.where(place == at, low[at * SMALL : (at + 1) * SMALL], held)
        small.append(held)
    inverse = [
        jnp.where(small_differ == 0, 1.0, jnp.where(small_differ == 1, -one, 0.0)) for one in small
    ]
    size = 2
    while size < CHUNK:
        last = size == SMALL
        if last:
            band = (differ >= size) & (differ < 4 * size)
            inside = [jnp.where(band, low, 0.0).astype(BF16) for low in lower]
            inverse16 = [spread(one.astype(BF16)) for one in inverse]
            inverse = [spread(one) for one in inverse]
            wide16 = inverse16
        else:
            band = (small_differ >= size) & (small_differ < 4 * size)
            inside = [spread(jnp.where(band, one, 0.0).astype(BF16)) for one in small]
            inverse16 = [one.astype(BF16) for one in inverse]
            wide16 = [spread(one) for one in inverse16]
        between()
        step = [one.astype(BF16) for one in (each_mul if last else paired_mul)(inverse16, inside)]
        between()
        both = [
            mul(step[p], jnp.concatenate([step[p] if last else spread(step[p]), wide16[p]], 1))
            for p in range(count)
        ]
        between()
        inverse = [inverse[p] - both[p][:, CHUNK:] for p in range(count)]
        partial = [inverse[p].astype(BF16) for p in range(count)]
        squared = [one[:, :CHUNK] for one in both]
        if last:
            added = each_mul(squared, partial)
        else:
            added = paired_mul(squared, [spread(one) for one in partial])
        inverse = [inverse[p] + added[p] for p in range(count)]
        size *= 4

    solved = []
    for p in range(count):
        right = jnp.concatenate(
            [
                columns[:, count + p : count + p + 1] * value_of(p),
                columns[:, 2 * count + p : 2 * count + p + 1] * keys[p],
            ],
            1,
        )
        solved.append(mul(inverse[p], right))
    return solved


def later_kernel(
    key_ref, value_ref, key_taps, value_taps, beta_ref, decay_ref,
    solved_hbm, moves_hbm, unit_ref, key_padded, value_padded, solved_ref, moves_ref, sem,
):
    step, steps = pl.program_id(0), pl.num_programs(0)
    length, width = key_ref.shape
    chunks = range(1, length // CHUNK)
    key_heads = width // DK
    heads = value_ref.shape[1] // DV
    repeat_by = heads // key_heads
    packs = [(chunk, head) for chunk in chunks for head in range(heads)]
    skip = CHUNK - 16
    count = length - CHUNK
    widen(key_padded, 0, count + 16, key_ref[skip:, :])
    widen(value_padded, 0, count + 16, value_ref[skip:, :])
    key, turned = {}, {}
    for j in range(key_heads):
        unit = unit_rows(conv_silu(key_padded, 13, count, key_taps, j))
        unit_ref[:, head_of(j)] = unit.astype(BF16)
        for chunk in chunks:
            key[chunk, j] = unit[part_of(chunk - 1)]
            turned[chunk, j] = key[chunk, j].astype(BF16).T
    value = {}

    def make_value(head):
        value[head] = conv_silu(value_padded, 13, count, value_taps, head)

    def value_of(pack):
        chunk, head = packs[pack]
        return value[head][part_of(chunk - 1)]

    fade = log_fades(chunk_rows(decay_ref, heads, chunks))
    solved = solved_packs(
        fade,
        sigmoid(chunk_rows(beta_ref, heads, chunks)),
        [key[chunk, head // repeat_by] for chunk, head in packs],
        [turned[chunk, head // repeat_by] for chunk, head in packs],
        [functools.partial(make_value, head) for head in range(heads)],
        value_of,
    )
    tail = jnp.exp(fade[:, CHUNK - 1 : CHUNK] - fade)

    def leaving(held, out, at_step, kind):
        here = pl.ds(at_step * heads, heads)
        return pltpu.make_async_copy(held.at[here], out.at[here], sem.at[kind, at_step])

    for pack, (chunk, head) in enumerate(packs):
        solved_ref[step * heads + head, part_of(chunk - 1), :] = solved[pack].astype(BF16)
    leaving(solved_ref, solved_hbm, step, 0).start()
    for pack, (chunk, head) in enumerate(packs):
        moves_ref[step * heads + head, chunk - 1] = mul(
            turned[chunk, head // repeat_by].astype(F32) * tail[pack : pack + 1, :], solved[pack]
        ).astype(BF16)
    leaving(moves_ref, moves_hbm, step, 1).start()

    @pl.when(step == steps - 1)
    def _():
        for at_step in range(sem.shape[1]):
            leaving(solved_ref, solved_hbm, at_step, 0).wait()
            leaving(moves_ref, moves_hbm, at_step, 1).wait()


def states_kernel(
    key_ref, value_ref, key_before, value_before, key_taps, value_taps, beta_ref, decay_ref, moves_hbm,
    pairs_hbm, unit_ref, solved_hbm, starts_hbm,
    key_padded, value_padded, moves_ref, solved_ref, starts_ref, pairs_ref, in_sem, out_sem, pairs_sem,
):
    heads, length = decay_ref.shape
    chunks = length // CHUNK
    key_heads = key_ref.shape[1] // DK
    repeat_by = heads // key_heads
    incoming = pltpu.make_async_copy(moves_hbm, moves_ref, in_sem)
    incoming.start()

    widen(key_padded, 5, 3, key_before[...])
    widen(key_padded, 8, CHUNK, key_ref[...])
    widen(value_padded, 5, 3, value_before[...])
    widen(value_padded, 8, CHUNK, value_ref[...])
    key, turned = [], []
    for j in range(key_heads):
        key.append(unit_rows(conv_silu(key_padded, 5, CHUNK, key_taps, j)))
        unit_ref[:, head_of(j)] = key[j].astype(BF16)
        turned.append(key[j].astype(BF16).T)
    fade = log_fades(chunk_rows(decay_ref, heads, range(chunks)))
    value = {}

    def make_value(head):
        value[head] = conv_silu(value_padded, 5, CHUNK, value_taps, head)

    solved = solved_packs(
        fade[:heads],
        sigmoid(beta_ref[:, :CHUNK]),
        [key[head // repeat_by] for head in range(heads)],
        [turned[head // repeat_by] for head in range(heads)],
        [functools.partial(make_value, head) for head in range(heads)],
        lambda head: value[head],
    )
    last = jnp.exp(fade[:, CHUNK - 1 : CHUNK])
    tail = jnp.exp(fade[:, CHUNK - 1 : CHUNK] - fade)
    rows, cols = square_iotas()
    identity = jnp.where(rows == cols, 1.0, 0.0)

    state = []
    for head in range(heads):
        one = solved[head].astype(BF16)
        solved_ref[head] = one
        moved = mul(turned[head // repeat_by].astype(F32) * tail[head : head + 1, :], one)
        state.append(
            jnp.concatenate([moved[:, :DV], last[head : head + 1, :] * identity - moved[:, DV:]], 1)
        )
    each = min(HEADS_AT_ONCE, heads)
    outgoing = [pltpu.make_async_copy(solved_ref, solved_hbm, out_sem.at[0])]
    outgoing[0].start()
    incoming.wait()
    for chunk in range(1, chunks):
        for head in range(heads):
            pack = chunk * heads + head
            start = state[head].astype(BF16)
            starts_ref[chunk - 1, head] = start
            moves = moves_ref[head, chunk - 1]
            moved = last[pack : pack + 1, :] * state[head] - mul(moves[:, DV:], start)
            state[head] = jnp.concatenate([moved[:, :DV] + moves[:, :DV].astype(F32), moved[:, DV:]], 1)
            if chunk == chunks - 1:
                pairs_ref[head] = state[head].astype(BF16)
                if (head + 1) % each == 0:
                    done = pl.ds(head + 1 - each, each)
                    outgoing.append(
                        pltpu.make_async_copy(
                            pairs_ref.at[done], pairs_hbm.at[done], pairs_sem.at[head // each]
                        )
                    )
                    outgoing[-1].start()
        outgoing.append(
            pltpu.make_async_copy(
                starts_ref.at[chunk - 1], starts_hbm.at[chunk - 1], out_sem.at[chunk]
            )
        )
        outgoing[-1].start()
    for copy in outgoing:
        copy.wait()


def local_kernel(
    query_ref, query_before, query_taps, first_unit, later_unit, decay_ref,
    first_solved, later_solved, starts_ref, gate_ref, gain_ref,
    parts_ref, gated_ref, padded,
):
    length, width = query_ref.shape
    chunks = length // CHUNK
    key_heads = width // DK
    heads = first_solved.shape[0]
    repeat_by = heads // key_heads

    rows, cols = square_iotas()
    within = rows >= cols
    fade = log_fades(chunk_rows(decay_ref, heads, range(chunks)))
    columns = as_columns((fade, jnp.exp(fade)))
    widen(padded, 5, 3, query_before[...])
    widen(padded, 8, length, query_ref[...])
    query = [conv_silu(padded, 5, length, query_taps, j).astype(BF16) for j in range(key_heads)]
    for head in range(heads):
        gate = gate_ref[:, head_of(head)].astype(F32)
        gated_ref[:, head_of(head)] = (gate * sigmoid(gate) * gain_ref[...]).astype(BF16)
    for chunk in range(chunks):
        part = part_of(chunk)
        for j in range(key_heads):
            own = query[j][part]
            unit = first_unit[:, head_of(j)] if chunk == 0 else later_unit[part_of(chunk - 1), head_of(j)]
            inner = lax.dot_general(
                own, unit, (((1,), (1,)), ((), ())), preferred_element_type=F32
            )
            for head in range(j * repeat_by, (j + 1) * repeat_by):
                pack = chunk * heads + head
                gap = columns[:, pack : pack + 1] - fade[pack : pack + 1, :]
                scores = inner * jnp.exp(jnp.where(within, gap, -1e30))
                grown = columns[:, chunks * heads + pack : chunks * heads + pack + 1]
                if chunk == 0:
                    updates, wide = first_solved[head, :, :DV], first_solved[head, :, DV:]
                    fresh = jnp.concatenate([updates, -wide], 1)
                    carried = jnp.concatenate(
                        [jnp.zeros((CHUNK, DV), F32), grown * own.astype(F32)], 1
                    )
                else:
                    solved = later_solved[head, part_of(chunk - 1), :]
                    both = mul(jnp.concatenate([solved[:, DV:], own], 0), starts_ref[chunk - 1, head])
                    taken = both[:CHUNK]
                    fresh = jnp.concatenate(
                        [solved[:, :DV].astype(F32) - taken[:, :DV], -taken[:, DV:]], 1
                    )
                    carried = grown * both[CHUNK:]
                parts_ref[head, part, :] = (carried + mul(scores, fresh)).astype(BF16)


def columns_of(rows, width, first=0):
    return pl.BlockSpec((rows, width), lambda step: (0, step + first))


def in_vmem(mib):
    return pltpu.CompilerParams(vmem_limit_bytes=mib * 1024 * 1024)


def local_steps(raws, before, taps, beta_logit, decay_logit, gate_raw, norm_gain):
    length = raws[0].shape[0]
    key_heads = raws[0].shape[1] // DK
    value_heads = raws[2].shape[1] // DV
    repeat_by = value_heads // key_heads
    chunks = length // CHUNK
    beta, decay = beta_logit.T, decay_logit.T
    work = CHUNK * length * DV * value_heads
    hbm = pl.BlockSpec(memory_space=pltpu.HBM)

    def split(each):
        heads = each * repeat_by
        held = max(heads, math.gcd(8, value_heads))
        of_heads = lambda *shape: pl.BlockSpec((heads,) + shape, lambda step: (step,) + (0,) * len(shape))
        logits = pl.BlockSpec((held, length), lambda step: (step * heads // held, 0))
        return key_heads // each, each * DK, heads * DV, of_heads, logits

    each = math.gcd(4, key_heads)
    steps, narrow, wide, of_heads, logits = split(each)
    later = length - CHUNK
    solved, moves, later_unit = pl.pallas_call(
        later_kernel,
        grid=(steps,),
        in_specs=[
            columns_of(length, narrow), columns_of(length, wide),
            columns_of(4, narrow), columns_of(4, wide), logits, logits,
        ],
        out_specs=[hbm, hbm, columns_of(later, narrow)],
        out_shape=[
            jax.ShapeDtypeStruct((value_heads, later, DV + DK), BF16),
            jax.ShapeDtypeStruct((value_heads, chunks - 1, DK, DV + DK), BF16),
            jax.ShapeDtypeStruct((later, key_heads * DK), BF16),
        ],
        scratch_shapes=[
            pltpu.VMEM((each, later + 16, DK), F32),
            pltpu.VMEM((each * repeat_by, later + 16, DV), F32),
            pltpu.VMEM((value_heads, later, DV + DK), BF16),
            pltpu.VMEM((value_heads, chunks - 1, DK, DV + DK), BF16),
            pltpu.SemaphoreType.DMA((2, steps)),
        ],
        compiler_params=in_vmem(60),
        cost_estimate=pl.CostEstimate(flops=30 * work, bytes_accessed=0, transcendentals=0),
        name="later",
    )(raws[1], raws[2], taps[1], taps[2], beta, decay)

    narrow, wide = key_heads * DK, value_heads * DV
    whole = lambda shape, *at: pl.BlockSpec(shape, lambda step: at or (0,) * len(shape))
    pairs, first_unit, first_solved, starts = pl.pallas_call(
        states_kernel,
        grid=(1,),
        in_specs=[
            whole((CHUNK, narrow)), whole((CHUNK, wide)),
            whole((3, narrow), 0, repeat_by + 1), whole((3, wide)),
            whole(taps[1].shape), whole(taps[2].shape), whole(beta.shape), whole(decay.shape), hbm,
        ],
        out_specs=[hbm, whole((CHUNK, narrow)), hbm, hbm],
        out_shape=[
            jax.ShapeDtypeStruct((value_heads, DK, DV + DK), BF16),
            jax.ShapeDtypeStruct((CHUNK, narrow), BF16),
            jax.ShapeDtypeStruct((value_heads, CHUNK, DV + DK), BF16),
            jax.ShapeDtypeStruct((chunks - 1, value_heads, DK, DV + DK), BF16),
        ],
        scratch_shapes=[
            pltpu.VMEM((key_heads, 8 + CHUNK, DK), F32),
            pltpu.VMEM((value_heads, 8 + CHUNK, DV), F32),
            pltpu.VMEM(moves.shape, BF16),
            pltpu.VMEM((value_heads, CHUNK, DV + DK), BF16),
            pltpu.VMEM((chunks - 1, value_heads, DK, DV + DK), BF16),
            pltpu.VMEM((value_heads, DK, DV + DK), BF16),
            pltpu.SemaphoreType.DMA,
            pltpu.SemaphoreType.DMA((chunks,)),
            pltpu.SemaphoreType.DMA((value_heads // min(HEADS_AT_ONCE, value_heads),)),
        ],
        compiler_params=in_vmem(54),
        cost_estimate=pl.CostEstimate(flops=20 * work, bytes_accessed=0, transcendentals=0),
        name="states",
    )(raws[1], raws[2], before, before, taps[1], taps[2], beta, decay, moves)
    gain = norm_gain.reshape(1, DV)

    def local():
        steps, narrow, wide, of_heads, logits = split(math.gcd(2, key_heads))
        heads = wide // DV
        return pl.pallas_call(
            local_kernel,
            grid=(steps,),
            in_specs=[
                columns_of(length, narrow), columns_of(3, narrow, repeat_by * steps), columns_of(4, narrow),
                columns_of(CHUNK, narrow), columns_of(later, narrow), logits,
                of_heads(CHUNK, DV + DK), of_heads(later, DV + DK),
                pl.BlockSpec((chunks - 1, heads, DK, DV + DK), lambda step: (0, step, 0, 0)),
                columns_of(length, wide), whole(gain.shape),
            ],
            out_specs=[of_heads(length, DV + DK), columns_of(length, wide)],
            out_shape=[
                jax.ShapeDtypeStruct((value_heads, length, DV + DK), BF16),
                jax.ShapeDtypeStruct(gate_raw.shape, BF16),
            ],
            scratch_shapes=[pltpu.VMEM((narrow // DK, 8 + length, DK), F32)],
            compiler_params=in_vmem(60),
            cost_estimate=pl.CostEstimate(flops=12 * work, bytes_accessed=0, transcendentals=0),
            name="local",
        )(
            raws[0], before, taps[0], first_unit, later_unit, decay,
            first_solved, solved, starts, gate_raw, gain,
        )

    return pairs, local


def prefix_kernel(pairs_ref, prefix_ref, total_ref):
    count, heads = pairs_ref.shape[:2]
    running = [None] * heads
    for hop in range(count):
        for head in range(heads):
            now = pairs_ref[hop, head]
            if hop == 0:
                rows = lax.broadcasted_iota(jnp.int32, (DK, DV + DK), 0)
                cols = lax.broadcasted_iota(jnp.int32, (DK, DV + DK), 1)
                prefix_ref[hop, head] = jnp.where(cols == rows + DV, 1.0, 0.0).astype(BF16)
                running[head] = now.astype(F32)
            else:
                before = running[head].astype(BF16)
                prefix_ref[hop, head] = before
                own = jnp.concatenate([now[:, :DV].astype(F32), jnp.zeros((DK, DK), F32)], 1)
                running[head] = own + mul(now[:, DV:], before)
    for head in range(heads):
        total_ref[head] = running[head][:, : total_ref.shape[2]].astype(BF16)


def apply_kernel(prefix_ref, start_ref, starts_ref):
    count, heads = prefix_ref.shape[:2]
    for hop in range(count):
        for head in range(heads):
            starts_ref[hop, head] = (
                prefix_ref[hop, head, :, :DV].astype(F32)
                + mul(prefix_ref[hop, head, :, DV:], start_ref[head])
            ).astype(BF16)


def shifted(value, axis, by):
    count = lax.axis_size(axis)
    return lax.ppermute(value, axis, [(i, i + by) for i in range(count - by)])


def group_start(total, axis, group):
    groups = lax.axis_size(axis) // group
    running = shifted(total, axis, group)
    by = 1
    while by < groups - 1:
        earlier = shifted(running, axis, by * group)
        product = jnp.einsum("bkl,blv->bkv", running[..., DV:], earlier, preferred_element_type=F32)
        own = jnp.pad(running[..., :DV], ((0, 0), (0, 0), (0, DK)))
        running = (product + own.astype(F32)).astype(BF16)
        by *= 2
    return running[..., :DV]


def starts_of(pairs, axis, beside):
    size = lax.axis_size(axis)
    heads = pairs.shape[0]
    group = math.gcd(math.gcd(size, heads), GROUP)
    groups = [[g * group + i for i in range(group)] for g in range(size // group)]
    each = heads // group
    wide = DV if size // group == 2 else DV + DK
    by_head = lax.all_to_all(pairs, axis, 0, 0, axis_index_groups=groups, tiled=True)
    by_head, done = lax.optimization_barrier((by_head, beside()))
    prefix, total = pl.pallas_call(
        prefix_kernel,
        out_shape=[
            jax.ShapeDtypeStruct((group, each, DK, DV + DK), BF16),
            jax.ShapeDtypeStruct((each, DK, wide), BF16),
        ],
        compiler_params=in_vmem(16),
        name="prefix",
    )(by_head.reshape(group, each, DK, DV + DK))
    starts = pl.pallas_call(
        apply_kernel,
        out_shape=jax.ShapeDtypeStruct((group, each, DK, DV), BF16),
        compiler_params=in_vmem(16),
        name="apply",
    )(prefix, group_start(total, axis, group))
    starts = lax.all_to_all(
        starts.reshape(heads, DK, DV), axis, 0, 0, axis_index_groups=groups, tiled=True
    )
    return starts, done


def project_kernel(
    place_ref, starts_ref, gated_ref, parts_hbm, weight_hbm, away_ref, own_ref,
    parts_ref, weight_ref, total, parts_sem, weight_sem,
):
    heads, length = parts_ref.shape[:2]
    width = weight_ref.shape[1]
    each = min(HEADS_AT_ONCE, heads)
    block = min(512, width)
    groups = heads // each

    def parts(g):
        here = pl.ds(g * each, each)
        return pltpu.make_async_copy(parts_hbm.at[here], parts_ref.at[here], parts_sem.at[g])

    def weights(g):
        rows = pl.ds(g * each * DV, each * DV)
        return pltpu.make_async_copy(weight_hbm.at[rows], weight_ref.at[rows], weight_sem.at[g])

    def normed_group(g):
        normed = []
        for head in range(g * each, (g + 1) * each):
            core = parts_ref[head, :, :DV].astype(F32) + mul(
                parts_ref[head, :, DV:], starts_ref[head]
            )
            scale = lax.rsqrt(jnp.mean(core * core, -1, keepdims=True) + EPSILON)
            normed.append((core * scale * gated_ref[:, head_of(head)].astype(F32)).astype(BF16))
        return jnp.concatenate(normed, 1)

    parts(0).start()
    weights(0).start()
    parts(0).wait()
    if groups > 1:
        parts(1).start()
        weights(1).start()
    following = normed_group(0)
    for g in range(groups):
        weights(g).wait()
        if g + 2 < groups:
            weights(g + 2).start()
        if g + 1 < groups:
            parts(g + 1).wait()
        if g + 2 < groups:
            parts(g + 2).start()
        normed = following
        if g + 1 < groups:
            following = normed_group(g + 1)
        for at in range(0, width, block):
            added = jnp.dot(
                normed, weight_ref[g * each * DV : (g + 1) * each * DV, at : at + block],
                preferred_element_type=F32,
            )
            if g > 0:
                added = added + total[:, at : at + block]
            if g < groups - 1:
                total[:, at : at + block] = added
            elif own_ref is None:
                away_ref[:, at : at + block] = added.astype(BF16)
            else:
                first = place_ref[0] == 0
                low, high = added[: length // 2], added[length // 2 :]
                own_ref[:, at : at + block] = jnp.where(first, low, high).astype(BF16)
                away_ref[:, at : at + block] = jnp.where(first, high, low).astype(BF16)


def whole_kernel(place_ref, starts_ref, gated_ref, parts_hbm, weight_hbm, out_ref, *scratch):
    project_kernel(place_ref, starts_ref, gated_ref, parts_hbm, weight_hbm, out_ref, None, *scratch)


def projected(parts, starts, gated, out_weight, axis):
    heads, length = parts.shape[:2]
    width = out_weight.shape[1]
    halves = lax.axis_size(axis) == 2
    vmem = pl.BlockSpec(memory_space=pltpu.VMEM)
    hbm = pl.BlockSpec(memory_space=pltpu.HBM)
    groups = heads // min(HEADS_AT_ONCE, heads)
    here = lax.axis_index(axis).astype(jnp.int32).reshape(1)
    out = jax.ShapeDtypeStruct((length // 2 if halves else length, width), BF16)
    partial = pl.pallas_call(
        project_kernel if halves else whole_kernel,
        in_specs=[pl.BlockSpec(memory_space=pltpu.SMEM), vmem, vmem, hbm, hbm],
        out_specs=[vmem, vmem] if halves else vmem,
        out_shape=[out, out] if halves else out,
        scratch_shapes=[
            pltpu.VMEM(parts.shape, BF16),
            pltpu.VMEM(out_weight.shape, BF16),
            pltpu.VMEM((length, width), F32),
            pltpu.SemaphoreType.DMA((groups,)),
            pltpu.SemaphoreType.DMA((groups,)),
        ],
        compiler_params=in_vmem(50),
        name="project",
    )(here, starts, gated, parts, out_weight)
    if not halves:
        return lax.psum_scatter(partial, axis, scatter_dimension=0, tiled=True)
    away, own = partial
    other = lax.ppermute(away, axis, [(0, 1), (1, 0)])
    return (own.astype(F32) + other.astype(F32)).astype(BF16)


def tails_kernel(value_hbm, query_hbm, key_hbm, out_ref, value_ref, query_ref, key_ref, sem):
    pairs = ((value_hbm, value_ref), (query_hbm, query_ref), (key_hbm, key_ref))
    copies = [
        pltpu.make_async_copy(source.at[pl.ds(source.shape[0] - 16, 16)], held, sem.at[i])
        for i, (source, held) in enumerate(pairs)
    ]
    for copy in copies:
        copy.start()
    at = 0
    for copy, (_, held) in zip(copies, pairs):
        copy.wait()
        width = held.shape[1]
        out_ref[:, at : at + width] = held[...].astype(F32)[13:16].astype(BF16)
        at += width


def tails(raws):
    order = (raws[2], raws[0], raws[1])
    width = sum(raw.shape[1] for raw in order)
    return pl.pallas_call(
        tails_kernel,
        in_specs=[pl.BlockSpec(memory_space=pltpu.HBM)] * 3,
        out_shape=jax.ShapeDtypeStruct((3, width), BF16),
        scratch_shapes=[pltpu.VMEM((16, raw.shape[1]), BF16) for raw in order]
        + [pltpu.SemaphoreType.DMA((3,))],
        compiler_params=in_vmem(60),
        name="tails",
    )(*order)


def shards(
    query_raw, key_raw, value_raw, gate_raw, query_taps, key_taps, value_taps,
    beta_logit, decay_logit, norm_gain, out_weight,
):
    raws = (query_raw, key_raw, value_raw)
    before = shifted(tails(raws), "seq", 1)
    pairs, local = local_steps(
        raws, before, (query_taps, key_taps, value_taps), beta_logit, decay_logit, gate_raw, norm_gain
    )
    starts, (parts, gated) = starts_of(pairs, "seq", local)
    return projected(parts, starts, gated, out_weight, "head")


def solution(mesh):
    placed = (
        P("seq", "head"), P("seq", "head"), P("seq", "head"), P("seq", "head"),
        P(None, "head"), P(None, "head"), P(None, "head"),
        P("seq", "head"), P("seq", "head"), P(), P("head", None),
    )
    return jax.shard_map(
        shards, mesh=mesh, in_specs=placed, out_specs=P(("seq", "head"), None), check_vma=False
    )
```

```python
import functools
import math

import jax
import jax.numpy as jnp
from jax import lax
from jax.experimental import pallas as pl
from jax.experimental.pallas import tpu as pltpu
from jax.sharding import PartitionSpec as P

DK = 128
DV = 128
CHUNK = 128
TINY = 8
SMALL = 32
GROUP = 8
HEADS_AT_ONCE = 4
EPSILON = 1e-06
F32 = jnp.float32
BF16 = jnp.bfloat16


def mul(left, right):
    return jnp.dot(left.astype(BF16), right.astype(BF16), preferred_element_type=F32)


def sigmoid(x):
    return 0.5 + 0.5 * jnp.tanh(0.5 * x)


def conv_silu(padded, first, rows, taps_ref, head):
    taps = taps_ref[:, head_of(head)]
    summed = taps[0:1] * padded[head, first : first + rows, :]
    for offset in range(1, 4):
        summed = summed + taps[offset : offset + 1] * padded[head, first + offset : first + offset + rows, :]
    return summed * sigmoid(summed)


def widen(padded, first, rows, raw):
    for head in range(padded.shape[0]):
        padded[head, first : first + rows, :] = raw[:, head_of(head)].astype(F32)


def unit_rows(key):
    return key * lax.rsqrt(jnp.sum(key * key, -1, keepdims=True) + EPSILON)


def part_of(chunk):
    return slice(chunk * CHUNK, (chunk + 1) * CHUNK)


def head_of(head):
    return slice(head * DK, (head + 1) * DK)


def chunk_rows(ref, heads, chunks):
    held = ref.shape[0]
    first = (pl.program_id(0) * heads) % held
    rows = ref[:heads, :]
    for at in range(heads, held, heads):
        rows = jnp.where(first == at, ref[at : at + heads, :], rows)
    return jnp.concatenate([rows[:, part_of(c)] for c in chunks], 0)


def square_iotas(rows=CHUNK):
    return (
        lax.broadcasted_iota(jnp.int32, (rows, CHUNK), 0),
        lax.broadcasted_iota(jnp.int32, (rows, CHUNK), 1),
    )


def log_fades(logit):
    rows, cols = square_iotas()
    decay = -(jnp.maximum(logit, 0.0) + jnp.log(1.0 + jnp.exp(-jnp.abs(logit))))
    return jnp.dot(
        decay, (rows <= cols).astype(F32), precision=lax.Precision.HIGHEST, preferred_element_type=F32
    )


def as_columns(blocks):
    rows = sum(block.shape[0] for block in blocks)
    return jnp.concatenate(list(blocks) + [jnp.zeros((CHUNK - rows, CHUNK), F32)], 0).T


def tiny_inverses(lower):
    lanes = lax.broadcasted_iota(jnp.int32, (TINY, CHUNK), 1)
    rows = lax.broadcasted_iota(jnp.int32, (TINY, CHUNK), 0)
    blocks = []
    for low in lower:
        block = low[:TINY]
        for at in range(1, CHUNK // TINY):
            block = jnp.where(lanes // TINY == at, low[at * TINY : (at + 1) * TINY], block)
        blocks.append(block)
    stacked = jnp.concatenate(blocks, 0)
    all_lanes = lax.broadcasted_iota(jnp.int32, stacked.shape, 1)
    factors = [
        jnp.take_along_axis(
            stacked, all_lanes // TINY * TINY + c, axis=1, mode="promise_in_bounds"
        )
        for c in range(TINY - 1)
    ]
    inverses = []
    for p in range(len(lower)):
        inverse = jnp.where(lanes % TINY == rows, 1.0, 0.0)
        for c in range(TINY - 1):
            inverse = inverse - factors[c][p * TINY : (p + 1) * TINY] * inverse[c : c + 1]
        inverses.append(inverse)
    return inverses


def solved_packs(fade, beta, keys, key_cols, value_work, value_of):
    count = len(keys)
    stages = 6
    done = [0, 0]

    def between():
        done[1] += 1
        while done[0] < len(value_work) and done[0] * stages < len(value_work) * done[1]:
            value_work[done[0]]()
            done[0] += 1

    rows, cols = square_iotas()
    strict = rows > cols
    differ = rows ^ cols
    columns = as_columns((fade, beta, beta * jnp.exp(fade)))
    inner = {}
    for key, turned in zip(keys, key_cols):
        if id(key) not in inner:
            inner[id(key)] = mul(key, turned)
    lower = []
    for p in range(count):
        gap = columns[:, p : p + 1] - fade[p : p + 1, :]
        ratio = jnp.exp(jnp.where(strict, gap, -1e30))
        lower.append(columns[:, count + p : count + p + 1] * ratio * inner[id(keys[p])])

    small_rows, small_cols = square_iotas(SMALL)
    small_differ = small_rows ^ (small_cols % SMALL)
    place = small_cols // SMALL
    blocks = jnp.where(rows // SMALL == cols // SMALL, 1.0, 0.0)
    blocks16 = blocks.astype(BF16)

    def spread(small):
        return jnp.concatenate([small] * (CHUNK // SMALL), 0) * (blocks16 if small.dtype == BF16 else blocks)

    small = []
    for low in lower:
        held = low[:SMALL]
        for at in range(1, CHUNK // SMALL):
            held = jnp.where(place == at, low[at * SMALL : (at + 1) * SMALL], held)
        small.append(held)
    tiny_inverse = tiny_inverses(lower)
    held = (small_cols % SMALL) // TINY == small_rows // TINY
    inverse = [
        jnp.where(held, jnp.concatenate([one] * (SMALL // TINY), 0), 0.0) for one in tiny_inverse
    ]
    size = TINY
    while size < CHUNK:
        last = size == SMALL
        if last:
            band = (differ >= size) & (differ < 4 * size)
            inside = [jnp.where(band, low, 0.0).astype(BF16) for low in lower]
            inverse16 = [spread(one.astype(BF16)) for one in inverse]
            inverse = [spread(one) for one in inverse]
            wide16 = inverse16
        else:
            band = (small_differ >= size) & (small_differ < 4 * size)
            inside = [spread(jnp.where(band, one, 0.0).astype(BF16)) for one in small]
            inverse16 = [one.astype(BF16) for one in inverse]
            wide16 = [spread(one) for one in inverse16]
        between()
        step = [mul(inverse16[p], inside[p]).astype(BF16) for p in range(count)]
        between()
        both = [
            mul(step[p], jnp.concatenate([step[p] if last else spread(step[p]), wide16[p]], 1))
            for p in range(count)
        ]
        between()
        inverse = [inverse[p] - both[p][:, CHUNK:] for p in range(count)]
        partial = [inverse[p].astype(BF16) for p in range(count)]
        inverse = [
            inverse[p] + mul(both[p][:, :CHUNK], partial[p] if last else spread(partial[p]))
            for p in range(count)
        ]
        size *= 4

    solved = []
    for p in range(count):
        right = jnp.concatenate(
            [
                columns[:, count + p : count + p + 1] * value_of(p),
                columns[:, 2 * count + p : 2 * count + p + 1] * keys[p],
            ],
            1,
        )
        solved.append(mul(inverse[p], right))
    return solved


def later_kernel(
    key_ref, value_ref, key_taps, value_taps, beta_ref, decay_ref,
    solved_ref, moves_ref, unit_ref, key_padded, value_padded,
):
    length, width = key_ref.shape
    chunks = range(1, length // CHUNK)
    key_heads = width // DK
    heads = value_ref.shape[1] // DV
    repeat_by = heads // key_heads
    packs = [(chunk, head) for chunk in chunks for head in range(heads)]
    skip = CHUNK - 16
    count = length - CHUNK
    widen(key_padded, 0, count + 16, key_ref[skip:, :])
    widen(value_padded, 0, count + 16, value_ref[skip:, :])
    key, turned = {}, {}
    for j in range(key_heads):
        unit = unit_rows(conv_silu(key_padded, 13, count, key_taps, j))
        unit_ref[:, head_of(j)] = unit.astype(BF16)
        for chunk in chunks:
            key[chunk, j] = unit[part_of(chunk - 1)]
            turned[chunk, j] = key[chunk, j].T
    value = {}

    def make_value(head):
        value[head] = conv_silu(value_padded, 13, count, value_taps, head)

    def value_of(pack):
        chunk, head = packs[pack]
        return value[head][part_of(chunk - 1)]

    fade = log_fades(chunk_rows(decay_ref, heads, chunks))
    solved = solved_packs(
        fade,
        sigmoid(chunk_rows(beta_ref, heads, chunks)),
        [key[chunk, head // repeat_by] for chunk, head in packs],
        [turned[chunk, head // repeat_by] for chunk, head in packs],
        [functools.partial(make_value, head) for head in range(heads)],
        value_of,
    )
    tail = jnp.exp(fade[:, CHUNK - 1 : CHUNK] - fade)
    for pack, (chunk, head) in enumerate(packs):
        one = solved[pack].astype(BF16)
        solved_ref[head, part_of(chunk - 1), :] = one
        moves_ref[head, chunk - 1] = mul(
            turned[chunk, head // repeat_by] * tail[pack : pack + 1, :], one
        ).astype(BF16)


def states_kernel(
    key_ref, value_ref, key_before, value_before, key_taps, value_taps, beta_ref, decay_ref, moves_hbm,
    pairs_hbm, unit_ref, solved_hbm, starts_hbm,
    key_padded, value_padded, moves_ref, solved_ref, starts_ref, pairs_ref, in_sem, out_sem, pairs_sem,
):
    heads, length = decay_ref.shape
    chunks = length // CHUNK
    key_heads = key_ref.shape[1] // DK
    repeat_by = heads // key_heads
    incoming = pltpu.make_async_copy(moves_hbm, moves_ref, in_sem)
    incoming.start()

    widen(key_padded, 5, 3, key_before[...])
    widen(key_padded, 8, CHUNK, key_ref[...])
    widen(value_padded, 5, 3, value_before[...])
    widen(value_padded, 8, CHUNK, value_ref[...])
    key, turned = [], []
    for j in range(key_heads):
        key.append(unit_rows(conv_silu(key_padded, 5, CHUNK, key_taps, j)))
        unit_ref[:, head_of(j)] = key[j].astype(BF16)
        turned.append(key[j].T)
    fade = log_fades(chunk_rows(decay_ref, heads, range(chunks)))
    value = {}

    def make_value(head):
        value[head] = conv_silu(value_padded, 5, CHUNK, value_taps, head)

    solved = solved_packs(
        fade[:heads],
        sigmoid(beta_ref[:, :CHUNK]),
        [key[head // repeat_by] for head in range(heads)],
        [turned[head // repeat_by] for head in range(heads)],
        [functools.partial(make_value, head) for head in range(heads)],
        lambda head: value[head],
    )
    last = jnp.exp(fade[:, CHUNK - 1 : CHUNK])
    tail = jnp.exp(fade[:, CHUNK - 1 : CHUNK] - fade)
    rows, cols = square_iotas()
    identity = jnp.where(rows == cols, 1.0, 0.0)

    state = []
    for head in range(heads):
        one = solved[head].astype(BF16)
        solved_ref[head] = one
        moved = mul(turned[head // repeat_by] * tail[head : head + 1, :], one)
        state.append(
            jnp.concatenate([moved[:, :DV], last[head : head + 1, :] * identity - moved[:, DV:]], 1)
        )
    each = min(HEADS_AT_ONCE, heads)
    outgoing = [pltpu.make_async_copy(solved_ref, solved_hbm, out_sem.at[0])]
    outgoing[0].start()
    incoming.wait()
    for chunk in range(1, chunks):
        for head in range(heads):
            pack = chunk * heads + head
            start = state[head].astype(BF16)
            starts_ref[chunk - 1, head] = start
            moves = moves_ref[head, chunk - 1]
            moved = last[pack : pack + 1, :] * state[head] - mul(moves[:, DV:], start)
            state[head] = jnp.concatenate([moved[:, :DV] + moves[:, :DV].astype(F32), moved[:, DV:]], 1)
            if chunk == chunks - 1:
                pairs_ref[head] = state[head].astype(BF16)
                if (head + 1) % each == 0:
                    done = pl.ds(head + 1 - each, each)
                    outgoing.append(
                        pltpu.make_async_copy(
                            pairs_ref.at[done], pairs_hbm.at[done], pairs_sem.at[head // each]
                        )
                    )
                    outgoing[-1].start()
        outgoing.append(
            pltpu.make_async_copy(
                starts_ref.at[chunk - 1], starts_hbm.at[chunk - 1], out_sem.at[chunk]
            )
        )
        outgoing[-1].start()
    for copy in outgoing:
        copy.wait()


def local_kernel(
    query_ref, query_before, query_taps, first_unit, later_unit, decay_ref,
    first_solved, later_solved, starts_ref, gate_ref, gain_ref,
    parts_ref, gated_ref, padded,
):
    length, width = query_ref.shape
    chunks = length // CHUNK
    key_heads = width // DK
    heads = first_solved.shape[0]
    repeat_by = heads // key_heads

    rows, cols = square_iotas()
    within = rows >= cols
    fade = log_fades(chunk_rows(decay_ref, heads, range(chunks)))
    columns = as_columns((fade, jnp.exp(fade)))
    widen(padded, 5, 3, query_before[...])
    widen(padded, 8, length, query_ref[...])
    query = [conv_silu(padded, 5, length, query_taps, j).astype(BF16) for j in range(key_heads)]
    for head in range(heads):
        gate = gate_ref[:, head_of(head)].astype(F32)
        gated_ref[:, head_of(head)] = (gate * sigmoid(gate) * gain_ref[...]).astype(BF16)
    for chunk in range(chunks):
        part = part_of(chunk)
        for j in range(key_heads):
            own = query[j][part]
            unit = first_unit[:, head_of(j)] if chunk == 0 else later_unit[part_of(chunk - 1), head_of(j)]
            inner = lax.dot_general(
                own, unit, (((1,), (1,)), ((), ())), preferred_element_type=F32
            )
            for head in range(j * repeat_by, (j + 1) * repeat_by):
                pack = chunk * heads + head
                gap = columns[:, pack : pack + 1] - fade[pack : pack + 1, :]
                scores = inner * jnp.exp(jnp.where(within, gap, -1e30))
                grown = columns[:, chunks * heads + pack : chunks * heads + pack + 1]
                if chunk == 0:
                    updates, wide = first_solved[head, :, :DV], first_solved[head, :, DV:]
                    fresh = jnp.concatenate([updates, -wide], 1)
                    carried = jnp.concatenate(
                        [jnp.zeros((CHUNK, DV), F32), grown * own.astype(F32)], 1
                    )
                else:
                    solved = later_solved[head, part_of(chunk - 1), :]
                    both = mul(jnp.concatenate([solved[:, DV:], own], 0), starts_ref[chunk - 1, head])
                    taken = both[:CHUNK]
                    fresh = jnp.concatenate(
                        [solved[:, :DV].astype(F32) - taken[:, :DV], -taken[:, DV:]], 1
                    )
                    carried = grown * both[CHUNK:]
                parts_ref[head, part, :] = (carried + mul(scores, fresh)).astype(BF16)


def columns_of(rows, width, first=0):
    return pl.BlockSpec((rows, width), lambda step: (0, step + first))


def in_vmem(mib):
    return pltpu.CompilerParams(vmem_limit_bytes=mib * 1024 * 1024)


def local_steps(raws, before, taps, beta_logit, decay_logit, gate_raw, norm_gain):
    length = raws[0].shape[0]
    key_heads = raws[0].shape[1] // DK
    value_heads = raws[2].shape[1] // DV
    repeat_by = value_heads // key_heads
    chunks = length // CHUNK
    beta, decay = beta_logit.T, decay_logit.T
    work = CHUNK * length * DV * value_heads
    hbm = pl.BlockSpec(memory_space=pltpu.HBM)

    def split(each):
        heads = each * repeat_by
        held = max(heads, math.gcd(8, value_heads))
        of_heads = lambda *shape: pl.BlockSpec((heads,) + shape, lambda step: (step,) + (0,) * len(shape))
        logits = pl.BlockSpec((held, length), lambda step: (step * heads // held, 0))
        return key_heads // each, each * DK, heads * DV, of_heads, logits

    each = math.gcd(4, key_heads)
    steps, narrow, wide, of_heads, logits = split(each)
    later = length - CHUNK
    solved, moves, later_unit = pl.pallas_call(
        later_kernel,
        grid=(steps,),
        in_specs=[
            columns_of(length, narrow), columns_of(length, wide),
            columns_of(4, narrow), columns_of(4, wide), logits, logits,
        ],
        out_specs=[
            of_heads(later, DV + DK), of_heads(chunks - 1, DK, DV + DK), columns_of(later, narrow),
        ],
        out_shape=[
            jax.ShapeDtypeStruct((value_heads, later, DV + DK), BF16),
            jax.ShapeDtypeStruct((value_heads, chunks - 1, DK, DV + DK), BF16),
            jax.ShapeDtypeStruct((later, key_heads * DK), BF16),
        ],
        scratch_shapes=[
            pltpu.VMEM((each, later + 16, DK), F32),
            pltpu.VMEM((each * repeat_by, later + 16, DV), F32),
        ],
        compiler_params=in_vmem(60),
        cost_estimate=pl.CostEstimate(flops=30 * work, bytes_accessed=0, transcendentals=0),
        name="later",
    )(raws[1], raws[2], taps[1], taps[2], beta, decay)

    narrow, wide = key_heads * DK, value_heads * DV
    whole = lambda shape, *at: pl.BlockSpec(shape, lambda step: at or (0,) * len(shape))
    pairs, first_unit, first_solved, starts = pl.pallas_call(
        states_kernel,
        grid=(1,),
        in_specs=[
            whole((CHUNK, narrow)), whole((CHUNK, wide)),
            whole((3, narrow), 0, repeat_by + 1), whole((3, wide)),
            whole(taps[1].shape), whole(taps[2].shape), whole(beta.shape), whole(decay.shape), hbm,
        ],
        out_specs=[hbm, whole((CHUNK, narrow)), hbm, hbm],
        out_shape=[
            jax.ShapeDtypeStruct((value_heads, DK, DV + DK), BF16),
            jax.ShapeDtypeStruct((CHUNK, narrow), BF16),
            jax.ShapeDtypeStruct((value_heads, CHUNK, DV + DK), BF16),
            jax.ShapeDtypeStruct((chunks - 1, value_heads, DK, DV + DK), BF16),
        ],
        scratch_shapes=[
            pltpu.VMEM((key_heads, 8 + CHUNK, DK), F32),
            pltpu.VMEM((value_heads, 8 + CHUNK, DV), F32),
            pltpu.VMEM(moves.shape, BF16),
            pltpu.VMEM((value_heads, CHUNK, DV + DK), BF16),
            pltpu.VMEM((chunks - 1, value_heads, DK, DV + DK), BF16),
            pltpu.VMEM((value_heads, DK, DV + DK), BF16),
            pltpu.SemaphoreType.DMA,
            pltpu.SemaphoreType.DMA((chunks,)),
            pltpu.SemaphoreType.DMA((value_heads // min(HEADS_AT_ONCE, value_heads),)),
        ],
        compiler_params=in_vmem(54),
        cost_estimate=pl.CostEstimate(flops=20 * work, bytes_accessed=0, transcendentals=0),
        name="states",
    )(raws[1], raws[2], before, before, taps[1], taps[2], beta, decay, moves)
    gain = norm_gain.reshape(1, DV)

    def local():
        steps, narrow, wide, of_heads, logits = split(math.gcd(2, key_heads))
        heads = wide // DV
        return pl.pallas_call(
            local_kernel,
            grid=(steps,),
            in_specs=[
                columns_of(length, narrow), columns_of(3, narrow, repeat_by * steps), columns_of(4, narrow),
                columns_of(CHUNK, narrow), columns_of(later, narrow), logits,
                of_heads(CHUNK, DV + DK), of_heads(later, DV + DK),
                pl.BlockSpec((chunks - 1, heads, DK, DV + DK), lambda step: (0, step, 0, 0)),
                columns_of(length, wide), whole(gain.shape),
            ],
            out_specs=[of_heads(length, DV + DK), columns_of(length, wide)],
            out_shape=[
                jax.ShapeDtypeStruct((value_heads, length, DV + DK), BF16),
                jax.ShapeDtypeStruct(gate_raw.shape, BF16),
            ],
            scratch_shapes=[pltpu.VMEM((narrow // DK, 8 + length, DK), F32)],
            compiler_params=in_vmem(60),
            cost_estimate=pl.CostEstimate(flops=12 * work, bytes_accessed=0, transcendentals=0),
            name="local",
        )(
            raws[0], before, taps[0], first_unit, later_unit, decay,
            first_solved, solved, starts, gate_raw, gain,
        )

    return pairs, local


def prefix_kernel(pairs_ref, prefix_ref, total_ref):
    count, heads = pairs_ref.shape[:2]
    running = [None] * heads
    for hop in range(count):
        for head in range(heads):
            now = pairs_ref[hop, head]
            if hop == 0:
                rows = lax.broadcasted_iota(jnp.int32, (DK, DV + DK), 0)
                cols = lax.broadcasted_iota(jnp.int32, (DK, DV + DK), 1)
                prefix_ref[hop, head] = jnp.where(cols == rows + DV, 1.0, 0.0).astype(BF16)
                running[head] = now.astype(F32)
            else:
                before = running[head].astype(BF16)
                prefix_ref[hop, head] = before
                own = jnp.concatenate([now[:, :DV].astype(F32), jnp.zeros((DK, DK), F32)], 1)
                running[head] = own + mul(now[:, DV:], before)
    for head in range(heads):
        total_ref[head] = running[head][:, : total_ref.shape[2]].astype(BF16)


def apply_kernel(prefix_ref, start_ref, starts_ref):
    count, heads = prefix_ref.shape[:2]
    for hop in range(count):
        for head in range(heads):
            starts_ref[hop, head] = (
                prefix_ref[hop, head, :, :DV].astype(F32)
                + mul(prefix_ref[hop, head, :, DV:], start_ref[head])
            ).astype(BF16)


def shifted(value, axis, by):
    count = lax.axis_size(axis)
    return lax.ppermute(value, axis, [(i, i + by) for i in range(count - by)])


def group_start(total, axis, group):
    groups = lax.axis_size(axis) // group
    running = shifted(total, axis, group)
    by = 1
    while by < groups - 1:
        earlier = shifted(running, axis, by * group)
        product = jnp.einsum("bkl,blv->bkv", running[..., DV:], earlier, preferred_element_type=F32)
        own = jnp.pad(running[..., :DV], ((0, 0), (0, 0), (0, DK)))
        running = (product + own.astype(F32)).astype(BF16)
        by *= 2
    return running[..., :DV]


def starts_of(pairs, axis, beside):
    size = lax.axis_size(axis)
    heads = pairs.shape[0]
    group = math.gcd(math.gcd(size, heads), GROUP)
    groups = [[g * group + i for i in range(group)] for g in range(size // group)]
    each = heads // group
    wide = DV if size // group == 2 else DV + DK
    by_head = lax.all_to_all(pairs, axis, 0, 0, axis_index_groups=groups, tiled=True)
    by_head, done = lax.optimization_barrier((by_head, beside()))
    prefix, total = pl.pallas_call(
        prefix_kernel,
        out_shape=[
            jax.ShapeDtypeStruct((group, each, DK, DV + DK), BF16),
            jax.ShapeDtypeStruct((each, DK, wide), BF16),
        ],
        compiler_params=in_vmem(16),
        name="prefix",
    )(by_head.reshape(group, each, DK, DV + DK))
    starts = pl.pallas_call(
        apply_kernel,
        out_shape=jax.ShapeDtypeStruct((group, each, DK, DV), BF16),
        compiler_params=in_vmem(16),
        name="apply",
    )(prefix, group_start(total, axis, group))
    starts = lax.all_to_all(
        starts.reshape(heads, DK, DV), axis, 0, 0, axis_index_groups=groups, tiled=True
    )
    return starts, done


def project_kernel(
    place_ref, starts_ref, gated_ref, parts_hbm, weight_hbm, away_ref, own_ref,
    parts_ref, weight_ref, total, parts_sem, weight_sem,
):
    heads, length = parts_ref.shape[:2]
    width = weight_ref.shape[1]
    each = min(HEADS_AT_ONCE, heads)
    block = min(512, width)
    groups = heads // each

    def parts(g):
        here = pl.ds(g * each, each)
        return pltpu.make_async_copy(parts_hbm.at[here], parts_ref.at[here], parts_sem.at[g])

    def weights(g):
        rows = pl.ds(g * each * DV, each * DV)
        return pltpu.make_async_copy(weight_hbm.at[rows], weight_ref.at[rows], weight_sem.at[g])

    def normed_group(g):
        normed = []
        for head in range(g * each, (g + 1) * each):
            core = parts_ref[head, :, :DV].astype(F32) + mul(
                parts_ref[head, :, DV:], starts_ref[head]
            )
            scale = lax.rsqrt(jnp.mean(core * core, -1, keepdims=True) + EPSILON)
            normed.append((core * scale * gated_ref[:, head_of(head)].astype(F32)).astype(BF16))
        return jnp.concatenate(normed, 1)

    parts(0).start()
    weights(0).start()
    parts(0).wait()
    if groups > 1:
        parts(1).start()
        weights(1).start()
    following = normed_group(0)
    for g in range(groups):
        weights(g).wait()
        if g + 2 < groups:
            weights(g + 2).start()
        if g + 1 < groups:
            parts(g + 1).wait()
        if g + 2 < groups:
            parts(g + 2).start()
        normed = following
        if g + 1 < groups:
            following = normed_group(g + 1)
        for at in range(0, width, block):
            added = jnp.dot(
                normed, weight_ref[g * each * DV : (g + 1) * each * DV, at : at + block],
                preferred_element_type=F32,
            )
            if g > 0:
                added = added + total[:, at : at + block]
            if g < groups - 1:
                total[:, at : at + block] = added
            elif own_ref is None:
                away_ref[:, at : at + block] = added.astype(BF16)
            else:
                first = place_ref[0] == 0
                low, high = added[: length // 2], added[length // 2 :]
                own_ref[:, at : at + block] = jnp.where(first, low, high).astype(BF16)
                away_ref[:, at : at + block] = jnp.where(first, high, low).astype(BF16)


def whole_kernel(place_ref, starts_ref, gated_ref, parts_hbm, weight_hbm, out_ref, *scratch):
    project_kernel(place_ref, starts_ref, gated_ref, parts_hbm, weight_hbm, out_ref, None, *scratch)


def projected(parts, starts, gated, out_weight, axis):
    heads, length = parts.shape[:2]
    width = out_weight.shape[1]
    halves = lax.axis_size(axis) == 2
    vmem = pl.BlockSpec(memory_space=pltpu.VMEM)
    hbm = pl.BlockSpec(memory_space=pltpu.HBM)
    groups = heads // min(HEADS_AT_ONCE, heads)
    here = lax.axis_index(axis).astype(jnp.int32).reshape(1)
    out = jax.ShapeDtypeStruct((length // 2 if halves else length, width), BF16)
    partial = pl.pallas_call(
        project_kernel if halves else whole_kernel,
        in_specs=[pl.BlockSpec(memory_space=pltpu.SMEM), vmem, vmem, hbm, hbm],
        out_specs=[vmem, vmem] if halves else vmem,
        out_shape=[out, out] if halves else out,
        scratch_shapes=[
            pltpu.VMEM(parts.shape, BF16),
            pltpu.VMEM(out_weight.shape, BF16),
            pltpu.VMEM((length, width), F32),
            pltpu.SemaphoreType.DMA((groups,)),
            pltpu.SemaphoreType.DMA((groups,)),
        ],
        compiler_params=in_vmem(50),
        name="project",
    )(here, starts, gated, parts, out_weight)
    if not halves:
        return lax.psum_scatter(partial, axis, scatter_dimension=0, tiled=True)
    away, own = partial
    other = lax.ppermute(away, axis, [(0, 1), (1, 0)])
    return (own.astype(F32) + other.astype(F32)).astype(BF16)


def tails_kernel(value_hbm, query_hbm, key_hbm, out_ref, value_ref, query_ref, key_ref, sem):
    pairs = ((value_hbm, value_ref), (query_hbm, query_ref), (key_hbm, key_ref))
    copies = [
        pltpu.make_async_copy(source.at[pl.ds(source.shape[0] - 16, 16)], held, sem.at[i])
        for i, (source, held) in enumerate(pairs)
    ]
    for copy in copies:
        copy.start()
    at = 0
    for copy, (_, held) in zip(copies, pairs):
        copy.wait()
        width = held.shape[1]
        out_ref[:, at : at + width] = held[...].astype(F32)[13:16].astype(BF16)
        at += width


def tails(raws):
    order = (raws[2], raws[0], raws[1])
    width = sum(raw.shape[1] for raw in order)
    return pl.pallas_call(
        tails_kernel,
        in_specs=[pl.BlockSpec(memory_space=pltpu.HBM)] * 3,
        out_shape=jax.ShapeDtypeStruct((3, width), BF16),
        scratch_shapes=[pltpu.VMEM((16, raw.shape[1]), BF16) for raw in order]
        + [pltpu.SemaphoreType.DMA((3,))],
        compiler_params=in_vmem(60),
        name="tails",
    )(*order)


def shards(
    query_raw, key_raw, value_raw, gate_raw, query_taps, key_taps, value_taps,
    beta_logit, decay_logit, norm_gain, out_weight,
):
    raws = (query_raw, key_raw, value_raw)
    before = shifted(tails(raws), "seq", 1)
    pairs, local = local_steps(
        raws, before, (query_taps, key_taps, value_taps), beta_logit, decay_logit, gate_raw, norm_gain
    )
    starts, (parts, gated) = starts_of(pairs, "seq", local)
    return projected(parts, starts, gated, out_weight, "head")


def solution(mesh):
    placed = (
        P("seq", "head"), P("seq", "head"), P("seq", "head"), P("seq", "head"),
        P(None, "head"), P(None, "head"), P(None, "head"),
        P("seq", "head"), P("seq", "head"), P(), P("head", None),
    )
    return jax.shard_map(
        shards, mesh=mesh, in_specs=placed, out_specs=P(("seq", "head"), None), check_vma=False
    )
```

```python
import functools
import math

import jax
import jax.numpy as jnp
from jax import lax
from jax.experimental import pallas as pl
from jax.experimental.pallas import tpu as pltpu
from jax.sharding import PartitionSpec as P

DK = 128
DV = 128
CHUNK = 128
TINY = 8
SMALL = 32
GROUP = 8
HEADS_AT_ONCE = 4
EPSILON = 1e-06
F32 = jnp.float32
BF16 = jnp.bfloat16


def mul(left, right):
    return jnp.dot(left.astype(BF16), right.astype(BF16), preferred_element_type=F32)


def sigmoid(x):
    return 0.5 + 0.5 * jnp.tanh(0.5 * x)


def conv_silu(padded, first, rows, taps_ref, head):
    taps = taps_ref[:, head_of(head)]
    summed = taps[0:1] * padded[head, first : first + rows, :]
    for offset in range(1, 4):
        summed = summed + taps[offset : offset + 1] * padded[head, first + offset : first + offset + rows, :]
    return summed * sigmoid(summed)


def widen(padded, first, rows, raw):
    for head in range(padded.shape[0]):
        padded[head, first : first + rows, :] = raw[:, head_of(head)].astype(F32)


def row_sums(values, factor):
    return mul(values, jnp.full((CHUNK, CHUNK), factor, BF16))


def unit_rows(key):
    return key * lax.rsqrt(row_sums(key * key, 1.0) + EPSILON)


def softplus(x):
    return jnp.maximum(x, 0.0) + jnp.log(1.0 + jnp.exp(-jnp.abs(x)))


def part_of(chunk):
    return slice(chunk * CHUNK, (chunk + 1) * CHUNK)


def head_of(head):
    return slice(head * DK, (head + 1) * DK)


def chunk_rows(ref, heads, chunks):
    held = ref.shape[0]
    first = (pl.program_id(0) * heads) % held
    rows = ref[:heads, :]
    for at in range(heads, held, heads):
        rows = jnp.where(first == at, ref[at : at + heads, :], rows)
    return jnp.concatenate([rows[:, part_of(c)] for c in chunks], 0)


def square_iotas(rows=CHUNK):
    return (
        lax.broadcasted_iota(jnp.int32, (rows, CHUNK), 0),
        lax.broadcasted_iota(jnp.int32, (rows, CHUNK), 1),
    )


def log_fades(logit):
    rows, cols = square_iotas()
    return jnp.dot(
        -softplus(logit), (rows <= cols).astype(F32), precision=lax.Precision.HIGHEST, preferred_element_type=F32
    )


def as_columns(blocks):
    rows = sum(block.shape[0] for block in blocks)
    return jnp.concatenate(list(blocks) + [jnp.zeros((CHUNK - rows, CHUNK), F32)], 0).T


def tiny_inverses(lower):
    lanes = lax.broadcasted_iota(jnp.int32, (TINY, CHUNK), 1)
    rows = lax.broadcasted_iota(jnp.int32, (TINY, CHUNK), 0)
    blocks = []
    for low in lower:
        block = low[:TINY]
        for at in range(1, CHUNK // TINY):
            block = jnp.where(lanes // TINY == at, low[at * TINY : (at + 1) * TINY], block)
        blocks.append(block)
    stacked = jnp.concatenate(blocks, 0)
    all_lanes = lax.broadcasted_iota(jnp.int32, stacked.shape, 1)
    factors = [
        jnp.take_along_axis(
            stacked, all_lanes // TINY * TINY + c, axis=1, mode="promise_in_bounds"
        )
        for c in range(TINY - 1)
    ]
    inverses = []
    for p in range(len(lower)):
        inverse = jnp.where(lanes % TINY == rows, 1.0, 0.0)
        for c in range(TINY - 1):
            inverse = inverse - factors[c][p * TINY : (p + 1) * TINY] * inverse[c : c + 1]
        inverses.append(inverse)
    return inverses


def solved_packs(fade, beta_logit, keys, key_cols, value_work, value_of):
    count = len(keys)
    stages = 6
    done = [0, 0]

    def between():
        done[1] += 1
        while done[0] < len(value_work) and done[0] * stages < len(value_work) * done[1]:
            value_work[done[0]]()
            done[0] += 1

    rows, cols = square_iotas()
    strict = rows > cols
    differ = rows ^ cols
    columns = as_columns((fade - softplus(-beta_logit),))
    beta = sigmoid(beta_logit)
    beta_grown = beta * jnp.exp(fade)
    inner = {}
    for key, turned in zip(keys, key_cols):
        if id(key) not in inner:
            inner[id(key)] = mul(key, turned)
    lower = []
    for p in range(count):
        gap = columns[:, p : p + 1] - fade[p : p + 1, :]
        lower.append(jnp.exp(jnp.where(strict, gap, -1e30)) * inner[id(keys[p])])

    small_rows, small_cols = square_iotas(SMALL)
    small_differ = small_rows ^ (small_cols % SMALL)
    place = small_cols // SMALL
    blocks = jnp.where(rows // SMALL == cols // SMALL, 1.0, 0.0)
    blocks16 = blocks.astype(BF16)

    def spread(small):
        return jnp.concatenate([small] * (CHUNK // SMALL), 0) * (blocks16 if small.dtype == BF16 else blocks)

    small = []
    for low in lower:
        held = low[:SMALL]
        for at in range(1, CHUNK // SMALL):
            held = jnp.where(place == at, low[at * SMALL : (at + 1) * SMALL], held)
        small.append(held)
    tiny_inverse = tiny_inverses(lower)
    held = (small_cols % SMALL) // TINY == small_rows // TINY
    inverse = [
        jnp.where(held, jnp.concatenate([one] * (SMALL // TINY), 0), 0.0) for one in tiny_inverse
    ]
    size = TINY
    while size < CHUNK:
        last = size == SMALL
        if last:
            band = (differ >= size) & (differ < 4 * size)
            inside = [jnp.where(band, low, 0.0).astype(BF16) for low in lower]
            inverse16 = [spread(one.astype(BF16)) for one in inverse]
            inverse = [spread(one) for one in inverse]
            wide16 = inverse16
        else:
            band = (small_differ >= size) & (small_differ < 4 * size)
            inside = [spread(jnp.where(band, one, 0.0).astype(BF16)) for one in small]
            inverse16 = [one.astype(BF16) for one in inverse]
            wide16 = [spread(one) for one in inverse16]
        between()
        step = [mul(inverse16[p], inside[p]).astype(BF16) for p in range(count)]
        between()
        both = [
            mul(step[p], jnp.concatenate([step[p] if last else spread(step[p]), wide16[p]], 1))
            for p in range(count)
        ]
        between()
        inverse = [inverse[p] - both[p][:, CHUNK:] for p in range(count)]
        partial = [inverse[p].astype(BF16) for p in range(count)]
        inverse = [
            inverse[p] + mul(both[p][:, :CHUNK], partial[p] if last else spread(partial[p]))
            for p in range(count)
        ]
        size *= 4

    return [
        jnp.concatenate(
            [
                mul(inverse[p] * beta[p : p + 1, :], value_of(p)),
                mul(inverse[p] * beta_grown[p : p + 1, :], keys[p]),
            ],
            1,
        )
        for p in range(count)
    ]


def later_kernel(
    key_ref, value_ref, key_taps, value_taps, beta_ref, decay_ref,
    solved_ref, moves_ref, unit_ref, key_padded, value_padded,
):
    length, width = key_ref.shape
    chunks = range(1, length // CHUNK)
    key_heads = width // DK
    heads = value_ref.shape[1] // DV
    repeat_by = heads // key_heads
    packs = [(chunk, head) for chunk in chunks for head in range(heads)]
    skip = CHUNK - 16
    count = length - CHUNK
    widen(key_padded, 0, count + 16, key_ref[skip:, :])
    widen(value_padded, 0, count + 16, value_ref[skip:, :])
    key, turned = {}, {}
    for j in range(key_heads):
        unit = unit_rows(conv_silu(key_padded, 13, count, key_taps, j))
        unit_ref[:, head_of(j)] = unit.astype(BF16)
        for chunk in chunks:
            key[chunk, j] = unit[part_of(chunk - 1)]
            turned[chunk, j] = key[chunk, j].T
    value = {}

    def make_value(head):
        value[head] = conv_silu(value_padded, 13, count, value_taps, head)

    def value_of(pack):
        chunk, head = packs[pack]
        return value[head][part_of(chunk - 1)]

    fade = log_fades(chunk_rows(decay_ref, heads, chunks))
    solved = solved_packs(
        fade,
        chunk_rows(beta_ref, heads, chunks),
        [key[chunk, head // repeat_by] for chunk, head in packs],
        [turned[chunk, head // repeat_by] for chunk, head in packs],
        [functools.partial(make_value, head) for head in range(heads)],
        value_of,
    )
    tail = jnp.exp(fade[:, CHUNK - 1 : CHUNK] - fade)
    for pack, (chunk, head) in enumerate(packs):
        one = solved[pack].astype(BF16)
        solved_ref[head, part_of(chunk - 1), :] = one
        moves_ref[head, chunk - 1] = mul(
            turned[chunk, head // repeat_by] * tail[pack : pack + 1, :], one
        ).astype(BF16)


def states_kernel(
    key_ref, value_ref, key_before, value_before, key_taps, value_taps, beta_ref, decay_ref, moves_hbm,
    pairs_hbm, unit_ref, solved_hbm, starts_hbm,
    key_padded, value_padded, moves_ref, solved_ref, starts_ref, pairs_ref, in_sem, out_sem, pairs_sem,
):
    heads, length = decay_ref.shape
    chunks = length // CHUNK
    key_heads = key_ref.shape[1] // DK
    repeat_by = heads // key_heads
    incoming = pltpu.make_async_copy(moves_hbm, moves_ref, in_sem)
    incoming.start()

    widen(key_padded, 5, 3, key_before[...])
    widen(key_padded, 8, CHUNK, key_ref[...])
    widen(value_padded, 5, 3, value_before[...])
    widen(value_padded, 8, CHUNK, value_ref[...])
    key, turned = [], []
    for j in range(key_heads):
        key.append(unit_rows(conv_silu(key_padded, 5, CHUNK, key_taps, j)))
        unit_ref[:, head_of(j)] = key[j].astype(BF16)
        turned.append(key[j].T)
    fade = log_fades(chunk_rows(decay_ref, heads, range(chunks)))
    value = {}

    def make_value(head):
        value[head] = conv_silu(value_padded, 5, CHUNK, value_taps, head)

    solved = solved_packs(
        fade[:heads],
        beta_ref[:, :CHUNK],
        [key[head // repeat_by] for head in range(heads)],
        [turned[head // repeat_by] for head in range(heads)],
        [functools.partial(make_value, head) for head in range(heads)],
        lambda head: value[head],
    )
    last = jnp.exp(fade[:, CHUNK - 1 : CHUNK])
    tail = jnp.exp(fade[:, CHUNK - 1 : CHUNK] - fade)
    rows, cols = square_iotas()
    identity = jnp.where(rows == cols, 1.0, 0.0)

    state = []
    for head in range(heads):
        one = solved[head].astype(BF16)
        solved_ref[head] = one
        moved = mul(turned[head // repeat_by] * tail[head : head + 1, :], one)
        state.append(
            jnp.concatenate([moved[:, :DV], last[head : head + 1, :] * identity - moved[:, DV:]], 1)
        )
    each = min(HEADS_AT_ONCE, heads)
    outgoing = [pltpu.make_async_copy(solved_ref, solved_hbm, out_sem.at[0])]
    outgoing[0].start()
    incoming.wait()
    for chunk in range(1, chunks):
        for head in range(heads):
            pack = chunk * heads + head
            start = state[head].astype(BF16)
            starts_ref[chunk - 1, head] = start
            moves = moves_ref[head, chunk - 1]
            moved = last[pack : pack + 1, :] * state[head] - mul(moves[:, DV:], start)
            state[head] = jnp.concatenate([moved[:, :DV] + moves[:, :DV].astype(F32), moved[:, DV:]], 1)
            if chunk == chunks - 1:
                pairs_ref[head] = state[head].astype(BF16)
                if (head + 1) % each == 0:
                    done = pl.ds(head + 1 - each, each)
                    outgoing.append(
                        pltpu.make_async_copy(
                            pairs_ref.at[done], pairs_hbm.at[done], pairs_sem.at[head // each]
                        )
                    )
                    outgoing[-1].start()
        outgoing.append(
            pltpu.make_async_copy(
                starts_ref.at[chunk - 1], starts_hbm.at[chunk - 1], out_sem.at[chunk]
            )
        )
        outgoing[-1].start()
    for copy in outgoing:
        copy.wait()


def local_kernel(
    query_ref, query_before, query_taps, first_unit, later_unit, decay_ref,
    first_solved, later_solved, starts_ref, gate_ref, gain_ref,
    parts_ref, gated_ref, padded,
):
    length, width = query_ref.shape
    chunks = length // CHUNK
    key_heads = width // DK
    heads = first_solved.shape[0]
    repeat_by = heads // key_heads

    rows, cols = square_iotas()
    within = rows >= cols
    fade = log_fades(chunk_rows(decay_ref, heads, range(chunks)))
    columns = as_columns((fade,))
    widen(padded, 5, 3, query_before[...])
    widen(padded, 8, length, query_ref[...])
    query = [conv_silu(padded, 5, length, query_taps, j).astype(BF16) for j in range(key_heads)]
    for head in range(heads):
        gate = gate_ref[:, head_of(head)].astype(F32)
        gated_ref[:, head_of(head)] = (gate * sigmoid(gate) * gain_ref[...]).astype(BF16)
    for chunk in range(chunks):
        part = part_of(chunk)
        for j in range(key_heads):
            own = query[j][part]
            unit = first_unit[:, head_of(j)] if chunk == 0 else later_unit[part_of(chunk - 1), head_of(j)]
            inner = lax.dot_general(
                own, unit, (((1,), (1,)), ((), ())), preferred_element_type=F32
            )
            for head in range(j * repeat_by, (j + 1) * repeat_by):
                pack = chunk * heads + head
                column = jnp.broadcast_to(columns[:, pack : pack + 1], (CHUNK, CHUNK))
                scores = inner * jnp.exp(jnp.where(within, column - fade[pack : pack + 1, :], -1e30))
                grown = jnp.exp(column)
                if chunk == 0:
                    updates, wide = first_solved[head, :, :DV], first_solved[head, :, DV:]
                    fresh = jnp.concatenate([updates, -wide], 1)
                    carried = jnp.concatenate(
                        [jnp.zeros((CHUNK, DV), F32), grown * own.astype(F32)], 1
                    )
                else:
                    solved = later_solved[head, part_of(chunk - 1), :]
                    both = mul(jnp.concatenate([solved[:, DV:], own], 0), starts_ref[chunk - 1, head])
                    taken = both[:CHUNK]
                    fresh = jnp.concatenate(
                        [solved[:, :DV].astype(F32) - taken[:, :DV], -taken[:, DV:]], 1
                    )
                    carried = jnp.concatenate(
                        [grown * both[CHUNK:, :DV], grown * both[CHUNK:, DV:]], 1
                    )
                parts_ref[head, part, :] = (carried + mul(scores, fresh)).astype(BF16)


def columns_of(rows, width, first=0):
    return pl.BlockSpec((rows, width), lambda step: (0, step + first))


def in_vmem(mib):
    return pltpu.CompilerParams(vmem_limit_bytes=mib * 1024 * 1024)


def local_steps(raws, before, taps, beta_logit, decay_logit, gate_raw, norm_gain):
    length = raws[0].shape[0]
    key_heads = raws[0].shape[1] // DK
    value_heads = raws[2].shape[1] // DV
    repeat_by = value_heads // key_heads
    chunks = length // CHUNK
    beta, decay = beta_logit.T, decay_logit.T
    work = CHUNK * length * DV * value_heads
    hbm = pl.BlockSpec(memory_space=pltpu.HBM)

    def split(each):
        heads = each * repeat_by
        held = max(heads, math.gcd(8, value_heads))
        of_heads = lambda *shape: pl.BlockSpec((heads,) + shape, lambda step: (step,) + (0,) * len(shape))
        logits = pl.BlockSpec((held, length), lambda step: (step * heads // held, 0))
        return key_heads // each, each * DK, heads * DV, of_heads, logits

    each = math.gcd(4, key_heads)
    steps, narrow, wide, of_heads, logits = split(each)
    later = length - CHUNK
    solved, moves, later_unit = pl.pallas_call(
        later_kernel,
        grid=(steps,),
        in_specs=[
            columns_of(length, narrow), columns_of(length, wide),
            columns_of(4, narrow), columns_of(4, wide), logits, logits,
        ],
        out_specs=[
            of_heads(later, DV + DK), of_heads(chunks - 1, DK, DV + DK), columns_of(later, narrow),
        ],
        out_shape=[
            jax.ShapeDtypeStruct((value_heads, later, DV + DK), BF16),
            jax.ShapeDtypeStruct((value_heads, chunks - 1, DK, DV + DK), BF16),
            jax.ShapeDtypeStruct((later, key_heads * DK), BF16),
        ],
        scratch_shapes=[
            pltpu.VMEM((each, later + 16, DK), F32),
            pltpu.VMEM((each * repeat_by, later + 16, DV), F32),
        ],
        compiler_params=in_vmem(60),
        cost_estimate=pl.CostEstimate(flops=30 * work, bytes_accessed=0, transcendentals=0),
        name="later",
    )(raws[1], raws[2], taps[1], taps[2], beta, decay)

    narrow, wide = key_heads * DK, value_heads * DV
    whole = lambda shape, *at: pl.BlockSpec(shape, lambda step: at or (0,) * len(shape))
    pairs, first_unit, first_solved, starts = pl.pallas_call(
        states_kernel,
        grid=(1,),
        in_specs=[
            whole((CHUNK, narrow)), whole((CHUNK, wide)),
            whole((3, narrow), 0, repeat_by + 1), whole((3, wide)),
            whole(taps[1].shape), whole(taps[2].shape), whole(beta.shape), whole(decay.shape), hbm,
        ],
        out_specs=[hbm, whole((CHUNK, narrow)), hbm, hbm],
        out_shape=[
            jax.ShapeDtypeStruct((value_heads, DK, DV + DK), BF16),
            jax.ShapeDtypeStruct((CHUNK, narrow), BF16),
            jax.ShapeDtypeStruct((value_heads, CHUNK, DV + DK), BF16),
            jax.ShapeDtypeStruct((chunks - 1, value_heads, DK, DV + DK), BF16),
        ],
        scratch_shapes=[
            pltpu.VMEM((key_heads, 8 + CHUNK, DK), F32),
            pltpu.VMEM((value_heads, 8 + CHUNK, DV), F32),
            pltpu.VMEM(moves.shape, BF16),
            pltpu.VMEM((value_heads, CHUNK, DV + DK), BF16),
            pltpu.VMEM((chunks - 1, value_heads, DK, DV + DK), BF16),
            pltpu.VMEM((value_heads, DK, DV + DK), BF16),
            pltpu.SemaphoreType.DMA,
            pltpu.SemaphoreType.DMA((chunks,)),
            pltpu.SemaphoreType.DMA((value_heads // min(HEADS_AT_ONCE, value_heads),)),
        ],
        compiler_params=in_vmem(54),
        cost_estimate=pl.CostEstimate(flops=20 * work, bytes_accessed=0, transcendentals=0),
        name="states",
    )(raws[1], raws[2], before, before, taps[1], taps[2], beta, decay, moves)
    gain = norm_gain.reshape(1, DV)

    def local():
        steps, narrow, wide, of_heads, logits = split(math.gcd(2, key_heads))
        heads = wide // DV
        return pl.pallas_call(
            local_kernel,
            grid=(steps,),
            in_specs=[
                columns_of(length, narrow), columns_of(3, narrow, repeat_by * steps), columns_of(4, narrow),
                columns_of(CHUNK, narrow), columns_of(later, narrow), logits,
                of_heads(CHUNK, DV + DK), of_heads(later, DV + DK),
                pl.BlockSpec((chunks - 1, heads, DK, DV + DK), lambda step: (0, step, 0, 0)),
                columns_of(length, wide), whole(gain.shape),
            ],
            out_specs=[of_heads(length, DV + DK), columns_of(length, wide)],
            out_shape=[
                jax.ShapeDtypeStruct((value_heads, length, DV + DK), BF16),
                jax.ShapeDtypeStruct(gate_raw.shape, BF16),
            ],
            scratch_shapes=[pltpu.VMEM((narrow // DK, 8 + length, DK), F32)],
            compiler_params=in_vmem(60),
            cost_estimate=pl.CostEstimate(flops=12 * work, bytes_accessed=0, transcendentals=0),
            name="local",
        )(
            raws[0], before, taps[0], first_unit, later_unit, decay,
            first_solved, solved, starts, gate_raw, gain,
        )

    return pairs, local


def prefix_kernel(pairs_ref, prefix_ref, total_ref):
    count, heads = pairs_ref.shape[:2]
    running = [None] * heads
    for hop in range(count):
        for head in range(heads):
            now = pairs_ref[hop, head]
            if hop == 0:
                rows = lax.broadcasted_iota(jnp.int32, (DK, DV + DK), 0)
                cols = lax.broadcasted_iota(jnp.int32, (DK, DV + DK), 1)
                prefix_ref[hop, head] = jnp.where(cols == rows + DV, 1.0, 0.0).astype(BF16)
                running[head] = now.astype(F32)
            else:
                before = running[head].astype(BF16)
                prefix_ref[hop, head] = before
                own = jnp.concatenate([now[:, :DV].astype(F32), jnp.zeros((DK, DK), F32)], 1)
                running[head] = own + mul(now[:, DV:], before)
    for head in range(heads):
        total_ref[head] = running[head][:, : total_ref.shape[2]].astype(BF16)


def apply_kernel(prefix_ref, start_ref, starts_ref):
    count, heads = prefix_ref.shape[:2]
    for hop in range(count):
        for head in range(heads):
            starts_ref[hop, head] = (
                prefix_ref[hop, head, :, :DV].astype(F32)
                + mul(prefix_ref[hop, head, :, DV:], start_ref[head])
            ).astype(BF16)


def shifted(value, axis, by):
    count = lax.axis_size(axis)
    return lax.ppermute(value, axis, [(i, i + by) for i in range(count - by)])


def group_start(total, axis, group):
    groups = lax.axis_size(axis) // group
    running = shifted(total, axis, group)
    by = 1
    while by < groups - 1:
        earlier = shifted(running, axis, by * group)
        product = jnp.einsum("bkl,blv->bkv", running[..., DV:], earlier, preferred_element_type=F32)
        own = jnp.pad(running[..., :DV], ((0, 0), (0, 0), (0, DK)))
        running = (product + own.astype(F32)).astype(BF16)
        by *= 2
    return running[..., :DV]


def starts_of(pairs, axis, beside):
    size = lax.axis_size(axis)
    heads = pairs.shape[0]
    group = math.gcd(math.gcd(size, heads), GROUP)
    groups = [[g * group + i for i in range(group)] for g in range(size // group)]
    each = heads // group
    wide = DV if size // group == 2 else DV + DK
    by_head = lax.all_to_all(pairs, axis, 0, 0, axis_index_groups=groups, tiled=True)
    by_head, done = lax.optimization_barrier((by_head, beside()))
    prefix, total = pl.pallas_call(
        prefix_kernel,
        out_shape=[
            jax.ShapeDtypeStruct((group, each, DK, DV + DK), BF16),
            jax.ShapeDtypeStruct((each, DK, wide), BF16),
        ],
        compiler_params=in_vmem(16),
        name="prefix",
    )(by_head.reshape(group, each, DK, DV + DK))
    starts = pl.pallas_call(
        apply_kernel,
        out_shape=jax.ShapeDtypeStruct((group, each, DK, DV), BF16),
        compiler_params=in_vmem(16),
        name="apply",
    )(prefix, group_start(total, axis, group))
    starts = lax.all_to_all(
        starts.reshape(heads, DK, DV), axis, 0, 0, axis_index_groups=groups, tiled=True
    )
    return starts, done


def project_kernel(
    place_ref, starts_ref, gated_ref, parts_hbm, weight_hbm, away_ref, own_ref,
    parts_ref, weight_ref, total, parts_sem, weight_sem,
):
    heads, length = parts_ref.shape[:2]
    width = weight_ref.shape[1]
    each = min(HEADS_AT_ONCE, heads)
    block = min(512, width)
    groups = heads // each

    def parts(g):
        here = pl.ds(g * each, each)
        return pltpu.make_async_copy(parts_hbm.at[here], parts_ref.at[here], parts_sem.at[g])

    def weights(g):
        rows = pl.ds(g * each * DV, each * DV)
        return pltpu.make_async_copy(weight_hbm.at[rows], weight_ref.at[rows], weight_sem.at[g])

    def normed_group(g):
        normed = []
        for head in range(g * each, (g + 1) * each):
            core = parts_ref[head, :, :DV].astype(F32) + mul(
                parts_ref[head, :, DV:], starts_ref[head]
            )
            scale = lax.rsqrt(row_sums(core * core, 1.0 / DV) + EPSILON)
            normed.append((core * scale * gated_ref[:, head_of(head)].astype(F32)).astype(BF16))
        return jnp.concatenate(normed, 1)

    parts(0).start()
    weights(0).start()
    parts(0).wait()
    if groups > 1:
        parts(1).start()
        weights(1).start()
    following = normed_group(0)
    for g in range(groups):
        weights(g).wait()
        if g + 2 < groups:
            weights(g + 2).start()
        if g + 1 < groups:
            parts(g + 1).wait()
        if g + 2 < groups:
            parts(g + 2).start()
        normed = following
        if g + 1 < groups:
            following = normed_group(g + 1)
        for at in range(0, width, block):
            added = jnp.dot(
                normed, weight_ref[g * each * DV : (g + 1) * each * DV, at : at + block],
                preferred_element_type=F32,
            )
            if g > 0:
                added = added + total[:, at : at + block]
            if g < groups - 1:
                total[:, at : at + block] = added
            elif own_ref is None:
                away_ref[:, at : at + block] = added.astype(BF16)
            else:
                first = place_ref[0] == 0
                low, high = added[: length // 2], added[length // 2 :]
                own_ref[:, at : at + block] = jnp.where(first, low, high).astype(BF16)
                away_ref[:, at : at + block] = jnp.where(first, high, low).astype(BF16)


def whole_kernel(place_ref, starts_ref, gated_ref, parts_hbm, weight_hbm, out_ref, *scratch):
    project_kernel(place_ref, starts_ref, gated_ref, parts_hbm, weight_hbm, out_ref, None, *scratch)


def projected(parts, starts, gated, out_weight, axis):
    heads, length = parts.shape[:2]
    width = out_weight.shape[1]
    halves = lax.axis_size(axis) == 2
    vmem = pl.BlockSpec(memory_space=pltpu.VMEM)
    hbm = pl.BlockSpec(memory_space=pltpu.HBM)
    groups = heads // min(HEADS_AT_ONCE, heads)
    here = lax.axis_index(axis).astype(jnp.int32).reshape(1)
    out = jax.ShapeDtypeStruct((length // 2 if halves else length, width), BF16)
    partial = pl.pallas_call(
        project_kernel if halves else whole_kernel,
        in_specs=[pl.BlockSpec(memory_space=pltpu.SMEM), vmem, vmem, hbm, hbm],
        out_specs=[vmem, vmem] if halves else vmem,
        out_shape=[out, out] if halves else out,
        scratch_shapes=[
            pltpu.VMEM(parts.shape, BF16),
            pltpu.VMEM(out_weight.shape, BF16),
            pltpu.VMEM((length, width), F32),
            pltpu.SemaphoreType.DMA((groups,)),
            pltpu.SemaphoreType.DMA((groups,)),
        ],
        compiler_params=in_vmem(50),
        name="project",
    )(here, starts, gated, parts, out_weight)
    if not halves:
        return lax.psum_scatter(partial, axis, scatter_dimension=0, tiled=True)
    away, own = partial
    other = lax.ppermute(away, axis, [(0, 1), (1, 0)])
    return (own.astype(F32) + other.astype(F32)).astype(BF16)


def tails_kernel(value_hbm, query_hbm, key_hbm, out_ref, value_ref, query_ref, key_ref, sem):
    pairs = ((value_hbm, value_ref), (query_hbm, query_ref), (key_hbm, key_ref))
    copies = [
        pltpu.make_async_copy(source.at[pl.ds(source.shape[0] - 16, 16)], held, sem.at[i])
        for i, (source, held) in enumerate(pairs)
    ]
    for copy in copies:
        copy.start()
    at = 0
    for copy, (_, held) in zip(copies, pairs):
        copy.wait()
        width = held.shape[1]
        out_ref[:, at : at + width] = held[...].astype(F32)[13:16].astype(BF16)
        at += width


def tails(raws):
    order = (raws[2], raws[0], raws[1])
    width = sum(raw.shape[1] for raw in order)
    return pl.pallas_call(
        tails_kernel,
        in_specs=[pl.BlockSpec(memory_space=pltpu.HBM)] * 3,
        out_shape=jax.ShapeDtypeStruct((3, width), BF16),
        scratch_shapes=[pltpu.VMEM((16, raw.shape[1]), BF16) for raw in order]
        + [pltpu.SemaphoreType.DMA((3,))],
        compiler_params=in_vmem(60),
        name="tails",
    )(*order)


def shards(
    query_raw, key_raw, value_raw, gate_raw, query_taps, key_taps, value_taps,
    beta_logit, decay_logit, norm_gain, out_weight,
):
    raws = (query_raw, key_raw, value_raw)
    before = shifted(tails(raws), "seq", 1)
    pairs, local = local_steps(
        raws, before, (query_taps, key_taps, value_taps), beta_logit, decay_logit, gate_raw, norm_gain
    )
    starts, (parts, gated) = starts_of(pairs, "seq", local)
    return projected(parts, starts, gated, out_weight, "head")


def solution(mesh):
    placed = (
        P("seq", "head"), P("seq", "head"), P("seq", "head"), P("seq", "head"),
        P(None, "head"), P(None, "head"), P(None, "head"),
        P("seq", "head"), P("seq", "head"), P(), P("head", None),
    )
    return jax.shard_map(
        shards, mesh=mesh, in_specs=placed, out_specs=P(("seq", "head"), None), check_vma=False
    )
```

```python
import functools
import math

import jax
import jax.numpy as jnp
from jax import lax
from jax.experimental import pallas as pl
from jax.experimental.pallas import tpu as pltpu
from jax.sharding import PartitionSpec as P

DK = 128
DV = 128
CHUNK = 128
TINY = 8
SMALL = 32
GROUP = 8
HEADS_AT_ONCE = 4
EPSILON = 1e-06
F32 = jnp.float32
BF16 = jnp.bfloat16


def mul(left, right):
    return jnp.dot(left.astype(BF16), right.astype(BF16), preferred_element_type=F32)


def sigmoid(x):
    return 0.5 + 0.5 * jnp.tanh(0.5 * x)


def conv_silu(padded, first, rows, taps_ref, head):
    taps = taps_ref[:, head_of(head)]
    summed = taps[0:1] * padded[head, first : first + rows, :]
    for offset in range(1, 4):
        summed = summed + taps[offset : offset + 1] * padded[head, first + offset : first + offset + rows, :]
    return summed * sigmoid(summed)


def widen(padded, first, rows, raw):
    for head in range(padded.shape[0]):
        padded[head, first : first + rows, :] = raw[:, head_of(head)].astype(F32)


def row_sums(values):
    return mul(values, jnp.ones((CHUNK, CHUNK), BF16))


def unit_rows(key):
    return key * lax.rsqrt(row_sums(key * key) + EPSILON)


def softplus(x):
    return jnp.maximum(x, 0.0) + jnp.log(1.0 + jnp.exp(-jnp.abs(x)))


def part_of(chunk):
    return slice(chunk * CHUNK, (chunk + 1) * CHUNK)


def head_of(head):
    return slice(head * DK, (head + 1) * DK)


def chunk_rows(ref, heads, chunks):
    held = ref.shape[0]
    first = (pl.program_id(0) * heads) % held
    rows = ref[:heads, :]
    for at in range(heads, held, heads):
        rows = jnp.where(first == at, ref[at : at + heads, :], rows)
    return jnp.concatenate([rows[:, part_of(c)] for c in chunks], 0)


def square_iotas(rows=CHUNK):
    return (
        lax.broadcasted_iota(jnp.int32, (rows, CHUNK), 0),
        lax.broadcasted_iota(jnp.int32, (rows, CHUNK), 1),
    )


def log_fades(logit):
    rows, cols = square_iotas()
    return jnp.dot(
        -softplus(logit), (rows <= cols).astype(F32), precision=lax.Precision.HIGHEST, preferred_element_type=F32
    )


def as_columns(blocks):
    rows = sum(block.shape[0] for block in blocks)
    return jnp.concatenate(list(blocks) + [jnp.zeros((CHUNK - rows, CHUNK), F32)], 0).T


def tiny_inverses(lower):
    lanes = lax.broadcasted_iota(jnp.int32, (TINY, CHUNK), 1)
    rows = lax.broadcasted_iota(jnp.int32, (TINY, CHUNK), 0)
    blocks = []
    for low in lower:
        block = low[:TINY]
        for at in range(1, CHUNK // TINY):
            block = jnp.where(lanes // TINY == at, low[at * TINY : (at + 1) * TINY], block)
        blocks.append(block)
    stacked = jnp.concatenate(blocks, 0)
    all_lanes = lax.broadcasted_iota(jnp.int32, stacked.shape, 1)
    factors = [
        jnp.take_along_axis(
            stacked, all_lanes // TINY * TINY + c, axis=1, mode="promise_in_bounds"
        )
        for c in range(TINY - 1)
    ]
    inverses = []
    for p in range(len(lower)):
        inverse = jnp.where(lanes % TINY == rows, 1.0, 0.0)
        for c in range(TINY - 1):
            inverse = inverse - factors[c][p * TINY : (p + 1) * TINY] * inverse[c : c + 1]
        inverses.append(inverse)
    return inverses


def solved_packs(fade, beta_logit, keys, key_cols, value_work, value_of):
    count = len(keys)
    stages = 6
    done = [0, 0]

    def between():
        done[1] += 1
        while done[0] < len(value_work) and done[0] * stages < len(value_work) * done[1]:
            value_work[done[0]]()
            done[0] += 1

    rows, cols = square_iotas()
    strict = rows > cols
    differ = rows ^ cols
    columns = as_columns((fade - softplus(-beta_logit),))
    beta = sigmoid(beta_logit)
    beta_grown = beta * jnp.exp(fade)
    inner = {}
    for key, turned in zip(keys, key_cols):
        if id(key) not in inner:
            inner[id(key)] = mul(key, turned)
    lower = []
    for p in range(count):
        gap = columns[:, p : p + 1] - fade[p : p + 1, :]
        lower.append(jnp.exp(jnp.where(strict, gap, -1e30)) * inner[id(keys[p])])

    small_rows, small_cols = square_iotas(SMALL)
    small_differ = small_rows ^ (small_cols % SMALL)
    place = small_cols // SMALL
    blocks = jnp.where(rows // SMALL == cols // SMALL, 1.0, 0.0)
    blocks16 = blocks.astype(BF16)

    def spread(small):
        return jnp.concatenate([small] * (CHUNK // SMALL), 0) * (blocks16 if small.dtype == BF16 else blocks)

    small = []
    for low in lower:
        held = low[:SMALL]
        for at in range(1, CHUNK // SMALL):
            held = jnp.where(place == at, low[at * SMALL : (at + 1) * SMALL], held)
        small.append(held)
    tiny_inverse = tiny_inverses(lower)
    held = (small_cols % SMALL) // TINY == small_rows // TINY
    inverse = [
        jnp.where(held, jnp.concatenate([one] * (SMALL // TINY), 0), 0.0) for one in tiny_inverse
    ]
    size = TINY
    while size < CHUNK:
        last = size == SMALL
        if last:
            band = (differ >= size) & (differ < 4 * size)
            inside = [jnp.where(band, low, 0.0).astype(BF16) for low in lower]
            inverse16 = [spread(one.astype(BF16)) for one in inverse]
            inverse = [spread(one) for one in inverse]
            wide16 = inverse16
        else:
            band = (small_differ >= size) & (small_differ < 4 * size)
            inside = [spread(jnp.where(band, one, 0.0).astype(BF16)) for one in small]
            inverse16 = [one.astype(BF16) for one in inverse]
            wide16 = [spread(one) for one in inverse16]
        between()
        step = [mul(inverse16[p], inside[p]).astype(BF16) for p in range(count)]
        between()
        both = [
            mul(step[p], jnp.concatenate([step[p] if last else spread(step[p]), wide16[p]], 1))
            for p in range(count)
        ]
        between()
        inverse = [inverse[p] - both[p][:, CHUNK:] for p in range(count)]
        partial = [inverse[p].astype(BF16) for p in range(count)]
        inverse = [
            inverse[p] + mul(both[p][:, :CHUNK], partial[p] if last else spread(partial[p]))
            for p in range(count)
        ]
        size *= 4

    return [
        jnp.concatenate(
            [
                mul(inverse[p] * beta[p : p + 1, :], value_of(p)),
                mul(inverse[p] * beta_grown[p : p + 1, :], keys[p]),
            ],
            1,
        )
        for p in range(count)
    ]


def later_kernel(
    key_ref, value_ref, key_taps, value_taps, beta_ref, decay_ref,
    solved_ref, moves_ref, key_padded, value_padded,
):
    length, width = key_ref.shape
    chunks = range(1, length // CHUNK)
    key_heads = width // DK
    heads = value_ref.shape[1] // DV
    repeat_by = heads // key_heads
    packs = [(chunk, head) for chunk in chunks for head in range(heads)]
    skip = CHUNK - 16
    count = length - CHUNK
    widen(key_padded, 0, count + 16, key_ref[skip:, :])
    widen(value_padded, 0, count + 16, value_ref[skip:, :])
    key, turned = {}, {}
    for j in range(key_heads):
        unit = unit_rows(conv_silu(key_padded, 13, count, key_taps, j))
        for head in range(j * repeat_by, (j + 1) * repeat_by):
            solved_ref[head, :, DV + DK :] = unit.astype(BF16)
        for chunk in chunks:
            key[chunk, j] = unit[part_of(chunk - 1)]
            turned[chunk, j] = key[chunk, j].T
    value = {}

    def make_value(head):
        value[head] = conv_silu(value_padded, 13, count, value_taps, head)

    def value_of(pack):
        chunk, head = packs[pack]
        return value[head][part_of(chunk - 1)]

    fade = log_fades(chunk_rows(decay_ref, heads, chunks))
    solved = solved_packs(
        fade,
        chunk_rows(beta_ref, heads, chunks),
        [key[chunk, head // repeat_by] for chunk, head in packs],
        [turned[chunk, head // repeat_by] for chunk, head in packs],
        [functools.partial(make_value, head) for head in range(heads)],
        value_of,
    )
    tail = jnp.exp(fade[:, CHUNK - 1 : CHUNK] - fade)
    for pack, (chunk, head) in enumerate(packs):
        one = solved[pack].astype(BF16)
        solved_ref[head, part_of(chunk - 1), : DV + DK] = one
        moves_ref[head, chunk - 1] = mul(
            turned[chunk, head // repeat_by] * tail[pack : pack + 1, :], one
        ).astype(BF16)


def states_kernel(
    key_ref, value_ref, key_before, value_before, key_taps, value_taps, beta_ref, decay_ref, moves_hbm,
    pairs_hbm, solved_hbm, starts_hbm,
    key_padded, value_padded, moves_ref, solved_ref, starts_ref, pairs_ref, in_sem, out_sem, pairs_sem,
):
    heads, length = decay_ref.shape
    chunks = length // CHUNK
    key_heads = key_ref.shape[1] // DK
    repeat_by = heads // key_heads
    incoming = pltpu.make_async_copy(moves_hbm, moves_ref, in_sem)
    incoming.start()

    widen(key_padded, 5, 3, key_before[...])
    widen(key_padded, 8, CHUNK, key_ref[...])
    widen(value_padded, 5, 3, value_before[...])
    widen(value_padded, 8, CHUNK, value_ref[...])
    key, turned = [], []
    for j in range(key_heads):
        key.append(unit_rows(conv_silu(key_padded, 5, CHUNK, key_taps, j)))
        for head in range(j * repeat_by, (j + 1) * repeat_by):
            solved_ref[head, :, DV + DK :] = key[j].astype(BF16)
        turned.append(key[j].T)
    fade = log_fades(chunk_rows(decay_ref, heads, range(chunks)))
    value = {}

    def make_value(head):
        value[head] = conv_silu(value_padded, 5, CHUNK, value_taps, head)

    solved = solved_packs(
        fade[:heads],
        beta_ref[:, :CHUNK],
        [key[head // repeat_by] for head in range(heads)],
        [turned[head // repeat_by] for head in range(heads)],
        [functools.partial(make_value, head) for head in range(heads)],
        lambda head: value[head],
    )
    last = jnp.exp(fade[:, CHUNK - 1 : CHUNK])
    tail = jnp.exp(fade[:, CHUNK - 1 : CHUNK] - fade)
    rows, cols = square_iotas()
    identity = jnp.where(rows == cols, 1.0, 0.0)

    state = []
    for head in range(heads):
        one = solved[head].astype(BF16)
        solved_ref[head, :, : DV + DK] = one
        moved = mul(turned[head // repeat_by] * tail[head : head + 1, :], one)
        state.append(
            jnp.concatenate([moved[:, :DV], last[head : head + 1, :] * identity - moved[:, DV:]], 1)
        )
    each = min(HEADS_AT_ONCE, heads)
    outgoing = [pltpu.make_async_copy(solved_ref, solved_hbm, out_sem.at[0])]
    outgoing[0].start()
    incoming.wait()
    for chunk in range(1, chunks):
        for head in range(heads):
            pack = chunk * heads + head
            start = state[head].astype(BF16)
            starts_ref[chunk - 1, head] = start
            moves = moves_ref[head, chunk - 1]
            moved = last[pack : pack + 1, :] * state[head] - mul(moves[:, DV:], start)
            state[head] = jnp.concatenate([moved[:, :DV] + moves[:, :DV].astype(F32), moved[:, DV:]], 1)
            if chunk == chunks - 1:
                pairs_ref[head] = state[head].astype(BF16)
                if (head + 1) % each == 0:
                    done = pl.ds(head + 1 - each, each)
                    outgoing.append(
                        pltpu.make_async_copy(
                            pairs_ref.at[done], pairs_hbm.at[done], pairs_sem.at[head // each]
                        )
                    )
                    outgoing[-1].start()
        outgoing.append(
            pltpu.make_async_copy(
                starts_ref.at[chunk - 1], starts_hbm.at[chunk - 1], out_sem.at[chunk]
            )
        )
        outgoing[-1].start()
    for copy in outgoing:
        copy.wait()


def local_kernel(
    query_ref, query_before, query_taps, decay_ref,
    first_solved, later_solved, starts_ref, gate_ref, gain_ref,
    parts_ref, gated_ref, padded,
):
    length, width = query_ref.shape
    chunks = length // CHUNK
    key_heads = width // DK
    heads = first_solved.shape[0]
    repeat_by = heads // key_heads

    rows, cols = square_iotas()
    within = rows >= cols
    fade = log_fades(chunk_rows(decay_ref, heads, range(chunks)))
    columns = as_columns((fade,))
    widen(padded, 5, 3, query_before[...])
    widen(padded, 8, length, query_ref[...])
    query = [conv_silu(padded, 5, length, query_taps, j).astype(BF16) for j in range(key_heads)]
    for head in range(heads):
        gate = gate_ref[:, head_of(head)].astype(F32)
        gated_ref[:, head_of(head)] = (gate * sigmoid(gate) * gain_ref[...]).astype(BF16)
    for chunk in range(chunks):
        part = part_of(chunk)
        for j in range(key_heads):
            own = query[j][part]
            if chunk == 0:
                unit = first_solved[j * repeat_by, :, DV + DK :]
            else:
                unit = later_solved[j * repeat_by, part_of(chunk - 1), DV + DK :]
            inner = lax.dot_general(
                own, unit, (((1,), (1,)), ((), ())), preferred_element_type=F32
            )
            for head in range(j * repeat_by, (j + 1) * repeat_by):
                pack = chunk * heads + head
                column = jnp.broadcast_to(columns[:, pack : pack + 1], (CHUNK, CHUNK))
                scores = inner * jnp.exp(jnp.where(within, column - fade[pack : pack + 1, :], -1e30))
                grown = jnp.exp(column)
                if chunk == 0:
                    updates, wide = first_solved[head, :, :DV], first_solved[head, :, DV : DV + DK]
                    fresh = jnp.concatenate([updates, -wide], 1)
                    carried = jnp.concatenate(
                        [jnp.zeros((CHUNK, DV), F32), grown * own.astype(F32)], 1
                    )
                else:
                    solved = later_solved[head, part_of(chunk - 1), : DV + DK]
                    both = mul(jnp.concatenate([solved[:, DV:], own], 0), starts_ref[chunk - 1, head])
                    taken = both[:CHUNK]
                    fresh = jnp.concatenate(
                        [solved[:, :DV].astype(F32) - taken[:, :DV], -taken[:, DV:]], 1
                    )
                    carried = jnp.concatenate(
                        [grown * both[CHUNK:, :DV], grown * both[CHUNK:, DV:]], 1
                    )
                parts_ref[head, part, :] = (carried + mul(scores, fresh)).astype(BF16)


def columns_of(rows, width, first=0):
    return pl.BlockSpec((rows, width), lambda step: (0, step + first))


def in_vmem(mib):
    return pltpu.CompilerParams(vmem_limit_bytes=mib * 1024 * 1024)


def local_steps(raws, before, taps, beta_logit, decay_logit, gate_raw, norm_gain):
    length = raws[0].shape[0]
    key_heads = raws[0].shape[1] // DK
    value_heads = raws[2].shape[1] // DV
    repeat_by = value_heads // key_heads
    chunks = length // CHUNK
    beta, decay = beta_logit.T, decay_logit.T
    work = CHUNK * length * DV * value_heads
    hbm = pl.BlockSpec(memory_space=pltpu.HBM)

    def split(each):
        heads = each * repeat_by
        held = max(heads, math.gcd(8, value_heads))
        of_heads = lambda *shape: pl.BlockSpec((heads,) + shape, lambda step: (step,) + (0,) * len(shape))
        logits = pl.BlockSpec((held, length), lambda step: (step * heads // held, 0))
        return key_heads // each, each * DK, heads * DV, of_heads, logits

    each = math.gcd(4, key_heads)
    steps, narrow, wide, of_heads, logits = split(each)
    later = length - CHUNK
    solved, moves = pl.pallas_call(
        later_kernel,
        grid=(steps,),
        in_specs=[
            columns_of(length, narrow), columns_of(length, wide),
            columns_of(4, narrow), columns_of(4, wide), logits, logits,
        ],
        out_specs=[
            of_heads(later, DV + 2 * DK), of_heads(chunks - 1, DK, DV + DK),
        ],
        out_shape=[
            jax.ShapeDtypeStruct((value_heads, later, DV + 2 * DK), BF16),
            jax.ShapeDtypeStruct((value_heads, chunks - 1, DK, DV + DK), BF16),
        ],
        scratch_shapes=[
            pltpu.VMEM((each, later + 16, DK), F32),
            pltpu.VMEM((each * repeat_by, later + 16, DV), F32),
        ],
        compiler_params=in_vmem(50),
        cost_estimate=pl.CostEstimate(flops=30 * work, bytes_accessed=0, transcendentals=0),
        name="later",
    )(raws[1], raws[2], taps[1], taps[2], beta, decay)

    narrow, wide = key_heads * DK, value_heads * DV
    whole = lambda shape, *at: pl.BlockSpec(shape, lambda step: at or (0,) * len(shape))
    pairs, first_solved, starts = pl.pallas_call(
        states_kernel,
        grid=(1,),
        in_specs=[
            whole((CHUNK, narrow)), whole((CHUNK, wide)),
            whole((3, narrow), 0, repeat_by + 1), whole((3, wide)),
            whole(taps[1].shape), whole(taps[2].shape), whole(beta.shape), whole(decay.shape), hbm,
        ],
        out_specs=[hbm, hbm, hbm],
        out_shape=[
            jax.ShapeDtypeStruct((value_heads, DK, DV + DK), BF16),
            jax.ShapeDtypeStruct((value_heads, CHUNK, DV + 2 * DK), BF16),
            jax.ShapeDtypeStruct((chunks - 1, value_heads, DK, DV + DK), BF16),
        ],
        scratch_shapes=[
            pltpu.VMEM((key_heads, 8 + CHUNK, DK), F32),
            pltpu.VMEM((value_heads, 8 + CHUNK, DV), F32),
            pltpu.VMEM(moves.shape, BF16),
            pltpu.VMEM((value_heads, CHUNK, DV + 2 * DK), BF16),
            pltpu.VMEM((chunks - 1, value_heads, DK, DV + DK), BF16),
            pltpu.VMEM((value_heads, DK, DV + DK), BF16),
            pltpu.SemaphoreType.DMA,
            pltpu.SemaphoreType.DMA((chunks,)),
            pltpu.SemaphoreType.DMA((value_heads // min(HEADS_AT_ONCE, value_heads),)),
        ],
        compiler_params=in_vmem(52),
        cost_estimate=pl.CostEstimate(flops=20 * work, bytes_accessed=0, transcendentals=0),
        name="states",
    )(raws[1], raws[2], before, before, taps[1], taps[2], beta, decay, moves)
    gain = norm_gain.reshape(1, DV)

    def local():
        steps, narrow, wide, of_heads, logits = split(math.gcd(2, key_heads))
        heads = wide // DV
        return pl.pallas_call(
            local_kernel,
            grid=(steps,),
            in_specs=[
                columns_of(length, narrow), columns_of(3, narrow, repeat_by * steps), columns_of(4, narrow),
                logits, of_heads(CHUNK, DV + 2 * DK), of_heads(later, DV + 2 * DK),
                pl.BlockSpec((chunks - 1, heads, DK, DV + DK), lambda step: (0, step, 0, 0)),
                columns_of(length, wide), whole(gain.shape),
            ],
            out_specs=[of_heads(length, DV + DK), columns_of(length, wide)],
            out_shape=[
                jax.ShapeDtypeStruct((value_heads, length, DV + DK), BF16),
                jax.ShapeDtypeStruct(gate_raw.shape, BF16),
            ],
            scratch_shapes=[pltpu.VMEM((narrow // DK, 8 + length, DK), F32)],
            compiler_params=in_vmem(60),
            cost_estimate=pl.CostEstimate(flops=12 * work, bytes_accessed=0, transcendentals=0),
            name="local",
        )(
            raws[0], before, taps[0], decay, first_solved, solved, starts, gate_raw, gain,
        )

    return pairs, local


def prefix_kernel(pairs_ref, prefix_ref, total_ref):
    count, heads = pairs_ref.shape[:2]
    running = [None] * heads
    for hop in range(count):
        for head in range(heads):
            now = pairs_ref[hop, head]
            if hop == 0:
                rows = lax.broadcasted_iota(jnp.int32, (DK, DV + DK), 0)
                cols = lax.broadcasted_iota(jnp.int32, (DK, DV + DK), 1)
                prefix_ref[hop, head] = jnp.where(cols == rows + DV, 1.0, 0.0).astype(BF16)
                running[head] = now.astype(F32)
            else:
                before = running[head].astype(BF16)
                prefix_ref[hop, head] = before
                own = jnp.concatenate([now[:, :DV].astype(F32), jnp.zeros((DK, DK), F32)], 1)
                running[head] = own + mul(now[:, DV:], before)
    for head in range(heads):
        total_ref[head] = running[head][:, : total_ref.shape[2]].astype(BF16)


def apply_kernel(prefix_ref, start_ref, starts_ref):
    count, heads = prefix_ref.shape[:2]
    for hop in range(count):
        for head in range(heads):
            starts_ref[hop, head] = (
                prefix_ref[hop, head, :, :DV].astype(F32)
                + mul(prefix_ref[hop, head, :, DV:], start_ref[head])
            ).astype(BF16)


def shifted(value, axis, by):
    count = lax.axis_size(axis)
    return lax.ppermute(value, axis, [(i, i + by) for i in range(count - by)])


def group_start(total, axis, group):
    groups = lax.axis_size(axis) // group
    running = shifted(total, axis, group)
    by = 1
    while by < groups - 1:
        earlier = shifted(running, axis, by * group)
        product = jnp.einsum("bkl,blv->bkv", running[..., DV:], earlier, preferred_element_type=F32)
        own = jnp.pad(running[..., :DV], ((0, 0), (0, 0), (0, DK)))
        running = (product + own.astype(F32)).astype(BF16)
        by *= 2
    return running[..., :DV]


def starts_of(pairs, axis, beside):
    size = lax.axis_size(axis)
    heads = pairs.shape[0]
    group = math.gcd(math.gcd(size, heads), GROUP)
    groups = [[g * group + i for i in range(group)] for g in range(size // group)]
    each = heads // group
    wide = DV if size // group == 2 else DV + DK
    by_head = lax.all_to_all(pairs, axis, 0, 0, axis_index_groups=groups, tiled=True)
    by_head, done = lax.optimization_barrier((by_head, beside()))
    prefix, total = pl.pallas_call(
        prefix_kernel,
        out_shape=[
            jax.ShapeDtypeStruct((group, each, DK, DV + DK), BF16),
            jax.ShapeDtypeStruct((each, DK, wide), BF16),
        ],
        compiler_params=in_vmem(16),
        name="prefix",
    )(by_head.reshape(group, each, DK, DV + DK))
    starts = pl.pallas_call(
        apply_kernel,
        out_shape=jax.ShapeDtypeStruct((group, each, DK, DV), BF16),
        compiler_params=in_vmem(16),
        name="apply",
    )(prefix, group_start(total, axis, group))
    starts = lax.all_to_all(
        starts.reshape(heads, DK, DV), axis, 0, 0, axis_index_groups=groups, tiled=True
    )
    return starts, done


def project_kernel(
    place_ref, starts_ref, gated_ref, parts_hbm, weight_hbm, away_ref, own_ref,
    parts_ref, weight_ref, total, parts_sem, weight_sem,
):
    heads, length = parts_ref.shape[:2]
    width = weight_ref.shape[1]
    each = min(HEADS_AT_ONCE, heads)
    block = min(512, width)
    groups = heads // each

    def parts(g):
        here = pl.ds(g * each, each)
        return pltpu.make_async_copy(parts_hbm.at[here], parts_ref.at[here], parts_sem.at[g])

    def weights(g):
        rows = pl.ds(g * each * DV, each * DV)
        return pltpu.make_async_copy(weight_hbm.at[rows], weight_ref.at[rows], weight_sem.at[g])

    def normed_group(g):
        normed = []
        for head in range(g * each, (g + 1) * each):
            core = parts_ref[head, :, :DV].astype(F32) + mul(
                parts_ref[head, :, DV:], starts_ref[head]
            )
            scale = lax.rsqrt(jnp.mean(core * core, -1, keepdims=True) + EPSILON)
            normed.append((core * scale * gated_ref[:, head_of(head)].astype(F32)).astype(BF16))
        return jnp.concatenate(normed, 1)

    parts(0).start()
    weights(0).start()
    parts(0).wait()
    if groups > 1:
        parts(1).start()
        weights(1).start()
    following = normed_group(0)
    for g in range(groups):
        weights(g).wait()
        if g + 2 < groups:
            weights(g + 2).start()
        if g + 1 < groups:
            parts(g + 1).wait()
        if g + 2 < groups:
            parts(g + 2).start()
        normed = following
        if g + 1 < groups:
            following = normed_group(g + 1)
        for at in range(0, width, block):
            added = jnp.dot(
                normed, weight_ref[g * each * DV : (g + 1) * each * DV, at : at + block],
                preferred_element_type=F32,
            )
            if g > 0:
                added = added + total[:, at : at + block]
            if g < groups - 1:
                total[:, at : at + block] = added
            elif own_ref is None:
                away_ref[:, at : at + block] = added.astype(BF16)
            else:
                first = place_ref[0] == 0
                low, high = added[: length // 2], added[length // 2 :]
                own_ref[:, at : at + block] = jnp.where(first, low, high).astype(BF16)
                away_ref[:, at : at + block] = jnp.where(first, high, low).astype(BF16)


def whole_kernel(place_ref, starts_ref, gated_ref, parts_hbm, weight_hbm, out_ref, *scratch):
    project_kernel(place_ref, starts_ref, gated_ref, parts_hbm, weight_hbm, out_ref, None, *scratch)


def projected(parts, starts, gated, out_weight, axis):
    heads, length = parts.shape[:2]
    width = out_weight.shape[1]
    halves = lax.axis_size(axis) == 2
    vmem = pl.BlockSpec(memory_space=pltpu.VMEM)
    hbm = pl.BlockSpec(memory_space=pltpu.HBM)
    groups = heads // min(HEADS_AT_ONCE, heads)
    here = lax.axis_index(axis).astype(jnp.int32).reshape(1)
    out = jax.ShapeDtypeStruct((length // 2 if halves else length, width), BF16)
    partial = pl.pallas_call(
        project_kernel if halves else whole_kernel,
        in_specs=[pl.BlockSpec(memory_space=pltpu.SMEM), vmem, vmem, hbm, hbm],
        out_specs=[vmem, vmem] if halves else vmem,
        out_shape=[out, out] if halves else out,
        scratch_shapes=[
            pltpu.VMEM(parts.shape, BF16),
            pltpu.VMEM(out_weight.shape, BF16),
            pltpu.VMEM((length, width), F32),
            pltpu.SemaphoreType.DMA((groups,)),
            pltpu.SemaphoreType.DMA((groups,)),
        ],
        compiler_params=in_vmem(50),
        name="project",
    )(here, starts, gated, parts, out_weight)
    if not halves:
        return lax.psum_scatter(partial, axis, scatter_dimension=0, tiled=True)
    away, own = partial
    other = lax.ppermute(away, axis, [(0, 1), (1, 0)])
    return (own.astype(F32) + other.astype(F32)).astype(BF16)


def tails_kernel(value_hbm, query_hbm, key_hbm, out_ref, value_ref, query_ref, key_ref, sem):
    pairs = ((value_hbm, value_ref), (query_hbm, query_ref), (key_hbm, key_ref))
    copies = [
        pltpu.make_async_copy(source.at[pl.ds(source.shape[0] - 16, 16)], held, sem.at[i])
        for i, (source, held) in enumerate(pairs)
    ]
    for copy in copies:
        copy.start()
    at = 0
    for copy, (_, held) in zip(copies, pairs):
        copy.wait()
        width = held.shape[1]
        out_ref[:, at : at + width] = held[...].astype(F32)[13:16].astype(BF16)
        at += width


def tails(raws):
    order = (raws[2], raws[0], raws[1])
    width = sum(raw.shape[1] for raw in order)
    return pl.pallas_call(
        tails_kernel,
        in_specs=[pl.BlockSpec(memory_space=pltpu.HBM)] * 3,
        out_shape=jax.ShapeDtypeStruct((3, width), BF16),
        scratch_shapes=[pltpu.VMEM((16, raw.shape[1]), BF16) for raw in order]
        + [pltpu.SemaphoreType.DMA((3,))],
        compiler_params=in_vmem(60),
        name="tails",
    )(*order)


def shards(
    query_raw, key_raw, value_raw, gate_raw, query_taps, key_taps, value_taps,
    beta_logit, decay_logit, norm_gain, out_weight,
):
    raws = (query_raw, key_raw, value_raw)
    before = shifted(tails(raws), "seq", 1)
    pairs, local = local_steps(
        raws, before, (query_taps, key_taps, value_taps), beta_logit, decay_logit, gate_raw, norm_gain
    )
    starts, (parts, gated) = starts_of(pairs, "seq", local)
    return projected(parts, starts, gated, out_weight, "head")


def solution(mesh):
    placed = (
        P("seq", "head"), P("seq", "head"), P("seq", "head"), P("seq", "head"),
        P(None, "head"), P(None, "head"), P(None, "head"),
        P("seq", "head"), P("seq", "head"), P(), P("head", None),
    )
    return jax.shard_map(
        shards, mesh=mesh, in_specs=placed, out_specs=P(("seq", "head"), None), check_vma=False
    )
```

```python
import functools
import math

import jax
import jax.numpy as jnp
from jax import lax
from jax.experimental import pallas as pl
from jax.experimental.pallas import tpu as pltpu
from jax.sharding import PartitionSpec as P

DK = 128
DV = 128
CHUNK = 128
TINY = 8
SMALL = 32
GROUP = 8
HEADS_AT_ONCE = 4
EPSILON = 1e-06
F32 = jnp.float32
BF16 = jnp.bfloat16


def mul(left, right):
    return jnp.dot(left.astype(BF16), right.astype(BF16), preferred_element_type=F32)


def sigmoid(x):
    return 0.5 + 0.5 * jnp.tanh(0.5 * x)


def conv_silu(padded, first, rows, taps_ref, head):
    taps = taps_ref[:, head_of(head)]
    summed = taps[0:1] * padded[head, first : first + rows, :]
    for offset in range(1, 4):
        summed = summed + taps[offset : offset + 1] * padded[head, first + offset : first + offset + rows, :]
    return summed * sigmoid(summed)


def widen(padded, first, rows, raw):
    for head in range(padded.shape[0]):
        padded[head, first : first + rows, :] = raw[:, head_of(head)].astype(F32)


def row_sums(values):
    return mul(values, jnp.ones((CHUNK, CHUNK), BF16))


def unit_rows(key):
    return key * lax.rsqrt(row_sums(key * key) + EPSILON)


def softplus(x):
    return jnp.maximum(x, 0.0) + jnp.log(1.0 + jnp.exp(-jnp.abs(x)))


def part_of(chunk):
    return slice(chunk * CHUNK, (chunk + 1) * CHUNK)


def head_of(head):
    return slice(head * DK, (head + 1) * DK)


def chunk_rows(ref, heads, chunks):
    held = ref.shape[0]
    first = (pl.program_id(0) * heads) % held
    rows = ref[:heads, :]
    for at in range(heads, held, heads):
        rows = jnp.where(first == at, ref[at : at + heads, :], rows)
    return jnp.concatenate([rows[:, part_of(c)] for c in chunks], 0)


def square_iotas(rows=CHUNK):
    return (
        lax.broadcasted_iota(jnp.int32, (rows, CHUNK), 0),
        lax.broadcasted_iota(jnp.int32, (rows, CHUNK), 1),
    )


def log_fades(logit):
    rows, cols = square_iotas()
    return jnp.dot(
        -softplus(logit), (rows <= cols).astype(F32), precision=lax.Precision.HIGHEST, preferred_element_type=F32
    )


def as_columns(blocks):
    rows = sum(block.shape[0] for block in blocks)
    return jnp.concatenate(list(blocks) + [jnp.zeros((CHUNK - rows, CHUNK), F32)], 0).T


def tiny_inverses(lower):
    lanes = lax.broadcasted_iota(jnp.int32, (TINY, CHUNK), 1)
    rows = lax.broadcasted_iota(jnp.int32, (TINY, CHUNK), 0)
    blocks = []
    for low in lower:
        block = low[:TINY]
        for at in range(1, CHUNK // TINY):
            block = jnp.where(lanes // TINY == at, low[at * TINY : (at + 1) * TINY], block)
        blocks.append(block)
    stacked = jnp.concatenate(blocks, 0)
    all_lanes = lax.broadcasted_iota(jnp.int32, stacked.shape, 1)
    factors = [
        jnp.take_along_axis(
            stacked, all_lanes // TINY * TINY + c, axis=1, mode="promise_in_bounds"
        )
        for c in range(TINY - 1)
    ]
    inverses = []
    for p in range(len(lower)):
        inverse = jnp.where(lanes % TINY == rows, 1.0, 0.0)
        for c in range(TINY - 1):
            inverse = inverse - factors[c][p * TINY : (p + 1) * TINY] * inverse[c : c + 1]
        inverses.append(inverse)
    return inverses


def solved_packs(fade, beta_logit, keys, key_cols, value_work, value_of):
    count = len(keys)
    stages = 6
    done = [0, 0]

    def between():
        done[1] += 1
        while done[0] < len(value_work) and done[0] * stages < len(value_work) * done[1]:
            value_work[done[0]]()
            done[0] += 1

    rows, cols = square_iotas()
    strict = rows > cols
    differ = rows ^ cols
    columns = as_columns((fade - softplus(-beta_logit),))
    beta = sigmoid(beta_logit)
    beta_grown = beta * jnp.exp(fade)
    inner = {}
    for key, turned in zip(keys, key_cols):
        if id(key) not in inner:
            inner[id(key)] = mul(key, turned)
    lower = []
    for p in range(count):
        gap = columns[:, p : p + 1] - fade[p : p + 1, :]
        lower.append(jnp.exp(jnp.where(strict, gap, -1e30)) * inner[id(keys[p])])

    small_rows, small_cols = square_iotas(SMALL)
    small_differ = small_rows ^ (small_cols % SMALL)
    place = small_cols // SMALL
    blocks = jnp.where(rows // SMALL == cols // SMALL, 1.0, 0.0)
    blocks16 = blocks.astype(BF16)

    def spread(small):
        return jnp.concatenate([small] * (CHUNK // SMALL), 0) * (blocks16 if small.dtype == BF16 else blocks)

    small = []
    for low in lower:
        held = low[:SMALL]
        for at in range(1, CHUNK // SMALL):
            held = jnp.where(place == at, low[at * SMALL : (at + 1) * SMALL], held)
        small.append(held)
    tiny_inverse = tiny_inverses(lower)
    held = (small_cols % SMALL) // TINY == small_rows // TINY
    inverse = [
        jnp.where(held, jnp.concatenate([one] * (SMALL // TINY), 0), 0.0) for one in tiny_inverse
    ]
    size = TINY
    while size < CHUNK:
        last = size == SMALL
        if last:
            band = (differ >= size) & (differ < 4 * size)
            inside = [jnp.where(band, low, 0.0).astype(BF16) for low in lower]
            inverse16 = [spread(one.astype(BF16)) for one in inverse]
            inverse = [spread(one) for one in inverse]
            wide16 = inverse16
        else:
            band = (small_differ >= size) & (small_differ < 4 * size)
            inside = [spread(jnp.where(band, one, 0.0).astype(BF16)) for one in small]
            inverse16 = [one.astype(BF16) for one in inverse]
            wide16 = [spread(one) for one in inverse16]
        between()
        step = [mul(inverse16[p], inside[p]).astype(BF16) for p in range(count)]
        between()
        both = [
            mul(step[p], jnp.concatenate([step[p] if last else spread(step[p]), wide16[p]], 1))
            for p in range(count)
        ]
        between()
        inverse = [inverse[p] - both[p][:, CHUNK:] for p in range(count)]
        partial = [inverse[p].astype(BF16) for p in range(count)]
        inverse = [
            inverse[p] + mul(both[p][:, :CHUNK], partial[p] if last else spread(partial[p]))
            for p in range(count)
        ]
        size *= 4

    return [
        jnp.concatenate(
            [
                mul(inverse[p] * beta[p : p + 1, :], value_of(p)),
                mul(inverse[p] * beta_grown[p : p + 1, :], keys[p]),
            ],
            1,
        )
        for p in range(count)
    ]


def later_kernel(
    key_ref, value_ref, key_taps, value_taps, beta_ref, decay_ref,
    solved_ref, moves_ref, key_padded, value_padded,
):
    length = key_ref.shape[0]
    chunks = range(1, length // CHUNK)
    key_heads, heads = key_padded.shape[0], value_padded.shape[0]
    step = pl.program_id(0)
    repeat_by = heads // key_heads
    packs = [(chunk, head) for chunk in chunks for head in range(heads)]
    skip = CHUNK - 16
    count = length - CHUNK
    for padded, raw_ref in ((key_padded, key_ref), (value_padded, value_ref)):
        for head in range(padded.shape[0]):
            first = pl.multiple_of((step * padded.shape[0] + head) * DK, DK)
            padded[head] = raw_ref[skip:, pl.ds(first, DK)].astype(F32)
    key, turned = {}, {}
    for j in range(key_heads):
        unit = unit_rows(conv_silu(key_padded, 13, count, key_taps, j))
        for head in range(j * repeat_by, (j + 1) * repeat_by):
            solved_ref[head, :, DV + DK :] = unit.astype(BF16)
        for chunk in chunks:
            key[chunk, j] = unit[part_of(chunk - 1)]
            turned[chunk, j] = key[chunk, j].T
    value = {}

    def make_value(head):
        value[head] = conv_silu(value_padded, 13, count, value_taps, head)

    def value_of(pack):
        chunk, head = packs[pack]
        return value[head][part_of(chunk - 1)]

    fade = log_fades(chunk_rows(decay_ref, heads, chunks))
    solved = solved_packs(
        fade,
        chunk_rows(beta_ref, heads, chunks),
        [key[chunk, head // repeat_by] for chunk, head in packs],
        [turned[chunk, head // repeat_by] for chunk, head in packs],
        [functools.partial(make_value, head) for head in range(heads)],
        value_of,
    )
    tail = jnp.exp(fade[:, CHUNK - 1 : CHUNK] - fade)
    for pack, (chunk, head) in enumerate(packs):
        one = solved[pack].astype(BF16)
        solved_ref[head, part_of(chunk - 1), : DV + DK] = one
        moves_ref[head, chunk - 1] = mul(
            turned[chunk, head // repeat_by] * tail[pack : pack + 1, :], one
        ).astype(BF16)


def states_kernel(
    key_ref, value_ref, key_before, value_before, key_taps, value_taps, beta_ref, decay_ref, moves_hbm,
    pairs_hbm, solved_hbm, starts_hbm,
    key_padded, value_padded, moves_ref, solved_ref, starts_ref, pairs_ref, in_sem, out_sem, pairs_sem,
):
    heads, length = decay_ref.shape
    chunks = length // CHUNK
    key_heads = key_ref.shape[1] // DK
    repeat_by = heads // key_heads
    incoming = pltpu.make_async_copy(moves_hbm, moves_ref, in_sem)
    incoming.start()

    widen(key_padded, 5, 3, key_before[...])
    widen(key_padded, 8, CHUNK, key_ref[...])
    widen(value_padded, 5, 3, value_before[...])
    widen(value_padded, 8, CHUNK, value_ref[...])
    key, turned = [], []
    for j in range(key_heads):
        key.append(unit_rows(conv_silu(key_padded, 5, CHUNK, key_taps, j)))
        for head in range(j * repeat_by, (j + 1) * repeat_by):
            solved_ref[head, :, DV + DK :] = key[j].astype(BF16)
        turned.append(key[j].T)
    fade = log_fades(chunk_rows(decay_ref, heads, range(chunks)))
    value = {}

    def make_value(head):
        value[head] = conv_silu(value_padded, 5, CHUNK, value_taps, head)

    solved = solved_packs(
        fade[:heads],
        beta_ref[:, :CHUNK],
        [key[head // repeat_by] for head in range(heads)],
        [turned[head // repeat_by] for head in range(heads)],
        [functools.partial(make_value, head) for head in range(heads)],
        lambda head: value[head],
    )
    last = jnp.exp(fade[:, CHUNK - 1 : CHUNK])
    tail = jnp.exp(fade[:, CHUNK - 1 : CHUNK] - fade)
    rows, cols = square_iotas()
    identity = jnp.where(rows == cols, 1.0, 0.0)

    state = []
    for head in range(heads):
        one = solved[head].astype(BF16)
        solved_ref[head, :, : DV + DK] = one
        moved = mul(turned[head // repeat_by] * tail[head : head + 1, :], one)
        state.append(
            jnp.concatenate([moved[:, :DV], last[head : head + 1, :] * identity - moved[:, DV:]], 1)
        )
    each = min(HEADS_AT_ONCE, heads)
    outgoing = [pltpu.make_async_copy(solved_ref, solved_hbm, out_sem.at[0])]
    outgoing[0].start()
    incoming.wait()
    for chunk in range(1, chunks):
        for head in range(heads):
            pack = chunk * heads + head
            start = state[head].astype(BF16)
            starts_ref[chunk - 1, head] = start
            moves = moves_ref[head, chunk - 1]
            moved = last[pack : pack + 1, :] * state[head] - mul(moves[:, DV:], start)
            state[head] = jnp.concatenate([moved[:, :DV] + moves[:, :DV].astype(F32), moved[:, DV:]], 1)
            if chunk == chunks - 1:
                pairs_ref[head] = state[head].astype(BF16)
                if (head + 1) % each == 0:
                    done = pl.ds(head + 1 - each, each)
                    outgoing.append(
                        pltpu.make_async_copy(
                            pairs_ref.at[done], pairs_hbm.at[done], pairs_sem.at[head // each]
                        )
                    )
                    outgoing[-1].start()
        outgoing.append(
            pltpu.make_async_copy(
                starts_ref.at[chunk - 1], starts_hbm.at[chunk - 1], out_sem.at[chunk]
            )
        )
        outgoing[-1].start()
    for copy in outgoing:
        copy.wait()


def local_kernel(
    query_ref, query_before, query_taps, decay_ref,
    first_solved, later_solved, starts_ref, gate_ref, gain_ref,
    ahead_ref, parts_ref, padded,
):
    step = pl.program_id(0)
    length, width = query_ref.shape
    chunks = length // CHUNK
    key_heads = width // DK
    heads = first_solved.shape[0]
    repeat_by = heads // key_heads

    rows, cols = square_iotas()
    within = rows >= cols
    fade = log_fades(chunk_rows(decay_ref, heads, range(chunks)))
    columns = as_columns((fade,))
    widen(padded, 5, 3, query_before[...])
    widen(padded, 8, length, query_ref[...])
    query = [conv_silu(padded, 5, length, query_taps, j).astype(BF16) for j in range(key_heads)]
    for head in range(heads):
        gate = gate_ref[:, head_of(head)].astype(F32)
        parts_ref[heads + head // 2, :, head_of(head % 2)] = (
            gate * sigmoid(gate) * gain_ref[...]
        ).astype(BF16)
    for chunk in range(chunks):
        part = part_of(chunk)
        for j in range(key_heads):
            own = query[j][part]
            if chunk == 0:
                unit = first_solved[j * repeat_by, :, DV + DK :]
            else:
                unit = later_solved[j * repeat_by, part_of(chunk - 1), DV + DK :]
            inner = lax.dot_general(
                own, unit, (((1,), (1,)), ((), ())), preferred_element_type=F32
            )
            for head in range(j * repeat_by, (j + 1) * repeat_by):
                pack = chunk * heads + head
                column = jnp.broadcast_to(columns[:, pack : pack + 1], (CHUNK, CHUNK))
                scores = inner * jnp.exp(jnp.where(within, column - fade[pack : pack + 1, :], -1e30))
                grown = jnp.exp(column)
                if chunk == 0:
                    updates, wide = first_solved[head, :, :DV], first_solved[head, :, DV : DV + DK]
                    fresh = jnp.concatenate([updates, -wide], 1)
                    carried = jnp.concatenate(
                        [jnp.zeros((CHUNK, DV), F32), grown * own.astype(F32)], 1
                    )
                else:
                    solved = later_solved[head, part_of(chunk - 1), : DV + DK]
                    both = mul(jnp.concatenate([solved[:, DV:], own], 0), starts_ref[chunk - 1, head])
                    taken = both[:CHUNK]
                    fresh = jnp.concatenate(
                        [solved[:, :DV].astype(F32) - taken[:, :DV], -taken[:, DV:]], 1
                    )
                    carried = jnp.concatenate(
                        [grown * both[CHUNK:, :DV], grown * both[CHUNK:, DV:]], 1
                    )
                parts_ref[head, part, :] = (carried + mul(scores, fresh)).astype(BF16)

    @pl.when(step == 0)
    def _():
        ahead_ref[...] = parts_ref[...]


def columns_of(rows, width, first=0):
    return pl.BlockSpec((rows, width), lambda step: (0, step + first))


def in_vmem(mib):
    return pltpu.CompilerParams(vmem_limit_bytes=mib * 1024 * 1024)


def local_steps(raws, before, taps, beta_logit, decay_logit, gate_raw, norm_gain):
    length = raws[0].shape[0]
    key_heads = raws[0].shape[1] // DK
    value_heads = raws[2].shape[1] // DV
    repeat_by = value_heads // key_heads
    chunks = length // CHUNK
    beta, decay = beta_logit.T, decay_logit.T
    work = CHUNK * length * DV * value_heads
    hbm = pl.BlockSpec(memory_space=pltpu.HBM)
    vmem = pl.BlockSpec(memory_space=pltpu.VMEM)

    def split(each):
        heads = each * repeat_by
        held = max(heads, math.gcd(8, value_heads))
        of_heads = lambda *shape: pl.BlockSpec((heads,) + shape, lambda step: (step,) + (0,) * len(shape))
        logits = pl.BlockSpec((held, length), lambda step: (step * heads // held, 0))
        return key_heads // each, each * DK, heads * DV, of_heads, logits

    each = math.gcd(4, key_heads)
    steps, narrow, wide, of_heads, logits = split(each)
    later = length - CHUNK
    solved, moves = pl.pallas_call(
        later_kernel,
        grid=(steps,),
        in_specs=[
            vmem, vmem, columns_of(4, narrow), columns_of(4, wide), logits, logits,
        ],
        out_specs=[
            of_heads(later, DV + 2 * DK), of_heads(chunks - 1, DK, DV + DK),
        ],
        out_shape=[
            jax.ShapeDtypeStruct((value_heads, later, DV + 2 * DK), BF16),
            jax.ShapeDtypeStruct((value_heads, chunks - 1, DK, DV + DK), BF16),
        ],
        scratch_shapes=[
            pltpu.VMEM((each, later + 16, DK), F32),
            pltpu.VMEM((each * repeat_by, later + 16, DV), F32),
        ],
        compiler_params=in_vmem(50),
        cost_estimate=pl.CostEstimate(flops=30 * work, bytes_accessed=0, transcendentals=0),
        name="later",
    )(raws[1], raws[2], taps[1], taps[2], beta, decay)

    narrow, wide = key_heads * DK, value_heads * DV
    whole = lambda shape, *at: pl.BlockSpec(shape, lambda step: at or (0,) * len(shape))
    pairs, first_solved, starts = pl.pallas_call(
        states_kernel,
        grid=(1,),
        in_specs=[
            whole((CHUNK, narrow)), whole((CHUNK, wide)),
            whole((3, narrow), 0, repeat_by + 1), whole((3, wide)),
            whole(taps[1].shape), whole(taps[2].shape), whole(beta.shape), whole(decay.shape), hbm,
        ],
        out_specs=[hbm, hbm, hbm],
        out_shape=[
            jax.ShapeDtypeStruct((value_heads, DK, DV + DK), BF16),
            jax.ShapeDtypeStruct((value_heads, CHUNK, DV + 2 * DK), BF16),
            jax.ShapeDtypeStruct((chunks - 1, value_heads, DK, DV + DK), BF16),
        ],
        scratch_shapes=[
            pltpu.VMEM((key_heads, 8 + CHUNK, DK), F32),
            pltpu.VMEM((value_heads, 8 + CHUNK, DV), F32),
            pltpu.VMEM(moves.shape, BF16),
            pltpu.VMEM((value_heads, CHUNK, DV + 2 * DK), BF16),
            pltpu.VMEM((chunks - 1, value_heads, DK, DV + DK), BF16),
            pltpu.VMEM((value_heads, DK, DV + DK), BF16),
            pltpu.SemaphoreType.DMA,
            pltpu.SemaphoreType.DMA((chunks,)),
            pltpu.SemaphoreType.DMA((value_heads // min(HEADS_AT_ONCE, value_heads),)),
        ],
        compiler_params=in_vmem(52),
        cost_estimate=pl.CostEstimate(flops=20 * work, bytes_accessed=0, transcendentals=0),
        name="states",
    )(raws[1], raws[2], before, before, taps[1], taps[2], beta, decay, moves)
    gain = norm_gain.reshape(1, DV)

    def local():
        steps, narrow, wide, of_heads, logits = split(math.gcd(2, key_heads))
        heads = wide // DV
        ahead = (heads + heads // 2, length, DV + DK)
        return pl.pallas_call(
            local_kernel,
            grid=(steps,),
            in_specs=[
                columns_of(length, narrow), columns_of(3, narrow, repeat_by * steps), columns_of(4, narrow),
                logits, of_heads(CHUNK, DV + 2 * DK), of_heads(later, DV + 2 * DK),
                pl.BlockSpec((chunks - 1, heads, DK, DV + DK), lambda step: (0, step, 0, 0)),
                columns_of(length, wide), whole(gain.shape),
            ],
            out_specs=[
                whole(ahead),
                pl.BlockSpec(ahead, lambda step: (jnp.maximum(step - 1, 0), 0, 0)),
            ],
            out_shape=[
                jax.ShapeDtypeStruct(ahead, BF16),
                jax.ShapeDtypeStruct((max(steps - 1, 1) * ahead[0],) + ahead[1:], BF16),
            ],
            scratch_shapes=[pltpu.VMEM((narrow // DK, 8 + length, DK), F32)],
            compiler_params=in_vmem(60),
            cost_estimate=pl.CostEstimate(flops=12 * work, bytes_accessed=0, transcendentals=0),
            name="local",
        )(
            raws[0], before, taps[0], decay, first_solved, solved, starts, gate_raw, gain,
        )

    return pairs, local


def prefix_kernel(pairs_ref, prefix_ref, total_ref):
    count, heads = pairs_ref.shape[:2]
    running = [None] * heads
    for hop in range(count):
        for head in range(heads):
            now = pairs_ref[hop, head]
            if hop == 0:
                rows = lax.broadcasted_iota(jnp.int32, (DK, DV + DK), 0)
                cols = lax.broadcasted_iota(jnp.int32, (DK, DV + DK), 1)
                prefix_ref[hop, head] = jnp.where(cols == rows + DV, 1.0, 0.0).astype(BF16)
                running[head] = now.astype(F32)
            else:
                before = running[head].astype(BF16)
                prefix_ref[hop, head] = before
                own = jnp.concatenate([now[:, :DV].astype(F32), jnp.zeros((DK, DK), F32)], 1)
                running[head] = own + mul(now[:, DV:], before)
    for head in range(heads):
        total_ref[head] = running[head][:, : total_ref.shape[2]].astype(BF16)


def apply_kernel(prefix_ref, start_ref, starts_ref):
    count, heads = prefix_ref.shape[:2]
    for hop in range(count):
        for head in range(heads):
            starts_ref[hop, head] = (
                prefix_ref[hop, head, :, :DV].astype(F32)
                + mul(prefix_ref[hop, head, :, DV:], start_ref[head])
            ).astype(BF16)


def shifted(value, axis, by):
    count = lax.axis_size(axis)
    return lax.ppermute(value, axis, [(i, i + by) for i in range(count - by)])


def group_start(total, axis, group):
    groups = lax.axis_size(axis) // group
    running = shifted(total, axis, group)
    by = 1
    while by < groups - 1:
        earlier = shifted(running, axis, by * group)
        product = jnp.einsum("bkl,blv->bkv", running[..., DV:], earlier, preferred_element_type=F32)
        own = jnp.pad(running[..., :DV], ((0, 0), (0, 0), (0, DK)))
        running = (product + own.astype(F32)).astype(BF16)
        by *= 2
    return running[..., :DV]


def starts_of(pairs, axis, beside):
    size = lax.axis_size(axis)
    heads = pairs.shape[0]
    group = math.gcd(math.gcd(size, heads), GROUP)
    groups = [[g * group + i for i in range(group)] for g in range(size // group)]
    each = heads // group
    wide = DV if size // group == 2 else DV + DK
    by_head = lax.all_to_all(pairs, axis, 0, 0, axis_index_groups=groups, tiled=True)
    by_head, done = lax.optimization_barrier((by_head, beside()))
    prefix, total = pl.pallas_call(
        prefix_kernel,
        out_shape=[
            jax.ShapeDtypeStruct((group, each, DK, DV + DK), BF16),
            jax.ShapeDtypeStruct((each, DK, wide), BF16),
        ],
        compiler_params=in_vmem(16),
        name="prefix",
    )(by_head.reshape(group, each, DK, DV + DK))
    starts = pl.pallas_call(
        apply_kernel,
        out_shape=jax.ShapeDtypeStruct((group, each, DK, DV), BF16),
        compiler_params=in_vmem(16),
        name="apply",
    )(prefix, group_start(total, axis, group))
    starts = lax.all_to_all(
        starts.reshape(heads, DK, DV), axis, 0, 0, axis_index_groups=groups, tiled=True
    )
    return starts, done


def project_kernel(
    place_ref, starts_ref, ahead_ref, parts_hbm, weight_hbm, away_ref, own_ref,
    parts_ref, weight_ref, total, parts_sem, weight_sem,
):
    heads = starts_ref.shape[0]
    entries, length = ahead_ref.shape[:2]
    each = entries * 2 // 3
    width = weight_ref.shape[1]
    block = min(512, width)
    groups = heads // each

    def parts(g):
        here = pl.ds((g - 1) * entries, entries)
        return pltpu.make_async_copy(parts_hbm.at[here], parts_ref.at[here], parts_sem.at[g])

    def weights(g):
        rows = pl.ds(g * each * DV, each * DV)
        return pltpu.make_async_copy(weight_hbm.at[rows], weight_ref.at[rows], weight_sem.at[g])

    def normed_group(g):
        normed = []
        for head in range(g * each, (g + 1) * each):
            held, at = (ahead_ref, head) if g == 0 else (parts_ref, (g - 1) * entries + head - g * each)
            core = held[at, :, :DV].astype(F32) + mul(held[at, :, DV:], starts_ref[head])
            scale = lax.rsqrt(jnp.mean(core * core, -1, keepdims=True) + EPSILON)
            gated = held[at - head % each + each + head % each // 2, :, head_of(head % 2)]
            normed.append((core * scale * gated.astype(F32)).astype(BF16))
        return jnp.concatenate(normed, 1)

    weights(0).start()
    if groups > 1:
        parts(1).start()
        weights(1).start()
    following = normed_group(0)
    for g in range(groups):
        weights(g).wait()
        if g + 2 < groups:
            weights(g + 2).start()
        if g + 1 < groups:
            parts(g + 1).wait()
        if g + 2 < groups:
            parts(g + 2).start()
        normed = following
        if g + 1 < groups:
            following = normed_group(g + 1)
        for at in range(0, width, block):
            added = jnp.dot(
                normed, weight_ref[g * each * DV : (g + 1) * each * DV, at : at + block],
                preferred_element_type=F32,
            )
            if g > 0:
                added = added + total[:, at : at + block]
            if g < groups - 1:
                total[:, at : at + block] = added
            elif own_ref is None:
                away_ref[:, at : at + block] = added.astype(BF16)
            else:
                first = place_ref[0] == 0
                low, high = added[: length // 2], added[length // 2 :]
                own_ref[:, at : at + block] = jnp.where(first, low, high).astype(BF16)
                away_ref[:, at : at + block] = jnp.where(first, high, low).astype(BF16)


def whole_kernel(place_ref, starts_ref, ahead_ref, parts_hbm, weight_hbm, out_ref, *scratch):
    project_kernel(place_ref, starts_ref, ahead_ref, parts_hbm, weight_hbm, out_ref, None, *scratch)


def projected(ahead, parts, starts, out_weight, axis):
    length = parts.shape[1]
    width = out_weight.shape[1]
    halves = lax.axis_size(axis) == 2
    vmem = pl.BlockSpec(memory_space=pltpu.VMEM)
    hbm = pl.BlockSpec(memory_space=pltpu.HBM)
    heads = starts.shape[0]
    groups = heads // (ahead.shape[0] * 2 // 3)
    here = lax.axis_index(axis).astype(jnp.int32).reshape(1)
    out = jax.ShapeDtypeStruct((length // 2 if halves else length, width), BF16)
    partial = pl.pallas_call(
        project_kernel if halves else whole_kernel,
        in_specs=[pl.BlockSpec(memory_space=pltpu.SMEM), vmem, vmem, hbm, hbm],
        out_specs=[vmem, vmem] if halves else vmem,
        out_shape=[out, out] if halves else out,
        scratch_shapes=[
            pltpu.VMEM(parts.shape, BF16),
            pltpu.VMEM(out_weight.shape, BF16),
            pltpu.VMEM((length, width), F32),
            pltpu.SemaphoreType.DMA((groups,)),
            pltpu.SemaphoreType.DMA((groups,)),
        ],
        compiler_params=in_vmem(50),
        name="project",
    )(here, starts, ahead, parts, out_weight)
    if not halves:
        return lax.psum_scatter(partial, axis, scatter_dimension=0, tiled=True)
    away, own = partial
    other = lax.ppermute(away, axis, [(0, 1), (1, 0)])
    return (own.astype(F32) + other.astype(F32)).astype(BF16)


def tails_kernel(value_hbm, query_hbm, key_hbm, out_ref, value_ref, query_ref, key_ref, sem):
    pairs = ((value_hbm, value_ref), (query_hbm, query_ref), (key_hbm, key_ref))
    copies = [
        pltpu.make_async_copy(source.at[pl.ds(source.shape[0] - 16, 16)], held, sem.at[i])
        for i, (source, held) in enumerate(pairs)
    ]
    for copy in copies:
        copy.start()
    at = 0
    for copy, (_, held) in zip(copies, pairs):
        copy.wait()
        width = held.shape[1]
        out_ref[:, at : at + width] = held[...].astype(F32)[13:16].astype(BF16)
        at += width


def tails(raws):
    order = (raws[2], raws[0], raws[1])
    width = sum(raw.shape[1] for raw in order)
    return pl.pallas_call(
        tails_kernel,
        in_specs=[pl.BlockSpec(memory_space=pltpu.HBM)] * 3,
        out_shape=jax.ShapeDtypeStruct((3, width), BF16),
        scratch_shapes=[pltpu.VMEM((16, raw.shape[1]), BF16) for raw in order]
        + [pltpu.SemaphoreType.DMA((3,))],
        compiler_params=in_vmem(60),
        name="tails",
    )(*order)


def shards(
    query_raw, key_raw, value_raw, gate_raw, query_taps, key_taps, value_taps,
    beta_logit, decay_logit, norm_gain, out_weight,
):
    raws = (query_raw, key_raw, value_raw)
    before = shifted(tails(raws), "seq", 1)
    pairs, local = local_steps(
        raws, before, (query_taps, key_taps, value_taps), beta_logit, decay_logit, gate_raw, norm_gain
    )
    starts, (ahead, parts) = starts_of(pairs, "seq", local)
    return projected(ahead, parts, starts, out_weight, "head")


def solution(mesh):
    placed = (
        P("seq", "head"), P("seq", "head"), P("seq", "head"), P("seq", "head"),
        P(None, "head"), P(None, "head"), P(None, "head"),
        P("seq", "head"), P("seq", "head"), P(), P("head", None),
    )
    return jax.shard_map(
        shards, mesh=mesh, in_specs=placed, out_specs=P(("seq", "head"), None), check_vma=False
    )
```

```python
import functools
import math

import jax
import jax.numpy as jnp
from jax import lax
from jax.experimental import pallas as pl
from jax.experimental.pallas import tpu as pltpu
from jax.sharding import PartitionSpec as P

DK = 128
DV = 128
CHUNK = 128
TINY = 8
SMALL = 32
GROUP = 8
HEADS_AT_ONCE = 4
EPSILON = 1e-06
F32 = jnp.float32
BF16 = jnp.bfloat16


def mul(left, right):
    return jnp.dot(left.astype(BF16), right.astype(BF16), preferred_element_type=F32)


def sigmoid(x):
    return 0.5 + 0.5 * jnp.tanh(0.5 * x)


def conv_silu(padded, first, rows, taps_ref, head, before=0):
    taps = taps_ref[:, pl.ds(pl.multiple_of((before + head) * DK, DK), DK)]
    summed = taps[0:1] * padded[head, first : first + rows, :]
    for offset in range(1, 4):
        summed = summed + taps[offset : offset + 1] * padded[head, first + offset : first + offset + rows, :]
    return summed * sigmoid(summed)


def widen(padded, first, rows, raw):
    for head in range(padded.shape[0]):
        padded[head, first : first + rows, :] = raw[:, head_of(head)].astype(F32)


def row_sums(values):
    return mul(values, jnp.ones((CHUNK, CHUNK), BF16))


def unit_rows(key):
    return key * lax.rsqrt(row_sums(key * key) + EPSILON)


def softplus(x):
    return jnp.maximum(x, 0.0) + jnp.log(1.0 + jnp.exp(-jnp.abs(x)))


def part_of(chunk):
    return slice(chunk * CHUNK, (chunk + 1) * CHUNK)


def head_of(head):
    return slice(head * DK, (head + 1) * DK)


def chunk_rows(ref, heads, chunks):
    held = ref.shape[0]
    first = (pl.program_id(0) * heads) % held
    rows = ref[:heads, :]
    for at in range(heads, held, heads):
        rows = jnp.where(first == at, ref[at : at + heads, :], rows)
    return jnp.concatenate([rows[:, part_of(c)] for c in chunks], 0)


def square_iotas(rows=CHUNK):
    return (
        lax.broadcasted_iota(jnp.int32, (rows, CHUNK), 0),
        lax.broadcasted_iota(jnp.int32, (rows, CHUNK), 1),
    )


def log_fades(logit):
    rows, cols = square_iotas()
    return jnp.dot(
        -softplus(logit), (rows <= cols).astype(F32), precision=lax.Precision.HIGHEST, preferred_element_type=F32
    )


def as_columns(blocks):
    rows = sum(block.shape[0] for block in blocks)
    return jnp.concatenate(list(blocks) + [jnp.zeros((CHUNK - rows, CHUNK), F32)], 0).T


def tiny_inverses(lower):
    lanes = lax.broadcasted_iota(jnp.int32, (TINY, CHUNK), 1)
    rows = lax.broadcasted_iota(jnp.int32, (TINY, CHUNK), 0)
    blocks = []
    for low in lower:
        block = low[:TINY]
        for at in range(1, CHUNK // TINY):
            block = jnp.where(lanes // TINY == at, low[at * TINY : (at + 1) * TINY], block)
        blocks.append(block)
    stacked = jnp.concatenate(blocks, 0)
    all_lanes = lax.broadcasted_iota(jnp.int32, stacked.shape, 1)
    factors = [
        jnp.take_along_axis(
            stacked, all_lanes // TINY * TINY + c, axis=1, mode="promise_in_bounds"
        )
        for c in range(TINY - 1)
    ]
    inverses = []
    for p in range(len(lower)):
        inverse = jnp.where(lanes % TINY == rows, 1.0, 0.0)
        for c in range(TINY - 1):
            inverse = inverse - factors[c][p * TINY : (p + 1) * TINY] * inverse[c : c + 1]
        inverses.append(inverse)
    return inverses


def solved_packs(fade, beta_logit, keys, key_cols, value_work, value_of):
    count = len(keys)
    stages = 6
    done = [0, 0]

    def between():
        done[1] += 1
        while done[0] < len(value_work) and done[0] * stages < len(value_work) * done[1]:
            value_work[done[0]]()
            done[0] += 1

    rows, cols = square_iotas()
    strict = rows > cols
    differ = rows ^ cols
    columns = as_columns((fade - softplus(-beta_logit),))
    beta = sigmoid(beta_logit)
    beta_grown = beta * jnp.exp(fade)
    inner = {}
    for key, turned in zip(keys, key_cols):
        if id(key) not in inner:
            inner[id(key)] = mul(key, turned)
    lower = []
    for p in range(count):
        gap = columns[:, p : p + 1] - fade[p : p + 1, :]
        lower.append(jnp.exp(jnp.where(strict, gap, -1e30)) * inner[id(keys[p])])

    small_rows, small_cols = square_iotas(SMALL)
    small_differ = small_rows ^ (small_cols % SMALL)
    place = small_cols // SMALL
    blocks = jnp.where(rows // SMALL == cols // SMALL, 1.0, 0.0)
    blocks16 = blocks.astype(BF16)

    def spread(small):
        return jnp.concatenate([small] * (CHUNK // SMALL), 0) * (blocks16 if small.dtype == BF16 else blocks)

    small = []
    for low in lower:
        held = low[:SMALL]
        for at in range(1, CHUNK // SMALL):
            held = jnp.where(place == at, low[at * SMALL : (at + 1) * SMALL], held)
        small.append(held)
    tiny_inverse = tiny_inverses(lower)
    held = (small_cols % SMALL) // TINY == small_rows // TINY
    inverse = [
        jnp.where(held, jnp.concatenate([one] * (SMALL // TINY), 0), 0.0) for one in tiny_inverse
    ]
    size = TINY
    while size < CHUNK:
        last = size == SMALL
        if last:
            band = (differ >= size) & (differ < 4 * size)
            inside = [jnp.where(band, low, 0.0).astype(BF16) for low in lower]
            inverse16 = [spread(one.astype(BF16)) for one in inverse]
            inverse = [spread(one) for one in inverse]
            wide16 = inverse16
        else:
            band = (small_differ >= size) & (small_differ < 4 * size)
            inside = [spread(jnp.where(band, one, 0.0).astype(BF16)) for one in small]
            inverse16 = [one.astype(BF16) for one in inverse]
            wide16 = [spread(one) for one in inverse16]
        between()
        step = [mul(inverse16[p], inside[p]).astype(BF16) for p in range(count)]
        between()
        both = [
            mul(step[p], jnp.concatenate([step[p] if last else spread(step[p]), wide16[p]], 1))
            for p in range(count)
        ]
        between()
        inverse = [inverse[p] - both[p][:, CHUNK:] for p in range(count)]
        partial = [inverse[p].astype(BF16) for p in range(count)]
        inverse = [
            inverse[p] + mul(both[p][:, :CHUNK], partial[p] if last else spread(partial[p]))
            for p in range(count)
        ]
        size *= 4

    return [
        jnp.concatenate(
            [
                mul(inverse[p] * beta[p : p + 1, :], value_of(p)),
                mul(inverse[p] * beta_grown[p : p + 1, :], keys[p]),
            ],
            1,
        )
        for p in range(count)
    ]


def later_kernel(
    key_ref, value_ref, key_taps, value_taps, beta_ref, decay_ref,
    solved_hbm, moves_hbm, key_padded, value_padded, solved_ref, moves_ref, sem,
):
    length = key_ref.shape[0]
    chunks = range(1, length // CHUNK)
    key_heads, heads = key_padded.shape[0], value_padded.shape[0]
    step = pl.program_id(0)
    repeat_by = heads // key_heads
    packs = [(chunk, head) for chunk in chunks for head in range(heads)]
    skip = CHUNK - 16
    count = length - CHUNK
    for padded, raw_ref in ((key_padded, key_ref), (value_padded, value_ref)):
        for head in range(padded.shape[0]):
            first = pl.multiple_of((step * padded.shape[0] + head) * DK, DK)
            padded[head] = raw_ref[skip:, pl.ds(first, DK)].astype(F32)
    key, turned = {}, {}
    for j in range(key_heads):
        unit = unit_rows(conv_silu(key_padded, 13, count, key_taps, j, step * key_heads))
        for head in range(j * repeat_by, (j + 1) * repeat_by):
            solved_ref[step * heads + head, :, DV + DK :] = unit.astype(BF16)
        for chunk in chunks:
            key[chunk, j] = unit[part_of(chunk - 1)]
            turned[chunk, j] = key[chunk, j].T
    value = {}

    def make_value(head):
        value[head] = conv_silu(value_padded, 13, count, value_taps, head, step * heads)

    def value_of(pack):
        chunk, head = packs[pack]
        return value[head][part_of(chunk - 1)]

    fade = log_fades(chunk_rows(decay_ref, heads, chunks))
    solved = solved_packs(
        fade,
        chunk_rows(beta_ref, heads, chunks),
        [key[chunk, head // repeat_by] for chunk, head in packs],
        [turned[chunk, head // repeat_by] for chunk, head in packs],
        [functools.partial(make_value, head) for head in range(heads)],
        value_of,
    )
    tail = jnp.exp(fade[:, CHUNK - 1 : CHUNK] - fade)

    def leaving(held, out, at_step, kind):
        here = pl.ds(at_step * heads, heads)
        return pltpu.make_async_copy(held.at[here], out.at[here], sem.at[kind, at_step])

    solved = [one.astype(BF16) for one in solved]
    for pack, (chunk, head) in enumerate(packs):
        solved_ref[step * heads + head, part_of(chunk - 1), : DV + DK] = solved[pack]
    leaving(solved_ref, solved_hbm, step, 0).start()
    for pack, (chunk, head) in enumerate(packs):
        moves_ref[step * heads + head, chunk - 1] = mul(
            turned[chunk, head // repeat_by] * tail[pack : pack + 1, :], solved[pack]
        ).astype(BF16)
    leaving(moves_ref, moves_hbm, step, 1).start()

    @pl.when(step == pl.num_programs(0) - 1)
    def _():
        for at_step in range(sem.shape[1]):
            leaving(solved_ref, solved_hbm, at_step, 0).wait()
            leaving(moves_ref, moves_hbm, at_step, 1).wait()


def states_kernel(
    key_ref, value_hbm, before_ref, key_taps, value_taps, beta_ref, decay_ref, moves_hbm,
    pairs_hbm, solved_hbm, starts_hbm,
    key_padded, value_padded, value_ref, moves_ref, solved_ref, starts_ref, pairs_ref,
    value_sem, in_sem, out_sem, pairs_sem,
):
    heads, length = decay_ref.shape
    chunks = length // CHUNK
    key_heads = key_ref.shape[1] // DK
    repeat_by = heads // key_heads
    value_copy = pltpu.make_async_copy(value_hbm.at[pl.ds(0, CHUNK)], value_ref, value_sem)
    value_copy.start()
    incoming = pltpu.make_async_copy(moves_hbm, moves_ref, in_sem)
    incoming.start()

    key_at = before_ref.shape[1] - key_ref.shape[1]
    widen(key_padded, 5, 3, before_ref[:, key_at:])
    widen(key_padded, 8, CHUNK, key_ref[:CHUNK, :])
    key, turned = [], []
    for j in range(key_heads):
        key.append(unit_rows(conv_silu(key_padded, 5, CHUNK, key_taps, j)))
        for head in range(j * repeat_by, (j + 1) * repeat_by):
            solved_ref[head, :, DV + DK :] = key[j].astype(BF16)
        turned.append(key[j].T)
    fade = log_fades(chunk_rows(decay_ref, heads, range(chunks)))
    value = {}

    def value_rows():
        value_copy.wait()
        widen(value_padded, 5, 3, before_ref[:, : value_ref.shape[1]])
        widen(value_padded, 8, CHUNK, value_ref[...])

    def make_value(head):
        value[head] = conv_silu(value_padded, 5, CHUNK, value_taps, head)

    solved = solved_packs(
        fade[:heads],
        beta_ref[:, :CHUNK],
        [key[head // repeat_by] for head in range(heads)],
        [turned[head // repeat_by] for head in range(heads)],
        [value_rows] + [functools.partial(make_value, head) for head in range(heads)],
        lambda head: value[head],
    )
    last = jnp.exp(fade[:, CHUNK - 1 : CHUNK])
    tail = jnp.exp(fade[:, CHUNK - 1 : CHUNK] - fade)
    rows, cols = square_iotas()
    identity = jnp.where(rows == cols, 1.0, 0.0)

    state = []
    for head in range(heads):
        one = solved[head].astype(BF16)
        solved_ref[head, :, : DV + DK] = one
        moved = mul(turned[head // repeat_by] * tail[head : head + 1, :], one)
        state.append(
            jnp.concatenate([moved[:, :DV], last[head : head + 1, :] * identity - moved[:, DV:]], 1)
        )
    each = min(HEADS_AT_ONCE, heads)
    outgoing = [pltpu.make_async_copy(solved_ref, solved_hbm, out_sem.at[0])]
    outgoing[0].start()
    incoming.wait()
    for chunk in range(1, chunks):
        for head in range(heads):
            pack = chunk * heads + head
            start = state[head].astype(BF16)
            starts_ref[chunk - 1, head] = start
            moves = moves_ref[head, chunk - 1]
            moved = last[pack : pack + 1, :] * state[head] - mul(moves[:, DV:], start)
            state[head] = jnp.concatenate([moved[:, :DV] + moves[:, :DV].astype(F32), moved[:, DV:]], 1)
            if chunk == chunks - 1:
                pairs_ref[head] = state[head].astype(BF16)
                if (head + 1) % each == 0:
                    done = pl.ds(head + 1 - each, each)
                    outgoing.append(
                        pltpu.make_async_copy(
                            pairs_ref.at[done], pairs_hbm.at[done], pairs_sem.at[head // each]
                        )
                    )
                    outgoing[-1].start()
        outgoing.append(
            pltpu.make_async_copy(
                starts_ref.at[chunk - 1], starts_hbm.at[chunk - 1], out_sem.at[chunk]
            )
        )
        outgoing[-1].start()
    for copy in outgoing:
        copy.wait()


def local_kernel(
    query_ref, query_before, query_taps, decay_ref,
    first_solved, later_solved, starts_ref, gate_ref, gain_ref,
    ahead_ref, parts_ref, padded,
):
    step = pl.program_id(0)
    length, width = query_ref.shape
    chunks = length // CHUNK
    key_heads = width // DK
    heads = first_solved.shape[0]
    repeat_by = heads // key_heads

    rows, cols = square_iotas()
    within = rows >= cols
    fade = log_fades(chunk_rows(decay_ref, heads, range(chunks)))
    columns = as_columns((fade,))
    widen(padded, 5, 3, query_before[...])
    widen(padded, 8, length, query_ref[...])
    query = [conv_silu(padded, 5, length, query_taps, j).astype(BF16) for j in range(key_heads)]
    for head in range(heads):
        gate = gate_ref[:, head_of(head)].astype(F32)
        parts_ref[heads + head // 2, :, head_of(head % 2)] = (
            gate * sigmoid(gate) * gain_ref[...]
        ).astype(BF16)
    for chunk in range(chunks):
        part = part_of(chunk)
        for j in range(key_heads):
            own = query[j][part]
            if chunk == 0:
                unit = first_solved[j * repeat_by, :, DV + DK :]
            else:
                unit = later_solved[j * repeat_by, part_of(chunk - 1), DV + DK :]
            inner = lax.dot_general(
                own, unit, (((1,), (1,)), ((), ())), preferred_element_type=F32
            )
            for head in range(j * repeat_by, (j + 1) * repeat_by):
                pack = chunk * heads + head
                column = jnp.broadcast_to(columns[:, pack : pack + 1], (CHUNK, CHUNK))
                scores = inner * jnp.exp(jnp.where(within, column - fade[pack : pack + 1, :], -1e30))
                grown = jnp.exp(column)
                if chunk == 0:
                    updates, wide = first_solved[head, :, :DV], first_solved[head, :, DV : DV + DK]
                    fresh = jnp.concatenate([updates, -wide], 1)
                    carried = jnp.concatenate(
                        [jnp.zeros((CHUNK, DV), F32), grown * own.astype(F32)], 1
                    )
                else:
                    solved = later_solved[head, part_of(chunk - 1), : DV + DK]
                    both = mul(jnp.concatenate([solved[:, DV:], own], 0), starts_ref[chunk - 1, head])
                    taken = both[:CHUNK]
                    fresh = jnp.concatenate(
                        [solved[:, :DV].astype(F32) - taken[:, :DV], -taken[:, DV:]], 1
                    )
                    carried = jnp.concatenate(
                        [grown * both[CHUNK:, :DV], grown * both[CHUNK:, DV:]], 1
                    )
                parts_ref[head, part, :] = (carried + mul(scores, fresh)).astype(BF16)

    @pl.when(step == 0)
    def _():
        ahead_ref[...] = parts_ref[...]


def columns_of(rows, width, first=0):
    return pl.BlockSpec((rows, width), lambda step: (0, step + first))


def in_vmem(mib):
    return pltpu.CompilerParams(vmem_limit_bytes=mib * 1024 * 1024)


def local_steps(raws, before, taps, beta_logit, decay_logit, gate_raw, norm_gain):
    length = raws[0].shape[0]
    key_heads = raws[0].shape[1] // DK
    value_heads = raws[2].shape[1] // DV
    repeat_by = value_heads // key_heads
    chunks = length // CHUNK
    beta, decay = beta_logit.T, decay_logit.T
    work = CHUNK * length * DV * value_heads
    hbm = pl.BlockSpec(memory_space=pltpu.HBM)
    vmem = pl.BlockSpec(memory_space=pltpu.VMEM)

    def split(each):
        heads = each * repeat_by
        held = max(heads, math.gcd(8, value_heads))
        of_heads = lambda *shape: pl.BlockSpec((heads,) + shape, lambda step: (step,) + (0,) * len(shape))
        logits = pl.BlockSpec((held, length), lambda step: (step * heads // held, 0))
        return key_heads // each, each * DK, heads * DV, of_heads, logits

    each = math.gcd(4, key_heads)
    steps, narrow, wide, of_heads, logits = split(each)
    later = length - CHUNK
    solved, moves = pl.pallas_call(
        later_kernel,
        grid=(steps,),
        in_specs=[
            vmem, vmem, vmem, vmem, vmem, vmem,
        ],
        out_specs=[hbm, hbm],
        out_shape=[
            jax.ShapeDtypeStruct((value_heads, later, DV + 2 * DK), BF16),
            jax.ShapeDtypeStruct((value_heads, chunks - 1, DK, DV + DK), BF16),
        ],
        scratch_shapes=[
            pltpu.VMEM((each, later + 16, DK), F32),
            pltpu.VMEM((each * repeat_by, later + 16, DV), F32),
            pltpu.VMEM((value_heads, later, DV + 2 * DK), BF16),
            pltpu.VMEM((value_heads, chunks - 1, DK, DV + DK), BF16),
            pltpu.SemaphoreType.DMA((2, steps)),
        ],
        compiler_params=in_vmem(50),
        cost_estimate=pl.CostEstimate(flops=30 * work, bytes_accessed=0, transcendentals=0),
        name="later",
    )(raws[1], raws[2], taps[1], taps[2], beta, decay)

    narrow, wide = key_heads * DK, value_heads * DV
    whole = lambda shape, *at: pl.BlockSpec(shape, lambda step: at or (0,) * len(shape))
    pairs, first_solved, starts = pl.pallas_call(
        states_kernel,
        grid=(1,),
        in_specs=[
            vmem, hbm, vmem, vmem, vmem, vmem, vmem, hbm,
        ],
        out_specs=[hbm, hbm, hbm],
        out_shape=[
            jax.ShapeDtypeStruct((value_heads, DK, DV + DK), BF16),
            jax.ShapeDtypeStruct((value_heads, CHUNK, DV + 2 * DK), BF16),
            jax.ShapeDtypeStruct((chunks - 1, value_heads, DK, DV + DK), BF16),
        ],
        scratch_shapes=[
            pltpu.VMEM((key_heads, 8 + CHUNK, DK), F32),
            pltpu.VMEM((value_heads, 8 + CHUNK, DV), F32),
            pltpu.VMEM((CHUNK, wide), BF16),
            pltpu.VMEM(moves.shape, BF16),
            pltpu.VMEM((value_heads, CHUNK, DV + 2 * DK), BF16),
            pltpu.VMEM((chunks - 1, value_heads, DK, DV + DK), BF16),
            pltpu.VMEM((value_heads, DK, DV + DK), BF16),
            pltpu.SemaphoreType.DMA,
            pltpu.SemaphoreType.DMA,
            pltpu.SemaphoreType.DMA((chunks,)),
            pltpu.SemaphoreType.DMA((value_heads // min(HEADS_AT_ONCE, value_heads),)),
        ],
        compiler_params=in_vmem(52),
        cost_estimate=pl.CostEstimate(flops=20 * work, bytes_accessed=0, transcendentals=0),
        name="states",
    )(raws[1], raws[2], before, taps[1], taps[2], beta, decay, moves)
    gain = norm_gain.reshape(1, DV)

    def local():
        steps, narrow, wide, of_heads, logits = split(math.gcd(2, key_heads))
        heads = wide // DV
        ahead = (heads + heads // 2, length, DV + DK)
        return pl.pallas_call(
            local_kernel,
            grid=(steps,),
            in_specs=[
                columns_of(length, narrow), columns_of(3, narrow, repeat_by * steps), columns_of(4, narrow),
                logits, of_heads(CHUNK, DV + 2 * DK), of_heads(later, DV + 2 * DK),
                pl.BlockSpec((chunks - 1, heads, DK, DV + DK), lambda step: (0, step, 0, 0)),
                columns_of(length, wide), whole(gain.shape),
            ],
            out_specs=[
                whole(ahead),
                pl.BlockSpec(ahead, lambda step: (jnp.maximum(step - 1, 0), 0, 0)),
            ],
            out_shape=[
                jax.ShapeDtypeStruct(ahead, BF16),
                jax.ShapeDtypeStruct((max(steps - 1, 1) * ahead[0],) + ahead[1:], BF16),
            ],
            scratch_shapes=[pltpu.VMEM((narrow // DK, 8 + length, DK), F32)],
            compiler_params=in_vmem(60),
            cost_estimate=pl.CostEstimate(flops=12 * work, bytes_accessed=0, transcendentals=0),
            name="local",
        )(
            raws[0], before, taps[0], decay, first_solved, solved, starts, gate_raw, gain,
        )

    return pairs, local


def prefix_kernel(pairs_ref, prefix_ref, total_ref):
    count, heads = pairs_ref.shape[:2]
    running = [None] * heads
    for hop in range(count):
        for head in range(heads):
            now = pairs_ref[hop, head]
            if hop == 0:
                rows = lax.broadcasted_iota(jnp.int32, (DK, DV + DK), 0)
                cols = lax.broadcasted_iota(jnp.int32, (DK, DV + DK), 1)
                prefix_ref[hop, head] = jnp.where(cols == rows + DV, 1.0, 0.0).astype(BF16)
                running[head] = now.astype(F32)
            else:
                before = running[head].astype(BF16)
                prefix_ref[hop, head] = before
                own = jnp.concatenate([now[:, :DV].astype(F32), jnp.zeros((DK, DK), F32)], 1)
                running[head] = own + mul(now[:, DV:], before)
    for head in range(heads):
        total_ref[head] = running[head][:, : total_ref.shape[2]].astype(BF16)


def apply_kernel(prefix_ref, start_ref, starts_ref):
    count, heads = prefix_ref.shape[:2]
    for hop in range(count):
        for head in range(heads):
            starts_ref[hop, head] = (
                prefix_ref[hop, head, :, :DV].astype(F32)
                + mul(prefix_ref[hop, head, :, DV:], start_ref[head])
            ).astype(BF16)


def shifted(value, axis, by):
    count = lax.axis_size(axis)
    return lax.ppermute(value, axis, [(i, i + by) for i in range(count - by)])


def group_start(total, axis, group):
    groups = lax.axis_size(axis) // group
    running = shifted(total, axis, group)
    by = 1
    while by < groups - 1:
        earlier = shifted(running, axis, by * group)
        product = jnp.einsum("bkl,blv->bkv", running[..., DV:], earlier, preferred_element_type=F32)
        own = jnp.pad(running[..., :DV], ((0, 0), (0, 0), (0, DK)))
        running = (product + own.astype(F32)).astype(BF16)
        by *= 2
    return running[..., :DV]


def starts_of(pairs, axis, beside):
    size = lax.axis_size(axis)
    heads = pairs.shape[0]
    group = math.gcd(math.gcd(size, heads), GROUP)
    groups = [[g * group + i for i in range(group)] for g in range(size // group)]
    each = heads // group
    wide = DV if size // group == 2 else DV + DK
    by_head = lax.all_to_all(pairs, axis, 0, 0, axis_index_groups=groups, tiled=True)
    by_head, done = lax.optimization_barrier((by_head, beside()))
    prefix, total = pl.pallas_call(
        prefix_kernel,
        out_shape=[
            jax.ShapeDtypeStruct((group, each, DK, DV + DK), BF16),
            jax.ShapeDtypeStruct((each, DK, wide), BF16),
        ],
        compiler_params=in_vmem(16),
        name="prefix",
    )(by_head.reshape(group, each, DK, DV + DK))
    starts = pl.pallas_call(
        apply_kernel,
        out_shape=jax.ShapeDtypeStruct((group, each, DK, DV), BF16),
        compiler_params=in_vmem(16),
        name="apply",
    )(prefix, group_start(total, axis, group))
    starts = lax.all_to_all(
        starts.reshape(heads, DK, DV), axis, 0, 0, axis_index_groups=groups, tiled=True
    )
    return starts, done


def project_kernel(
    place_ref, starts_ref, ahead_ref, parts_hbm, weight_hbm, away_ref, own_ref,
    parts_ref, weight_ref, total, parts_sem, weight_sem,
):
    heads = starts_ref.shape[0]
    entries, length = ahead_ref.shape[:2]
    each = entries * 2 // 3
    width = weight_ref.shape[1]
    block = min(512, width)
    groups = heads // each

    def parts(g):
        here = pl.ds((g - 1) * entries, entries)
        return pltpu.make_async_copy(parts_hbm.at[here], parts_ref.at[here], parts_sem.at[g])

    def weights(g):
        rows = pl.ds(g * each * DV, each * DV)
        return pltpu.make_async_copy(weight_hbm.at[rows], weight_ref.at[rows], weight_sem.at[g])

    def normed_group(g):
        normed = []
        for head in range(g * each, (g + 1) * each):
            held, at = (ahead_ref, head) if g == 0 else (parts_ref, (g - 1) * entries + head - g * each)
            core = held[at, :, :DV].astype(F32) + mul(held[at, :, DV:], starts_ref[head])
            scale = lax.rsqrt(jnp.mean(core * core, -1, keepdims=True) + EPSILON)
            gated = held[at - head % each + each + head % each // 2, :, head_of(head % 2)]
            normed.append((core * scale * gated.astype(F32)).astype(BF16))
        return jnp.concatenate(normed, 1)

    weights(0).start()
    if groups > 1:
        parts(1).start()
        weights(1).start()
    following = normed_group(0)
    for g in range(groups):
        weights(g).wait()
        if g + 2 < groups:
            weights(g + 2).start()
        if g + 1 < groups:
            parts(g + 1).wait()
        if g + 2 < groups:
            parts(g + 2).start()
        normed = following
        if g + 1 < groups:
            following = normed_group(g + 1)
        for at in range(0, width, block):
            added = jnp.dot(
                normed, weight_ref[g * each * DV : (g + 1) * each * DV, at : at + block],
                preferred_element_type=F32,
            )
            if g > 0:
                added = added + total[:, at : at + block]
            if g < groups - 1:
                total[:, at : at + block] = added
            elif own_ref is None:
                away_ref[:, at : at + block] = added.astype(BF16)
            else:
                first = place_ref[0] == 0
                low, high = added[: length // 2], added[length // 2 :]
                own_ref[:, at : at + block] = jnp.where(first, low, high).astype(BF16)
                away_ref[:, at : at + block] = jnp.where(first, high, low).astype(BF16)


def whole_kernel(place_ref, starts_ref, ahead_ref, parts_hbm, weight_hbm, out_ref, *scratch):
    project_kernel(place_ref, starts_ref, ahead_ref, parts_hbm, weight_hbm, out_ref, None, *scratch)


def projected(ahead, parts, starts, out_weight, axis):
    length = parts.shape[1]
    width = out_weight.shape[1]
    halves = lax.axis_size(axis) == 2
    vmem = pl.BlockSpec(memory_space=pltpu.VMEM)
    hbm = pl.BlockSpec(memory_space=pltpu.HBM)
    heads = starts.shape[0]
    groups = heads // (ahead.shape[0] * 2 // 3)
    here = lax.axis_index(axis).astype(jnp.int32).reshape(1)
    out = jax.ShapeDtypeStruct((length // 2 if halves else length, width), BF16)
    partial = pl.pallas_call(
        project_kernel if halves else whole_kernel,
        in_specs=[pl.BlockSpec(memory_space=pltpu.SMEM), vmem, vmem, hbm, hbm],
        out_specs=[vmem, vmem] if halves else vmem,
        out_shape=[out, out] if halves else out,
        scratch_shapes=[
            pltpu.VMEM(parts.shape, BF16),
            pltpu.VMEM(out_weight.shape, BF16),
            pltpu.VMEM((length, width), F32),
            pltpu.SemaphoreType.DMA((groups,)),
            pltpu.SemaphoreType.DMA((groups,)),
        ],
        compiler_params=in_vmem(50),
        name="project",
    )(here, starts, ahead, parts, out_weight)
    if not halves:
        return lax.psum_scatter(partial, axis, scatter_dimension=0, tiled=True)
    away, own = partial
    other = lax.ppermute(away, axis, [(0, 1), (1, 0)])
    return (own.astype(F32) + other.astype(F32)).astype(BF16)


def tails_kernel(value_hbm, query_hbm, key_hbm, out_ref, value_ref, query_ref, key_ref, sem):
    pairs = ((value_hbm, value_ref), (query_hbm, query_ref), (key_hbm, key_ref))
    copies = [
        pltpu.make_async_copy(source.at[pl.ds(source.shape[0] - 16, 16)], held, sem.at[i])
        for i, (source, held) in enumerate(pairs)
    ]
    for copy in copies:
        copy.start()
    at = 0
    for copy, (_, held) in zip(copies, pairs):
        copy.wait()
        width = held.shape[1]
        out_ref[:, at : at + width] = held[...].astype(F32)[13:16].astype(BF16)
        at += width


def tails(raws):
    order = (raws[2], raws[0], raws[1])
    width = sum(raw.shape[1] for raw in order)
    return pl.pallas_call(
        tails_kernel,
        in_specs=[pl.BlockSpec(memory_space=pltpu.HBM)] * 3,
        out_shape=jax.ShapeDtypeStruct((3, width), BF16),
        scratch_shapes=[pltpu.VMEM((16, raw.shape[1]), BF16) for raw in order]
        + [pltpu.SemaphoreType.DMA((3,))],
        compiler_params=in_vmem(60),
        name="tails",
    )(*order)


def shards(
    query_raw, key_raw, value_raw, gate_raw, query_taps, key_taps, value_taps,
    beta_logit, decay_logit, norm_gain, out_weight,
):
    raws = (query_raw, key_raw, value_raw)
    before = shifted(tails(raws), "seq", 1)
    pairs, local = local_steps(
        raws, before, (query_taps, key_taps, value_taps), beta_logit, decay_logit, gate_raw, norm_gain
    )
    starts, (ahead, parts) = starts_of(pairs, "seq", local)
    return projected(ahead, parts, starts, out_weight, "head")


def solution(mesh):
    placed = (
        P("seq", "head"), P("seq", "head"), P("seq", "head"), P("seq", "head"),
        P(None, "head"), P(None, "head"), P(None, "head"),
        P("seq", "head"), P("seq", "head"), P(), P("head", None),
    )
    return jax.shard_map(
        shards, mesh=mesh, in_specs=placed, out_specs=P(("seq", "head"), None), check_vma=False
    )
```

```python
import functools
import math

import jax
import jax.numpy as jnp
from jax import lax
from jax.experimental import pallas as pl
from jax.experimental.pallas import tpu as pltpu
from jax.sharding import PartitionSpec as P

DK = 128
DV = 128
CHUNK = 128
TINY = 8
SMALL = 32
GROUP = 8
HEADS_AT_ONCE = 4
EPSILON = 1e-06
F32 = jnp.float32
BF16 = jnp.bfloat16


def mul(left, right):
    return jnp.dot(left.astype(BF16), right.astype(BF16), preferred_element_type=F32)


def sigmoid(x):
    return 0.5 + 0.5 * jnp.tanh(0.5 * x)


def conv_silu(padded, first, rows, taps_ref, head, before=0):
    taps = taps_ref[:, pl.ds(pl.multiple_of((before + head) * DK, DK), DK)]
    summed = taps[0:1] * padded[head, first : first + rows, :]
    for offset in range(1, 4):
        summed = summed + taps[offset : offset + 1] * padded[head, first + offset : first + offset + rows, :]
    return summed * sigmoid(summed)


def widen(padded, first, rows, raw):
    for head in range(padded.shape[0]):
        padded[head, first : first + rows, :] = raw[:, head_of(head)].astype(F32)


def row_sums(values):
    return mul(values, jnp.ones((CHUNK, CHUNK), BF16))


def unit_rows(key):
    return key * lax.rsqrt(row_sums(key * key) + EPSILON)


def softplus(x):
    return jnp.maximum(x, 0.0) + jnp.log(1.0 + jnp.exp(-jnp.abs(x)))


def part_of(chunk):
    return slice(chunk * CHUNK, (chunk + 1) * CHUNK)


def head_of(head):
    return slice(head * DK, (head + 1) * DK)


def chunk_rows(ref, heads, chunks):
    held = ref.shape[0]
    first = (pl.program_id(0) * heads) % held
    rows = ref[:heads, :]
    for at in range(heads, held, heads):
        rows = jnp.where(first == at, ref[at : at + heads, :], rows)
    return jnp.concatenate([rows[:, part_of(c)] for c in chunks], 0)


def square_iotas(rows=CHUNK):
    return (
        lax.broadcasted_iota(jnp.int32, (rows, CHUNK), 0),
        lax.broadcasted_iota(jnp.int32, (rows, CHUNK), 1),
    )


def log_fades(logit):
    rows, cols = square_iotas()
    return jnp.dot(
        -softplus(logit), (rows <= cols).astype(F32), precision=lax.Precision.HIGHEST, preferred_element_type=F32
    )


def as_columns(blocks):
    rows = sum(block.shape[0] for block in blocks)
    return jnp.concatenate(list(blocks) + [jnp.zeros((CHUNK - rows, CHUNK), F32)], 0).T


def tiny_inverses(lower):
    lanes = lax.broadcasted_iota(jnp.int32, (TINY, CHUNK), 1)
    rows = lax.broadcasted_iota(jnp.int32, (TINY, CHUNK), 0)
    blocks = []
    for low in lower:
        block = low[:TINY]
        for at in range(1, CHUNK // TINY):
            block = jnp.where(lanes // TINY == at, low[at * TINY : (at + 1) * TINY], block)
        blocks.append(block)
    stacked = jnp.concatenate(blocks, 0)
    all_lanes = lax.broadcasted_iota(jnp.int32, stacked.shape, 1)
    factors = [
        jnp.take_along_axis(
            stacked, all_lanes // TINY * TINY + c, axis=1, mode="promise_in_bounds"
        )
        for c in range(TINY - 1)
    ]
    inverses = []
    for p in range(len(lower)):
        inverse = jnp.where(lanes % TINY == rows, 1.0, 0.0)
        for c in range(TINY - 1):
            inverse = inverse - factors[c][p * TINY : (p + 1) * TINY] * inverse[c : c + 1]
        inverses.append(inverse)
    return inverses


def solved_packs(fade, beta_logit, keys, key_cols, value_work, value_of):
    count = len(keys)
    stages = 6
    done = [0, 0]

    def between():
        done[1] += 1
        while done[0] < len(value_work) and done[0] * stages < len(value_work) * done[1]:
            value_work[done[0]]()
            done[0] += 1

    rows, cols = square_iotas()
    strict = rows > cols
    differ = rows ^ cols
    columns = as_columns((fade - softplus(-beta_logit),))
    beta = sigmoid(beta_logit)
    beta_grown = beta * jnp.exp(fade)
    inner = {}
    for key, turned in zip(keys, key_cols):
        if id(key) not in inner:
            inner[id(key)] = mul(key, turned)
    lower = []
    for p in range(count):
        gap = columns[:, p : p + 1] - fade[p : p + 1, :]
        lower.append(jnp.exp(jnp.where(strict, gap, -1e30)) * inner[id(keys[p])])

    small_rows, small_cols = square_iotas(SMALL)
    small_differ = small_rows ^ (small_cols % SMALL)
    place = small_cols // SMALL
    blocks = jnp.where(rows // SMALL == cols // SMALL, 1.0, 0.0)
    blocks16 = blocks.astype(BF16)

    def spread(small):
        return jnp.concatenate([small] * (CHUNK // SMALL), 0) * (blocks16 if small.dtype == BF16 else blocks)

    small = []
    for low in lower:
        held = low[:SMALL]
        for at in range(1, CHUNK // SMALL):
            held = jnp.where(place == at, low[at * SMALL : (at + 1) * SMALL], held)
        small.append(held)
    tiny_inverse = tiny_inverses(lower)
    held = (small_cols % SMALL) // TINY == small_rows // TINY
    inverse = [
        jnp.where(held, jnp.concatenate([one] * (SMALL // TINY), 0), 0.0) for one in tiny_inverse
    ]
    size = TINY
    while size < CHUNK:
        last = size == SMALL
        if last:
            band = (differ >= size) & (differ < 4 * size)
            inside = [jnp.where(band, low, 0.0).astype(BF16) for low in lower]
            inverse16 = [spread(one.astype(BF16)) for one in inverse]
            inverse = [spread(one) for one in inverse]
            wide16 = inverse16
        else:
            band = (small_differ >= size) & (small_differ < 4 * size)
            inside = [spread(jnp.where(band, one, 0.0).astype(BF16)) for one in small]
            inverse16 = [one.astype(BF16) for one in inverse]
            wide16 = [spread(one) for one in inverse16]
        between()
        step = [mul(inverse16[p], inside[p]).astype(BF16) for p in range(count)]
        between()
        both = [
            mul(step[p], jnp.concatenate([step[p] if last else spread(step[p]), wide16[p]], 1))
            for p in range(count)
        ]
        between()
        inverse = [inverse[p] - both[p][:, CHUNK:] for p in range(count)]
        partial = [inverse[p].astype(BF16) for p in range(count)]
        inverse = [
            inverse[p] + mul(both[p][:, :CHUNK], partial[p] if last else spread(partial[p]))
            for p in range(count)
        ]
        size *= 4

    return [
        jnp.concatenate(
            [
                mul(inverse[p] * beta[p : p + 1, :], value_of(p)),
                mul(inverse[p] * beta_grown[p : p + 1, :], keys[p]),
            ],
            1,
        )
        for p in range(count)
    ]


def later_kernel(
    key_ref, value_ref, key_taps, value_taps, beta_ref, decay_ref,
    solved_hbm, moves_hbm, key_padded, value_padded, solved_ref, moves_ref, sem,
):
    length = key_ref.shape[0]
    chunks = range(1, length // CHUNK)
    key_heads, heads = key_padded.shape[0], value_padded.shape[0]
    step = pl.program_id(0)
    repeat_by = heads // key_heads
    packs = [(chunk, head) for chunk in chunks for head in range(heads)]
    skip = CHUNK - 16
    count = length - CHUNK
    for padded, raw_ref in ((key_padded, key_ref), (value_padded, value_ref)):
        for head in range(padded.shape[0]):
            first = pl.multiple_of((step * padded.shape[0] + head) * DK, DK)
            padded[head] = raw_ref[skip:, pl.ds(first, DK)].astype(F32)
    key, turned = {}, {}
    for j in range(key_heads):
        unit = unit_rows(conv_silu(key_padded, 13, count, key_taps, j, step * key_heads))
        for head in range(j * repeat_by, (j + 1) * repeat_by):
            solved_ref[step * heads + head, :, DV + DK :] = unit.astype(BF16)
        for chunk in chunks:
            key[chunk, j] = unit[part_of(chunk - 1)]
            turned[chunk, j] = key[chunk, j].T
    value = {}

    def make_value(head):
        value[head] = conv_silu(value_padded, 13, count, value_taps, head, step * heads)

    def value_of(pack):
        chunk, head = packs[pack]
        return value[head][part_of(chunk - 1)]

    fade = log_fades(chunk_rows(decay_ref, heads, chunks))
    solved = solved_packs(
        fade,
        chunk_rows(beta_ref, heads, chunks),
        [key[chunk, head // repeat_by] for chunk, head in packs],
        [turned[chunk, head // repeat_by] for chunk, head in packs],
        [functools.partial(make_value, head) for head in range(heads)],
        value_of,
    )
    tail = jnp.exp(fade[:, CHUNK - 1 : CHUNK] - fade)

    def leaving(held, out, at_step, kind):
        here = pl.ds(at_step * heads, heads)
        return pltpu.make_async_copy(held.at[here], out.at[here], sem.at[kind, at_step])

    solved = [one.astype(BF16) for one in solved]
    for pack, (chunk, head) in enumerate(packs):
        solved_ref[step * heads + head, part_of(chunk - 1), : DV + DK] = solved[pack]
    leaving(solved_ref, solved_hbm, step, 0).start()
    for pack, (chunk, head) in enumerate(packs):
        moves_ref[step * heads + head, chunk - 1] = mul(
            turned[chunk, head // repeat_by] * tail[pack : pack + 1, :], solved[pack]
        ).astype(BF16)
    leaving(moves_ref, moves_hbm, step, 1).start()

    @pl.when(step == pl.num_programs(0) - 1)
    def _():
        for at_step in range(sem.shape[1]):
            leaving(solved_ref, solved_hbm, at_step, 0).wait()
            leaving(moves_ref, moves_hbm, at_step, 1).wait()


def states_kernel(
    key_ref, value_hbm, before_ref, key_taps, value_taps, beta_ref, decay_ref, moves_hbm,
    pairs_hbm, solved_hbm, starts_hbm,
    key_padded, value_padded, value_ref, moves_ref, solved_ref, starts_ref, pairs_ref,
    value_sem, in_sem, out_sem, pairs_sem,
):
    heads, length = decay_ref.shape
    chunks = length // CHUNK
    key_heads = key_ref.shape[1] // DK
    repeat_by = heads // key_heads
    value_copy = pltpu.make_async_copy(value_hbm.at[pl.ds(0, CHUNK)], value_ref, value_sem)
    value_copy.start()
    incoming = pltpu.make_async_copy(moves_hbm, moves_ref, in_sem)
    incoming.start()

    key_at = before_ref.shape[1] - key_ref.shape[1]
    widen(key_padded, 5, 3, before_ref[:, key_at:])
    widen(key_padded, 8, CHUNK, key_ref[:CHUNK, :])
    key, turned = [], []
    for j in range(key_heads):
        key.append(unit_rows(conv_silu(key_padded, 5, CHUNK, key_taps, j)))
        for head in range(j * repeat_by, (j + 1) * repeat_by):
            solved_ref[head, :, DV + DK :] = key[j].astype(BF16)
        turned.append(key[j].T)
    fade = log_fades(chunk_rows(decay_ref, heads, range(chunks)))
    value = {}

    def value_rows():
        value_copy.wait()
        widen(value_padded, 5, 3, before_ref[:, : value_ref.shape[1]])
        widen(value_padded, 8, CHUNK, value_ref[...])

    def make_value(head):
        value[head] = conv_silu(value_padded, 5, CHUNK, value_taps, head)

    solved = solved_packs(
        fade[:heads],
        beta_ref[:, :CHUNK],
        [key[head // repeat_by] for head in range(heads)],
        [turned[head // repeat_by] for head in range(heads)],
        [value_rows] + [functools.partial(make_value, head) for head in range(heads)],
        lambda head: value[head],
    )
    last = jnp.exp(fade[:, CHUNK - 1 : CHUNK])
    tail = jnp.exp(fade[:, CHUNK - 1 : CHUNK] - fade)
    rows, cols = square_iotas()
    identity = jnp.where(rows == cols, 1.0, 0.0)

    state = []
    for head in range(heads):
        one = solved[head].astype(BF16)
        solved_ref[head, :, : DV + DK] = one
        moved = mul(turned[head // repeat_by] * tail[head : head + 1, :], one)
        state.append(
            jnp.concatenate([moved[:, :DV], last[head : head + 1, :] * identity - moved[:, DV:]], 1)
        )
    each = min(HEADS_AT_ONCE, heads)
    outgoing = [pltpu.make_async_copy(solved_ref, solved_hbm, out_sem.at[0])]
    outgoing[0].start()
    incoming.wait()
    for chunk in range(1, chunks):
        for head in range(heads):
            pack = chunk * heads + head
            start = state[head].astype(BF16)
            starts_ref[chunk - 1, head] = start
            moves = moves_ref[head, chunk - 1]
            moved = last[pack : pack + 1, :] * state[head] - mul(moves[:, DV:], start)
            state[head] = jnp.concatenate([moved[:, :DV] + moves[:, :DV].astype(F32), moved[:, DV:]], 1)
            if chunk == chunks - 1:
                pairs_ref[head] = state[head].astype(BF16)
                if (head + 1) % each == 0:
                    done = pl.ds(head + 1 - each, each)
                    outgoing.append(
                        pltpu.make_async_copy(
                            pairs_ref.at[done], pairs_hbm.at[done], pairs_sem.at[head // each]
                        )
                    )
                    outgoing[-1].start()
        outgoing.append(
            pltpu.make_async_copy(
                starts_ref.at[chunk - 1], starts_hbm.at[chunk - 1], out_sem.at[chunk]
            )
        )
        outgoing[-1].start()
    for copy in outgoing:
        copy.wait()


def local_kernel(
    query_ref, query_before, query_taps, decay_ref,
    first_solved, later_solved, starts_ref, gate_ref, gain_ref,
    ahead_ref, parts_ref, padded,
):
    step = pl.program_id(0)
    length, width = query_ref.shape
    chunks = length // CHUNK
    key_heads = width // DK
    heads = first_solved.shape[0]
    repeat_by = heads // key_heads

    rows, cols = square_iotas()
    within = rows >= cols
    fade = log_fades(chunk_rows(decay_ref, heads, range(chunks)))
    columns = as_columns((fade,))
    widen(padded, 5, 3, query_before[...])
    widen(padded, 8, length, query_ref[...])
    query = [conv_silu(padded, 5, length, query_taps, j).astype(BF16) for j in range(key_heads)]
    for head in range(heads):
        gate = gate_ref[:, head_of(head)].astype(F32)
        parts_ref[heads + head // 2, :, head_of(head % 2)] = (
            gate * sigmoid(gate) * gain_ref[...]
        ).astype(BF16)
    for chunk in range(chunks):
        part = part_of(chunk)
        for j in range(key_heads):
            own = query[j][part]
            if chunk == 0:
                unit = first_solved[j * repeat_by, :, DV + DK :]
            else:
                unit = later_solved[j * repeat_by, part_of(chunk - 1), DV + DK :]
            inner = lax.dot_general(
                own, unit, (((1,), (1,)), ((), ())), preferred_element_type=F32
            )
            for head in range(j * repeat_by, (j + 1) * repeat_by):
                pack = chunk * heads + head
                column = jnp.broadcast_to(columns[:, pack : pack + 1], (CHUNK, CHUNK))
                scores = inner * jnp.exp(jnp.where(within, column - fade[pack : pack + 1, :], -1e30))
                grown = jnp.exp(column)
                if chunk == 0:
                    updates, wide = first_solved[head, :, :DV], first_solved[head, :, DV : DV + DK]
                    fresh = jnp.concatenate([updates, -wide], 1)
                    carried = jnp.concatenate(
                        [jnp.zeros((CHUNK, DV), F32), grown * own.astype(F32)], 1
                    )
                else:
                    solved = later_solved[head, part_of(chunk - 1), : DV + DK]
                    both = mul(jnp.concatenate([solved[:, DV:], own], 0), starts_ref[chunk - 1, head])
                    taken = both[:CHUNK]
                    fresh = jnp.concatenate(
                        [solved[:, :DV].astype(F32) - taken[:, :DV], -taken[:, DV:]], 1
                    )
                    carried = jnp.concatenate(
                        [grown * both[CHUNK:, :DV], grown * both[CHUNK:, DV:]], 1
                    )
                parts_ref[head, part, :] = (carried + mul(scores, fresh)).astype(BF16)

    @pl.when(step == 0)
    def _():
        ahead_ref[...] = parts_ref[...]


def columns_of(rows, width, first=0):
    return pl.BlockSpec((rows, width), lambda step: (0, step + first))


def in_vmem(mib):
    return pltpu.CompilerParams(vmem_limit_bytes=mib * 1024 * 1024)


def local_steps(raws, before, taps, beta_logit, decay_logit, gate_raw, norm_gain):
    length = raws[0].shape[0]
    key_heads = raws[0].shape[1] // DK
    value_heads = raws[2].shape[1] // DV
    repeat_by = value_heads // key_heads
    chunks = length // CHUNK
    beta, decay = beta_logit.T, decay_logit.T
    work = CHUNK * length * DV * value_heads
    hbm = pl.BlockSpec(memory_space=pltpu.HBM)
    vmem = pl.BlockSpec(memory_space=pltpu.VMEM)

    def split(each):
        heads = each * repeat_by
        held = max(heads, math.gcd(8, value_heads))
        of_heads = lambda *shape: pl.BlockSpec((heads,) + shape, lambda step: (step,) + (0,) * len(shape))
        logits = pl.BlockSpec((held, length), lambda step: (step * heads // held, 0))
        return key_heads // each, each * DK, heads * DV, of_heads, logits

    each = math.gcd(4, key_heads)
    steps, narrow, wide, of_heads, logits = split(each)
    later = length - CHUNK
    solved, moves = pl.pallas_call(
        later_kernel,
        grid=(steps,),
        in_specs=[
            vmem, vmem, vmem, vmem, vmem, vmem,
        ],
        out_specs=[hbm, hbm],
        out_shape=[
            jax.ShapeDtypeStruct((value_heads, later, DV + 2 * DK), BF16),
            jax.ShapeDtypeStruct((value_heads, chunks - 1, DK, DV + DK), BF16),
        ],
        scratch_shapes=[
            pltpu.VMEM((each, later + 16, DK), F32),
            pltpu.VMEM((each * repeat_by, later + 16, DV), F32),
            pltpu.VMEM((value_heads, later, DV + 2 * DK), BF16),
            pltpu.VMEM((value_heads, chunks - 1, DK, DV + DK), BF16),
            pltpu.SemaphoreType.DMA((2, steps)),
        ],
        compiler_params=in_vmem(50),
        cost_estimate=pl.CostEstimate(flops=30 * work, bytes_accessed=0, transcendentals=0),
        name="later",
    )(raws[1], raws[2], taps[1], taps[2], beta, decay)

    narrow, wide = key_heads * DK, value_heads * DV
    whole = lambda shape, *at: pl.BlockSpec(shape, lambda step: at or (0,) * len(shape))
    pairs, first_solved, starts = pl.pallas_call(
        states_kernel,
        grid=(1,),
        in_specs=[
            vmem, hbm, vmem, vmem, vmem, vmem, vmem, hbm,
        ],
        out_specs=[hbm, hbm, hbm],
        out_shape=[
            jax.ShapeDtypeStruct((value_heads, DK, DV + DK), BF16),
            jax.ShapeDtypeStruct((value_heads, CHUNK, DV + 2 * DK), BF16),
            jax.ShapeDtypeStruct((chunks - 1, value_heads, DK, DV + DK), BF16),
        ],
        scratch_shapes=[
            pltpu.VMEM((key_heads, 8 + CHUNK, DK), F32),
            pltpu.VMEM((value_heads, 8 + CHUNK, DV), F32),
            pltpu.VMEM((CHUNK, wide), BF16),
            pltpu.VMEM(moves.shape, BF16),
            pltpu.VMEM((value_heads, CHUNK, DV + 2 * DK), BF16),
            pltpu.VMEM((chunks - 1, value_heads, DK, DV + DK), BF16),
            pltpu.VMEM((value_heads, DK, DV + DK), BF16),
            pltpu.SemaphoreType.DMA,
            pltpu.SemaphoreType.DMA,
            pltpu.SemaphoreType.DMA((chunks,)),
            pltpu.SemaphoreType.DMA((value_heads // min(HEADS_AT_ONCE, value_heads),)),
        ],
        compiler_params=in_vmem(52),
        cost_estimate=pl.CostEstimate(flops=20 * work, bytes_accessed=0, transcendentals=0),
        name="states",
    )(raws[1], raws[2], before, taps[1], taps[2], beta, decay, moves)
    gain = norm_gain.reshape(1, DV)

    def local():
        steps, narrow, wide, of_heads, logits = split(math.gcd(2, key_heads))
        heads = wide // DV
        ahead = (heads + heads // 2, length, DV + DK)
        return pl.pallas_call(
            local_kernel,
            grid=(steps,),
            in_specs=[
                columns_of(length, narrow), columns_of(3, narrow, repeat_by * steps), columns_of(4, narrow),
                logits, of_heads(CHUNK, DV + 2 * DK), of_heads(later, DV + 2 * DK),
                pl.BlockSpec((chunks - 1, heads, DK, DV + DK), lambda step: (0, step, 0, 0)),
                columns_of(length, wide), whole(gain.shape),
            ],
            out_specs=[
                whole(ahead),
                pl.BlockSpec(ahead, lambda step: (jnp.maximum(step - 1, 0), 0, 0)),
            ],
            out_shape=[
                jax.ShapeDtypeStruct(ahead, BF16),
                jax.ShapeDtypeStruct((max(steps - 1, 1) * ahead[0],) + ahead[1:], BF16),
            ],
            scratch_shapes=[pltpu.VMEM((narrow // DK, 8 + length, DK), F32)],
            compiler_params=in_vmem(60),
            cost_estimate=pl.CostEstimate(flops=12 * work, bytes_accessed=0, transcendentals=0),
            name="local",
        )(
            raws[0], before, taps[0], decay, first_solved, solved, starts, gate_raw, gain,
        )

    return pairs, local


def prefix_kernel(pairs_ref, prefix_ref, total_ref):
    count, heads = pairs_ref.shape[:2]
    running = [None] * heads
    for hop in range(count):
        for head in range(heads):
            now = pairs_ref[hop, head]
            if hop == 0:
                rows = lax.broadcasted_iota(jnp.int32, (DK, DV + DK), 0)
                cols = lax.broadcasted_iota(jnp.int32, (DK, DV + DK), 1)
                prefix_ref[hop, head] = jnp.where(cols == rows + DV, 1.0, 0.0).astype(BF16)
                running[head] = now.astype(F32)
            else:
                before = running[head].astype(BF16)
                prefix_ref[hop, head] = before
                own = jnp.concatenate([now[:, :DV].astype(F32), jnp.zeros((DK, DK), F32)], 1)
                running[head] = own + mul(now[:, DV:], before)
    for head in range(heads):
        total_ref[head] = running[head][:, : total_ref.shape[2]].astype(BF16)


def apply_kernel(prefix_ref, start_ref, starts_ref):
    count, heads = prefix_ref.shape[:2]
    for hop in range(count):
        for head in range(heads):
            starts_ref[hop, head] = (
                prefix_ref[hop, head, :, :DV].astype(F32)
                + mul(prefix_ref[hop, head, :, DV:], start_ref[head])
            ).astype(BF16)


def shifted(value, axis, by):
    count = lax.axis_size(axis)
    return lax.ppermute(value, axis, [(i, i + by) for i in range(count - by)])


def group_start(total, axis, group):
    groups = lax.axis_size(axis) // group
    running = shifted(total, axis, group)
    by = 1
    while by < groups - 1:
        earlier = shifted(running, axis, by * group)
        product = jnp.einsum("bkl,blv->bkv", running[..., DV:], earlier, preferred_element_type=F32)
        own = jnp.pad(running[..., :DV], ((0, 0), (0, 0), (0, DK)))
        running = (product + own.astype(F32)).astype(BF16)
        by *= 2
    return running[..., :DV]


def starts_of(pairs, axis, beside):
    size = lax.axis_size(axis)
    heads = pairs.shape[0]
    group = math.gcd(math.gcd(size, heads), GROUP)
    groups = [[g * group + i for i in range(group)] for g in range(size // group)]
    each = heads // group
    wide = DV if size // group == 2 else DV + DK
    by_head = lax.all_to_all(pairs, axis, 0, 0, axis_index_groups=groups, tiled=True)
    by_head, done = lax.optimization_barrier((by_head, beside()))
    prefix, total = pl.pallas_call(
        prefix_kernel,
        out_shape=[
            jax.ShapeDtypeStruct((group, each, DK, DV + DK), BF16),
            jax.ShapeDtypeStruct((each, DK, wide), BF16),
        ],
        compiler_params=in_vmem(16),
        name="prefix",
    )(by_head.reshape(group, each, DK, DV + DK))
    starts = pl.pallas_call(
        apply_kernel,
        out_shape=jax.ShapeDtypeStruct((group, each, DK, DV), BF16),
        compiler_params=in_vmem(16),
        name="apply",
    )(prefix, group_start(total, axis, group))
    starts = lax.all_to_all(
        starts.reshape(heads, DK, DV), axis, 0, 0, axis_index_groups=groups, tiled=True
    )
    return starts, done


def project_kernel(
    place_ref, starts_ref, ahead_ref, parts_hbm, weight_hbm, away_ref, own_ref,
    parts_ref, weight_ref, total, parts_sem, weight_sem,
):
    heads = starts_ref.shape[0]
    entries, length = ahead_ref.shape[:2]
    each = entries * 2 // 3
    width = weight_ref.shape[1]
    block = min(512, width)
    groups = heads // each

    def parts(g):
        here = pl.ds((g - 1) * entries, entries)
        return pltpu.make_async_copy(parts_hbm.at[here], parts_ref.at[here], parts_sem.at[g])

    def weights(g):
        rows = pl.ds(g * each * DV, each * DV)
        return pltpu.make_async_copy(weight_hbm.at[rows], weight_ref.at[rows], weight_sem.at[g])

    def normed_group(g):
        normed = []
        for head in range(g * each, (g + 1) * each):
            held, at = (ahead_ref, head) if g == 0 else (parts_ref, (g - 1) * entries + head - g * each)
            core = held[at, :, :DV].astype(F32) + mul(held[at, :, DV:], starts_ref[head])
            scale = lax.rsqrt(jnp.mean(core * core, -1, keepdims=True) + EPSILON)
            gated = held[at - head % each + each + head % each // 2, :, head_of(head % 2)]
            normed.append((core * scale * gated.astype(F32)).astype(BF16))
        return jnp.concatenate(normed, 1)

    weights(0).start()
    if groups > 1:
        parts(1).start()
    following = normed_group(0)
    if groups > 1:
        weights(1).start()
    if groups > 2:
        parts(2).start()
    for g in range(groups):
        weights(g).wait()
        if g + 1 < groups:
            parts(g + 1).wait()
        if g + 2 < groups:
            weights(g + 2).start()
        if g + 3 < groups:
            parts(g + 3).start()
        normed = following
        if g + 1 < groups:
            following = normed_group(g + 1)
        for at in range(0, width, block):
            added = jnp.dot(
                normed, weight_ref[g * each * DV : (g + 1) * each * DV, at : at + block],
                preferred_element_type=F32,
            )
            if g > 0:
                added = added + total[:, at : at + block]
            if g < groups - 1:
                total[:, at : at + block] = added
            elif own_ref is None:
                away_ref[:, at : at + block] = added.astype(BF16)
            else:
                first = place_ref[0] == 0
                low, high = added[: length // 2], added[length // 2 :]
                own_ref[:, at : at + block] = jnp.where(first, low, high).astype(BF16)
                away_ref[:, at : at + block] = jnp.where(first, high, low).astype(BF16)


def whole_kernel(place_ref, starts_ref, ahead_ref, parts_hbm, weight_hbm, out_ref, *scratch):
    project_kernel(place_ref, starts_ref, ahead_ref, parts_hbm, weight_hbm, out_ref, None, *scratch)


def projected(ahead, parts, starts, out_weight, axis):
    length = parts.shape[1]
    width = out_weight.shape[1]
    halves = lax.axis_size(axis) == 2
    vmem = pl.BlockSpec(memory_space=pltpu.VMEM)
    hbm = pl.BlockSpec(memory_space=pltpu.HBM)
    heads = starts.shape[0]
    groups = heads // (ahead.shape[0] * 2 // 3)
    here = lax.axis_index(axis).astype(jnp.int32).reshape(1)
    out = jax.ShapeDtypeStruct((length // 2 if halves else length, width), BF16)
    partial = pl.pallas_call(
        project_kernel if halves else whole_kernel,
        in_specs=[pl.BlockSpec(memory_space=pltpu.SMEM), vmem, vmem, hbm, hbm],
        out_specs=[vmem, vmem] if halves else vmem,
        out_shape=[out, out] if halves else out,
        scratch_shapes=[
            pltpu.VMEM(parts.shape, BF16),
            pltpu.VMEM(out_weight.shape, BF16),
            pltpu.VMEM((length, width), F32),
            pltpu.SemaphoreType.DMA((groups,)),
            pltpu.SemaphoreType.DMA((groups,)),
        ],
        compiler_params=in_vmem(50),
        name="project",
    )(here, starts, ahead, parts, out_weight)
    if not halves:
        return lax.psum_scatter(partial, axis, scatter_dimension=0, tiled=True)
    away, own = partial
    other = lax.ppermute(away, axis, [(0, 1), (1, 0)])
    return (own.astype(F32) + other.astype(F32)).astype(BF16)


def tails_kernel(value_hbm, query_hbm, key_hbm, out_ref, value_ref, query_ref, key_ref, sem):
    pairs = ((value_hbm, value_ref), (query_hbm, query_ref), (key_hbm, key_ref))
    copies = [
        pltpu.make_async_copy(source.at[pl.ds(source.shape[0] - 16, 16)], held, sem.at[i])
        for i, (source, held) in enumerate(pairs)
    ]
    for copy in copies:
        copy.start()
    at = 0
    for copy, (_, held) in zip(copies, pairs):
        copy.wait()
        width = held.shape[1]
        out_ref[:, at : at + width] = held[...].astype(F32)[13:16].astype(BF16)
        at += width


def tails(raws):
    order = (raws[2], raws[0], raws[1])
    width = sum(raw.shape[1] for raw in order)
    return pl.pallas_call(
        tails_kernel,
        in_specs=[pl.BlockSpec(memory_space=pltpu.HBM)] * 3,
        out_shape=jax.ShapeDtypeStruct((3, width), BF16),
        scratch_shapes=[pltpu.VMEM((16, raw.shape[1]), BF16) for raw in order]
        + [pltpu.SemaphoreType.DMA((3,))],
        compiler_params=in_vmem(60),
        name="tails",
    )(*order)


def shards(
    query_raw, key_raw, value_raw, gate_raw, query_taps, key_taps, value_taps,
    beta_logit, decay_logit, norm_gain, out_weight,
):
    raws = (query_raw, key_raw, value_raw)
    before = shifted(tails(raws), "seq", 1)
    pairs, local = local_steps(
        raws, before, (query_taps, key_taps, value_taps), beta_logit, decay_logit, gate_raw, norm_gain
    )
    starts, (ahead, parts) = starts_of(pairs, "seq", local)
    return projected(ahead, parts, starts, out_weight, "head")


def solution(mesh):
    placed = (
        P("seq", "head"), P("seq", "head"), P("seq", "head"), P("seq", "head"),
        P(None, "head"), P(None, "head"), P(None, "head"),
        P("seq", "head"), P("seq", "head"), P(), P("head", None),
    )
    return jax.shard_map(
        shards, mesh=mesh, in_specs=placed, out_specs=P(("seq", "head"), None), check_vma=False
    )
```

```python
import functools
import math

import jax
import jax.numpy as jnp
from jax import lax
from jax.experimental import pallas as pl
from jax.experimental.pallas import tpu as pltpu
from jax.sharding import PartitionSpec as P

DK = 128
DV = 128
CHUNK = 128
TINY = 8
SMALL = 32
GROUP = 8
HEADS_AT_ONCE = 4
EPSILON = 1e-06
F32 = jnp.float32
BF16 = jnp.bfloat16


def mul(left, right):
    return jnp.dot(left.astype(BF16), right.astype(BF16), preferred_element_type=F32)


def sigmoid(x):
    return 0.5 + 0.5 * jnp.tanh(0.5 * x)


def conv_silu(padded, first, rows, taps_ref, head, before=0):
    taps = taps_ref[:, pl.ds(pl.multiple_of((before + head) * DK, DK), DK)]
    summed = taps[0:1] * padded[head, first : first + rows, :]
    for offset in range(1, 4):
        summed = summed + taps[offset : offset + 1] * padded[head, first + offset : first + offset + rows, :]
    return summed * sigmoid(summed)


def widen(padded, first, rows, raw):
    for head in range(padded.shape[0]):
        padded[head, first : first + rows, :] = raw[:, head_of(head)].astype(F32)


def row_sums(values):
    return mul(values, jnp.ones((CHUNK, CHUNK), BF16))


def unit_rows(key):
    return key * lax.rsqrt(row_sums(key * key) + EPSILON)


def softplus(x):
    return jnp.maximum(x, 0.0) + jnp.log(1.0 + jnp.exp(-jnp.abs(x)))


def part_of(chunk):
    return slice(chunk * CHUNK, (chunk + 1) * CHUNK)


def head_of(head):
    return slice(head * DK, (head + 1) * DK)


def chunk_rows(ref, heads, chunks):
    held = ref.shape[0]
    first = (pl.program_id(0) * heads) % held
    rows = ref[:heads, :]
    for at in range(heads, held, heads):
        rows = jnp.where(first == at, ref[at : at + heads, :], rows)
    return jnp.concatenate([rows[:, part_of(c)] for c in chunks], 0)


def square_iotas(rows=CHUNK):
    return (
        lax.broadcasted_iota(jnp.int32, (rows, CHUNK), 0),
        lax.broadcasted_iota(jnp.int32, (rows, CHUNK), 1),
    )


def log_fades(logit):
    rows, cols = square_iotas()
    return jnp.dot(
        -softplus(logit), (rows <= cols).astype(F32), precision=lax.Precision.HIGHEST, preferred_element_type=F32
    )


def as_columns(blocks):
    rows = sum(block.shape[0] for block in blocks)
    return jnp.concatenate(list(blocks) + [jnp.zeros((CHUNK - rows, CHUNK), F32)], 0).T


def tiny_inverses(lower):
    lanes = lax.broadcasted_iota(jnp.int32, (TINY, CHUNK), 1)
    rows = lax.broadcasted_iota(jnp.int32, (TINY, CHUNK), 0)
    blocks = []
    for low in lower:
        block = low[:TINY]
        for at in range(1, CHUNK // TINY):
            block = jnp.where(lanes // TINY == at, low[at * TINY : (at + 1) * TINY], block)
        blocks.append(block)
    stacked = jnp.concatenate(blocks, 0)
    all_lanes = lax.broadcasted_iota(jnp.int32, stacked.shape, 1)
    factors = [
        jnp.take_along_axis(
            stacked, all_lanes // TINY * TINY + c, axis=1, mode="promise_in_bounds"
        )
        for c in range(TINY - 1)
    ]
    inverses = []
    for p in range(len(lower)):
        inverse = jnp.where(lanes % TINY == rows, 1.0, 0.0)
        for c in range(TINY - 1):
            inverse = inverse - factors[c][p * TINY : (p + 1) * TINY] * inverse[c : c + 1]
        inverses.append(inverse)
    return inverses


def solved_packs(fade, beta_logit, keys, key_cols, value_work, value_of):
    count = len(keys)
    stages = 6
    done = [0, 0]

    def between():
        done[1] += 1
        while done[0] < len(value_work) and done[0] * stages < len(value_work) * done[1]:
            value_work[done[0]]()
            done[0] += 1

    rows, cols = square_iotas()
    strict = rows > cols
    differ = rows ^ cols
    columns = as_columns((fade - softplus(-beta_logit),))
    beta = sigmoid(beta_logit)
    beta_grown = beta * jnp.exp(fade)
    inner = {}
    for key, turned in zip(keys, key_cols):
        if id(key) not in inner:
            inner[id(key)] = mul(key, turned)
    lower = []
    for p in range(count):
        gap = columns[:, p : p + 1] - fade[p : p + 1, :]
        lower.append(jnp.exp(jnp.where(strict, gap, -1e30)) * inner[id(keys[p])])

    small_rows, small_cols = square_iotas(SMALL)
    small_differ = small_rows ^ (small_cols % SMALL)
    place = small_cols // SMALL
    blocks = jnp.where(rows // SMALL == cols // SMALL, 1.0, 0.0)
    blocks16 = blocks.astype(BF16)

    def spread(small):
        return jnp.concatenate([small] * (CHUNK // SMALL), 0) * (blocks16 if small.dtype == BF16 else blocks)

    small = []
    for low in lower:
        held = low[:SMALL]
        for at in range(1, CHUNK // SMALL):
            held = jnp.where(place == at, low[at * SMALL : (at + 1) * SMALL], held)
        small.append(held)
    tiny_inverse = tiny_inverses(lower)
    held = (small_cols % SMALL) // TINY == small_rows // TINY
    inverse = [
        jnp.where(held, jnp.concatenate([one] * (SMALL // TINY), 0), 0.0) for one in tiny_inverse
    ]
    size = TINY
    while size < CHUNK:
        last = size == SMALL
        if last:
            band = (differ >= size) & (differ < 4 * size)
            inside = [jnp.where(band, low, 0.0).astype(BF16) for low in lower]
            inverse16 = [spread(one.astype(BF16)) for one in inverse]
            inverse = [spread(one) for one in inverse]
            wide16 = inverse16
        else:
            band = (small_differ >= size) & (small_differ < 4 * size)
            inside = [spread(jnp.where(band, one, 0.0).astype(BF16)) for one in small]
            inverse16 = [one.astype(BF16) for one in inverse]
            wide16 = [spread(one) for one in inverse16]
        between()
        step = [mul(inverse16[p], inside[p]).astype(BF16) for p in range(count)]
        between()
        both = [
            mul(step[p], jnp.concatenate([step[p] if last else spread(step[p]), wide16[p]], 1))
            for p in range(count)
        ]
        between()
        inverse = [inverse[p] - both[p][:, CHUNK:] for p in range(count)]
        partial = [inverse[p].astype(BF16) for p in range(count)]
        inverse = [
            inverse[p] + mul(both[p][:, :CHUNK], partial[p] if last else spread(partial[p]))
            for p in range(count)
        ]
        size *= 4

    return [
        jnp.concatenate(
            [
                mul(inverse[p] * beta[p : p + 1, :], value_of(p)),
                mul(inverse[p] * beta_grown[p : p + 1, :], keys[p]),
            ],
            1,
        )
        for p in range(count)
    ]


def later_kernel(
    key_ref, value_ref, key_taps, value_taps, beta_ref, decay_ref,
    solved_hbm, moves_hbm, key_padded, value_padded, solved_ref, moves_ref, sem,
):
    length = key_ref.shape[0]
    chunks = range(1, length // CHUNK)
    key_heads, heads = key_padded.shape[0], value_padded.shape[0]
    step = pl.program_id(0)
    repeat_by = heads // key_heads
    packs = [(chunk, head) for chunk in chunks for head in range(heads)]
    skip = CHUNK - 16
    count = length - CHUNK
    for padded, raw_ref in ((key_padded, key_ref), (value_padded, value_ref)):
        for head in range(padded.shape[0]):
            first = pl.multiple_of((step * padded.shape[0] + head) * DK, DK)
            padded[head] = raw_ref[skip:, pl.ds(first, DK)].astype(F32)
    key, turned = {}, {}
    for j in range(key_heads):
        unit = unit_rows(conv_silu(key_padded, 13, count, key_taps, j, step * key_heads))
        for head in range(j * repeat_by, (j + 1) * repeat_by):
            solved_ref[step * heads + head, :, DV + DK :] = unit.astype(BF16)
        for chunk in chunks:
            key[chunk, j] = unit[part_of(chunk - 1)]
            turned[chunk, j] = key[chunk, j].T
    value = {}

    def make_value(head):
        value[head] = conv_silu(value_padded, 13, count, value_taps, head, step * heads)

    def value_of(pack):
        chunk, head = packs[pack]
        return value[head][part_of(chunk - 1)]

    fade = log_fades(chunk_rows(decay_ref, heads, chunks))
    solved = solved_packs(
        fade,
        chunk_rows(beta_ref, heads, chunks),
        [key[chunk, head // repeat_by] for chunk, head in packs],
        [turned[chunk, head // repeat_by] for chunk, head in packs],
        [functools.partial(make_value, head) for head in range(heads)],
        value_of,
    )
    tail = jnp.exp(fade[:, CHUNK - 1 : CHUNK] - fade)

    several = min(HEADS_AT_ONCE, heads)

    def leaving(held, out, group, kind):
        here = pl.ds(group * several, several)
        return pltpu.make_async_copy(held.at[here], out.at[here], sem.at[kind, group])

    for at in range(0, heads, several):
        group = (step * heads + at) // several
        own = [(pack, c, head) for pack, (c, head) in enumerate(packs) if at <= head < at + several]
        for pack, chunk, head in own:
            solved_ref[step * heads + head, part_of(chunk - 1), : DV + DK] = solved[pack].astype(BF16)
        leaving(solved_ref, solved_hbm, group, 0).start()
        for pack, chunk, head in own:
            moves_ref[step * heads + head, chunk - 1] = mul(
                turned[chunk, head // repeat_by] * tail[pack : pack + 1, :], solved[pack]
            ).astype(BF16)
        leaving(moves_ref, moves_hbm, group, 1).start()

    @pl.when(step == pl.num_programs(0) - 1)
    def _():
        for group in range(sem.shape[1]):
            leaving(solved_ref, solved_hbm, group, 0).wait()
            leaving(moves_ref, moves_hbm, group, 1).wait()


def states_kernel(
    key_ref, value_hbm, before_ref, key_taps, value_taps, beta_ref, decay_ref, moves_hbm,
    pairs_hbm, solved_hbm, starts_hbm,
    key_padded, value_padded, value_ref, moves_ref, solved_ref, starts_ref, pairs_ref,
    value_sem, in_sem, out_sem, pairs_sem,
):
    heads, length = decay_ref.shape
    chunks = length // CHUNK
    key_heads = key_ref.shape[1] // DK
    repeat_by = heads // key_heads
    value_copy = pltpu.make_async_copy(value_hbm.at[pl.ds(0, CHUNK)], value_ref, value_sem)
    value_copy.start()
    incoming = pltpu.make_async_copy(moves_hbm, moves_ref, in_sem)
    incoming.start()

    key_at = before_ref.shape[1] - key_ref.shape[1]
    widen(key_padded, 5, 3, before_ref[:, key_at:])
    widen(key_padded, 8, CHUNK, key_ref[:CHUNK, :])
    key, turned = [], []
    for j in range(key_heads):
        key.append(unit_rows(conv_silu(key_padded, 5, CHUNK, key_taps, j)))
        for head in range(j * repeat_by, (j + 1) * repeat_by):
            solved_ref[head, :, DV + DK :] = key[j].astype(BF16)
        turned.append(key[j].T)
    fade = log_fades(chunk_rows(decay_ref, heads, range(chunks)))
    value = {}

    def value_rows():
        value_copy.wait()
        widen(value_padded, 5, 3, before_ref[:, : value_ref.shape[1]])
        widen(value_padded, 8, CHUNK, value_ref[...])

    def make_value(head):
        value[head] = conv_silu(value_padded, 5, CHUNK, value_taps, head)

    solved = solved_packs(
        fade[:heads],
        beta_ref[:, :CHUNK],
        [key[head // repeat_by] for head in range(heads)],
        [turned[head // repeat_by] for head in range(heads)],
        [value_rows] + [functools.partial(make_value, head) for head in range(heads)],
        lambda head: value[head],
    )
    last = jnp.exp(fade[:, CHUNK - 1 : CHUNK])
    tail = jnp.exp(fade[:, CHUNK - 1 : CHUNK] - fade)
    rows, cols = square_iotas()
    identity = jnp.where(rows == cols, 1.0, 0.0)

    state = []
    for head in range(heads):
        one = solved[head].astype(BF16)
        solved_ref[head, :, : DV + DK] = one
        moved = mul(turned[head // repeat_by] * tail[head : head + 1, :], one)
        state.append(
            jnp.concatenate([moved[:, :DV], last[head : head + 1, :] * identity - moved[:, DV:]], 1)
        )
    each = min(HEADS_AT_ONCE, heads)
    outgoing = [pltpu.make_async_copy(solved_ref, solved_hbm, out_sem.at[0])]
    outgoing[0].start()
    incoming.wait()
    for chunk in range(1, chunks):
        for head in range(heads):
            pack = chunk * heads + head
            start = state[head].astype(BF16)
            starts_ref[chunk - 1, head] = start
            moves = moves_ref[head, chunk - 1]
            moved = last[pack : pack + 1, :] * state[head] - mul(moves[:, DV:], start)
            state[head] = jnp.concatenate([moved[:, :DV] + moves[:, :DV].astype(F32), moved[:, DV:]], 1)
            if chunk == chunks - 1:
                pairs_ref[head] = state[head].astype(BF16)
                if (head + 1) % each == 0:
                    done = pl.ds(head + 1 - each, each)
                    outgoing.append(
                        pltpu.make_async_copy(
                            pairs_ref.at[done], pairs_hbm.at[done], pairs_sem.at[head // each]
                        )
                    )
                    outgoing[-1].start()
        outgoing.append(
            pltpu.make_async_copy(
                starts_ref.at[chunk - 1], starts_hbm.at[chunk - 1], out_sem.at[chunk]
            )
        )
        outgoing[-1].start()
    for copy in outgoing:
        copy.wait()


def local_kernel(
    query_ref, query_before, query_taps, decay_ref,
    first_solved, later_solved, starts_ref, gate_ref, gain_ref,
    ahead_ref, parts_ref, padded,
):
    step = pl.program_id(0)
    length, width = query_ref.shape
    chunks = length // CHUNK
    key_heads = width // DK
    heads = first_solved.shape[0]
    repeat_by = heads // key_heads

    rows, cols = square_iotas()
    within = rows >= cols
    fade = log_fades(chunk_rows(decay_ref, heads, range(chunks)))
    columns = as_columns((fade,))
    widen(padded, 5, 3, query_before[...])
    widen(padded, 8, length, query_ref[...])
    query = [conv_silu(padded, 5, length, query_taps, j).astype(BF16) for j in range(key_heads)]
    for head in range(heads):
        gate = gate_ref[:, head_of(head)].astype(F32)
        parts_ref[heads + head // 2, :, head_of(head % 2)] = (
            gate * sigmoid(gate) * gain_ref[...]
        ).astype(BF16)
    for chunk in range(chunks):
        part = part_of(chunk)
        for j in range(key_heads):
            own = query[j][part]
            if chunk == 0:
                unit = first_solved[j * repeat_by, :, DV + DK :]
            else:
                unit = later_solved[j * repeat_by, part_of(chunk - 1), DV + DK :]
            inner = lax.dot_general(
                own, unit, (((1,), (1,)), ((), ())), preferred_element_type=F32
            )
            for head in range(j * repeat_by, (j + 1) * repeat_by):
                pack = chunk * heads + head
                column = jnp.broadcast_to(columns[:, pack : pack + 1], (CHUNK, CHUNK))
                scores = inner * jnp.exp(jnp.where(within, column - fade[pack : pack + 1, :], -1e30))
                grown = jnp.exp(column)
                if chunk == 0:
                    updates, wide = first_solved[head, :, :DV], first_solved[head, :, DV : DV + DK]
                    fresh = jnp.concatenate([updates, -wide], 1)
                    carried = jnp.concatenate(
                        [jnp.zeros((CHUNK, DV), F32), grown * own.astype(F32)], 1
                    )
                else:
                    solved = later_solved[head, part_of(chunk - 1), : DV + DK]
                    both = mul(jnp.concatenate([solved[:, DV:], own], 0), starts_ref[chunk - 1, head])
                    taken = both[:CHUNK]
                    fresh = jnp.concatenate(
                        [solved[:, :DV].astype(F32) - taken[:, :DV], -taken[:, DV:]], 1
                    )
                    carried = jnp.concatenate(
                        [grown * both[CHUNK:, :DV], grown * both[CHUNK:, DV:]], 1
                    )
                parts_ref[head, part, :] = (carried + mul(scores, fresh)).astype(BF16)

    @pl.when(step == 0)
    def _():
        ahead_ref[...] = parts_ref[...]


def columns_of(rows, width, first=0):
    return pl.BlockSpec((rows, width), lambda step: (0, step + first))


def in_vmem(mib):
    return pltpu.CompilerParams(vmem_limit_bytes=mib * 1024 * 1024)


def local_steps(raws, before, taps, beta_logit, decay_logit, gate_raw, norm_gain):
    length = raws[0].shape[0]
    key_heads = raws[0].shape[1] // DK
    value_heads = raws[2].shape[1] // DV
    repeat_by = value_heads // key_heads
    chunks = length // CHUNK
    beta, decay = beta_logit.T, decay_logit.T
    work = CHUNK * length * DV * value_heads
    hbm = pl.BlockSpec(memory_space=pltpu.HBM)
    vmem = pl.BlockSpec(memory_space=pltpu.VMEM)

    def split(each):
        heads = each * repeat_by
        held = max(heads, math.gcd(8, value_heads))
        of_heads = lambda *shape: pl.BlockSpec((heads,) + shape, lambda step: (step,) + (0,) * len(shape))
        logits = pl.BlockSpec((held, length), lambda step: (step * heads // held, 0))
        return key_heads // each, each * DK, heads * DV, of_heads, logits

    each = math.gcd(8, key_heads)
    steps, narrow, wide, of_heads, logits = split(each)
    later = length - CHUNK
    solved, moves = pl.pallas_call(
        later_kernel,
        grid=(steps,),
        in_specs=[
            vmem, vmem, vmem, vmem, vmem, vmem,
        ],
        out_specs=[hbm, hbm],
        out_shape=[
            jax.ShapeDtypeStruct((value_heads, later, DV + 2 * DK), BF16),
            jax.ShapeDtypeStruct((value_heads, chunks - 1, DK, DV + DK), BF16),
        ],
        scratch_shapes=[
            pltpu.VMEM((each, later + 16, DK), F32),
            pltpu.VMEM((each * repeat_by, later + 16, DV), F32),
            pltpu.VMEM((value_heads, later, DV + 2 * DK), BF16),
            pltpu.VMEM((value_heads, chunks - 1, DK, DV + DK), BF16),
            pltpu.SemaphoreType.DMA((2, value_heads // min(HEADS_AT_ONCE, wide // DV))),
        ],
        compiler_params=in_vmem(50),
        cost_estimate=pl.CostEstimate(flops=30 * work, bytes_accessed=0, transcendentals=0),
        name="later",
    )(raws[1], raws[2], taps[1], taps[2], beta, decay)

    narrow, wide = key_heads * DK, value_heads * DV
    whole = lambda shape, *at: pl.BlockSpec(shape, lambda step: at or (0,) * len(shape))
    pairs, first_solved, starts = pl.pallas_call(
        states_kernel,
        grid=(1,),
        in_specs=[
            vmem, hbm, vmem, vmem, vmem, vmem, vmem, hbm,
        ],
        out_specs=[hbm, hbm, hbm],
        out_shape=[
            jax.ShapeDtypeStruct((value_heads, DK, DV + DK), BF16),
            jax.ShapeDtypeStruct((value_heads, CHUNK, DV + 2 * DK), BF16),
            jax.ShapeDtypeStruct((chunks - 1, value_heads, DK, DV + DK), BF16),
        ],
        scratch_shapes=[
            pltpu.VMEM((key_heads, 8 + CHUNK, DK), F32),
            pltpu.VMEM((value_heads, 8 + CHUNK, DV), F32),
            pltpu.VMEM((CHUNK, wide), BF16),
            pltpu.VMEM(moves.shape, BF16),
            pltpu.VMEM((value_heads, CHUNK, DV + 2 * DK), BF16),
            pltpu.VMEM((chunks - 1, value_heads, DK, DV + DK), BF16),
            pltpu.VMEM((value_heads, DK, DV + DK), BF16),
            pltpu.SemaphoreType.DMA,
            pltpu.SemaphoreType.DMA,
            pltpu.SemaphoreType.DMA((chunks,)),
            pltpu.SemaphoreType.DMA((value_heads // min(HEADS_AT_ONCE, value_heads),)),
        ],
        compiler_params=in_vmem(52),
        cost_estimate=pl.CostEstimate(flops=20 * work, bytes_accessed=0, transcendentals=0),
        name="states",
    )(raws[1], raws[2], before, taps[1], taps[2], beta, decay, moves)
    gain = norm_gain.reshape(1, DV)

    def local():
        steps, narrow, wide, of_heads, logits = split(math.gcd(2, key_heads))
        heads = wide // DV
        ahead = (heads + heads // 2, length, DV + DK)
        return pl.pallas_call(
            local_kernel,
            grid=(steps,),
            in_specs=[
                columns_of(length, narrow), columns_of(3, narrow, repeat_by * steps), columns_of(4, narrow),
                logits, of_heads(CHUNK, DV + 2 * DK), of_heads(later, DV + 2 * DK),
                pl.BlockSpec((chunks - 1, heads, DK, DV + DK), lambda step: (0, step, 0, 0)),
                columns_of(length, wide), whole(gain.shape),
            ],
            out_specs=[
                whole(ahead),
                pl.BlockSpec(ahead, lambda step: (jnp.maximum(step - 1, 0), 0, 0)),
            ],
            out_shape=[
                jax.ShapeDtypeStruct(ahead, BF16),
                jax.ShapeDtypeStruct((max(steps - 1, 1) * ahead[0],) + ahead[1:], BF16),
            ],
            scratch_shapes=[pltpu.VMEM((narrow // DK, 8 + length, DK), F32)],
            compiler_params=in_vmem(60),
            cost_estimate=pl.CostEstimate(flops=12 * work, bytes_accessed=0, transcendentals=0),
            name="local",
        )(
            raws[0], before, taps[0], decay, first_solved, solved, starts, gate_raw, gain,
        )

    return pairs, local


def prefix_kernel(pairs_ref, prefix_ref, total_ref):
    count, heads = pairs_ref.shape[:2]
    running = [None] * heads
    for hop in range(count):
        for head in range(heads):
            now = pairs_ref[hop, head]
            if hop == 0:
                rows = lax.broadcasted_iota(jnp.int32, (DK, DV + DK), 0)
                cols = lax.broadcasted_iota(jnp.int32, (DK, DV + DK), 1)
                prefix_ref[hop, head] = jnp.where(cols == rows + DV, 1.0, 0.0).astype(BF16)
                running[head] = now.astype(F32)
            else:
                before = running[head].astype(BF16)
                prefix_ref[hop, head] = before
                own = jnp.concatenate([now[:, :DV].astype(F32), jnp.zeros((DK, DK), F32)], 1)
                running[head] = own + mul(now[:, DV:], before)
    for head in range(heads):
        total_ref[head] = running[head][:, : total_ref.shape[2]].astype(BF16)


def apply_kernel(prefix_ref, start_ref, starts_ref):
    count, heads = prefix_ref.shape[:2]
    for hop in range(count):
        for head in range(heads):
            starts_ref[hop, head] = (
                prefix_ref[hop, head, :, :DV].astype(F32)
                + mul(prefix_ref[hop, head, :, DV:], start_ref[head])
            ).astype(BF16)


def shifted(value, axis, by):
    count = lax.axis_size(axis)
    return lax.ppermute(value, axis, [(i, i + by) for i in range(count - by)])


def group_start(total, axis, group):
    groups = lax.axis_size(axis) // group
    running = shifted(total, axis, group)
    by = 1
    while by < groups - 1:
        earlier = shifted(running, axis, by * group)
        product = jnp.einsum("bkl,blv->bkv", running[..., DV:], earlier, preferred_element_type=F32)
        own = jnp.pad(running[..., :DV], ((0, 0), (0, 0), (0, DK)))
        running = (product + own.astype(F32)).astype(BF16)
        by *= 2
    return running[..., :DV]


def starts_of(pairs, axis, beside):
    size = lax.axis_size(axis)
    heads = pairs.shape[0]
    group = math.gcd(math.gcd(size, heads), GROUP)
    groups = [[g * group + i for i in range(group)] for g in range(size // group)]
    each = heads // group
    wide = DV if size // group == 2 else DV + DK
    by_head = lax.all_to_all(pairs, axis, 0, 0, axis_index_groups=groups, tiled=True)
    by_head, done = lax.optimization_barrier((by_head, beside()))
    prefix, total = pl.pallas_call(
        prefix_kernel,
        out_shape=[
            jax.ShapeDtypeStruct((group, each, DK, DV + DK), BF16),
            jax.ShapeDtypeStruct((each, DK, wide), BF16),
        ],
        compiler_params=in_vmem(16),
        name="prefix",
    )(by_head.reshape(group, each, DK, DV + DK))
    starts = pl.pallas_call(
        apply_kernel,
        out_shape=jax.ShapeDtypeStruct((group, each, DK, DV), BF16),
        compiler_params=in_vmem(16),
        name="apply",
    )(prefix, group_start(total, axis, group))
    starts = lax.all_to_all(
        starts.reshape(heads, DK, DV), axis, 0, 0, axis_index_groups=groups, tiled=True
    )
    return starts, done


def project_kernel(
    place_ref, starts_ref, ahead_ref, parts_hbm, weight_hbm, away_ref, own_ref,
    parts_ref, weight_ref, total, parts_sem, weight_sem,
):
    heads = starts_ref.shape[0]
    entries, length = ahead_ref.shape[:2]
    each = entries * 2 // 3
    width = weight_ref.shape[1]
    block = min(512, width)
    groups = heads // each

    def parts(g):
        here = pl.ds((g - 1) * entries, entries)
        return pltpu.make_async_copy(parts_hbm.at[here], parts_ref.at[here], parts_sem.at[g])

    def weights(g):
        rows = pl.ds(g * each * DV, each * DV)
        return pltpu.make_async_copy(weight_hbm.at[rows], weight_ref.at[rows], weight_sem.at[g])

    def normed_group(g):
        normed = []
        for head in range(g * each, (g + 1) * each):
            held, at = (ahead_ref, head) if g == 0 else (parts_ref, (g - 1) * entries + head - g * each)
            core = held[at, :, :DV].astype(F32) + mul(held[at, :, DV:], starts_ref[head])
            scale = lax.rsqrt(jnp.mean(core * core, -1, keepdims=True) + EPSILON)
            gated = held[at - head % each + each + head % each // 2, :, head_of(head % 2)]
            normed.append((core * scale * gated.astype(F32)).astype(BF16))
        return jnp.concatenate(normed, 1)

    weights(0).start()
    if groups > 1:
        parts(1).start()
    following = normed_group(0)
    if groups > 1:
        weights(1).start()
    if groups > 2:
        parts(2).start()
    for g in range(groups):
        weights(g).wait()
        if g + 1 < groups:
            parts(g + 1).wait()
        if g + 2 < groups:
            weights(g + 2).start()
        if g + 3 < groups:
            parts(g + 3).start()
        normed = following
        if g + 1 < groups:
            following = normed_group(g + 1)
        for at in range(0, width, block):
            added = jnp.dot(
                normed, weight_ref[g * each * DV : (g + 1) * each * DV, at : at + block],
                preferred_element_type=F32,
            )
            if g > 0:
                added = added + total[:, at : at + block]
            if g < groups - 1:
                total[:, at : at + block] = added
            elif own_ref is None:
                away_ref[:, at : at + block] = added.astype(BF16)
            else:
                first = place_ref[0] == 0
                low, high = added[: length // 2], added[length // 2 :]
                own_ref[:, at : at + block] = jnp.where(first, low, high).astype(BF16)
                away_ref[:, at : at + block] = jnp.where(first, high, low).astype(BF16)


def whole_kernel(place_ref, starts_ref, ahead_ref, parts_hbm, weight_hbm, out_ref, *scratch):
    project_kernel(place_ref, starts_ref, ahead_ref, parts_hbm, weight_hbm, out_ref, None, *scratch)


def projected(ahead, parts, starts, out_weight, axis):
    length = parts.shape[1]
    width = out_weight.shape[1]
    halves = lax.axis_size(axis) == 2
    vmem = pl.BlockSpec(memory_space=pltpu.VMEM)
    hbm = pl.BlockSpec(memory_space=pltpu.HBM)
    heads = starts.shape[0]
    groups = heads // (ahead.shape[0] * 2 // 3)
    here = lax.axis_index(axis).astype(jnp.int32).reshape(1)
    out = jax.ShapeDtypeStruct((length // 2 if halves else length, width), BF16)
    partial = pl.pallas_call(
        project_kernel if halves else whole_kernel,
        in_specs=[pl.BlockSpec(memory_space=pltpu.SMEM), vmem, vmem, hbm, hbm],
        out_specs=[vmem, vmem] if halves else vmem,
        out_shape=[out, out] if halves else out,
        scratch_shapes=[
            pltpu.VMEM(parts.shape, BF16),
            pltpu.VMEM(out_weight.shape, BF16),
            pltpu.VMEM((length, width), F32),
            pltpu.SemaphoreType.DMA((groups,)),
            pltpu.SemaphoreType.DMA((groups,)),
        ],
        compiler_params=in_vmem(50),
        name="project",
    )(here, starts, ahead, parts, out_weight)
    if not halves:
        return lax.psum_scatter(partial, axis, scatter_dimension=0, tiled=True)
    away, own = partial
    other = lax.ppermute(away, axis, [(0, 1), (1, 0)])
    return (own.astype(F32) + other.astype(F32)).astype(BF16)


def tails_kernel(value_hbm, query_hbm, key_hbm, out_ref, value_ref, query_ref, key_ref, sem):
    pairs = ((value_hbm, value_ref), (query_hbm, query_ref), (key_hbm, key_ref))
    copies = [
        pltpu.make_async_copy(source.at[pl.ds(source.shape[0] - 16, 16)], held, sem.at[i])
        for i, (source, held) in enumerate(pairs)
    ]
    for copy in copies:
        copy.start()
    at = 0
    for copy, (_, held) in zip(copies, pairs):
        copy.wait()
        width = held.shape[1]
        out_ref[:, at : at + width] = held[...].astype(F32)[13:16].astype(BF16)
        at += width


def tails(raws):
    order = (raws[2], raws[0], raws[1])
    width = sum(raw.shape[1] for raw in order)
    return pl.pallas_call(
        tails_kernel,
        in_specs=[pl.BlockSpec(memory_space=pltpu.HBM)] * 3,
        out_shape=jax.ShapeDtypeStruct((3, width), BF16),
        scratch_shapes=[pltpu.VMEM((16, raw.shape[1]), BF16) for raw in order]
        + [pltpu.SemaphoreType.DMA((3,))],
        compiler_params=in_vmem(60),
        name="tails",
    )(*order)


def shards(
    query_raw, key_raw, value_raw, gate_raw, query_taps, key_taps, value_taps,
    beta_logit, decay_logit, norm_gain, out_weight,
):
    raws = (query_raw, key_raw, value_raw)
    before = shifted(tails(raws), "seq", 1)
    pairs, local = local_steps(
        raws, before, (query_taps, key_taps, value_taps), beta_logit, decay_logit, gate_raw, norm_gain
    )
    starts, (ahead, parts) = starts_of(pairs, "seq", local)
    return projected(ahead, parts, starts, out_weight, "head")


def solution(mesh):
    placed = (
        P("seq", "head"), P("seq", "head"), P("seq", "head"), P("seq", "head"),
        P(None, "head"), P(None, "head"), P(None, "head"),
        P("seq", "head"), P("seq", "head"), P(), P("head", None),
    )
    return jax.shard_map(
        shards, mesh=mesh, in_specs=placed, out_specs=P(("seq", "head"), None), check_vma=False
    )
```

```python
import functools
import math

import jax
import jax.numpy as jnp
from jax import lax
from jax.experimental import pallas as pl
from jax.experimental.pallas import tpu as pltpu
from jax.sharding import PartitionSpec as P

DK = 128
DV = 128
CHUNK = 128
TINY = 8
SMALL = 32
GROUP = 8
HEADS_AT_ONCE = 4
EPSILON = 1e-06
F32 = jnp.float32
BF16 = jnp.bfloat16


def mul(left, right):
    return jnp.dot(left.astype(BF16), right.astype(BF16), preferred_element_type=F32)


def sigmoid(x):
    return 0.5 + 0.5 * jnp.tanh(0.5 * x)


def conv_silu(padded, first, rows, taps_ref, head, before=0):
    taps = taps_ref[:, pl.ds(pl.multiple_of((before + head) * DK, DK), DK)]
    summed = taps[0:1] * padded[head, first : first + rows, :]
    for offset in range(1, 4):
        summed = summed + taps[offset : offset + 1] * padded[head, first + offset : first + offset + rows, :]
    return summed * sigmoid(summed)


def widen(padded, first, rows, raw):
    for head in range(padded.shape[0]):
        padded[head, first : first + rows, :] = raw[:, head_of(head)].astype(F32)


def row_sums(values):
    return mul(values, jnp.ones((CHUNK, CHUNK), BF16))


def unit_rows(key):
    return key * lax.rsqrt(row_sums(key * key) + EPSILON)


def softplus(x):
    return jnp.maximum(x, 0.0) + jnp.log(1.0 + jnp.exp(-jnp.abs(x)))


def part_of(chunk):
    return slice(chunk * CHUNK, (chunk + 1) * CHUNK)


def head_of(head):
    return slice(head * DK, (head + 1) * DK)


def chunk_rows(ref, heads, chunks):
    held = ref.shape[0]
    first = (pl.program_id(0) * heads) % held
    rows = ref[:heads, :]
    for at in range(heads, held, heads):
        rows = jnp.where(first == at, ref[at : at + heads, :], rows)
    return jnp.concatenate([rows[:, part_of(c)] for c in chunks], 0)


def square_iotas(rows=CHUNK):
    return (
        lax.broadcasted_iota(jnp.int32, (rows, CHUNK), 0),
        lax.broadcasted_iota(jnp.int32, (rows, CHUNK), 1),
    )


def log_fades(logit):
    rows, cols = square_iotas()
    return jnp.dot(
        -softplus(logit), (rows <= cols).astype(F32), precision=lax.Precision.HIGHEST, preferred_element_type=F32
    )


def as_columns(blocks):
    rows = sum(block.shape[0] for block in blocks)
    return jnp.concatenate(list(blocks) + [jnp.zeros((CHUNK - rows, CHUNK), F32)], 0).T


def tiny_inverses(lower):
    lanes = lax.broadcasted_iota(jnp.int32, (TINY, CHUNK), 1)
    rows = lax.broadcasted_iota(jnp.int32, (TINY, CHUNK), 0)
    blocks = []
    for low in lower:
        block = low[:TINY]
        for at in range(1, CHUNK // TINY):
            block = jnp.where(lanes // TINY == at, low[at * TINY : (at + 1) * TINY], block)
        blocks.append(block)
    stacked = jnp.concatenate(blocks, 0)
    all_lanes = lax.broadcasted_iota(jnp.int32, stacked.shape, 1)
    factors = [
        jnp.take_along_axis(
            stacked, all_lanes // TINY * TINY + c, axis=1, mode="promise_in_bounds"
        )
        for c in range(TINY - 1)
    ]
    inverses = []
    for p in range(len(lower)):
        inverse = jnp.where(lanes % TINY == rows, 1.0, 0.0)
        for c in range(TINY - 1):
            inverse = inverse - factors[c][p * TINY : (p + 1) * TINY] * inverse[c : c + 1]
        inverses.append(inverse)
    return inverses


def solved_packs(fade, beta_logit, keys, key_cols, value_work, value_of):
    count = len(keys)
    stages = 6
    done = [0, 0]

    def between():
        done[1] += 1
        while done[0] < len(value_work) and done[0] * stages < len(value_work) * done[1]:
            value_work[done[0]]()
            done[0] += 1

    rows, cols = square_iotas()
    strict = rows > cols
    differ = rows ^ cols
    columns = as_columns((fade - softplus(-beta_logit),))
    beta = sigmoid(beta_logit)
    beta_grown = beta * jnp.exp(fade)
    inner = {}
    for key, turned in zip(keys, key_cols):
        if id(key) not in inner:
            inner[id(key)] = mul(key, turned)
    lower = []
    for p in range(count):
        gap = columns[:, p : p + 1] - fade[p : p + 1, :]
        lower.append(jnp.exp(jnp.where(strict, gap, -1e30)) * inner[id(keys[p])])

    small_rows, small_cols = square_iotas(SMALL)
    small_differ = small_rows ^ (small_cols % SMALL)
    place = small_cols // SMALL
    blocks = jnp.where(rows // SMALL == cols // SMALL, 1.0, 0.0)
    blocks16 = blocks.astype(BF16)

    def spread(small):
        return jnp.concatenate([small] * (CHUNK // SMALL), 0) * (blocks16 if small.dtype == BF16 else blocks)

    small = []
    for low in lower:
        held = low[:SMALL]
        for at in range(1, CHUNK // SMALL):
            held = jnp.where(place == at, low[at * SMALL : (at + 1) * SMALL], held)
        small.append(held)
    tiny_inverse = tiny_inverses(lower)
    held = (small_cols % SMALL) // TINY == small_rows // TINY
    inverse = [
        jnp.where(held, jnp.concatenate([one] * (SMALL // TINY), 0), 0.0) for one in tiny_inverse
    ]
    size = TINY
    while size < CHUNK:
        last = size == SMALL
        if last:
            band = (differ >= size) & (differ < 4 * size)
            inside = [jnp.where(band, low, 0.0).astype(BF16) for low in lower]
            inverse16 = [spread(one.astype(BF16)) for one in inverse]
            inverse = [spread(one) for one in inverse]
            wide16 = inverse16
        else:
            band = (small_differ >= size) & (small_differ < 4 * size)
            inside = [spread(jnp.where(band, one, 0.0).astype(BF16)) for one in small]
            inverse16 = [one.astype(BF16) for one in inverse]
            wide16 = [spread(one) for one in inverse16]
        between()
        step = [mul(inverse16[p], inside[p]).astype(BF16) for p in range(count)]
        between()
        both = [
            mul(step[p], jnp.concatenate([step[p] if last else spread(step[p]), wide16[p]], 1))
            for p in range(count)
        ]
        between()
        inverse = [inverse[p] - both[p][:, CHUNK:] for p in range(count)]
        partial = [inverse[p].astype(BF16) for p in range(count)]
        inverse = [
            inverse[p] + mul(both[p][:, :CHUNK], partial[p] if last else spread(partial[p]))
            for p in range(count)
        ]
        size *= 4

    return [
        jnp.concatenate(
            [
                mul(inverse[p] * beta[p : p + 1, :], value_of(p)),
                mul(inverse[p] * beta_grown[p : p + 1, :], keys[p]),
            ],
            1,
        )
        for p in range(count)
    ]


def later_kernel(
    key_ref, value_ref, key_taps, value_taps, beta_ref, decay_ref,
    solved_hbm, moves_hbm, key_padded, value_padded, solved_ref, moves_ref, sem,
):
    length = key_ref.shape[0]
    chunks = range(1, length // CHUNK)
    key_heads, heads = key_padded.shape[0], value_padded.shape[0]
    step = pl.program_id(0)
    repeat_by = heads // key_heads
    packs = [(chunk, head) for chunk in chunks for head in range(heads)]
    skip = CHUNK - 16
    count = length - CHUNK
    for padded, raw_ref in ((key_padded, key_ref), (value_padded, value_ref)):
        for head in range(padded.shape[0]):
            first = pl.multiple_of((step * padded.shape[0] + head) * DK, DK)
            padded[head] = raw_ref[skip:, pl.ds(first, DK)].astype(F32)
    key, turned = {}, {}
    for j in range(key_heads):
        unit = unit_rows(conv_silu(key_padded, 13, count, key_taps, j, step * key_heads))
        for head in range(j * repeat_by, (j + 1) * repeat_by):
            solved_ref[step * heads + head, :, DV + DK :] = unit.astype(BF16)
        for chunk in chunks:
            key[chunk, j] = unit[part_of(chunk - 1)]
            turned[chunk, j] = key[chunk, j].T
    value = {}

    def make_value(head):
        value[head] = conv_silu(value_padded, 13, count, value_taps, head, step * heads)

    def value_of(pack):
        chunk, head = packs[pack]
        return value[head][part_of(chunk - 1)]

    fade = log_fades(chunk_rows(decay_ref, heads, chunks))
    solved = solved_packs(
        fade,
        chunk_rows(beta_ref, heads, chunks),
        [key[chunk, head // repeat_by] for chunk, head in packs],
        [turned[chunk, head // repeat_by] for chunk, head in packs],
        [functools.partial(make_value, head) for head in range(heads)],
        value_of,
    )
    tail = jnp.exp(fade[:, CHUNK - 1 : CHUNK] - fade)

    several = min(HEADS_AT_ONCE, heads)

    def leaving(held, out, group, kind):
        here = pl.ds(group * several, several)
        return pltpu.make_async_copy(held.at[here], out.at[here], sem.at[kind, group])

    for at in range(0, heads, several):
        group = (step * heads + at) // several
        own = [(pack, c, head) for pack, (c, head) in enumerate(packs) if at <= head < at + several]
        for pack, chunk, head in own:
            solved_ref[step * heads + head, part_of(chunk - 1), : DV + DK] = solved[pack].astype(BF16)
        leaving(solved_ref, solved_hbm, group, 0).start()
        for pack, chunk, head in own:
            moves_ref[step * heads + head, chunk - 1] = mul(
                turned[chunk, head // repeat_by] * tail[pack : pack + 1, :], solved[pack]
            ).astype(BF16)
        leaving(moves_ref, moves_hbm, group, 1).start()

    @pl.when(step == pl.num_programs(0) - 1)
    def _():
        for group in range(sem.shape[1]):
            leaving(solved_ref, solved_hbm, group, 0).wait()
            leaving(moves_ref, moves_hbm, group, 1).wait()


def states_kernel(
    key_ref, value_hbm, before_ref, key_taps, value_taps, beta_ref, decay_ref, moves_hbm,
    pairs_hbm, solved_hbm, starts_hbm,
    key_padded, value_padded, value_ref, moves_ref, solved_ref, starts_ref, pairs_ref,
    value_sem, in_sem, out_sem, pairs_sem,
):
    heads, length = decay_ref.shape
    chunks = length // CHUNK
    key_heads = key_ref.shape[1] // DK
    repeat_by = heads // key_heads
    value_copy = pltpu.make_async_copy(value_hbm.at[pl.ds(0, CHUNK)], value_ref, value_sem)
    value_copy.start()
    incoming = pltpu.make_async_copy(moves_hbm, moves_ref, in_sem)

    key_at = before_ref.shape[1] - key_ref.shape[1]
    widen(key_padded, 5, 3, before_ref[:, key_at:])
    widen(key_padded, 8, CHUNK, key_ref[:CHUNK, :])
    key, turned = [], []
    for j in range(key_heads):
        key.append(unit_rows(conv_silu(key_padded, 5, CHUNK, key_taps, j)))
        for head in range(j * repeat_by, (j + 1) * repeat_by):
            solved_ref[head, :, DV + DK :] = key[j].astype(BF16)
        turned.append(key[j].T)
    fade = log_fades(chunk_rows(decay_ref, heads, range(chunks)))
    value = {}

    def value_rows():
        value_copy.wait()
        incoming.start()
        widen(value_padded, 5, 3, before_ref[:, : value_ref.shape[1]])
        widen(value_padded, 8, CHUNK, value_ref[...])

    def make_value(head):
        value[head] = conv_silu(value_padded, 5, CHUNK, value_taps, head)

    solved = solved_packs(
        fade[:heads],
        beta_ref[:, :CHUNK],
        [key[head // repeat_by] for head in range(heads)],
        [turned[head // repeat_by] for head in range(heads)],
        [value_rows] + [functools.partial(make_value, head) for head in range(heads)],
        lambda head: value[head],
    )
    last = jnp.exp(fade[:, CHUNK - 1 : CHUNK])
    tail = jnp.exp(fade[:, CHUNK - 1 : CHUNK] - fade)
    rows, cols = square_iotas()
    identity = jnp.where(rows == cols, 1.0, 0.0)

    state = []
    for head in range(heads):
        one = solved[head].astype(BF16)
        solved_ref[head, :, : DV + DK] = one
        moved = mul(turned[head // repeat_by] * tail[head : head + 1, :], one)
        state.append(
            jnp.concatenate([moved[:, :DV], last[head : head + 1, :] * identity - moved[:, DV:]], 1)
        )
    each = min(HEADS_AT_ONCE, heads)
    outgoing = [pltpu.make_async_copy(solved_ref, solved_hbm, out_sem.at[0])]
    outgoing[0].start()
    incoming.wait()
    for chunk in range(1, chunks):
        for head in range(heads):
            pack = chunk * heads + head
            start = state[head].astype(BF16)
            starts_ref[chunk - 1, head] = start
            moves = moves_ref[head, chunk - 1]
            moved = last[pack : pack + 1, :] * state[head] - mul(moves[:, DV:], start)
            state[head] = jnp.concatenate([moved[:, :DV] + moves[:, :DV].astype(F32), moved[:, DV:]], 1)
            if chunk == chunks - 1:
                pairs_ref[head] = state[head].astype(BF16)
                if (head + 1) % each == 0:
                    done = pl.ds(head + 1 - each, each)
                    outgoing.append(
                        pltpu.make_async_copy(
                            pairs_ref.at[done], pairs_hbm.at[done], pairs_sem.at[head // each]
                        )
                    )
                    outgoing[-1].start()
        outgoing.append(
            pltpu.make_async_copy(
                starts_ref.at[chunk - 1], starts_hbm.at[chunk - 1], out_sem.at[chunk]
            )
        )
        outgoing[-1].start()
    for copy in outgoing:
        copy.wait()


def local_kernel(
    query_ref, query_before, query_taps, decay_ref,
    first_solved, later_solved, starts_ref, gate_ref, gain_ref,
    ahead_ref, parts_ref, padded,
):
    step = pl.program_id(0)
    length, width = query_ref.shape
    chunks = length // CHUNK
    key_heads = width // DK
    heads = first_solved.shape[0]
    repeat_by = heads // key_heads

    rows, cols = square_iotas()
    within = rows >= cols
    fade = log_fades(chunk_rows(decay_ref, heads, range(chunks)))
    columns = as_columns((fade,))
    widen(padded, 5, 3, query_before[...])
    widen(padded, 8, length, query_ref[...])
    query = [conv_silu(padded, 5, length, query_taps, j).astype(BF16) for j in range(key_heads)]
    for head in range(heads):
        gate = gate_ref[:, head_of(head)].astype(F32)
        parts_ref[heads + head // 2, :, head_of(head % 2)] = (
            gate * sigmoid(gate) * gain_ref[...]
        ).astype(BF16)
    for chunk in range(chunks):
        part = part_of(chunk)
        for j in range(key_heads):
            own = query[j][part]
            if chunk == 0:
                unit = first_solved[j * repeat_by, :, DV + DK :]
            else:
                unit = later_solved[j * repeat_by, part_of(chunk - 1), DV + DK :]
            inner = lax.dot_general(
                own, unit, (((1,), (1,)), ((), ())), preferred_element_type=F32
            )
            for head in range(j * repeat_by, (j + 1) * repeat_by):
                pack = chunk * heads + head
                column = jnp.broadcast_to(columns[:, pack : pack + 1], (CHUNK, CHUNK))
                scores = inner * jnp.exp(jnp.where(within, column - fade[pack : pack + 1, :], -1e30))
                grown = jnp.exp(column)
                if chunk == 0:
                    updates, wide = first_solved[head, :, :DV], first_solved[head, :, DV : DV + DK]
                    fresh = jnp.concatenate([updates, -wide], 1)
                    carried = jnp.concatenate(
                        [jnp.zeros((CHUNK, DV), F32), grown * own.astype(F32)], 1
                    )
                else:
                    solved = later_solved[head, part_of(chunk - 1), : DV + DK]
                    both = mul(jnp.concatenate([solved[:, DV:], own], 0), starts_ref[chunk - 1, head])
                    taken = both[:CHUNK]
                    fresh = jnp.concatenate(
                        [solved[:, :DV].astype(F32) - taken[:, :DV], -taken[:, DV:]], 1
                    )
                    carried = jnp.concatenate(
                        [grown * both[CHUNK:, :DV], grown * both[CHUNK:, DV:]], 1
                    )
                parts_ref[head, part, :] = (carried + mul(scores, fresh)).astype(BF16)

    @pl.when(step == 0)
    def _():
        ahead_ref[...] = parts_ref[...]


def columns_of(rows, width, first=0):
    return pl.BlockSpec((rows, width), lambda step: (0, step + first))


def in_vmem(mib):
    return pltpu.CompilerParams(vmem_limit_bytes=mib * 1024 * 1024)


def local_steps(raws, before, taps, beta_logit, decay_logit, gate_raw, norm_gain):
    length = raws[0].shape[0]
    key_heads = raws[0].shape[1] // DK
    value_heads = raws[2].shape[1] // DV
    repeat_by = value_heads // key_heads
    chunks = length // CHUNK
    beta, decay = beta_logit.T, decay_logit.T
    work = CHUNK * length * DV * value_heads
    hbm = pl.BlockSpec(memory_space=pltpu.HBM)
    vmem = pl.BlockSpec(memory_space=pltpu.VMEM)

    def split(each):
        heads = each * repeat_by
        held = max(heads, math.gcd(8, value_heads))
        of_heads = lambda *shape: pl.BlockSpec((heads,) + shape, lambda step: (step,) + (0,) * len(shape))
        logits = pl.BlockSpec((held, length), lambda step: (step * heads // held, 0))
        return key_heads // each, each * DK, heads * DV, of_heads, logits

    each = math.gcd(8, key_heads)
    steps, narrow, wide, of_heads, logits = split(each)
    later = length - CHUNK
    solved, moves = pl.pallas_call(
        later_kernel,
        grid=(steps,),
        in_specs=[
            vmem, vmem, vmem, vmem, vmem, vmem,
        ],
        out_specs=[hbm, hbm],
        out_shape=[
            jax.ShapeDtypeStruct((value_heads, later, DV + 2 * DK), BF16),
            jax.ShapeDtypeStruct((value_heads, chunks - 1, DK, DV + DK), BF16),
        ],
        scratch_shapes=[
            pltpu.VMEM((each, later + 16, DK), F32),
            pltpu.VMEM((each * repeat_by, later + 16, DV), F32),
            pltpu.VMEM((value_heads, later, DV + 2 * DK), BF16),
            pltpu.VMEM((value_heads, chunks - 1, DK, DV + DK), BF16),
            pltpu.SemaphoreType.DMA((2, value_heads // min(HEADS_AT_ONCE, wide // DV))),
        ],
        compiler_params=in_vmem(50),
        cost_estimate=pl.CostEstimate(flops=30 * work, bytes_accessed=0, transcendentals=0),
        name="later",
    )(raws[1], raws[2], taps[1], taps[2], beta, decay)

    narrow, wide = key_heads * DK, value_heads * DV
    whole = lambda shape, *at: pl.BlockSpec(shape, lambda step: at or (0,) * len(shape))
    pairs, first_solved, starts = pl.pallas_call(
        states_kernel,
        grid=(1,),
        in_specs=[
            vmem, hbm, vmem, vmem, vmem, vmem, vmem, hbm,
        ],
        out_specs=[hbm, hbm, hbm],
        out_shape=[
            jax.ShapeDtypeStruct((value_heads, DK, DV + DK), BF16),
            jax.ShapeDtypeStruct((value_heads, CHUNK, DV + 2 * DK), BF16),
            jax.ShapeDtypeStruct((chunks - 1, value_heads, DK, DV + DK), BF16),
        ],
        scratch_shapes=[
            pltpu.VMEM((key_heads, 8 + CHUNK, DK), F32),
            pltpu.VMEM((value_heads, 8 + CHUNK, DV), F32),
            pltpu.VMEM((CHUNK, wide), BF16),
            pltpu.VMEM(moves.shape, BF16),
            pltpu.VMEM((value_heads, CHUNK, DV + 2 * DK), BF16),
            pltpu.VMEM((chunks - 1, value_heads, DK, DV + DK), BF16),
            pltpu.VMEM((value_heads, DK, DV + DK), BF16),
            pltpu.SemaphoreType.DMA,
            pltpu.SemaphoreType.DMA,
            pltpu.SemaphoreType.DMA((chunks,)),
            pltpu.SemaphoreType.DMA((value_heads // min(HEADS_AT_ONCE, value_heads),)),
        ],
        compiler_params=in_vmem(52),
        cost_estimate=pl.CostEstimate(flops=20 * work, bytes_accessed=0, transcendentals=0),
        name="states",
    )(raws[1], raws[2], before, taps[1], taps[2], beta, decay, moves)
    gain = norm_gain.reshape(1, DV)

    def local():
        steps, narrow, wide, of_heads, logits = split(math.gcd(2, key_heads))
        heads = wide // DV
        ahead = (heads + heads // 2, length, DV + DK)
        return pl.pallas_call(
            local_kernel,
            grid=(steps,),
            in_specs=[
                columns_of(length, narrow), columns_of(3, narrow, repeat_by * steps), columns_of(4, narrow),
                logits, of_heads(CHUNK, DV + 2 * DK), of_heads(later, DV + 2 * DK),
                pl.BlockSpec((chunks - 1, heads, DK, DV + DK), lambda step: (0, step, 0, 0)),
                columns_of(length, wide), whole(gain.shape),
            ],
            out_specs=[
                whole(ahead),
                pl.BlockSpec(ahead, lambda step: (jnp.maximum(step - 1, 0), 0, 0)),
            ],
            out_shape=[
                jax.ShapeDtypeStruct(ahead, BF16),
                jax.ShapeDtypeStruct((max(steps - 1, 1) * ahead[0],) + ahead[1:], BF16),
            ],
            scratch_shapes=[pltpu.VMEM((narrow // DK, 8 + length, DK), F32)],
            compiler_params=in_vmem(60),
            cost_estimate=pl.CostEstimate(flops=12 * work, bytes_accessed=0, transcendentals=0),
            name="local",
        )(
            raws[0], before, taps[0], decay, first_solved, solved, starts, gate_raw, gain,
        )

    return pairs, local


def prefix_kernel(pairs_ref, prefix_ref, total_ref):
    count, heads = pairs_ref.shape[:2]
    running = [None] * heads
    for hop in range(count):
        for head in range(heads):
            now = pairs_ref[hop, head]
            if hop == 0:
                rows = lax.broadcasted_iota(jnp.int32, (DK, DV + DK), 0)
                cols = lax.broadcasted_iota(jnp.int32, (DK, DV + DK), 1)
                prefix_ref[hop, head] = jnp.where(cols == rows + DV, 1.0, 0.0).astype(BF16)
                running[head] = now.astype(F32)
            else:
                before = running[head].astype(BF16)
                prefix_ref[hop, head] = before
                own = jnp.concatenate([now[:, :DV].astype(F32), jnp.zeros((DK, DK), F32)], 1)
                running[head] = own + mul(now[:, DV:], before)
    for head in range(heads):
        total_ref[head] = running[head][:, : total_ref.shape[2]].astype(BF16)


def apply_kernel(prefix_ref, start_ref, starts_ref):
    count, heads = prefix_ref.shape[:2]
    for hop in range(count):
        for head in range(heads):
            starts_ref[hop, head] = (
                prefix_ref[hop, head, :, :DV].astype(F32)
                + mul(prefix_ref[hop, head, :, DV:], start_ref[head])
            ).astype(BF16)


def shifted(value, axis, by):
    count = lax.axis_size(axis)
    return lax.ppermute(value, axis, [(i, i + by) for i in range(count - by)])


def group_start(total, axis, group):
    groups = lax.axis_size(axis) // group
    running = shifted(total, axis, group)
    by = 1
    while by < groups - 1:
        earlier = shifted(running, axis, by * group)
        product = jnp.einsum("bkl,blv->bkv", running[..., DV:], earlier, preferred_element_type=F32)
        own = jnp.pad(running[..., :DV], ((0, 0), (0, 0), (0, DK)))
        running = (product + own.astype(F32)).astype(BF16)
        by *= 2
    return running[..., :DV]


def starts_of(pairs, axis, beside):
    size = lax.axis_size(axis)
    heads = pairs.shape[0]
    group = math.gcd(math.gcd(size, heads), GROUP)
    groups = [[g * group + i for i in range(group)] for g in range(size // group)]
    each = heads // group
    wide = DV if size // group == 2 else DV + DK
    by_head = lax.all_to_all(pairs, axis, 0, 0, axis_index_groups=groups, tiled=True)
    by_head, done = lax.optimization_barrier((by_head, beside()))
    prefix, total = pl.pallas_call(
        prefix_kernel,
        out_shape=[
            jax.ShapeDtypeStruct((group, each, DK, DV + DK), BF16),
            jax.ShapeDtypeStruct((each, DK, wide), BF16),
        ],
        compiler_params=in_vmem(16),
        name="prefix",
    )(by_head.reshape(group, each, DK, DV + DK))
    starts = pl.pallas_call(
        apply_kernel,
        out_shape=jax.ShapeDtypeStruct((group, each, DK, DV), BF16),
        compiler_params=in_vmem(16),
        name="apply",
    )(prefix, group_start(total, axis, group))
    starts = lax.all_to_all(
        starts.reshape(heads, DK, DV), axis, 0, 0, axis_index_groups=groups, tiled=True
    )
    return starts, done


def project_kernel(
    place_ref, starts_ref, ahead_ref, parts_hbm, weight_hbm, away_ref, own_ref,
    parts_ref, weight_ref, total, parts_sem, weight_sem,
):
    heads = starts_ref.shape[0]
    entries, length = ahead_ref.shape[:2]
    each = entries * 2 // 3
    width = weight_ref.shape[1]
    block = min(512, width)
    groups = heads // each

    def parts(g):
        here = pl.ds((g - 1) * entries, entries)
        return pltpu.make_async_copy(parts_hbm.at[here], parts_ref.at[here], parts_sem.at[g])

    def weights(g):
        rows = pl.ds(g * each * DV, each * DV)
        return pltpu.make_async_copy(weight_hbm.at[rows], weight_ref.at[rows], weight_sem.at[g])

    def normed_group(g):
        normed = []
        for head in range(g * each, (g + 1) * each):
            held, at = (ahead_ref, head) if g == 0 else (parts_ref, (g - 1) * entries + head - g * each)
            core = held[at, :, :DV].astype(F32) + mul(held[at, :, DV:], starts_ref[head])
            scale = lax.rsqrt(jnp.mean(core * core, -1, keepdims=True) + EPSILON)
            gated = held[at - head % each + each + head % each // 2, :, head_of(head % 2)]
            normed.append((core * scale * gated.astype(F32)).astype(BF16))
        return jnp.concatenate(normed, 1)

    weights(0).start()
    if groups > 1:
        parts(1).start()
    following = normed_group(0)
    if groups > 1:
        weights(1).start()
    if groups > 2:
        parts(2).start()
    for g in range(groups):
        weights(g).wait()
        if g + 2 < groups:
            weights(g + 2).start()
        normed = following
        for at in range(0, width, block):
            if g + 1 < groups and at == (width // block // 2 * block if g == 0 else 0):
                parts(g + 1).wait()
                if g + 3 < groups:
                    parts(g + 3).start()
                following = normed_group(g + 1)
            added = jnp.dot(
                normed, weight_ref[g * each * DV : (g + 1) * each * DV, at : at + block],
                preferred_element_type=F32,
            )
            if g > 0:
                added = added + total[:, at : at + block]
            if g < groups - 1:
                total[:, at : at + block] = added
            elif own_ref is None:
                away_ref[:, at : at + block] = added.astype(BF16)
            else:
                first = place_ref[0] == 0
                low, high = added[: length // 2], added[length // 2 :]
                own_ref[:, at : at + block] = jnp.where(first, low, high).astype(BF16)
                away_ref[:, at : at + block] = jnp.where(first, high, low).astype(BF16)


def whole_kernel(place_ref, starts_ref, ahead_ref, parts_hbm, weight_hbm, out_ref, *scratch):
    project_kernel(place_ref, starts_ref, ahead_ref, parts_hbm, weight_hbm, out_ref, None, *scratch)


def projected(ahead, parts, starts, out_weight, axis):
    length = parts.shape[1]
    width = out_weight.shape[1]
    halves = lax.axis_size(axis) == 2
    vmem = pl.BlockSpec(memory_space=pltpu.VMEM)
    hbm = pl.BlockSpec(memory_space=pltpu.HBM)
    heads = starts.shape[0]
    groups = heads // (ahead.shape[0] * 2 // 3)
    here = lax.axis_index(axis).astype(jnp.int32).reshape(1)
    out = jax.ShapeDtypeStruct((length // 2 if halves else length, width), BF16)
    partial = pl.pallas_call(
        project_kernel if halves else whole_kernel,
        in_specs=[pl.BlockSpec(memory_space=pltpu.SMEM), vmem, vmem, hbm, hbm],
        out_specs=[vmem, vmem] if halves else vmem,
        out_shape=[out, out] if halves else out,
        scratch_shapes=[
            pltpu.VMEM(parts.shape, BF16),
            pltpu.VMEM(out_weight.shape, BF16),
            pltpu.VMEM((length, width), F32),
            pltpu.SemaphoreType.DMA((groups,)),
            pltpu.SemaphoreType.DMA((groups,)),
        ],
        compiler_params=in_vmem(50),
        name="project",
    )(here, starts, ahead, parts, out_weight)
    if not halves:
        return lax.psum_scatter(partial, axis, scatter_dimension=0, tiled=True)
    away, own = partial
    other = lax.ppermute(away, axis, [(0, 1), (1, 0)])
    return (own.astype(F32) + other.astype(F32)).astype(BF16)


def tails_kernel(value_hbm, query_hbm, key_hbm, out_ref, value_ref, query_ref, key_ref, sem):
    pairs = ((value_hbm, value_ref), (query_hbm, query_ref), (key_hbm, key_ref))
    copies = [
        pltpu.make_async_copy(source.at[pl.ds(source.shape[0] - 16, 16)], held, sem.at[i])
        for i, (source, held) in enumerate(pairs)
    ]
    for copy in copies:
        copy.start()
    at = 0
    for copy, (_, held) in zip(copies, pairs):
        copy.wait()
        width = held.shape[1]
        out_ref[:, at : at + width] = held[...].astype(F32)[13:16].astype(BF16)
        at += width


def tails(raws):
    order = (raws[2], raws[0], raws[1])
    width = sum(raw.shape[1] for raw in order)
    return pl.pallas_call(
        tails_kernel,
        in_specs=[pl.BlockSpec(memory_space=pltpu.HBM)] * 3,
        out_shape=jax.ShapeDtypeStruct((3, width), BF16),
        scratch_shapes=[pltpu.VMEM((16, raw.shape[1]), BF16) for raw in order]
        + [pltpu.SemaphoreType.DMA((3,))],
        compiler_params=in_vmem(60),
        name="tails",
    )(*order)


def shards(
    query_raw, key_raw, value_raw, gate_raw, query_taps, key_taps, value_taps,
    beta_logit, decay_logit, norm_gain, out_weight,
):
    raws = (query_raw, key_raw, value_raw)
    before = shifted(tails(raws), "seq", 1)
    pairs, local = local_steps(
        raws, before, (query_taps, key_taps, value_taps), beta_logit, decay_logit, gate_raw, norm_gain
    )
    starts, (ahead, parts) = starts_of(pairs, "seq", local)
    return projected(ahead, parts, starts, out_weight, "head")


def solution(mesh):
    placed = (
        P("seq", "head"), P("seq", "head"), P("seq", "head"), P("seq", "head"),
        P(None, "head"), P(None, "head"), P(None, "head"),
        P("seq", "head"), P("seq", "head"), P(), P("head", None),
    )
    return jax.shard_map(
        shards, mesh=mesh, in_specs=placed, out_specs=P(("seq", "head"), None), check_vma=False
    )
```
